32 devices in a mesh: dp: 8 (over z, y), rows: 4 (over x, core).
Axes of the slice: x: 2, y: 2, z: 4, core: 2. Of those that a mesh axis runs over, the one named last changes fastest.
Arguments:
- views: bfloat16 [32, 2, 8, 8, 2048], P('dp', None, 'rows'), may hold values from -12 to 12
- crops: bfloat16 [32, 4, 4, 4, 2048], P('dp', None, 'rows'), may hold values from -12 to 12
- w_reduce: bfloat16 [2048, 512], P('dp'), may hold values from -0.125 to 0.125
- gain_one: bfloat16 [512], P('dp'), may hold values from 0.5 to 1.5
- shift_one: bfloat16 [512], P('dp'), may hold values from -2.5 to 2.5
- w_spatial: bfloat16 [3, 3, 512, 512], P(None, None, 'dp'), may hold values from -0.09375 to 0.09375
- gain_two: bfloat16 [512], P('dp'), may hold values from 0.5 to 1.5
- shift_two: bfloat16 [512], P('dp'), may hold values from -2.5 to 2.5
- w_expand: bfloat16 [512, 2048], P('dp'), may hold values from -0.25 to 0.25
- gain_three: bfloat16 [2048], P('dp'), may hold values from 0.5 to 1.5
- shift_three: bfloat16 [2048], P('dp'), may hold values from -2.5 to 2.5
- cot_views: bfloat16 [32, 2, 8, 8, 2048], P('dp', None, 'rows'), may hold values from -6 to 6
- cot_crops: bfloat16 [32, 4, 4, 4, 2048], P('dp', None, 'rows'), may hold values from -6 to 6
Outputs:
- out_views: bfloat16 [32, 2, 8, 8, 2048], P('dp', None, 'rows')
- out_crops: bfloat16 [32, 4, 4, 4, 2048], P('dp', None, 'rows')
- pooled: float32 [32, 6, 2048], P('dp')
- grad_views: bfloat16 [32, 2, 8, 8, 2048], P('dp', None, 'rows')
- grad_crops: bfloat16 [32, 4, 4, 4, 2048], P('dp', None, 'rows')
- grad_reduce: float32 [2048, 512], P('dp')
- grad_gain_one: float32 [512], P('dp')
- grad_shift_one: float32 [512], P('dp')
- grad_spatial: float32 [3, 3, 512, 512], P(None, None, 'dp')
- grad_gain_two: float32 [512], P('dp')
- grad_shift_two: float32 [512], P('dp')
- grad_expand: float32 [512, 2048], P('dp')
- grad_gain_three: float32 [2048], P('dp')
- grad_shift_three: float32 [2048], P('dp')
The draws below stay inside these ranges and needn't reach their ends.
All inputs are finite; a program needn't handle non-finite values.
Results may differ from the reference program's by a relative error of at most 0.0085.
Values may be sent and summed in bfloat16 or wider, within the bound.
A program may use at most 128 MiB of HBM per device.

```python
import math
import jax
import jax.numpy as jnp
from jax import lax

C = 2048
M = 512
IMG_DEV = 4
VIEWS = 2
CROPS = 4
VSIDE = 8
CSIDE = 4
IMAGES = 32
N_DP = 8


def scaled_field(key, base, side):
    key_pixel, key_channel = jax.random.split(key)
    shape = base.shape
    row_pos = lax.broadcasted_iota(jnp.float32, shape, 2)
    ramp = 0.6 * jnp.power(3.0, row_pos / (side - 1.0))
    pixel_scale = jnp.exp(jax.random.uniform(key_pixel, shape[:-1] + (1,), jnp.float32, math.log(0.6), math.log(1.6)))
    channel_scale = jnp.exp(jax.random.uniform(key_channel, (shape[-1],), jnp.float32, math.log(0.5), math.log(2.0)))
    return jnp.clip(base * ramp * pixel_scale * channel_scale, -12.0, 12.0).astype(jnp.bfloat16)


def draw_views(key, part):
    key = jax.random.fold_in(key, 11)
    key_base, key_scale = jax.random.split(key, 2)
    shape = (IMAGES, VIEWS, VSIDE, VSIDE, C)
    base = jnp.clip(jax.random.normal(key_base, shape, jnp.float32), -3.0, 3.0)
    return scaled_field(key_scale, base, VSIDE)


def draw_crops(key, part):
    key = jax.random.fold_in(key, 23)
    key_base, key_scale = jax.random.split(key, 2)
    shape = (IMAGES, CROPS, CSIDE, CSIDE, C)
    base = jnp.clip(jax.random.normal(key_base, shape, jnp.float32), -3.0, 3.0)
    return scaled_field(key_scale, base, CSIDE)


def block_scale(own_key, dims, cuts, low, high):
    level = 1.0
    for dim, shards_of in cuts:
        steps = jax.random.uniform(jax.random.fold_in(jax.random.fold_in(own_key, 6), dim), (shards_of,), jnp.float32, low / len(cuts), high / len(cuts))
        level = level * jnp.repeat(jnp.exp(steps), dims[dim] // shards_of).reshape((-1,) + (1,) * (len(dims) - 1 - dim))
    return level


def gaussian(key, extent, spread, reach, cuts=(), held_as=jnp.bfloat16):
    factor_of = block_scale(key, extent, cuts, -0.22, 0.18) if cuts else 1.0
    values = jax.random.normal(key, extent, jnp.float32) * spread * factor_of
    return jnp.minimum(jnp.maximum(values, -reach), reach).astype(held_as)


def setup_inputs(seed: int = 0) -> dict:
    keys = jax.random.split(jax.random.key(seed), 14)
    views = draw_views(jax.random.fold_in(keys[13], 71), 0)
    crops = draw_crops(jax.random.fold_in(keys[13], 71), 0)
    w_reduce = gaussian(keys[2], (C, M), C ** -0.5, 0.125, ((0, 8),))
    gain_one = jnp.clip(1.0 + 0.1 * jax.random.normal(keys[3], (M,), jnp.float32), 0.5, 1.5).astype(jnp.bfloat16)
    shift_one = gaussian(keys[4], (M,), 0.5, 2.5, ((0, 8),))
    w_spatial = gaussian(keys[5], (3, 3, M, M), (9 * M) ** -0.5, 0.09375, ((2, 8),))
    gain_two = jnp.clip(1.0 + 0.1 * jax.random.normal(keys[6], (M,), jnp.float32), 0.5, 1.5).astype(jnp.bfloat16)
    shift_two = gaussian(keys[7], (M,), 0.5, 2.5, ((0, 8),))
    w_expand = gaussian(keys[8], (M, C), M ** -0.5, 0.25, ((0, 8),))
    gain_three = jnp.clip(1.0 + 0.1 * jax.random.normal(keys[9], (C,), jnp.float32), 0.5, 1.5).astype(jnp.bfloat16)
    shift_three = gaussian(keys[10], (C,), 0.5, 2.5, ((0, 8),))
    cot_views = gaussian(keys[11], (IMAGES, VIEWS, VSIDE, VSIDE, C), 1.0, 6.0, ((0, 8), (2, 4)))
    cot_crops = gaussian(keys[12], (IMAGES, CROPS, CSIDE, CSIDE, C), 1.0, 6.0, ((0, 8), (2, 4)))
    return {"views": views, "crops": crops, "w_reduce": w_reduce, "gain_one": gain_one, "shift_one": shift_one, "w_spatial": w_spatial, "gain_two": gain_two, "shift_two": shift_two, "w_expand": w_expand, "gain_three": gain_three, "shift_three": shift_three, "cot_views": cot_views, "cot_crops": cot_crops}


EPSILON = 1e-05
HIGHEST = lax.Precision.HIGHEST

@jax.custom_vjp
def low(v):
    return lax.optimization_barrier(v.astype(jnp.bfloat16)).astype(jnp.float32)

@jax.custom_vjp
def low_back(v):
    return v

def low_keep(v):
    return (low(v), None)

def low_pass(kept, grad):
    return (grad,)

def back_keep(v):
    return (v, None)

def back_low(kept, grad):
    return (low(grad),)
low.defvjp(low_keep, low_pass)
low_back.defvjp(back_keep, back_low)

def normalize(values, gain_vec, shift_vec):
    channel_mean = lax.optimization_barrier(jnp.mean(values, axis=(0, 1, 2)))
    second = lax.optimization_barrier(jnp.mean(values * values, axis=(0, 1, 2)))
    return gain_vec * (values - channel_mean) * lax.rsqrt(second - channel_mean * channel_mean + EPSILON) + shift_vec

def block_map(map_batch, weight_reduce, gain_first, shift_first, weight_spatial, gain_second, shift_second, weight_expand, gain_third, shift_third):
    reduced = low_back(jnp.einsum('nhwc,cd->nhwd', map_batch, weight_reduce, precision=HIGHEST))
    first_act = low(jax.nn.silu(normalize(reduced, gain_first, shift_first)))
    spatial = low_back(lax.conv_general_dilated(first_act, weight_spatial, (1, 1), 'SAME', dimension_numbers=('NHWC', 'HWIO', 'NHWC'), precision=HIGHEST))
    second_act = low(jax.nn.silu(normalize(spatial, gain_second, shift_second)))
    expanded = low_back(jnp.einsum('nhwd,dc->nhwc', second_act, weight_expand, precision=HIGHEST))
    return jax.nn.silu(map_batch + normalize(expanded, gain_third, shift_third))

def reference(views, crops, w_reduce, gain_one, shift_one, w_spatial, gain_two, shift_two, w_expand, gain_three, shift_three, cot_views, cot_crops):
    params = tuple((param.astype(jnp.float32) for param in (w_reduce, gain_one, shift_one, w_spatial, gain_two, shift_two, w_expand, gain_three, shift_three)))

    def forward(view_maps, crop_maps, p_a, p_b, p_c, p_d, p_e, p_f, p_g, p_h, p_i):
        return (block_map(view_maps, p_a, p_b, p_c, p_d, p_e, p_f, p_g, p_h, p_i), block_map(crop_maps, p_a, p_b, p_c, p_d, p_e, p_f, p_g, p_h, p_i))

    def replica(totals, pieces):
        view_block, crop_block, view_cot, crop_cot = pieces
        outputs, pullback = jax.vjp(forward, view_block.astype(jnp.float32), crop_block.astype(jnp.float32), params[0], params[1], params[2], params[3], params[4], params[5], params[6], params[7], params[8])
        gradients = pullback((view_cot.astype(jnp.float32), crop_cot.astype(jnp.float32)))
        new_totals = tuple((total + grad for total, grad in zip(totals, gradients[2:])))
        pooled_block = jnp.concatenate([lax.optimization_barrier(jnp.mean(outputs[0], axis=(1, 2))).reshape(IMG_DEV, VIEWS, C), lax.optimization_barrier(jnp.mean(outputs[1], axis=(1, 2))).reshape(IMG_DEV, CROPS, C)], axis=1)
        return (new_totals, (outputs[0].astype(jnp.bfloat16), outputs[1].astype(jnp.bfloat16), pooled_block, gradients[0].astype(jnp.bfloat16), gradients[1].astype(jnp.bfloat16)))
    zero_grads = tuple((jnp.zeros(param.shape, jnp.float32) for param in params))
    blocks = (views.reshape(N_DP, IMG_DEV * VIEWS, VSIDE, VSIDE, C), crops.reshape(N_DP, IMG_DEV * CROPS, CSIDE, CSIDE, C), cot_views.reshape(N_DP, IMG_DEV * VIEWS, VSIDE, VSIDE, C), cot_crops.reshape(N_DP, IMG_DEV * CROPS, CSIDE, CSIDE, C))
    totals, stacked = lax.scan(replica, zero_grads, blocks)
    return (stacked[0].reshape(views.shape), stacked[1].reshape(crops.shape), stacked[2].reshape(IMAGES, VIEWS + CROPS, C), stacked[3].reshape(views.shape), stacked[4].reshape(crops.shape), totals[0], totals[1], totals[2], totals[3], totals[4], totals[5], totals[6], totals[7], totals[8])
```

```python
import functools

import jax
import jax.numpy as jnp
from jax import lax
from jax.experimental import pallas as pl
from jax.experimental.pallas import tpu as pltpu
from jax.sharding import PartitionSpec as P

EPSILON = 1e-05


def extended(cells, sides, width):
    for axis, dim in sides:
        count = lax.axis_size(axis)
        ends = count - 1
        head = lax.slice_in_dim(cells, 0, width, axis=dim)
        tail = lax.slice_in_dim(cells, cells.shape[dim] - width, cells.shape[dim], axis=dim)
        cells = jnp.concatenate(
            [
                lax.ppermute(tail, axis, [(i, (i + 1) % count) for i in range(ends)]),
                cells,
                lax.ppermute(head, axis, [((i + 1) % count, i) for i in range(ends)]),
            ],
            axis=dim,
        )
    return cells


def silu_slope(values):
    sigmoid_val = jax.nn.sigmoid(values)
    return sigmoid_val * (1.0 + values * (1.0 - sigmoid_val))


def standardize(reduced_pair, gain_vec, shift_vec):
    left_map = reduced_pair[0]
    right_map = reduced_pair[1]
    totals = lax.psum(
        (
            jnp.sum(left_map, 0),
            jnp.sum(left_map * left_map, 0),
            jnp.sum(right_map, 0),
            jnp.sum(right_map * right_map, 0),
        ),
        "rows",
    )
    results = []
    for member in range(2):
        values = reduced_pair[member]
        pixel_count = values.shape[0] * lax.axis_size("rows")
        channel_mean = totals[2 * member] / pixel_count
        inverse_scale = lax.rsqrt(
            totals[2 * member + 1] / pixel_count - channel_mean * channel_mean + EPSILON
        )
        centred = (values - channel_mean) * inverse_scale
        results.append((centred, inverse_scale, gain_vec * centred + shift_vec))
    return results


def unstandardize(slopes, saved, gain_vec):
    shift_left = jnp.sum(slopes[0], 0)
    gain_left = jnp.sum(slopes[0] * saved[0][0], 0)
    shift_right = jnp.sum(slopes[1], 0)
    gain_right = jnp.sum(slopes[1] * saved[1][0], 0)
    totals = lax.psum((shift_left, gain_left, shift_right, gain_right), "rows")
    results = []
    for member in range(2):
        pixel_count = slopes[member].shape[0] * lax.axis_size("rows")
        centred = saved[member][0]
        inverse_scale = saved[member][1]
        mean_slope = gain_vec * totals[2 * member] / pixel_count
        mean_cross = gain_vec * totals[2 * member + 1] / pixel_count
        results.append(
            inverse_scale * (gain_vec * slopes[member] - mean_slope - centred * mean_cross)
        )
    return (results, gain_left + gain_right, shift_left + shift_right)


def spread_rows(activity):
    return extended(activity, (("rows", 1),), 1)


def spread_grads(slopes):
    return extended(slopes, (("rows", 1),), 1)


def patches(padded, row_count, col_count, flipped):
    widened = jnp.pad(padded, ((0, 0), (0, 0), (1, 1), (0, 0)))
    tap_list = []
    for row_tap in range(3):
        for col_tap in range(3):
            row_start = 2 - row_tap if flipped else row_tap
            col_start = 2 - col_tap if flipped else col_tap
            tap_list.append(
                widened[:, row_start : row_start + row_count, col_start : col_start + col_count, :]
            )
    return jnp.concatenate(tap_list, axis=-1).reshape(-1, 9 * widened.shape[-1])


def body(
    views,
    crops,
    w_reduce,
    gain_one,
    shift_one,
    w_spatial,
    gain_two,
    shift_two,
    w_expand,
    gain_three,
    shift_three,
    cot_views,
    cot_crops,
):
    gathered = (
        lax.all_gather(w_reduce, "dp", axis=0, tiled=True),
        lax.all_gather(gain_one, "dp", axis=0, tiled=True),
        lax.all_gather(shift_one, "dp", axis=0, tiled=True),
        lax.all_gather(w_spatial, "dp", axis=2, tiled=True),
        lax.all_gather(gain_two, "dp", axis=0, tiled=True),
        lax.all_gather(shift_two, "dp", axis=0, tiled=True),
        lax.all_gather(w_expand, "dp", axis=0, tiled=True),
        lax.all_gather(gain_three, "dp", axis=0, tiled=True),
        lax.all_gather(shift_three, "dp", axis=0, tiled=True),
    )
    weight_reduce = gathered[0]
    weight_spatial = gathered[3]
    weight_expand = gathered[6]
    gain_first = gathered[1].astype(jnp.float32)
    shift_first = gathered[2].astype(jnp.float32)
    gain_second = gathered[4].astype(jnp.float32)
    shift_second = gathered[5].astype(jnp.float32)
    gain_third = gathered[7].astype(jnp.float32)
    shift_third = gathered[8].astype(jnp.float32)
    channels = views.shape[4]
    middle = weight_reduce.shape[1]
    map_shapes = [
        (views.shape[0] * views.shape[1], views.shape[2], views.shape[3]),
        (crops.shape[0] * crops.shape[1], crops.shape[2], crops.shape[3]),
    ]
    flat_inputs = [views.reshape(-1, channels), crops.reshape(-1, channels)]
    reduced = [
        jnp.dot(source, weight_reduce, preferred_element_type=jnp.float32) for source in flat_inputs
    ]
    first_norm = standardize(reduced, gain_first, shift_first)
    first_act = [jax.nn.silu(saved[2]).astype(jnp.bfloat16) for saved in first_norm]
    padded_act = [
        spread_rows(act.reshape(shape[0], shape[1], shape[2], middle))
        for act, shape in zip(first_act, map_shapes)
    ]
    patch_rows = [
        patches(padded, shape[1], shape[2], False) for padded, shape in zip(padded_act, map_shapes)
    ]
    kernel = weight_spatial.reshape(9 * middle, middle)
    spatial = [jnp.dot(patch, kernel, preferred_element_type=jnp.float32) for patch in patch_rows]
    second_norm = standardize(spatial, gain_second, shift_second)
    second_act = [jax.nn.silu(saved[2]).astype(jnp.bfloat16) for saved in second_norm]
    expanded = [
        jnp.dot(act, weight_expand, preferred_element_type=jnp.float32) for act in second_act
    ]
    third_norm = standardize(expanded, gain_third, shift_third)
    pre_list = [
        source.astype(jnp.float32) + saved[2] for source, saved in zip(flat_inputs, third_norm)
    ]
    activation = [jax.nn.silu(pre) for pre in pre_list]
    view_sums = jnp.sum(activation[0].reshape(views.shape[0], views.shape[1], -1, channels), axis=2)
    crop_sums = jnp.sum(activation[1].reshape(crops.shape[0], crops.shape[1], -1, channels), axis=2)
    pooled_sums = lax.psum((view_sums, crop_sums), "rows")
    pooled = jnp.concatenate(
        [
            pooled_sums[0] / (views.shape[3] * views.shape[3]),
            pooled_sums[1] / (crops.shape[3] * crops.shape[3]),
        ],
        axis=1,
    )
    cotangent = [
        cot_views.reshape(-1, channels).astype(jnp.float32),
        cot_crops.reshape(-1, channels).astype(jnp.float32),
    ]
    d_pre = [cot * silu_slope(pre) for cot, pre in zip(cotangent, pre_list)]
    d_expanded_f, gain_third_grad, shift_third_grad = unstandardize(d_pre, third_norm, gain_third)
    d_expanded = [grad.astype(jnp.bfloat16) for grad in d_expanded_f]
    expand_grad = jnp.einsum(
        "pm,pc->mc", second_act[0], d_expanded[0], preferred_element_type=jnp.float32
    ) + jnp.einsum("pm,pc->mc", second_act[1], d_expanded[1], preferred_element_type=jnp.float32)
    d_norm_two = [
        jnp.einsum("pc,mc->pm", grad, weight_expand, preferred_element_type=jnp.float32)
        * silu_slope(saved[2])
        for grad, saved in zip(d_expanded, second_norm)
    ]
    d_spatial_f, gain_second_grad, shift_second_grad = unstandardize(
        d_norm_two, second_norm, gain_second
    )
    d_spatial = [grad.astype(jnp.bfloat16) for grad in d_spatial_f]
    spatial_grad = (
        jnp.einsum("pk,pm->km", patch_rows[0], d_spatial[0], preferred_element_type=jnp.float32)
        + jnp.einsum("pk,pm->km", patch_rows[1], d_spatial[1], preferred_element_type=jnp.float32)
    ).reshape(3, 3, middle, middle)
    back_kernel = jnp.transpose(weight_spatial, (0, 1, 3, 2)).reshape(9 * middle, middle)
    padded_grads = [
        spread_grads(grad.reshape(shape[0], shape[1], shape[2], middle))
        for grad, shape in zip(d_spatial, map_shapes)
    ]
    d_norm_one = [
        jnp.dot(
            patches(padded, shape[1], shape[2], True),
            back_kernel,
            preferred_element_type=jnp.float32,
        )
        * silu_slope(saved[2])
        for padded, shape, saved in zip(padded_grads, map_shapes, first_norm)
    ]
    d_reduced_f, gain_first_grad, shift_first_grad = unstandardize(
        d_norm_one, first_norm, gain_first
    )
    d_reduced = [grad.astype(jnp.bfloat16) for grad in d_reduced_f]
    reduce_grad = jnp.einsum(
        "pc,pm->cm", flat_inputs[0], d_reduced[0], preferred_element_type=jnp.float32
    ) + jnp.einsum("pc,pm->cm", flat_inputs[1], d_reduced[1], preferred_element_type=jnp.float32)
    input_grads = [
        (
            pre_grad
            + jnp.einsum("pm,cm->pc", grad, weight_reduce, preferred_element_type=jnp.float32)
        ).astype(jnp.bfloat16)
        for pre_grad, grad in zip(d_pre, d_reduced)
    ]
    shares = (
        lax.psum_scatter(reduce_grad, "dp", scatter_dimension=0, tiled=True),
        lax.psum_scatter(gain_first_grad, "dp", scatter_dimension=0, tiled=True),
        lax.psum_scatter(shift_first_grad, "dp", scatter_dimension=0, tiled=True),
        lax.psum_scatter(spatial_grad, "dp", scatter_dimension=2, tiled=True),
        lax.psum_scatter(gain_second_grad, "dp", scatter_dimension=0, tiled=True),
        lax.psum_scatter(shift_second_grad, "dp", scatter_dimension=0, tiled=True),
        lax.psum_scatter(expand_grad, "dp", scatter_dimension=0, tiled=True),
        lax.psum_scatter(gain_third_grad, "dp", scatter_dimension=0, tiled=True),
        lax.psum_scatter(shift_third_grad, "dp", scatter_dimension=0, tiled=True),
    )
    summed = lax.psum(
        (
            shares[0],
            shares[1],
            shares[2],
            shares[3],
            shares[4],
            shares[5],
            shares[6],
            shares[7],
            shares[8],
        ),
        "rows",
    )
    return (
        activation[0].astype(jnp.bfloat16).reshape(views.shape),
        activation[1].astype(jnp.bfloat16).reshape(crops.shape),
        pooled,
        input_grads[0].reshape(views.shape),
        input_grads[1].reshape(crops.shape),
        summed[0],
        summed[1],
        summed[2],
        summed[3],
        summed[4],
        summed[5],
        summed[6],
        summed[7],
        summed[8],
    )


MESH = pl.DeviceIdType.MESH
F32 = jnp.float32
BF16 = jnp.bfloat16
NV = 512
NC = 256
N = NV + NC
KINDS = ((0, NV), (NV, NC))
NT = (((1,), (1,)), ((), ()))
TN = (((0,), (0,)), ((), ()))


def sigmoid(values):
    return 0.5 * jnp.tanh(0.5 * values) + 0.5


def dot(left, right, dims=(((1,), (0,)), ((), ()))):
    return lax.dot_general(left, right, dims, preferred_element_type=F32)


def moved(values, kind, step):
    rows, lanes = values.shape
    if step == 0:
        return values
    if kind == 0:
        maps = values.reshape(rows // 64, 64, lanes)
        gap = jnp.zeros((rows // 64, 8, lanes), values.dtype)
        parts = [gap, maps[:, :-8]] if step > 0 else [maps[:, 8:], gap]
        return jnp.concatenate(parts, axis=1).reshape(rows, lanes)
    gap = jnp.zeros((64, lanes), values.dtype)
    return jnp.concatenate([gap, values[:-64]] if step > 0 else [values[64:], gap], axis=0)


def turned(values, kind, step):
    if step == 0:
        return values
    rows, lanes = values.shape
    width = 8 if kind == 0 else 4
    col = lax.rem(lax.broadcasted_iota(jnp.int32, (rows, lanes), 0), width)
    edge = 0 if step > 0 else width - 1
    return jnp.where(col == edge, 0.0, pltpu.roll(values, 1 if step > 0 else rows - 1, axis=0))


def stats(values, rows):
    mean = jnp.sum(values, axis=0, keepdims=True) / rows
    second = jnp.sum(values * values, axis=0, keepdims=True) / rows
    return mean, lax.rsqrt(second - mean * mean + EPSILON)


def block_kernel(
    views, crops, w_reduce, w_spatial, w_expand, cot_views, cot_crops, params,
    out_views, out_crops, pooled, grad_views, grad_crops, grad_reduce, grad_spatial, grad_expand, grad_params,
    xv, xc, cv, cc, wr, ws, we, pg,
    part, csend, crecv, xsend, xrecv,
    act1, act2, dred, conv, xhat1, slope1, xhat2, slope2, ex, dpre, dex, pat, ov, oc, gv, gc, pool, own_pool,
    ge, gs, gr, ysend_e, yrecv_e, zsend_e, zrecv_e, ysend_s, yrecv_s, zsend_s, zrecv_s, ysend_r, yrecv_r, zsend_r, zrecv_r,
    fin_e, fin_s, fin_r, pgr, pgs,
    loc, sx, rx, sw, rw, spg, rpg, scs, rcs, sxs, rxs, sag, rag, sout, rout, sgy, rgy, sgz, rgz, sfin, rfin, spp, rpp, spool, rpool,
):
    i, r = lax.axis_index("dp"), lax.axis_index("rows")
    z, y = i // 2, i % 2
    x, c = r // 2, r % 2
    yp = (i + 1 - 2 * y, r)
    cp = (i, 2 * x + 1 - c)
    xp = (i, 2 * (1 - x) + c)
    xcp = (i, 2 * (1 - x) + 1 - c)

    def zpeer(dz):
        return (z + dz) % 4

    def copy(src, dst, send, recv, dev):
        return pltpu.make_async_remote_copy(
            src_ref=src, dst_ref=dst, send_sem=send, recv_sem=recv, device_id=dev, device_id_type=MESH
        )

    def got(dst, recv):
        copy(dst, dst, recv, recv, cp).wait_recv()

    def sent(src, send):
        copy(src, src, send, send, cp).wait_send()

    def lanes(k, xx, cc_):
        return pl.ds(pl.multiple_of(512 * k + 256 * cc_ + 128 * xx, 128), 128)

    local = []

    def stage(src, dst):
        cp_ = pltpu.make_async_copy(src, dst, loc.at[len(local)])
        cp_.start()
        local.append(cp_)

    @pl.when(y == c)
    def _():
        pltpu.make_async_copy(
            w_reduce.at[pl.ds(pl.multiple_of(128 * x, 128), 128)], wr.at[z], loc.at[23]
        ).start()

    stage(w_spatial.at[:, :, pl.ds(pl.multiple_of(128 * r, 128), 128)], ws.at[:, i])
    for k in range(4):
        stage(w_expand.at[:, lanes(k, x, c)], we.at[i, :, pl.ds(128 * k, 128)])
    stage(params, pg.at[i])
    for k in range(4):
        kl = pl.ds(128 * k, 128)
        stage(views.at[:, :, lanes(k, x, c)], xv.at[:, r, :, kl])
        stage(crops.at[:, lanes(k, x, c)], xc.at[r, :, kl])
    for k in range(4):
        kl = pl.ds(128 * k, 128)
        stage(cot_views.at[:, :, lanes(k, x, c)], cv.at[:, r, :, kl])
        stage(cot_crops.at[:, lanes(k, x, c)], cc.at[r, :, kl])

    bar = pltpu.get_barrier_semaphore()
    peers = [(2 * zpeer(dz) + y, r) for dz in (1, 2, 3)] + [(2 * zpeer(dz) + 1 - y, r) for dz in (0, 1, 2, 3)]
    peers += [cp, xp, xcp]
    for dev in peers:
        pl.semaphore_signal(bar, inc=1, device_id=dev, device_id_type=MESH)
    pl.semaphore_wait(bar, len(peers))

    wr_own, ws_own, we_own = wr.at[z], ws.at[:, i], we.at[i]

    @pl.when(y == c)
    def _():
        pltpu.make_async_copy(
            w_reduce.at[pl.ds(pl.multiple_of(128 * x, 128), 128)], wr.at[z], loc.at[23]
        ).wait()
        for dz in (1, 2, 3):
            copy(wr_own, wr_own, sw.at[0, dz], rw.at[0, z], (2 * zpeer(dz) + y, r)).start()
        copy(wr_own, wr_own, sw.at[0, 0], rw.at[0, z], yp).start()

    def spread(src_v, src_c, dst_v, dst_c, s):
        for dr in (1, 2, 3):
            rr = (r + dr) % 4
            for k in range(4):
                kl = pl.ds(128 * k, 128)
                copy(
                    src_v.at[:, :, lanes(k, rr // 2, rr % 2)], dst_v.at[:, r, :, kl], sx.at[s, 0, dr, k], rx.at[s, 0, r], (i, rr)
                ).start()
        for dr in (1, 2, 3):
            rr = (r + dr) % 4
            for k in range(4):
                kl = pl.ds(128 * k, 128)
                copy(src_c.at[:, lanes(k, rr // 2, rr % 2)], dst_c.at[r, :, kl], sx.at[s, 1, dr, k], rx.at[s, 1, r], (i, rr)).start()

    def spread_sent(src_v, src_c, s):
        for dr in (1, 2, 3):
            for k in range(4):
                kl = pl.ds(128 * k, 128)
                copy(src_v.at[:, :, kl], src_v.at[:, :, kl], sx.at[s, 0, dr, k], rx.at[s, 0, r], cp).wait_send()
                copy(src_c.at[:, kl], src_c.at[:, kl], sx.at[s, 1, dr, k], rx.at[s, 1, r], cp).wait_send()

    spread(views, crops, xv, xc, 0)

    local[5].wait()
    for n, dev in enumerate(peers[:7]):
        copy(pg.at[i], pg.at[i], spg.at[n], rpg.at[i], dev).start()

    local[0].wait()
    for dz in (1, 2, 3):
        copy(ws_own, ws_own, sw.at[1, dz], rw.at[1, i], (2 * zpeer(dz) + y, r)).start()
    copy(ws_own, ws_own, sw.at[1, 0], rw.at[1, i], yp).start()

    spread(cot_views, cot_crops, cv, cc, 1)

    for k in range(4):
        local[1 + k].wait()
    for dz in (1, 2, 3):
        copy(we_own, we_own, sw.at[2, dz], rw.at[2, i], (2 * zpeer(dz) + y, r)).start()
    copy(we_own, we_own, sw.at[2, 0], rw.at[2, i], yp).start()

    @pl.when(y == c)
    def _():
        for dz in (1, 2, 3):
            k = zpeer(dz)
            got(wr.at[k], rw.at[0, k])
            copy(wr.at[k], wr.at[k], sw.at[0, 3 + dz], rw.at[0, k], yp).start()

    @pl.when(y != c)
    def _():
        for k in range(4):
            got(wr.at[k], rw.at[0, k])

    def pass_on(a, slot):
        for dz in (1, 2, 3):
            ii = 2 * zpeer(dz) + y
            got(slot(ii), rw.at[a, ii])
            copy(slot(ii), slot(ii), sw.at[a, 3 + dz], rw.at[a, ii], yp).start()

    def arrived(a, slot):
        for dz in range(4):
            ii = 2 * zpeer(dz) + 1 - y
            got(slot(ii), rw.at[a, ii])

    for own in local[6:14]:
        own.wait()
    weight_r = wr[...].reshape(512, 512)

    def kind_rows(kind):
        start, rows = KINDS[kind]
        return pl.ds(start, rows)

    def scatter_start(op, kind, sums):
        rows = kind_rows(kind)
        for s in range(4):
            part[op, s, rows, :] = sums[:, 128 * s : 128 * s + 128]
        for xx in range(2):
            csend[op, kind, xx, pl.ds(0, KINDS[kind][1]), :] = part[op, 2 * xx + 1 - c, rows, :].astype(BF16)
        n = pl.ds(0, KINDS[kind][1])
        copy(csend.at[op, kind, :, n], crecv.at[op, kind, :, n], scs.at[op, kind], rcs.at[op, kind], cp).start()

    def scatter_mid(op, kind):
        rows = kind_rows(kind)
        n = pl.ds(0, KINDS[kind][1])
        got(crecv.at[op, kind, :, n], rcs.at[op, kind])
        far = part[op, 2 * (1 - x) + c, rows, :] + crecv[op, kind, 1 - x, n, :].astype(F32)
        xsend[op, kind, n, :] = far.astype(BF16)
        copy(xsend.at[op, kind, n], xrecv.at[op, kind, n], sxs.at[op, kind], rxs.at[op, kind], xp).start()

    def scatter_end(op, kind):
        rows = kind_rows(kind)
        n = pl.ds(0, KINDS[kind][1])
        near = part[op, 2 * x + c, rows, :] + crecv[op, kind, x, n, :].astype(F32)
        got(xrecv.at[op, kind, n], rxs.at[op, kind])
        return near + xrecv[op, kind, n, :].astype(F32)

    def gather_start(op, kind, buf, value):
        rows = kind_rows(kind)
        buf[r, rows, :] = value
        own = buf.at[r, rows]
        copy(own, own, sag.at[op, kind, 0], rag.at[op, kind, r], xp).start()
        copy(own, own, sag.at[op, kind, 1], rag.at[op, kind, r], cp).start()

    def gather_mid(op, kind, buf):
        rows = kind_rows(kind)
        far = buf.at[xp[1], rows]
        got(far, rag.at[op, kind, xp[1]])
        copy(far, far, sag.at[op, kind, 2], rag.at[op, kind, xp[1]], cp).start()

    def gather_end(op, kind, buf):
        rows = kind_rows(kind)
        got(buf.at[cp[1], rows], rag.at[op, kind, cp[1]])
        got(buf.at[xcp[1], rows], rag.at[op, kind, xcp[1]])
        return jnp.concatenate([buf[s, rows, :] for s in range(4)], axis=1)

    for dr in (1, 2, 3):
        rr = (r + dr) % 4
        got(xv.at[:, rr], rx.at[0, 0, rr])
    scatter_start(0, 0, dot(xv[...].reshape(NV, 512), weight_r))
    for dr in (1, 2, 3):
        rr = (r + dr) % 4
        got(xc.at[rr], rx.at[0, 1, rr])
    scatter_start(0, 1, dot(xc[...].reshape(NC, 512), weight_r))
    scatter_mid(0, 0)
    scatter_mid(0, 1)
    pass_on(1, lambda ii: ws.at[:, ii])

    for dz in (1, 2, 3):
        ii = 2 * zpeer(dz) + y
        got(pg.at[ii], rpg.at[ii])
    for dz in range(4):
        ii = 2 * zpeer(dz) + 1 - y
        got(pg.at[ii], rpg.at[ii])
    half = lax.broadcasted_iota(jnp.int32, (1, 128), 1) < 64
    gain1, shift1, gain2, shift2 = [
        jnp.where(half, pg[2 * r, q : q + 1, :], pg[2 * r + 1, q : q + 1, :]) for q in range(4)
    ]
    gain3 = jnp.concatenate([pg[2 * k + c, pl.ds(4 + x, 1), :] for k in range(4)], axis=1)
    shift3 = jnp.concatenate([pg[2 * k + c, pl.ds(6 + x, 1), :] for k in range(4)], axis=1)

    def norm_act(values, rows, gain, shift):
        mean, rstd = stats(values, rows)
        xhat = (values - mean) * rstd
        norm = gain * xhat + shift
        sig = sigmoid(norm)
        return rstd, xhat, sig * (1.0 + norm * (1.0 - sig)), (norm * sig).astype(BF16)

    rstd1, rstd2, rstd3 = [None, None], [None, None], [None, None]
    for kind in range(2):
        rows = KINDS[kind][1]
        rstd1[kind], xh, sl, act = norm_act(scatter_end(0, kind), rows, gain1, shift1)
        gather_start(0, kind, act1, act)
        xhat1[kind_rows(kind), :] = xh
        slope1[kind_rows(kind), :] = sl
    pass_on(2, lambda ii: we.at[ii])
    for kind in range(2):
        gather_mid(0, kind, act1)
    arrived(1, lambda ii: ws.at[:, ii])

    def weight_s():
        return jnp.concatenate([ws[t].reshape(512, 128) for t in range(9)], axis=1)

    for kind in range(2):
        rows = KINDS[kind][1]
        conv[kind_rows(kind), :] = dot(gather_end(0, kind, act1), weight_s())
        taps = [conv[kind_rows(kind), 128 * t : 128 * t + 128] for t in range(9)]
        spatial = None
        for j in range(3):
            col = taps[3 + j] + moved(taps[j], kind, 1) + moved(taps[6 + j], kind, -1)
            col = turned(col, kind, 1 - j)
            spatial = col if spatial is None else spatial + col
        rstd2[kind], xh, sl, act = norm_act(spatial, rows, gain2, shift2)
        gather_start(1, kind, act2, act)
        xhat2[kind_rows(kind), :] = xh
        slope2[kind_rows(kind), :] = sl
    for kind in range(2):
        gather_mid(1, kind, act2)
    arrived(2, lambda ii: we.at[ii])
    weight_e = we[...].reshape(512, 512)

    for own in local[14:]:
        own.wait()
    for dr in (1, 2, 3):
        rr = (r + dr) % 4
        got(cv.at[:, rr], rx.at[1, 0, rr])
        got(cc.at[rr], rx.at[1, 1, rr])
    sum_x3, sum_d3 = [], []
    pool[...] = jnp.zeros_like(pool)
    for kind in range(2):
        start, rows = KINDS[kind]
        full2 = gather_end(1, kind, act2)
        ex[kind_rows(kind), :] = dot(full2, weight_e)

        def moments(b, acc, start=start):
            e = ex[pl.ds(pl.multiple_of(start + 32 * b, 32), 32), :].reshape(4, 8, 512)
            return acc[0] + jnp.sum(e, axis=0), acc[1] + jnp.sum(e * e, axis=0)

        zero8 = jnp.zeros((8, 512), F32)
        tot, sq = lax.fori_loop(0, rows // 32, moments, (zero8, zero8))
        mean = jnp.sum(tot, axis=0, keepdims=True) / rows
        rstd = lax.rsqrt(jnp.sum(sq, axis=0, keepdims=True) / rows - mean * mean + EPSILON)
        rstd3[kind] = rstd

        def finish(b, acc, kind=kind, start=start, mean=mean, rstd=rstd):
            rs = pl.ds(pl.multiple_of(start + 16 * b, 16), 16)
            xhat = (ex[rs, :] - mean) * rstd
            ex[rs, :] = xhat
            if kind == 0:
                src = xv[b // 4, b % 4]
                cot = cv[b // 4, b % 4]
            else:
                qs = pl.ds(pl.multiple_of(16 * (b % 4), 16), 16)
                src = xc[b // 4, qs, :]
                cot = cc[b // 4, qs, :]
            pre = src.astype(F32) + (gain3 * xhat + shift3)
            sig = sigmoid(pre)
            activation = pre * sig
            d = cot.astype(F32) * (sig * (1.0 + pre * (1.0 - sig)))
            dpre[rs, :] = d
            if kind == 0:
                ov[b // 4, b % 4] = activation.astype(BF16)
                pool[b // 4] += activation[:8] + activation[8:]
            else:
                oc[b // 4, qs, :] = activation.astype(BF16)
                m = 8 + 2 * (b % 4)
                pool[m] += activation[:8]
                pool[m + 1] += activation[8:]
            dx = d * xhat
            return acc[0] + (d[:8] + d[8:]), acc[1] + (dx[:8] + dx[8:])

        sd, sxx = lax.fori_loop(0, rows // 16, finish, (zero8, zero8))
        sd, sxx = jnp.sum(sd, axis=0, keepdims=True), jnp.sum(sxx, axis=0, keepdims=True)
        sum_d3.append(sd)
        sum_x3.append(sxx)
        scale = gain3 * rstd
        mean_d, mean_x = sd / rows, sxx / rows

        def back(b, _, start=start, scale=scale, mean_d=mean_d, mean_x=mean_x):
            rs = pl.ds(pl.multiple_of(start + 32 * b, 32), 32)
            dex[rs, :] = (scale * (dpre[rs, :] - mean_d - ex[rs, :] * mean_x)).astype(BF16)
            return 0

        lax.fori_loop(0, rows // 32, back, 0)
        scatter_start(1, kind, dot(dex[kind_rows(kind), :], weight_e, NT))

    def hand_out(src_v, src_c, dst_v, dst_c, s):
        for dr in (1, 2, 3, 0):
            rr = (r + dr) % 4
            for k in range(4):
                kl = pl.ds(128 * k, 128)
                if dr:
                    copy(src_v.at[:, rr, :, kl], dst_v.at[:, :, lanes(k, x, c)], sout.at[s, 0, dr, k], rout.at[s, 0, r, k], (i, rr)).start()
                    copy(src_c.at[rr, :, kl], dst_c.at[:, lanes(k, x, c)], sout.at[s, 1, dr, k], rout.at[s, 1, r, k], (i, rr)).start()
                else:
                    pltpu.make_async_copy(src_v.at[:, r, :, kl], dst_v.at[:, :, lanes(k, x, c)], sout.at[s, 0, 0, k]).start()
                    pltpu.make_async_copy(src_c.at[r, :, kl], dst_c.at[:, lanes(k, x, c)], sout.at[s, 1, 0, k]).start()

    def handed(src_v, src_c, dst_v, dst_c, s):
        for dr in (1, 2, 3, 0):
            rr = (r + dr) % 4
            for k in range(4):
                kl = pl.ds(128 * k, 128)
                if dr:
                    copy(src_v.at[:, rr, :, kl], dst_v.at[:, :, lanes(k, x, c)], sout.at[s, 0, dr, k], rout.at[s, 0, r, k], (i, rr)).wait_send()
                    copy(src_c.at[rr, :, kl], dst_c.at[:, lanes(k, x, c)], sout.at[s, 1, dr, k], rout.at[s, 1, r, k], (i, rr)).wait_send()
                    got(dst_v.at[:, :, lanes(k, rr // 2, rr % 2)], rout.at[s, 0, rr, k])
                    got(dst_c.at[:, lanes(k, rr // 2, rr % 2)], rout.at[s, 1, rr, k])
                else:
                    pltpu.make_async_copy(src_v.at[:, r, :, kl], dst_v.at[:, :, lanes(k, x, c)], sout.at[s, 0, 0, k]).wait()
                    pltpu.make_async_copy(src_c.at[r, :, kl], dst_c.at[:, lanes(k, x, c)], sout.at[s, 1, 0, k]).wait()

    scatter_mid(1, 0)
    scatter_mid(1, 1)

    ge[...] = dot(jnp.concatenate([act2[s] for s in range(4)], axis=1), dex[...], TN).reshape(4, 2, 64, 512)

    def grad_y(full, send, recv, q):
        send[...] = full[:, 1 - y].astype(BF16)
        copy(send, recv, sgy.at[q], rgy.at[q], yp).start()

    def grad_z(full, yrecv, send, recv, q):
        got(yrecv, rgy.at[q])
        for dz in (1, 2, 3):
            k = zpeer(dz)
            send[k] = (full[k, y] + yrecv[k].astype(F32)).astype(BF16)
            copy(send.at[k], recv.at[z], sgz.at[q, dz], rgz.at[q, z], (2 * k + y, r)).start()

    def grad_sum(full, yrecv, recv, q):
        total = full[z, y] + yrecv[z].astype(F32)
        for dz in (1, 2, 3):
            k = zpeer(dz)
            got(recv.at[k], rgz.at[q, k])
            total = total + recv[k].astype(F32)
        return total

    def fin_start(buf, value, q):
        buf[r] = value.astype(BF16)
        copy(buf.at[r], buf.at[r], sfin.at[q, 0], rfin.at[q, r], xp).start()
        copy(buf.at[r], buf.at[r], sfin.at[q, 1], rfin.at[q, r], cp).start()

    def fin_mid(buf, q):
        got(buf.at[xp[1]], rfin.at[q, xp[1]])
        copy(buf.at[xp[1]], buf.at[xp[1]], sfin.at[q, 2], rfin.at[q, xp[1]], cp).start()

    def fin_end(buf, q):
        got(buf.at[cp[1]], rfin.at[q, cp[1]])
        got(buf.at[xcp[1]], rfin.at[q, xcp[1]])

    grad_y(ge, ysend_e, yrecv_e, 0)

    def norm_back(d, xhat, rstd, gain, rows):
        sd = jnp.sum(d, axis=0, keepdims=True)
        sxx = jnp.sum(d * xhat, axis=0, keepdims=True)
        return (gain * rstd) * (d - sd / rows - xhat * (sxx / rows)), sd, sxx

    sum_d2, sum_x2 = [], []
    for kind in range(2):
        start, rows = KINDS[kind]
        d = scatter_end(1, kind) * slope2[kind_rows(kind), :]
        dz_, sd, sxx = norm_back(d, xhat2[kind_rows(kind), :], rstd2[kind], gain2, rows)
        sum_d2.append(sd)
        sum_x2.append(sxx)
        dz_ = dz_.astype(BF16).astype(F32)
        for tj in range(3):
            col = turned(dz_, kind, tj - 1)
            for ti in range(3):
                t = 3 * ti + tj
                pat[kind_rows(kind), 128 * t : 128 * t + 128] = moved(col, kind, ti - 1).astype(BF16)
        scatter_start(2, kind, dot(pat[kind_rows(kind), :], weight_s(), NT))
    hand_out(ov, oc, out_views, out_crops, 0)
    grad_z(ge, yrecv_e, zsend_e, zrecv_e, 0)
    scatter_mid(2, 0)
    scatter_mid(2, 1)
    gs[...] = dot(jnp.concatenate([act1[s] for s in range(4)], axis=1), pat[...], TN).reshape(4, 2, 64, 1152)
    grad_y(gs, ysend_s, yrecv_s, 1)

    sum_d1, sum_x1 = [], []
    for kind in range(2):
        start, rows = KINDS[kind]
        d = scatter_end(2, kind) * slope1[kind_rows(kind), :]
        dz_, sd, sxx = norm_back(d, xhat1[kind_rows(kind), :], rstd1[kind], gain1, rows)
        sum_d1.append(sd)
        sum_x1.append(sxx)
        gather_start(2, kind, dred, dz_.astype(BF16))

    rows12 = [sum_x1[0] + sum_x1[1], sum_d1[0] + sum_d1[1], sum_x2[0] + sum_x2[1], sum_d2[0] + sum_d2[1]]
    gx3, gd3 = sum_x3[0] + sum_x3[1], sum_d3[0] + sum_d3[1]
    rows3 = [g[:, 128 * k : 128 * k + 128] for g in (gx3, gd3) for k in range(4)]
    pgr[i] = jnp.concatenate(rows12 + rows3 + [jnp.zeros((4, 128), F32)], axis=0)
    for n, dev in enumerate(peers[:7]):
        copy(pgr.at[i], pgr.at[i], spp.at[n], rpp.at[0, i], dev).start()
    grad_z(gs, yrecv_s, zsend_s, zrecv_s, 1)
    for kind in range(2):
        gather_mid(2, kind, dred)
    full_d = [gather_end(2, kind, dred) for kind in range(2)]

    for m in range(4):
        col = dot(xv[:, :, :, 128 * m : 128 * m + 128].reshape(NV, 128), full_d[0], TN)
        gr[m] = col + dot(xc[:, :, 128 * m : 128 * m + 128].reshape(NC, 128), full_d[1], TN)

    @pl.when(y != c)
    def _():
        ysend_r[...] = gr[...].astype(BF16)
        copy(ysend_r, yrecv_r, sgy.at[2], rgy.at[2], yp).start()

    for kind in range(2):
        start, rows = KINDS[kind]
        grad = (dpre[kind_rows(kind), :] + dot(full_d[kind], weight_r, NT)).astype(BF16)
        if kind == 0:
            gv[...] = grad.reshape(8, 4, 16, 512)
        else:
            gc[...] = grad.reshape(4, 64, 512)

    @pl.when(y == c)
    def _():
        got(yrecv_r, rgy.at[2])
        for dz in (1, 2, 3):
            k = zpeer(dz)
            zsend_r[k] = (gr[k] + yrecv_r[k].astype(F32)).astype(BF16)
            copy(zsend_r.at[k], zrecv_r.at[z], sgz.at[2, dz], rgz.at[2, z], (2 * k + y, r)).start()

    hand_out(gv, gc, grad_views, grad_crops, 1)
    fin_start(fin_e, grad_sum(ge, yrecv_e, zrecv_e, 0), 0)
    fin_start(fin_s, grad_sum(gs, yrecv_s, zrecv_s, 1), 1)

    for n in range(8):
        row = 4 * (n % 2) + n // 2
        own_pool[row : row + 1, :] = jnp.sum(pool[n], axis=0, keepdims=True) / 64.0
        for m in range(2):
            row = 4 * (2 + 2 * (n % 2) + m) + n // 2
            own_pool[row : row + 1, :] = jnp.sum(pool[8 + n, 4 * m : 4 * m + 4, :], axis=0, keepdims=True) / 16.0
    for k in range(4):
        kl = pl.ds(128 * k, 128)
        pltpu.make_async_copy(own_pool.at[:, kl], pooled.at[:, lanes(k, x, c)], spool.at[0, k]).start()
        for dr in (1, 2, 3):
            copy(own_pool.at[:, kl], pooled.at[:, lanes(k, x, c)], spool.at[dr, k], rpool.at[r, k], (i, (r + dr) % 4)).start()

    @pl.when(y == c)
    def _():
        total = gr[z] + yrecv_r[z].astype(F32)
        for dz in (1, 2, 3):
            k = zpeer(dz)
            got(zrecv_r.at[k], rgz.at[2, k])
            total = total + zrecv_r[k].astype(F32)
        fin_r[x] = total.astype(BF16)
        for n, dev in enumerate((xp, cp, xcp)):
            copy(fin_r.at[x], fin_r.at[x], sfin.at[2, n], rfin.at[2, x], dev).start()

    fin_mid(fin_e, 0)
    fin_mid(fin_s, 1)

    total = pgr[i]
    for n in range(7):
        ii = (i + 1 + n) % 8
        got(pgr.at[ii], rpp.at[0, ii])
        total = total + pgr[ii]
    pgs[r] = total
    for n, dev in enumerate((xp, cp, xcp)):
        copy(pgs.at[r], pgs.at[r], spp.at[7 + n], rpp.at[1, r], dev).start()

    fin_end(fin_e, 0)
    for s in range(4):
        for k in range(4):
            lo = 512 * k + 256 * (s % 2) + 128 * (s // 2)
            grad_expand[:, lo : lo + 128] = fin_e[s, :, 128 * k : 128 * k + 128].astype(F32)
    fin_end(fin_s, 1)
    for s in range(4):
        for t in range(9):
            grad_spatial[t, :, 128 * s : 128 * s + 128] = fin_s[s, :, 128 * t : 128 * t + 128].astype(F32)
    for dr in (1, 2, 3):
        rr = (r + dr) % 4
        got(pgs.at[rr], rpp.at[1, rr])
    grad_params[...] = pgs[...]

    got(fin_r.at[1 - x], rfin.at[2, 1 - x])

    @pl.when(y != c)
    def _():
        got(fin_r.at[x], rfin.at[2, x])

    for n in range(2):
        grad_reduce[128 * n : 128 * n + 128, :] = fin_r[n].astype(F32)

    handed(ov, oc, out_views, out_crops, 0)
    handed(gv, gc, grad_views, grad_crops, 1)
    for k in range(4):
        kl = pl.ds(128 * k, 128)
        pltpu.make_async_copy(own_pool.at[:, kl], pooled.at[:, lanes(k, x, c)], spool.at[0, k]).wait()
        for dr in (1, 2, 3):
            rr = (r + dr) % 4
            sent(own_pool.at[:, kl], spool.at[dr, k])
            got(pooled.at[:, lanes(k, rr // 2, rr % 2)], rpool.at[rr, k])
    spread_sent(views, crops, 0)
    spread_sent(cot_views, cot_crops, 1)
    for n in range(7):
        sent(pg.at[i], spg.at[n])
    for n in range(10):
        sent(pgs.at[r], spp.at[n])
    for n in range(7):
        sent(ws_own, sw.at[1, n])
        sent(we_own, sw.at[2, n])
    for kind in range(2):
        n = pl.ds(0, KINDS[kind][1])
        for op in range(3):
            sent(csend.at[op, kind, :, n], scs.at[op, kind])
            sent(xsend.at[op, kind, n], sxs.at[op, kind])
            for m in range(3):
                sent(act1.at[r, kind_rows(kind)], sag.at[op, kind, m])
    for q, (ys, zs, fin) in enumerate(((ysend_e, zsend_e, fin_e), (ysend_s, zsend_s, fin_s))):
        sent(ys, sgy.at[q])
        for dz in (1, 2, 3):
            sent(zs.at[z], sgz.at[q, dz])
        for n in range(3):
            sent(fin.at[r], sfin.at[q, n])

    @pl.when(y != c)
    def _():
        sent(ysend_r, sgy.at[2])

    @pl.when(y == c)
    def _():
        for n in range(7):
            sent(wr_own, sw.at[0, n])
        for dz in (1, 2, 3):
            sent(zsend_r.at[z], sgz.at[2, dz])
        for n in range(3):
            sent(fin_r.at[x], sfin.at[2, n])


def fused(views, crops, w_reduce, w_spatial, w_expand, cot_views, cot_crops, params):
    hbm, vmem = pl.BlockSpec(memory_space=pl.ANY), pl.BlockSpec(memory_space=pltpu.VMEM)

    def shape(dims, dtype):
        return jax.ShapeDtypeStruct(dims, dtype)

    def buf(dims, dtype=BF16):
        return pltpu.VMEM(dims, dtype)

    def dma(*dims):
        return pltpu.SemaphoreType.DMA(dims)

    return pl.pallas_call(
        block_kernel,
        out_shape=[
            shape((8, 16, 2048), BF16), shape((64, 2048), BF16), shape((24, 2048), F32),
            shape((8, 16, 2048), BF16), shape((64, 2048), BF16),
            shape((256, 512), F32), shape((9, 64, 512), F32), shape((64, 2048), F32), shape((4, 16, 128), F32),
        ],
        in_specs=[hbm] * 8,
        out_specs=[hbm] * 5 + [vmem] * 4,
        scratch_shapes=[
            buf((8, 4, 16, 512)), buf((4, 64, 512)), buf((8, 4, 16, 512)), buf((4, 64, 512)),
            buf((4, 128, 512)), buf((9, 8, 64, 128)), buf((8, 64, 512)), buf((8, 8, 128), F32),
            buf((3, 4, N, 128), F32), buf((3, 2, 2, NV, 128)), buf((3, 2, 2, NV, 128)),
            buf((3, 2, NV, 128)), buf((3, 2, NV, 128)),
            buf((4, N, 128)), buf((4, N, 128)), buf((4, N, 128)), buf((N, 1152), F32),
            buf((N, 128), F32), buf((N, 128), F32), buf((N, 128), F32), buf((N, 128), F32),
            buf((N, 512), F32), buf((N, 512), F32), buf((N, 512)), buf((N, 1152)),
            buf((8, 4, 16, 512)), buf((4, 64, 512)), buf((8, 4, 16, 512)), buf((4, 64, 512)),
            buf((16, 8, 512), F32), buf((24, 512), F32),
            buf((4, 2, 64, 512), F32), buf((4, 2, 64, 1152), F32), buf((4, 128, 512), F32),
            buf((4, 64, 512)), buf((4, 64, 512)), buf((4, 64, 512)), buf((4, 64, 512)),
            buf((4, 64, 1152)), buf((4, 64, 1152)), buf((4, 64, 1152)), buf((4, 64, 1152)),
            buf((4, 128, 512)), buf((4, 128, 512)), buf((4, 128, 512)), buf((4, 128, 512)),
            buf((4, 64, 512)), buf((4, 64, 1152)), buf((2, 128, 512)),
            buf((8, 16, 128), F32), buf((4, 16, 128), F32),
            dma(24), dma(2, 2, 4, 4), dma(2, 2, 4), dma(3, 7), dma(3, 8), dma(7), dma(8),
            dma(3, 2), dma(3, 2), dma(3, 2), dma(3, 2), dma(3, 2, 3), dma(3, 2, 4),
            dma(2, 2, 4, 4), dma(2, 2, 4, 4), dma(3), dma(3), dma(3, 4), dma(3, 4), dma(3, 3), dma(3, 4),
            dma(10), dma(2, 8), dma(4, 4), dma(4, 4),
        ],
        compiler_params=pltpu.CompilerParams(collective_id=0, has_side_effects=True, vmem_limit_bytes=56 << 20),
        cost_estimate=pl.CostEstimate(flops=5_200_000_000, bytes_accessed=8_000_000, transcendentals=2_000_000),
    )(views, crops, w_reduce, w_spatial, w_expand, cot_views, cot_crops, params)


def step(
    dp, rows, views, crops, w_reduce, gain_one, shift_one, w_spatial, gain_two, shift_two, w_expand, gain_three, shift_three,
    cot_views, cot_crops,
):
    args = (
        views, crops, w_reduce, gain_one, shift_one, w_spatial, gain_two, shift_two, w_expand, gain_three, shift_three,
        cot_views, cot_crops,
    )
    if (dp, rows) != (8, 4) or views.shape != (4, 2, 2, 8, 2048) or crops.shape != (4, 4, 1, 4, 2048):
        return body(*args)
    params = jnp.concatenate(
        [jnp.concatenate([v, v]) for v in (gain_one, shift_one, gain_two, shift_two)] + [gain_three, shift_three]
    ).astype(F32).reshape(8, 128)
    outs = fused(
        views.reshape(8, 16, 2048), crops.reshape(64, 2048), w_reduce, w_spatial.reshape(9, 64, 512), w_expand,
        cot_views.reshape(8, 16, 2048), cot_crops.reshape(64, 2048), params,
    )
    out_v, out_c, pooled, grad_v, grad_c, grad_r, grad_s, grad_e, grads = outs
    i = lax.axis_index("dp")
    small = lax.dynamic_index_in_dim(grads, i // 2, 0, keepdims=False)[:4]
    small = lax.dynamic_slice_in_dim(small, 64 * (i % 2), 64, axis=1)
    wide = grads.reshape(2, 2, 16, 128)[:, :, 4:12].reshape(2, 2, 2, 4, 128)
    wide = lax.dynamic_index_in_dim(wide, i % 2, 1, keepdims=False)
    wide = lax.dynamic_index_in_dim(wide, i // 2, 2, keepdims=False)
    return (
        out_v.reshape(views.shape),
        out_c.reshape(crops.shape),
        jnp.transpose(pooled.reshape(6, 4, 2048), (1, 0, 2)),
        grad_v.reshape(views.shape),
        grad_c.reshape(crops.shape),
        grad_r,
        small[0],
        small[1],
        grad_s.reshape(w_spatial.shape[:3] + (512,)),
        small[2],
        small[3],
        grad_e,
        wide[:, 0].reshape(256),
        wide[:, 1].reshape(256),
    )


def solution(mesh):
    return jax.shard_map(
        functools.partial(step, mesh.shape["dp"], mesh.shape["rows"]),
        mesh=mesh,
        in_specs=(
            P("dp", None, "rows", None, None),
            P("dp", None, "rows", None, None),
            P("dp", None),
            P("dp"),
            P("dp"),
            P(None, None, "dp", None),
            P("dp"),
            P("dp"),
            P("dp", None),
            P("dp"),
            P("dp"),
            P("dp", None, "rows", None, None),
            P("dp", None, "rows", None, None),
        ),
        out_specs=(
            P("dp", None, "rows", None, None),
            P("dp", None, "rows", None, None),
            P("dp", None, None),
            P("dp", None, "rows", None, None),
            P("dp", None, "rows", None, None),
            P("dp", None),
            P("dp"),
            P("dp"),
            P(None, None, "dp", None),
            P("dp"),
            P("dp"),
            P("dp", None),
            P("dp"),
            P("dp"),
        ),
        check_vma=False,
    )
```

```python
import functools

import jax
import jax.numpy as jnp
from jax import lax
from jax.experimental import pallas as pl
from jax.experimental.pallas import tpu as pltpu
from jax.sharding import PartitionSpec as P

EPSILON = 1e-05


def extended(cells, sides, width):
    for axis, dim in sides:
        count = lax.axis_size(axis)
        ends = count - 1
        head = lax.slice_in_dim(cells, 0, width, axis=dim)
        tail = lax.slice_in_dim(cells, cells.shape[dim] - width, cells.shape[dim], axis=dim)
        cells = jnp.concatenate(
            [
                lax.ppermute(tail, axis, [(i, (i + 1) % count) for i in range(ends)]),
                cells,
                lax.ppermute(head, axis, [((i + 1) % count, i) for i in range(ends)]),
            ],
            axis=dim,
        )
    return cells


def silu_slope(values):
    sigmoid_val = jax.nn.sigmoid(values)
    return sigmoid_val * (1.0 + values * (1.0 - sigmoid_val))


def standardize(reduced_pair, gain_vec, shift_vec):
    left_map = reduced_pair[0]
    right_map = reduced_pair[1]
    totals = lax.psum(
        (
            jnp.sum(left_map, 0),
            jnp.sum(left_map * left_map, 0),
            jnp.sum(right_map, 0),
            jnp.sum(right_map * right_map, 0),
        ),
        "rows",
    )
    results = []
    for member in range(2):
        values = reduced_pair[member]
        pixel_count = values.shape[0] * lax.axis_size("rows")
        channel_mean = totals[2 * member] / pixel_count
        inverse_scale = lax.rsqrt(
            totals[2 * member + 1] / pixel_count - channel_mean * channel_mean + EPSILON
        )
        centred = (values - channel_mean) * inverse_scale
        results.append((centred, inverse_scale, gain_vec * centred + shift_vec))
    return results


def unstandardize(slopes, saved, gain_vec):
    shift_left = jnp.sum(slopes[0], 0)
    gain_left = jnp.sum(slopes[0] * saved[0][0], 0)
    shift_right = jnp.sum(slopes[1], 0)
    gain_right = jnp.sum(slopes[1] * saved[1][0], 0)
    totals = lax.psum((shift_left, gain_left, shift_right, gain_right), "rows")
    results = []
    for member in range(2):
        pixel_count = slopes[member].shape[0] * lax.axis_size("rows")
        centred = saved[member][0]
        inverse_scale = saved[member][1]
        mean_slope = gain_vec * totals[2 * member] / pixel_count
        mean_cross = gain_vec * totals[2 * member + 1] / pixel_count
        results.append(
            inverse_scale * (gain_vec * slopes[member] - mean_slope - centred * mean_cross)
        )
    return (results, gain_left + gain_right, shift_left + shift_right)


def spread_rows(activity):
    return extended(activity, (("rows", 1),), 1)


def spread_grads(slopes):
    return extended(slopes, (("rows", 1),), 1)


def patches(padded, row_count, col_count, flipped):
    widened = jnp.pad(padded, ((0, 0), (0, 0), (1, 1), (0, 0)))
    tap_list = []
    for row_tap in range(3):
        for col_tap in range(3):
            row_start = 2 - row_tap if flipped else row_tap
            col_start = 2 - col_tap if flipped else col_tap
            tap_list.append(
                widened[:, row_start : row_start + row_count, col_start : col_start + col_count, :]
            )
    return jnp.concatenate(tap_list, axis=-1).reshape(-1, 9 * widened.shape[-1])


def body(
    views,
    crops,
    w_reduce,
    gain_one,
    shift_one,
    w_spatial,
    gain_two,
    shift_two,
    w_expand,
    gain_three,
    shift_three,
    cot_views,
    cot_crops,
):
    gathered = (
        lax.all_gather(w_reduce, "dp", axis=0, tiled=True),
        lax.all_gather(gain_one, "dp", axis=0, tiled=True),
        lax.all_gather(shift_one, "dp", axis=0, tiled=True),
        lax.all_gather(w_spatial, "dp", axis=2, tiled=True),
        lax.all_gather(gain_two, "dp", axis=0, tiled=True),
        lax.all_gather(shift_two, "dp", axis=0, tiled=True),
        lax.all_gather(w_expand, "dp", axis=0, tiled=True),
        lax.all_gather(gain_three, "dp", axis=0, tiled=True),
        lax.all_gather(shift_three, "dp", axis=0, tiled=True),
    )
    weight_reduce = gathered[0]
    weight_spatial = gathered[3]
    weight_expand = gathered[6]
    gain_first = gathered[1].astype(jnp.float32)
    shift_first = gathered[2].astype(jnp.float32)
    gain_second = gathered[4].astype(jnp.float32)
    shift_second = gathered[5].astype(jnp.float32)
    gain_third = gathered[7].astype(jnp.float32)
    shift_third = gathered[8].astype(jnp.float32)
    channels = views.shape[4]
    middle = weight_reduce.shape[1]
    map_shapes = [
        (views.shape[0] * views.shape[1], views.shape[2], views.shape[3]),
        (crops.shape[0] * crops.shape[1], crops.shape[2], crops.shape[3]),
    ]
    flat_inputs = [views.reshape(-1, channels), crops.reshape(-1, channels)]
    reduced = [
        jnp.dot(source, weight_reduce, preferred_element_type=jnp.float32) for source in flat_inputs
    ]
    first_norm = standardize(reduced, gain_first, shift_first)
    first_act = [jax.nn.silu(saved[2]).astype(jnp.bfloat16) for saved in first_norm]
    padded_act = [
        spread_rows(act.reshape(shape[0], shape[1], shape[2], middle))
        for act, shape in zip(first_act, map_shapes)
    ]
    patch_rows = [
        patches(padded, shape[1], shape[2], False) for padded, shape in zip(padded_act, map_shapes)
    ]
    kernel = weight_spatial.reshape(9 * middle, middle)
    spatial = [jnp.dot(patch, kernel, preferred_element_type=jnp.float32) for patch in patch_rows]
    second_norm = standardize(spatial, gain_second, shift_second)
    second_act = [jax.nn.silu(saved[2]).astype(jnp.bfloat16) for saved in second_norm]
    expanded = [
        jnp.dot(act, weight_expand, preferred_element_type=jnp.float32) for act in second_act
    ]
    third_norm = standardize(expanded, gain_third, shift_third)
    pre_list = [
        source.astype(jnp.float32) + saved[2] for source, saved in zip(flat_inputs, third_norm)
    ]
    activation = [jax.nn.silu(pre) for pre in pre_list]
    view_sums = jnp.sum(activation[0].reshape(views.shape[0], views.shape[1], -1, channels), axis=2)
    crop_sums = jnp.sum(activation[1].reshape(crops.shape[0], crops.shape[1], -1, channels), axis=2)
    pooled_sums = lax.psum((view_sums, crop_sums), "rows")
    pooled = jnp.concatenate(
        [
            pooled_sums[0] / (views.shape[3] * views.shape[3]),
            pooled_sums[1] / (crops.shape[3] * crops.shape[3]),
        ],
        axis=1,
    )
    cotangent = [
        cot_views.reshape(-1, channels).astype(jnp.float32),
        cot_crops.reshape(-1, channels).astype(jnp.float32),
    ]
    d_pre = [cot * silu_slope(pre) for cot, pre in zip(cotangent, pre_list)]
    d_expanded_f, gain_third_grad, shift_third_grad = unstandardize(d_pre, third_norm, gain_third)
    d_expanded = [grad.astype(jnp.bfloat16) for grad in d_expanded_f]
    expand_grad = jnp.einsum(
        "pm,pc->mc", second_act[0], d_expanded[0], preferred_element_type=jnp.float32
    ) + jnp.einsum("pm,pc->mc", second_act[1], d_expanded[1], preferred_element_type=jnp.float32)
    d_norm_two = [
        jnp.einsum("pc,mc->pm", grad, weight_expand, preferred_element_type=jnp.float32)
        * silu_slope(saved[2])
        for grad, saved in zip(d_expanded, second_norm)
    ]
    d_spatial_f, gain_second_grad, shift_second_grad = unstandardize(
        d_norm_two, second_norm, gain_second
    )
    d_spatial = [grad.astype(jnp.bfloat16) for grad in d_spatial_f]
    spatial_grad = (
        jnp.einsum("pk,pm->km", patch_rows[0], d_spatial[0], preferred_element_type=jnp.float32)
        + jnp.einsum("pk,pm->km", patch_rows[1], d_spatial[1], preferred_element_type=jnp.float32)
    ).reshape(3, 3, middle, middle)
    back_kernel = jnp.transpose(weight_spatial, (0, 1, 3, 2)).reshape(9 * middle, middle)
    padded_grads = [
        spread_grads(grad.reshape(shape[0], shape[1], shape[2], middle))
        for grad, shape in zip(d_spatial, map_shapes)
    ]
    d_norm_one = [
        jnp.dot(
            patches(padded, shape[1], shape[2], True),
            back_kernel,
            preferred_element_type=jnp.float32,
        )
        * silu_slope(saved[2])
        for padded, shape, saved in zip(padded_grads, map_shapes, first_norm)
    ]
    d_reduced_f, gain_first_grad, shift_first_grad = unstandardize(
        d_norm_one, first_norm, gain_first
    )
    d_reduced = [grad.astype(jnp.bfloat16) for grad in d_reduced_f]
    reduce_grad = jnp.einsum(
        "pc,pm->cm", flat_inputs[0], d_reduced[0], preferred_element_type=jnp.float32
    ) + jnp.einsum("pc,pm->cm", flat_inputs[1], d_reduced[1], preferred_element_type=jnp.float32)
    input_grads = [
        (
            pre_grad
            + jnp.einsum("pm,cm->pc", grad, weight_reduce, preferred_element_type=jnp.float32)
        ).astype(jnp.bfloat16)
        for pre_grad, grad in zip(d_pre, d_reduced)
    ]
    shares = (
        lax.psum_scatter(reduce_grad, "dp", scatter_dimension=0, tiled=True),
        lax.psum_scatter(gain_first_grad, "dp", scatter_dimension=0, tiled=True),
        lax.psum_scatter(shift_first_grad, "dp", scatter_dimension=0, tiled=True),
        lax.psum_scatter(spatial_grad, "dp", scatter_dimension=2, tiled=True),
        lax.psum_scatter(gain_second_grad, "dp", scatter_dimension=0, tiled=True),
        lax.psum_scatter(shift_second_grad, "dp", scatter_dimension=0, tiled=True),
        lax.psum_scatter(expand_grad, "dp", scatter_dimension=0, tiled=True),
        lax.psum_scatter(gain_third_grad, "dp", scatter_dimension=0, tiled=True),
        lax.psum_scatter(shift_third_grad, "dp", scatter_dimension=0, tiled=True),
    )
    summed = lax.psum(
        (
            shares[0],
            shares[1],
            shares[2],
            shares[3],
            shares[4],
            shares[5],
            shares[6],
            shares[7],
            shares[8],
        ),
        "rows",
    )
    return (
        activation[0].astype(jnp.bfloat16).reshape(views.shape),
        activation[1].astype(jnp.bfloat16).reshape(crops.shape),
        pooled,
        input_grads[0].reshape(views.shape),
        input_grads[1].reshape(crops.shape),
        summed[0],
        summed[1],
        summed[2],
        summed[3],
        summed[4],
        summed[5],
        summed[6],
        summed[7],
        summed[8],
    )


MESH = pl.DeviceIdType.MESH
F32 = jnp.float32
BF16 = jnp.bfloat16
NV = 512
NC = 256
N = NV + NC
KINDS = ((0, NV), (NV, NC))
NT = (((1,), (1,)), ((), ()))
TN = (((0,), (0,)), ((), ()))


def sigmoid(values):
    return 0.5 * jnp.tanh(0.5 * values) + 0.5


def dot(left, right, dims=(((1,), (0,)), ((), ()))):
    return lax.dot_general(left, right, dims, preferred_element_type=F32)


def moved(values, kind, step):
    rows, lanes = values.shape
    if step == 0:
        return values
    if kind == 0:
        maps = values.reshape(rows // 64, 64, lanes)
        gap = jnp.zeros((rows // 64, 8, lanes), values.dtype)
        parts = [gap, maps[:, :-8]] if step > 0 else [maps[:, 8:], gap]
        return jnp.concatenate(parts, axis=1).reshape(rows, lanes)
    gap = jnp.zeros((64, lanes), values.dtype)
    return jnp.concatenate([gap, values[:-64]] if step > 0 else [values[64:], gap], axis=0)


def turned(values, kind, step):
    if step == 0:
        return values
    rows, lanes = values.shape
    width = 8 if kind == 0 else 4
    col = lax.rem(lax.broadcasted_iota(jnp.int32, (rows, lanes), 0), width)
    edge = 0 if step > 0 else width - 1
    return jnp.where(col == edge, 0.0, pltpu.roll(values, 1 if step > 0 else rows - 1, axis=0))


def block_kernel(
    views, crops, w_reduce, w_spatial, w_expand, cot_views, cot_crops, gain_a, shift_a, gain_b, shift_b, gain_c, shift_c,
    out_views, out_crops, pooled, grad_views, grad_crops, fin_e, fin_s, fin_r, pgs,
    xv, xc4, xc, cv, cc4, cc, wr, ws, we, raw_a, raw_b, raw_c, raw_d, raw_e, raw_f, pg,
    part, csend, crecv, xsend, xrecv,
    act1, act2, dred, conv, xhat1, slope1, xhat2, slope2, ex, dpre, dex, pat, ov, oc, gv, gc, pool, rows_pool, own_pool,
    ge, gs, gr, ysend_e, yrecv_e, zsend_e, zrecv_e, ysend_s, yrecv_s, zsend_s, zrecv_s, ysend_r, yrecv_r, zsend_r, zrecv_r,
    relay_e, relay_s, relay_r, acc_e, acc_s, acc_r, pgr,
    loc, sx, rx, sw, rw, spg, rpg, scs, rcs, sxs, rxs, sag, rag, sout, rout, sgy, rgy, sgz, rgz, sfin, rfin, spp, rpp, spool, rpool,
):
    i, r = lax.axis_index("dp"), lax.axis_index("rows")
    z, y = i // 2, i % 2
    x, c = r // 2, r % 2
    yp = (i + 1 - 2 * y, r)
    cp = (i, 2 * x + 1 - c)
    xp = (i, 2 * (1 - x) + c)
    xcp = (i, 2 * (1 - x) + 1 - c)
    rest = (xp, xcp, cp)

    middle = (z + 1) // 2 == 1
    step = 1 - 2 * (z // 2)

    def on_line(places):
        return (2 * (z + places * step) + y, r)

    def copy(src, dst, send, recv, dev):
        return pltpu.make_async_remote_copy(
            src_ref=src, dst_ref=dst, send_sem=send, recv_sem=recv, device_id=dev, device_id_type=MESH
        )

    def got(dst, recv):
        copy(dst, dst, recv, recv, cp).wait_recv()

    def sent(src, send):
        copy(src, src, send, send, cp).wait_send()

    def lanes(k, xx, cc_):
        return pl.ds(pl.multiple_of(512 * k + 256 * cc_ + 128 * xx, 128), 128)

    def kl(k):
        return pl.ds(128 * k, 128)

    def kind_rows(kind):
        return pl.ds(*KINDS[kind])

    local = {}

    def stage(name, src, dst):
        cp_ = pltpu.make_async_copy(src, dst, loc.at[len(local)])
        cp_.start()
        local[name] = cp_

    wr_stage = pltpu.make_async_copy(w_reduce.at[pl.ds(pl.multiple_of(128 * x, 128), 128)], wr.at[z], loc.at[31])

    @pl.when(y == c)
    def _():
        wr_stage.start()

    stage("ws", w_spatial.at[:, :, pl.ds(pl.multiple_of(128 * r, 128), 128)], ws.at[:, i])
    raw = (raw_a, raw_b, raw_c, raw_d, raw_e, raw_f)
    for n, vec in enumerate((gain_a, shift_a, gain_b, shift_b, gain_c, shift_c)):
        stage(("g", n), vec, raw[n])
    for k in range(4):
        stage(("we", k), w_expand.at[:, lanes(k, x, c)], we.at[i, :, kl(k)])
    for k in range(4):
        stage(("xv", k), views.at[:, :, lanes(k, x, c)], xv.at[:, r, :, kl(k)])
        stage(("xc", k), crops.at[:, :, lanes(k, x, c)], xc4.at[r, :, :, kl(k)])
    for k in range(4):
        stage(("cv", k), cot_views.at[:, :, lanes(k, x, c)], cv.at[:, r, :, kl(k)])
        stage(("cc", k), cot_crops.at[:, :, lanes(k, x, c)], cc4.at[r, :, :, kl(k)])

    bar = pltpu.get_barrier_semaphore()
    peers = [((i + n) % 8, r) for n in range(1, 8)] + [cp, xp, xcp]
    for dev in peers:
        pl.semaphore_signal(bar, inc=1, device_id=dev, device_id_type=MESH)
    pl.semaphore_wait(bar, len(peers))

    def whole_wr(k):
        return (wr.at[k],)

    def parts_ws(k):
        return tuple(ws.at[pl.ds(3 * n, 3), 2 * k + y] for n in range(3))

    def parts_ws_other(k):
        return tuple(ws.at[pl.ds(3 * n, 3), 2 * k + 1 - y] for n in range(3))

    def whole_we(k):
        return (we.at[2 * k + y],)

    def whole_we_other(k):
        return (we.at[2 * k + 1 - y],)

    def line_send(a, parts):
        for h, own in enumerate(parts(z)):

            def go(n, dev, own=own, h=h):
                copy(own, own, sw.at[a, h, n], rw.at[a, h, y, z], dev).start()

            go(0, on_line(2))
            go(1, on_line(1))

            @pl.when(middle)
            def _(go=go):
                go(2, on_line(-1))

            go(3, yp)

    def line_pass(a, parts, h):
        def take(places, n, on=False):
            k = z + places * step
            ref = parts(k)[h]
            got(ref, rw.at[a, h, y, k])
            if on:
                copy(ref, ref, sw.at[a, h, 7], rw.at[a, h, y, k], on_line(-1)).start()
            copy(ref, ref, sw.at[a, h, 4 + n], rw.at[a, h, y, k], yp).start()

        @pl.when(middle)
        def _():
            take(2, 0, True)
            take(1, 1)
            take(-1, 2)

        @pl.when(jnp.logical_not(middle))
        def _():
            take(2, 0)
            take(1, 1)
            take(3, 2)

    def line_got(a, parts_other, h):
        for k in range(4):
            got(parts_other(k)[h], rw.at[a, h, 1 - y, k])

    def line_sent(a, parts):
        for h, own in enumerate(parts(z)):
            for n in (0, 1, 3, 4, 5, 6):
                sent(own, sw.at[a, h, n])

            @pl.when(middle)
            def _(own=own, h=h):
                sent(own, sw.at[a, h, 2])
                sent(own, sw.at[a, h, 7])

    @pl.when(y == c)
    def _():
        wr_stage.wait()
        line_send(0, whole_wr)

    def spread_v(src, dst, s, devs):
        for dev in devs:
            rr = dev[1]
            for k in range(4):
                dr = (rr + 4 - r) % 4
                copy(src.at[:, :, lanes(k, rr // 2, rr % 2)], dst.at[:, r, :, kl(k)], sx.at[s, 0, dr, k], rx.at[s, 0, r], dev).start()

    def spread_c(src, dst, s, devs):
        for dev in devs:
            rr = dev[1]
            for k in range(4):
                dr = (rr + 4 - r) % 4
                copy(src.at[:, :, lanes(k, rr // 2, rr % 2)], dst.at[r, :, :, kl(k)], sx.at[s, 1, dr, k], rx.at[s, 1, r], dev).start()

    spread_v(views, xv, 0, rest)
    spread_c(crops, xc4, 0, rest)

    spread_v(cot_views, cv, 1, rest[:1])

    for n in range(6):
        local["g", n].wait()
    pg[i] = jnp.zeros((8, 128), F32)
    for n in range(4):
        vec = raw[n][...].reshape(1, 64).astype(F32)
        pg[i, n : n + 1, :] = jnp.concatenate([vec, vec], axis=1)
    for n in range(2):
        for m in range(2):
            pg[i, 4 + 2 * n + m : 5 + 2 * n + m, :] = raw[4 + n][128 * m : 128 * m + 128].reshape(1, 128).astype(F32)
    for n, dev in enumerate(peers[:7]):
        copy(pg.at[i], pg.at[i], spg.at[n], rpg.at[i], dev).start()

    @pl.when(y == c)
    def _():
        line_pass(0, whole_wr, 0)

    @pl.when(y != c)
    def _():
        for k in range(4):
            got(wr.at[k], rw.at[0, 0, 1 - y, k])

    local["ws"].wait()
    line_send(1, parts_ws)

    def scatter_start(op, kind, sums):
        rows = kind_rows(kind)
        n = pl.ds(0, KINDS[kind][1])
        for s in range(4):
            part[op, s, rows, :] = sums[:, 128 * s : 128 * s + 128]
        for xx in (1 - x, x):
            csend[op, kind, xx, n, :] = part[op, 2 * xx + 1 - c, rows, :].astype(BF16)
            own = csend.at[op, kind, xx, n]
            copy(own, crecv.at[op, kind, xx, n], scs.at[op, kind, xx], rcs.at[op, kind, xx], cp).start()

    def scatter_mid(op, kind):
        rows = kind_rows(kind)
        n = pl.ds(0, KINDS[kind][1])
        got(crecv.at[op, kind, 1 - x, n], rcs.at[op, kind, 1 - x])
        far = part[op, 2 * (1 - x) + c, rows, :] + crecv[op, kind, 1 - x, n, :].astype(F32)
        xsend[op, kind, n, :] = far.astype(BF16)
        copy(xsend.at[op, kind, n], xrecv.at[op, kind, n], sxs.at[op, kind], rxs.at[op, kind], xp).start()

    def scatter_end(op, kind):
        rows = kind_rows(kind)
        n = pl.ds(0, KINDS[kind][1])
        got(crecv.at[op, kind, x, n], rcs.at[op, kind, x])
        near = part[op, 2 * x + c, rows, :] + crecv[op, kind, x, n, :].astype(F32)
        got(xrecv.at[op, kind, n], rxs.at[op, kind])
        return near + xrecv[op, kind, n, :].astype(F32)

    def gather_start(op, kind, buf, value):
        rows = kind_rows(kind)
        buf[r, rows, :] = value
        own = buf.at[r, rows]
        copy(own, own, sag.at[op, kind, 0], rag.at[op, kind, r], xp).start()
        copy(own, own, sag.at[op, kind, 1], rag.at[op, kind, r], cp).start()

    def gather_mid(op, kind, buf):
        rows = kind_rows(kind)
        far = buf.at[xp[1], rows]
        got(far, rag.at[op, kind, xp[1]])
        copy(far, far, sag.at[op, kind, 2], rag.at[op, kind, xp[1]], cp).start()

    def gather_end(op, kind, buf):
        rows = kind_rows(kind)
        got(buf.at[cp[1], rows], rag.at[op, kind, cp[1]])
        got(buf.at[xcp[1], rows], rag.at[op, kind, xcp[1]])
        return jnp.concatenate([buf[s, rows, :] for s in range(4)], axis=1)

    weight_r = wr[...].reshape(512, 512)
    for k in range(4):
        local["xv", k].wait()
    for dev in rest:
        got(xv.at[:, dev[1]], rx.at[0, 0, dev[1]])
    scatter_start(0, 0, dot(xv[...].reshape(NV, 512), weight_r))
    for k in range(4):
        local["xc", k].wait()
    for dev in rest:
        got(xc4.at[dev[1]], rx.at[0, 1, dev[1]])
    xc[...] = xc4[...].reshape(4, 64, 512)
    scatter_start(0, 1, dot(xc[...].reshape(NC, 512), weight_r))
    scatter_mid(0, 0)
    scatter_mid(0, 1)
    spread_c(cot_crops, cc4, 1, rest[:1])
    line_pass(1, parts_ws, 0)

    for dev in peers[:7]:
        got(pg.at[dev[0]], rpg.at[dev[0]])
    half = lax.broadcasted_iota(jnp.int32, (1, 128), 1) < 64
    gain1, shift1, gain2, shift2 = [
        jnp.where(half, pg[2 * r, q : q + 1, :], pg[2 * r + 1, q : q + 1, :]) for q in range(4)
    ]
    gain3 = jnp.concatenate([pg[2 * k + c, pl.ds(4 + x, 1), :] for k in range(4)], axis=1)
    shift3 = jnp.concatenate([pg[2 * k + c, pl.ds(6 + x, 1), :] for k in range(4)], axis=1)

    def norm_act(values, rows, gain, shift):
        mean = jnp.sum(values, axis=0, keepdims=True) / rows
        second = jnp.sum(values * values, axis=0, keepdims=True) / rows
        rstd = lax.rsqrt(second - mean * mean + EPSILON)
        xhat = (values - mean) * rstd
        norm = gain * xhat + shift
        sig = sigmoid(norm)
        return rstd, xhat, sig * (1.0 + norm * (1.0 - sig)), (norm * sig).astype(BF16)

    rstd1, rstd2, rstd3 = [None, None], [None, None], [None, None]
    for kind in range(2):
        rows = KINDS[kind][1]
        rstd1[kind], xh, sl, act = norm_act(scatter_end(0, kind), rows, gain1, shift1)
        gather_start(0, kind, act1, act)
        xhat1[kind_rows(kind), :] = xh
        slope1[kind_rows(kind), :] = sl
    spread_v(cot_views, cv, 1, rest[1:])
    spread_c(cot_crops, cc4, 1, rest[1:])
    line_pass(1, parts_ws, 1)
    line_pass(1, parts_ws, 2)
    for k in range(4):
        local["we", k].wait()
    line_send(2, whole_we)
    for kind in range(2):
        gather_mid(0, kind, act1)
    for h in range(3):
        line_got(1, parts_ws_other, h)

    def weight_s():
        return jnp.concatenate([ws[t].reshape(512, 128) for t in range(9)], axis=1)

    for kind in range(2):
        rows = KINDS[kind][1]
        conv[kind_rows(kind), :] = dot(gather_end(0, kind, act1), weight_s())
        taps = [conv[kind_rows(kind), 128 * t : 128 * t + 128] for t in range(9)]
        spatial = None
        for j in range(3):
            col = taps[3 + j] + moved(taps[j], kind, 1) + moved(taps[6 + j], kind, -1)
            col = turned(col, kind, 1 - j)
            spatial = col if spatial is None else spatial + col
        rstd2[kind], xh, sl, act = norm_act(spatial, rows, gain2, shift2)
        gather_start(1, kind, act2, act)
        xhat2[kind_rows(kind), :] = xh
        slope2[kind_rows(kind), :] = sl
    line_pass(2, whole_we, 0)
    pool[...] = jnp.zeros_like(pool)
    for kind in range(2):
        gather_mid(1, kind, act2)
    for k in range(4):
        local["cv", k].wait()
        local["cc", k].wait()
    for dev in rest:
        got(cv.at[:, dev[1]], rx.at[1, 0, dev[1]])
        got(cc4.at[dev[1]], rx.at[1, 1, dev[1]])
    cc[...] = cc4[...].reshape(4, 64, 512)
    line_got(2, whole_we_other, 0)
    weight_e = we[...].reshape(512, 512)

    sum_x3, sum_d3 = [], []
    zero8 = jnp.zeros((8, 512), F32)

    def expand(kind):
        start, rows = KINDS[kind]
        ex[kind_rows(kind), :] = dot(gather_end(1, kind, act2), weight_e)

        def moments(b, acc):
            e = ex[pl.ds(pl.multiple_of(start + 32 * b, 32), 32), :].reshape(4, 8, 512)
            return acc[0] + jnp.sum(e, axis=0), acc[1] + jnp.sum(e * e, axis=0)

        tot, sq = lax.fori_loop(0, rows // 32, moments, (zero8, zero8))
        mean = jnp.sum(tot, axis=0, keepdims=True) / rows
        rstd = lax.rsqrt(jnp.sum(sq, axis=0, keepdims=True) / rows - mean * mean + EPSILON)

        def finish(b, acc):
            rs = pl.ds(pl.multiple_of(start + 16 * b, 16), 16)
            qs = pl.ds(pl.multiple_of(16 * (b % 4), 16), 16)
            xhat = (ex[rs, :] - mean) * rstd
            ex[rs, :] = xhat
            src = xv[b // 4, b % 4] if kind == 0 else xc[b // 4, qs, :]
            cot = cv[b // 4, b % 4] if kind == 0 else cc[b // 4, qs, :]
            pre = src.astype(F32) + (gain3 * xhat + shift3)
            sig = sigmoid(pre)
            activation = pre * sig
            d = cot.astype(F32) * (sig * (1.0 + pre * (1.0 - sig)))
            dpre[rs, :] = d
            if kind == 0:
                ov[b // 4, b % 4] = activation.astype(BF16)
                pool[b // 4] += activation[:8] + activation[8:]
            else:
                oc[b // 4, qs, :] = activation.astype(BF16)
                pool[8 + 2 * (b % 4)] += activation[:8]
                pool[9 + 2 * (b % 4)] += activation[8:]
            dx = d * xhat
            return acc[0] + (d[:8] + d[8:]), acc[1] + (dx[:8] + dx[8:])

        sd, sxx = lax.fori_loop(0, rows // 16, finish, (zero8, zero8))
        sd, sxx = jnp.sum(sd, axis=0, keepdims=True), jnp.sum(sxx, axis=0, keepdims=True)
        sum_d3.append(sd)
        sum_x3.append(sxx)
        scale = gain3 * rstd
        mean_d, mean_x = sd / rows, sxx / rows

        def back(b, _):
            rs = pl.ds(pl.multiple_of(start + 32 * b, 32), 32)
            dex[rs, :] = (scale * (dpre[rs, :] - mean_d - ex[rs, :] * mean_x)).astype(BF16)
            return 0

        lax.fori_loop(0, rows // 32, back, 0)

    def hand_v(src, dst, s, devs):
        for dev in devs:
            dr = (dev[1] + 4 - r) % 4
            for k in range(4):
                copy(src.at[:, dev[1], :, kl(k)], dst.at[:, :, lanes(k, x, c)], sout.at[s, 0, dr, k], rout.at[s, 0, r, k], dev).start()

    def hand_c(src, dst, s, devs):
        for dev in devs:
            dr = (dev[1] + 4 - r) % 4
            for k in range(4):
                copy(src.at[dev[1], :, kl(k)], dst.at[:, lanes(k, x, c)], sout.at[s, 1, dr, k], rout.at[s, 1, r, k], dev).start()

    def hand_own(src_v, src_c, dst_v, dst_c, s, end=False):
        for k in range(4):
            for m, (src, dst) in enumerate(
                ((src_v.at[:, r, :, kl(k)], dst_v.at[:, :, lanes(k, x, c)]), (src_c.at[r, :, kl(k)], dst_c.at[:, lanes(k, x, c)]))
            ):
                own = pltpu.make_async_copy(src, dst, sout.at[s, m, 0, k])
                if end:
                    own.wait()
                else:
                    own.start()

    def handed(src_v, src_c, dst_v, dst_c, s):
        hand_own(src_v, src_c, dst_v, dst_c, s, True)
        for dev in rest:
            rr = dev[1]
            dr = (rr + 4 - r) % 4
            for k in range(4):
                sent(src_v.at[:, rr, :, kl(k)], sout.at[s, 0, dr, k])
                sent(src_c.at[rr, :, kl(k)], sout.at[s, 1, dr, k])
                got(dst_v.at[:, :, lanes(k, rr // 2, rr % 2)], rout.at[s, 0, rr, k])
                got(dst_c.at[:, lanes(k, rr // 2, rr % 2)], rout.at[s, 1, rr, k])

    far_of = jnp.where(middle, z + 2 * step, z + 3 * step)
    mid_of = jnp.where(middle, z - step, z + 2 * step)
    order = [far_of, mid_of, z + step, z]

    def grad_y(full, send, recv, q, both):
        for k in order:
            send[k] = (full[k, 1 - y] if both else full[k]).astype(BF16)
            copy(send.at[k], recv.at[k], sgy.at[q, k], rgy.at[q, k], yp).start()

    def grad_add(full, yrecv, q, k, both):
        got(yrecv.at[k], rgy.at[q, k])
        return (full[k, y] if both else full[k]) + yrecv[k].astype(F32)

    def grad_z(full, yrecv, send, recv, relay, q, n, both=True):
        k = order[n]
        if n == 0:

            @pl.when(jnp.logical_not(middle))
            def _():
                send[k] = grad_add(full, yrecv, q, k, both).astype(BF16)
                copy(send.at[k], relay, sgz.at[q, 0], rgz.at[q, 4], on_line(1)).start()

        else:
            send[k] = grad_add(full, yrecv, q, k, both).astype(BF16)
            copy(send.at[k], recv.at[z], sgz.at[q, n], rgz.at[q, z], (2 * k + y, r)).start()

    def grad_relay(full, yrecv, send, recv, relay, q, both=True):
        @pl.when(middle)
        def _():
            k = order[0]
            total = grad_add(full, yrecv, q, k, both)
            got(relay, rgz.at[q, 4])
            send[k] = (total + relay[...].astype(F32)).astype(BF16)
            copy(send.at[k], recv.at[z], sgz.at[q, 0], rgz.at[q, z], (2 * k + y, r)).start()

    def grad_sum(full, yrecv, recv, acc, q, both=True):
        acc[...] = grad_add(full, yrecv, q, z, both)
        for k in (z + step, z + 2 * step):
            got(recv.at[k], rgz.at[q, k])
            acc[...] += recv[k].astype(F32)

        @pl.when(middle)
        def _():
            k = z - step
            got(recv.at[k], rgz.at[q, k])
            acc[...] += recv[k].astype(F32)

        return acc[...]

    def fin_start(buf, value, q):
        buf[r] = value.astype(BF16)
        copy(buf.at[r], buf.at[r], sfin.at[q, 0], rfin.at[q, r], xp).start()
        copy(buf.at[r], buf.at[r], sfin.at[q, 1], rfin.at[q, r], cp).start()

    def fin_mid(buf, q):
        got(buf.at[xp[1]], rfin.at[q, xp[1]])
        copy(buf.at[xp[1]], buf.at[xp[1]], sfin.at[q, 2], rfin.at[q, xp[1]], cp).start()

    def fin_end(buf, q):
        got(buf.at[cp[1]], rfin.at[q, cp[1]])
        got(buf.at[xcp[1]], rfin.at[q, xcp[1]])

    expand(0)
    scatter_start(1, 0, dot(dex[kind_rows(0), :], weight_e, NT))
    expand(1)
    scatter_mid(1, 0)
    scatter_start(1, 1, dot(dex[kind_rows(1), :], weight_e, NT))
    ge[...] = dot(jnp.concatenate([act2[s] for s in range(4)], axis=1), dex[...], TN).reshape(4, 2, 64, 512)
    grad_y(ge, ysend_e, yrecv_e, 0, True)
    scatter_mid(1, 1)
    hand_v(ov, out_views, 0, rest[:1])
    hand_own(ov, oc, out_views, out_crops, 0)
    hand_v(ov, out_views, 0, rest[2:])
    hand_c(oc, out_crops, 0, rest[2:])

    def norm_back(d, xhat, rstd, gain, rows):
        sd = jnp.sum(d, axis=0, keepdims=True)
        sxx = jnp.sum(d * xhat, axis=0, keepdims=True)
        return (gain * rstd) * (d - sd / rows - xhat * (sxx / rows)), sd, sxx

    sum_d2, sum_x2 = [], []
    for kind in range(2):
        rows = KINDS[kind][1]
        d = scatter_end(1, kind) * slope2[kind_rows(kind), :]
        dz_, sd, sxx = norm_back(d, xhat2[kind_rows(kind), :], rstd2[kind], gain2, rows)
        sum_d2.append(sd)
        sum_x2.append(sxx)
        dz_ = dz_.astype(BF16).astype(F32)
        for tj in range(3):
            col = turned(dz_, kind, tj - 1)
            for ti in range(3):
                t = 3 * ti + tj
                pat[kind_rows(kind), 128 * t : 128 * t + 128] = moved(col, kind, ti - 1).astype(BF16)
        scatter_start(2, kind, dot(pat[kind_rows(kind), :], weight_s(), NT))
        if kind == 1:
            scatter_mid(2, 0)
    scatter_mid(2, 1)
    gs[...] = dot(jnp.concatenate([act1[s] for s in range(4)], axis=1), pat[...], TN).reshape(4, 2, 64, 1152)
    grad_y(gs, ysend_s, yrecv_s, 1, True)
    for n in range(4):
        if n < 3:
            grad_z(ge, yrecv_e, zsend_e, zrecv_e, relay_e, 0, n)
        else:
            grad_relay(ge, yrecv_e, zsend_e, zrecv_e, relay_e, 0)
    hand_v(ov, out_views, 0, rest[1:2])

    sum_d1, sum_x1 = [], []
    for kind in range(2):
        rows = KINDS[kind][1]
        d = scatter_end(2, kind) * slope1[kind_rows(kind), :]
        dz_, sd, sxx = norm_back(d, xhat1[kind_rows(kind), :], rstd1[kind], gain1, rows)
        sum_d1.append(sd)
        sum_x1.append(sxx)
        gather_start(2, kind, dred, dz_.astype(BF16))

    rows12 = [sum_x1[0] + sum_x1[1], sum_d1[0] + sum_d1[1], sum_x2[0] + sum_x2[1], sum_d2[0] + sum_d2[1]]
    gx3, gd3 = sum_x3[0] + sum_x3[1], sum_d3[0] + sum_d3[1]
    rows3 = [g[:, 128 * k : 128 * k + 128] for g in (gx3, gd3) for k in range(4)]
    pgr[i] = jnp.concatenate(rows12 + rows3 + [jnp.zeros((4, 128), F32)], axis=0)
    for n, dev in enumerate(peers[:7]):
        copy(pgr.at[i], pgr.at[i], spp.at[n], rpp.at[0, i], dev).start()
    hand_c(oc, out_crops, 0, rest[:2])

    rows_pool[...] = jnp.zeros_like(rows_pool)
    for n in range(8):
        row = 4 * (n % 2) + n // 2
        rows_pool[row : row + 1, :] = jnp.sum(pool[n], axis=0, keepdims=True) / 64.0
        for m in range(2):
            row = 4 * (2 + 2 * (n % 2) + m) + n // 2
            rows_pool[row : row + 1, :] = jnp.sum(pool[8 + n, 4 * m : 4 * m + 4, :], axis=0, keepdims=True) / 16.0
    own_pool[...] = rows_pool[...].astype(BF16)
    for k in range(4):
        pltpu.make_async_copy(own_pool.at[:, kl(k)], pooled.at[:, lanes(k, x, c)], spool.at[0, k]).start()
        for n, dev in enumerate(rest):
            copy(own_pool.at[:, kl(k)], pooled.at[:, lanes(k, x, c)], spool.at[1 + n, k], rpool.at[r, k], dev).start()

    grad_z(gs, yrecv_s, zsend_s, zrecv_s, relay_s, 1, 0)
    for kind in range(2):
        gather_mid(2, kind, dred)
    grad_z(gs, yrecv_s, zsend_s, zrecv_s, relay_s, 1, 1)
    full_d = [gather_end(2, kind, dred) for kind in range(2)]

    for m in range(4):
        col = dot(xv[:, :, :, 128 * m : 128 * m + 128].reshape(NV, 128), full_d[0], TN)
        gr[m] = col + dot(xc[:, :, 128 * m : 128 * m + 128].reshape(NC, 128), full_d[1], TN)

    @pl.when(y != c)
    def _():
        grad_y(gr, ysend_r, yrecv_r, 2, False)

    grad_z(gs, yrecv_s, zsend_s, zrecv_s, relay_s, 1, 2)
    grad_relay(gs, yrecv_s, zsend_s, zrecv_s, relay_s, 1)
    fin_start(fin_e, grad_sum(ge, yrecv_e, zrecv_e, acc_e, 0), 0)
    gv[...] = (dpre[kind_rows(0), :] + dot(full_d[0], weight_r, NT)).astype(BF16).reshape(8, 4, 16, 512)
    hand_v(gv, grad_views, 1, rest)
    gc[...] = (dpre[kind_rows(1), :] + dot(full_d[1], weight_r, NT)).astype(BF16).reshape(4, 64, 512)
    hand_c(gc, grad_crops, 1, rest)
    hand_own(gv, gc, grad_views, grad_crops, 1)

    @pl.when(y == c)
    def _():
        for n in range(3):
            grad_z(gr, yrecv_r, zsend_r, zrecv_r, relay_r, 2, n, False)
        grad_relay(gr, yrecv_r, zsend_r, zrecv_r, relay_r, 2, False)

    fin_start(fin_s, grad_sum(gs, yrecv_s, zrecv_s, acc_s, 1), 1)
    fin_mid(fin_e, 0)

    total = pgr[i]
    for n in range(7):
        ii = (i + 1 + n) % 8
        got(pgr.at[ii], rpp.at[0, ii])
        total = total + pgr[ii]
    pgs[r] = total
    for n, dev in enumerate(rest):
        copy(pgs.at[r], pgs.at[r], spp.at[7 + n], rpp.at[1, r], dev).start()

    @pl.when(y == c)
    def _():
        fin_r[x] = grad_sum(gr, yrecv_r, zrecv_r, acc_r, 2, False).astype(BF16)
        for n, dev in enumerate(rest):
            copy(fin_r.at[x], fin_r.at[x], sfin.at[2, n], rfin.at[2, x], dev).start()

    fin_mid(fin_s, 1)
    fin_end(fin_e, 0)
    fin_end(fin_s, 1)
    for dev in rest:
        got(pgs.at[dev[1]], rpp.at[1, dev[1]])
    handed(ov, oc, out_views, out_crops, 0)
    handed(gv, gc, grad_views, grad_crops, 1)
    for k in range(4):
        pltpu.make_async_copy(own_pool.at[:, kl(k)], pooled.at[:, lanes(k, x, c)], spool.at[0, k]).wait()
        for n, dev in enumerate(rest):
            sent(own_pool.at[:, kl(k)], spool.at[1 + n, k])
            got(pooled.at[:, lanes(k, dev[1] // 2, dev[1] % 2)], rpool.at[dev[1], k])
    got(fin_r.at[1 - x], rfin.at[2, 1 - x])

    @pl.when(y != c)
    def _():
        got(fin_r.at[x], rfin.at[2, x])

    for s, (src_v, src_c) in enumerate(((views, crops), (cot_views, cot_crops))):
        for dr in (1, 2, 3):
            for k in range(4):
                sent(src_v.at[:, :, kl(k)], sx.at[s, 0, dr, k])
                sent(src_c.at[:, :, kl(k)], sx.at[s, 1, dr, k])
    for n in range(7):
        sent(pg.at[i], spg.at[n])
    for n in range(10):
        sent(pgs.at[r], spp.at[n])
    line_sent(1, parts_ws)
    line_sent(2, whole_we)
    for kind in range(2):
        n = pl.ds(0, KINDS[kind][1])
        for op in range(3):
            for xx in range(2):
                sent(csend.at[op, kind, xx, n], scs.at[op, kind, xx])
            sent(xsend.at[op, kind, n], sxs.at[op, kind])
            for m in range(3):
                sent(act1.at[r, kind_rows(kind)], sag.at[op, kind, m])
    for q, (ys, zs, fin) in enumerate(((ysend_e, zsend_e, fin_e), (ysend_s, zsend_s, fin_s))):
        for k in range(4):
            sent(ys.at[k], sgy.at[q, k])
        for n in range(3):
            sent(zs.at[z], sgz.at[q, n])
        for n in range(3):
            sent(fin.at[r], sfin.at[q, n])

    @pl.when(y != c)
    def _():
        for k in range(4):
            sent(ysend_r.at[k], sgy.at[2, k])

    @pl.when(y == c)
    def _():
        line_sent(0, whole_wr)
        for n in range(3):
            sent(zsend_r.at[z], sgz.at[2, n])
        for n in range(3):
            sent(fin_r.at[x], sfin.at[2, n])


def store_kernel(
    out_v, out_c, pool, grad_v, grad_c, fin_e, fin_s, fin_r, sums,
    out_views, out_crops, pooled, grad_views, grad_crops, grad_reduce, grad_spatial, grad_expand,
    gain_a, shift_a, gain_b, shift_b, gain_c, shift_c,
    oc, pl_, gc, gr, gs, ge, sem,
):
    i = lax.axis_index("dp")
    z, y = i // 2, i % 2
    copies = []

    def store(src, dst):
        one = pltpu.make_async_copy(src, dst, sem.at[len(copies)])
        one.start()
        copies.append(one)

    store(out_v, out_views)
    store(grad_v, grad_views)
    for s in range(4):
        for t in range(9):
            gs[t, :, 128 * s : 128 * s + 128] = fin_s[s, :, 128 * t : 128 * t + 128].astype(F32)
    store(gs, grad_spatial)
    for s in range(4):
        for k in range(4):
            lo = 512 * k + 256 * (s % 2) + 128 * (s // 2)
            ge[:, lo : lo + 128] = fin_e[s, :, 128 * k : 128 * k + 128].astype(F32)
    store(ge, grad_expand)
    gr[...] = fin_r[...].astype(F32).reshape(256, 512)
    store(gr, grad_reduce)
    oc[...] = out_c[...].reshape(16, 4, 2048)
    store(oc, out_crops)
    gc[...] = grad_c[...].reshape(16, 4, 2048)
    store(gc, grad_crops)
    pl_[...] = pool[0:24, :].astype(F32).reshape(6, 4, 2048)
    store(pl_, pooled)
    for n, out in enumerate((gain_a, shift_a, gain_b, shift_b)):
        row = sums[i // 2, n : n + 1, :]
        out[...] = jnp.where(i % 2 == 0, row[:, :64], row[:, 64:]).reshape(64)
    for n, out in enumerate((gain_c, shift_c)):
        out[...] = jnp.concatenate([sums[2 * m + y, pl.ds(4 + 4 * n + z, 1), :] for m in range(2)], axis=1).reshape(256)
    for one in copies:
        one.wait()


def fused(views, crops, w_reduce, w_spatial, w_expand, cot_views, cot_crops, *params):
    hbm, vmem = pl.BlockSpec(memory_space=pltpu.HBM), pl.BlockSpec(memory_space=pltpu.VMEM)

    def shape(dims, dtype):
        return jax.ShapeDtypeStruct(dims, dtype)

    def buf(dims, dtype=BF16):
        return pltpu.VMEM(dims, dtype)

    def dma(*dims):
        return pltpu.SemaphoreType.DMA(dims)

    held = pl.pallas_call(
        block_kernel,
        out_shape=[
            buf((8, 16, 2048)), buf((64, 2048)), buf((32, 2048)), buf((8, 16, 2048)), buf((64, 2048)),
            buf((4, 64, 512)), buf((4, 64, 1152)), buf((2, 128, 512)), buf((4, 16, 128), F32),
        ],
        in_specs=[hbm] * 13,
        out_specs=[vmem] * 9,
        scratch_shapes=[
            buf((8, 4, 16, 512)), buf((4, 16, 4, 512)), buf((4, 64, 512)),
            buf((8, 4, 16, 512)), buf((4, 16, 4, 512)), buf((4, 64, 512)),
            buf((4, 128, 512)), buf((9, 8, 64, 128)), buf((8, 64, 512)), buf((64,)), buf((64,)), buf((64,)), buf((64,)), buf((256,)), buf((256,)), buf((8, 8, 128), F32),
            buf((3, 4, N, 128), F32), buf((3, 2, 2, NV, 128)), buf((3, 2, 2, NV, 128)),
            buf((3, 2, NV, 128)), buf((3, 2, NV, 128)),
            buf((4, N, 128)), buf((4, N, 128)), buf((4, N, 128)), buf((N, 1152), F32),
            buf((N, 128), F32), buf((N, 128), F32), buf((N, 128), F32), buf((N, 128), F32),
            buf((N, 512), F32), buf((N, 512), F32), buf((N, 512)), buf((N, 1152)),
            buf((8, 4, 16, 512)), buf((4, 64, 512)), buf((8, 4, 16, 512)), buf((4, 64, 512)),
            buf((16, 8, 512), F32), buf((32, 512), F32), buf((32, 512)),
            buf((4, 2, 64, 512), F32), buf((4, 2, 64, 1152), F32), buf((4, 128, 512), F32),
            buf((4, 64, 512)), buf((4, 64, 512)), buf((4, 64, 512)), buf((4, 64, 512)),
            buf((4, 64, 1152)), buf((4, 64, 1152)), buf((4, 64, 1152)), buf((4, 64, 1152)),
            buf((4, 128, 512)), buf((4, 128, 512)), buf((4, 128, 512)), buf((4, 128, 512)),
            buf((64, 512)), buf((64, 1152)), buf((128, 512)), buf((64, 512), F32), buf((64, 1152), F32), buf((128, 512), F32),
            buf((8, 16, 128), F32),
            dma(32), dma(2, 2, 4, 4), dma(2, 2, 4), dma(3, 3, 8), dma(3, 3, 2, 4), dma(7), dma(8),
            dma(3, 2, 2), dma(3, 2, 2), dma(3, 2), dma(3, 2), dma(3, 2, 3), dma(3, 2, 4),
            dma(2, 2, 4, 4), dma(2, 2, 4, 4), dma(3, 4), dma(3, 4), dma(3, 4), dma(3, 5), dma(3, 3), dma(3, 4),
            dma(10), dma(2, 8), dma(4, 4), dma(4, 4),
        ],
        compiler_params=pltpu.CompilerParams(collective_id=0, has_side_effects=True, vmem_limit_bytes=58 << 20),
        cost_estimate=pl.CostEstimate(flops=5_200_000_000, bytes_accessed=8_000_000, transcendentals=2_000_000),
    )(views, crops, w_reduce, w_spatial, w_expand, cot_views, cot_crops, *params)
    held = [pltpu.with_memory_space_constraint(one, pltpu.VMEM) for one in held]
    return pl.pallas_call(
        store_kernel,
        out_shape=[
            shape((8, 16, 2048), BF16), shape((16, 4, 2048), BF16), shape((6, 4, 2048), F32),
            shape((8, 16, 2048), BF16), shape((16, 4, 2048), BF16),
            shape((256, 512), F32), shape((9, 64, 512), F32), shape((64, 2048), F32),
            shape((64,), F32), shape((64,), F32), shape((64,), F32), shape((64,), F32), shape((256,), F32), shape((256,), F32),
        ],
        in_specs=[vmem] * 9,
        out_specs=[hbm] * 8 + [vmem] * 6,
        scratch_shapes=[
            buf((16, 4, 2048)), buf((6, 4, 2048), F32), buf((16, 4, 2048)),
            buf((256, 512), F32), buf((9, 64, 512), F32), buf((64, 2048), F32), dma(8),
        ],
        compiler_params=pltpu.CompilerParams(vmem_limit_bytes=16 << 20),
    )(*held)


def step(
    dp, rows, views, crops, w_reduce, gain_one, shift_one, w_spatial, gain_two, shift_two, w_expand, gain_three, shift_three,
    cot_views, cot_crops,
):
    args = (
        views, crops, w_reduce, gain_one, shift_one, w_spatial, gain_two, shift_two, w_expand, gain_three, shift_three,
        cot_views, cot_crops,
    )
    if (dp, rows) != (8, 4) or views.shape != (4, 2, 2, 8, 2048) or crops.shape != (4, 4, 1, 4, 2048):
        return body(*args)
    out_v, out_c, pooled, grad_v, grad_c, grad_r, grad_s, grad_e, ga, sa, gb, sb, gc, sc = fused(
        views.reshape(8, 16, 2048), crops.reshape(16, 4, 2048), w_reduce, w_spatial.reshape(9, 64, 512), w_expand,
        cot_views.reshape(8, 16, 2048), cot_crops.reshape(16, 4, 2048),
        gain_one, shift_one, gain_two, shift_two, gain_three, shift_three,
    )
    return (
        out_v.reshape(views.shape),
        out_c.reshape(crops.shape),
        jnp.transpose(pooled, (1, 0, 2)),
        grad_v.reshape(views.shape),
        grad_c.reshape(crops.shape),
        grad_r,
        ga,
        sa,
        grad_s.reshape(w_spatial.shape[:3] + (512,)),
        gb,
        sb,
        grad_e,
        gc,
        sc,
    )


def solution(mesh):
    return jax.shard_map(
        functools.partial(step, mesh.shape["dp"], mesh.shape["rows"]),
        mesh=mesh,
        in_specs=(
            P("dp", None, "rows", None, None),
            P("dp", None, "rows", None, None),
            P("dp", None),
            P("dp"),
            P("dp"),
            P(None, None, "dp", None),
            P("dp"),
            P("dp"),
            P("dp", None),
            P("dp"),
            P("dp"),
            P("dp", None, "rows", None, None),
            P("dp", None, "rows", None, None),
        ),
        out_specs=(
            P("dp", None, "rows", None, None),
            P("dp", None, "rows", None, None),
            P("dp", None, None),
            P("dp", None, "rows", None, None),
            P("dp", None, "rows", None, None),
            P("dp", None),
            P("dp"),
            P("dp"),
            P(None, None, "dp", None),
            P("dp"),
            P("dp"),
            P("dp", None),
            P("dp"),
            P("dp"),
        ),
        check_vma=False,
    )
```

```python
import functools

import jax
import jax.numpy as jnp
from jax import lax
from jax.experimental import pallas as pl
from jax.experimental.pallas import tpu as pltpu
from jax.sharding import PartitionSpec as P

EPSILON = 1e-05


def extended(cells, sides, width):
    for axis, dim in sides:
        count = lax.axis_size(axis)
        ends = count - 1
        head = lax.slice_in_dim(cells, 0, width, axis=dim)
        tail = lax.slice_in_dim(cells, cells.shape[dim] - width, cells.shape[dim], axis=dim)
        cells = jnp.concatenate(
            [
                lax.ppermute(tail, axis, [(i, (i + 1) % count) for i in range(ends)]),
                cells,
                lax.ppermute(head, axis, [((i + 1) % count, i) for i in range(ends)]),
            ],
            axis=dim,
        )
    return cells


def silu_slope(values):
    sigmoid_val = jax.nn.sigmoid(values)
    return sigmoid_val * (1.0 + values * (1.0 - sigmoid_val))


def standardize(reduced_pair, gain_vec, shift_vec):
    left_map = reduced_pair[0]
    right_map = reduced_pair[1]
    totals = lax.psum(
        (
            jnp.sum(left_map, 0),
            jnp.sum(left_map * left_map, 0),
            jnp.sum(right_map, 0),
            jnp.sum(right_map * right_map, 0),
        ),
        "rows",
    )
    results = []
    for member in range(2):
        values = reduced_pair[member]
        pixel_count = values.shape[0] * lax.axis_size("rows")
        channel_mean = totals[2 * member] / pixel_count
        inverse_scale = lax.rsqrt(
            totals[2 * member + 1] / pixel_count - channel_mean * channel_mean + EPSILON
        )
        centred = (values - channel_mean) * inverse_scale
        results.append((centred, inverse_scale, gain_vec * centred + shift_vec))
    return results


def unstandardize(slopes, saved, gain_vec):
    shift_left = jnp.sum(slopes[0], 0)
    gain_left = jnp.sum(slopes[0] * saved[0][0], 0)
    shift_right = jnp.sum(slopes[1], 0)
    gain_right = jnp.sum(slopes[1] * saved[1][0], 0)
    totals = lax.psum((shift_left, gain_left, shift_right, gain_right), "rows")
    results = []
    for member in range(2):
        pixel_count = slopes[member].shape[0] * lax.axis_size("rows")
        centred = saved[member][0]
        inverse_scale = saved[member][1]
        mean_slope = gain_vec * totals[2 * member] / pixel_count
        mean_cross = gain_vec * totals[2 * member + 1] / pixel_count
        results.append(
            inverse_scale * (gain_vec * slopes[member] - mean_slope - centred * mean_cross)
        )
    return (results, gain_left + gain_right, shift_left + shift_right)


def spread_rows(activity):
    return extended(activity, (("rows", 1),), 1)


def spread_grads(slopes):
    return extended(slopes, (("rows", 1),), 1)


def patches(padded, row_count, col_count, flipped):
    widened = jnp.pad(padded, ((0, 0), (0, 0), (1, 1), (0, 0)))
    tap_list = []
    for row_tap in range(3):
        for col_tap in range(3):
            row_start = 2 - row_tap if flipped else row_tap
            col_start = 2 - col_tap if flipped else col_tap
            tap_list.append(
                widened[:, row_start : row_start + row_count, col_start : col_start + col_count, :]
            )
    return jnp.concatenate(tap_list, axis=-1).reshape(-1, 9 * widened.shape[-1])


def body(
    views,
    crops,
    w_reduce,
    gain_one,
    shift_one,
    w_spatial,
    gain_two,
    shift_two,
    w_expand,
    gain_three,
    shift_three,
    cot_views,
    cot_crops,
):
    gathered = (
        lax.all_gather(w_reduce, "dp", axis=0, tiled=True),
        lax.all_gather(gain_one, "dp", axis=0, tiled=True),
        lax.all_gather(shift_one, "dp", axis=0, tiled=True),
        lax.all_gather(w_spatial, "dp", axis=2, tiled=True),
        lax.all_gather(gain_two, "dp", axis=0, tiled=True),
        lax.all_gather(shift_two, "dp", axis=0, tiled=True),
        lax.all_gather(w_expand, "dp", axis=0, tiled=True),
        lax.all_gather(gain_three, "dp", axis=0, tiled=True),
        lax.all_gather(shift_three, "dp", axis=0, tiled=True),
    )
    weight_reduce = gathered[0]
    weight_spatial = gathered[3]
    weight_expand = gathered[6]
    gain_first = gathered[1].astype(jnp.float32)
    shift_first = gathered[2].astype(jnp.float32)
    gain_second = gathered[4].astype(jnp.float32)
    shift_second = gathered[5].astype(jnp.float32)
    gain_third = gathered[7].astype(jnp.float32)
    shift_third = gathered[8].astype(jnp.float32)
    channels = views.shape[4]
    middle = weight_reduce.shape[1]
    map_shapes = [
        (views.shape[0] * views.shape[1], views.shape[2], views.shape[3]),
        (crops.shape[0] * crops.shape[1], crops.shape[2], crops.shape[3]),
    ]
    flat_inputs = [views.reshape(-1, channels), crops.reshape(-1, channels)]
    reduced = [
        jnp.dot(source, weight_reduce, preferred_element_type=jnp.float32) for source in flat_inputs
    ]
    first_norm = standardize(reduced, gain_first, shift_first)
    first_act = [jax.nn.silu(saved[2]).astype(jnp.bfloat16) for saved in first_norm]
    padded_act = [
        spread_rows(act.reshape(shape[0], shape[1], shape[2], middle))
        for act, shape in zip(first_act, map_shapes)
    ]
    patch_rows = [
        patches(padded, shape[1], shape[2], False) for padded, shape in zip(padded_act, map_shapes)
    ]
    kernel = weight_spatial.reshape(9 * middle, middle)
    spatial = [jnp.dot(patch, kernel, preferred_element_type=jnp.float32) for patch in patch_rows]
    second_norm = standardize(spatial, gain_second, shift_second)
    second_act = [jax.nn.silu(saved[2]).astype(jnp.bfloat16) for saved in second_norm]
    expanded = [
        jnp.dot(act, weight_expand, preferred_element_type=jnp.float32) for act in second_act
    ]
    third_norm = standardize(expanded, gain_third, shift_third)
    pre_list = [
        source.astype(jnp.float32) + saved[2] for source, saved in zip(flat_inputs, third_norm)
    ]
    activation = [jax.nn.silu(pre) for pre in pre_list]
    view_sums = jnp.sum(activation[0].reshape(views.shape[0], views.shape[1], -1, channels), axis=2)
    crop_sums = jnp.sum(activation[1].reshape(crops.shape[0], crops.shape[1], -1, channels), axis=2)
    pooled_sums = lax.psum((view_sums, crop_sums), "rows")
    pooled = jnp.concatenate(
        [
            pooled_sums[0] / (views.shape[3] * views.shape[3]),
            pooled_sums[1] / (crops.shape[3] * crops.shape[3]),
        ],
        axis=1,
    )
    cotangent = [
        cot_views.reshape(-1, channels).astype(jnp.float32),
        cot_crops.reshape(-1, channels).astype(jnp.float32),
    ]
    d_pre = [cot * silu_slope(pre) for cot, pre in zip(cotangent, pre_list)]
    d_expanded_f, gain_third_grad, shift_third_grad = unstandardize(d_pre, third_norm, gain_third)
    d_expanded = [grad.astype(jnp.bfloat16) for grad in d_expanded_f]
    expand_grad = jnp.einsum(
        "pm,pc->mc", second_act[0], d_expanded[0], preferred_element_type=jnp.float32
    ) + jnp.einsum("pm,pc->mc", second_act[1], d_expanded[1], preferred_element_type=jnp.float32)
    d_norm_two = [
        jnp.einsum("pc,mc->pm", grad, weight_expand, preferred_element_type=jnp.float32)
        * silu_slope(saved[2])
        for grad, saved in zip(d_expanded, second_norm)
    ]
    d_spatial_f, gain_second_grad, shift_second_grad = unstandardize(
        d_norm_two, second_norm, gain_second
    )
    d_spatial = [grad.astype(jnp.bfloat16) for grad in d_spatial_f]
    spatial_grad = (
        jnp.einsum("pk,pm->km", patch_rows[0], d_spatial[0], preferred_element_type=jnp.float32)
        + jnp.einsum("pk,pm->km", patch_rows[1], d_spatial[1], preferred_element_type=jnp.float32)
    ).reshape(3, 3, middle, middle)
    back_kernel = jnp.transpose(weight_spatial, (0, 1, 3, 2)).reshape(9 * middle, middle)
    padded_grads = [
        spread_grads(grad.reshape(shape[0], shape[1], shape[2], middle))
        for grad, shape in zip(d_spatial, map_shapes)
    ]
    d_norm_one = [
        jnp.dot(
            patches(padded, shape[1], shape[2], True),
            back_kernel,
            preferred_element_type=jnp.float32,
        )
        * silu_slope(saved[2])
        for padded, shape, saved in zip(padded_grads, map_shapes, first_norm)
    ]
    d_reduced_f, gain_first_grad, shift_first_grad = unstandardize(
        d_norm_one, first_norm, gain_first
    )
    d_reduced = [grad.astype(jnp.bfloat16) for grad in d_reduced_f]
    reduce_grad = jnp.einsum(
        "pc,pm->cm", flat_inputs[0], d_reduced[0], preferred_element_type=jnp.float32
    ) + jnp.einsum("pc,pm->cm", flat_inputs[1], d_reduced[1], preferred_element_type=jnp.float32)
    input_grads = [
        (
            pre_grad
            + jnp.einsum("pm,cm->pc", grad, weight_reduce, preferred_element_type=jnp.float32)
        ).astype(jnp.bfloat16)
        for pre_grad, grad in zip(d_pre, d_reduced)
    ]
    shares = (
        lax.psum_scatter(reduce_grad, "dp", scatter_dimension=0, tiled=True),
        lax.psum_scatter(gain_first_grad, "dp", scatter_dimension=0, tiled=True),
        lax.psum_scatter(shift_first_grad, "dp", scatter_dimension=0, tiled=True),
        lax.psum_scatter(spatial_grad, "dp", scatter_dimension=2, tiled=True),
        lax.psum_scatter(gain_second_grad, "dp", scatter_dimension=0, tiled=True),
        lax.psum_scatter(shift_second_grad, "dp", scatter_dimension=0, tiled=True),
        lax.psum_scatter(expand_grad, "dp", scatter_dimension=0, tiled=True),
        lax.psum_scatter(gain_third_grad, "dp", scatter_dimension=0, tiled=True),
        lax.psum_scatter(shift_third_grad, "dp", scatter_dimension=0, tiled=True),
    )
    summed = lax.psum(
        (
            shares[0],
            shares[1],
            shares[2],
            shares[3],
            shares[4],
            shares[5],
            shares[6],
            shares[7],
            shares[8],
        ),
        "rows",
    )
    return (
        activation[0].astype(jnp.bfloat16).reshape(views.shape),
        activation[1].astype(jnp.bfloat16).reshape(crops.shape),
        pooled,
        input_grads[0].reshape(views.shape),
        input_grads[1].reshape(crops.shape),
        summed[0],
        summed[1],
        summed[2],
        summed[3],
        summed[4],
        summed[5],
        summed[6],
        summed[7],
        summed[8],
    )


MESH = pl.DeviceIdType.MESH
SEMAPHORES = 159
F32 = jnp.float32
BF16 = jnp.bfloat16
NV = 512
NC = 256
N = NV + NC
KINDS = ((0, NV), (NV, NC))
NT = (((1,), (1,)), ((), ()))
TN = (((0,), (0,)), ((), ()))


def sigmoid(values):
    return 0.5 * jnp.tanh(0.5 * values) + 0.5


def dot(left, right, dims=(((1,), (0,)), ((), ()))):
    return lax.dot_general(left, right, dims, preferred_element_type=F32)


def moved(values, kind, step):
    rows, lanes = values.shape
    if step == 0:
        return values
    if kind == 0:
        maps = values.reshape(rows // 64, 64, lanes)
        gap = jnp.zeros((rows // 64, 8, lanes), values.dtype)
        parts = [gap, maps[:, :-8]] if step > 0 else [maps[:, 8:], gap]
        return jnp.concatenate(parts, axis=1).reshape(rows, lanes)
    gap = jnp.zeros((64, lanes), values.dtype)
    return jnp.concatenate([gap, values[:-64]] if step > 0 else [values[64:], gap], axis=0)


def turned(values, kind, step):
    if step == 0:
        return values
    rows, lanes = values.shape
    width = 8 if kind == 0 else 4
    col = lax.rem(lax.broadcasted_iota(jnp.int32, (rows, lanes), 0), width)
    edge = 0 if step > 0 else width - 1
    return jnp.where(col == edge, 0.0, pltpu.roll(values, 1 if step > 0 else rows - 1, axis=0))


def block_kernel(
    views, crops, w_reduce, w_spatial, w_expand, cot_views, cot_crops, gain_a, shift_a, gain_b, shift_b, gain_c, shift_c,
    out_views, out_crops, fin_p, grad_views, grad_crops, fin_e, fin_s, fin_r, pgs,
    xv, xc4, xc, cv, cc4, cc, wr, ws, we, raw_a, raw_b, raw_c, raw_d, raw_e, raw_f, pg,
    part, csend, crecv, xsend, xrecv,
    act1, act2, dred, conv, xhat1, slope1, xhat2, slope2, ex, dpre, dex, pat, ov, oc, gv, gc, pool, rows_pool,
    ge, gs, gr, ysend_e, yrecv_e, zsend_e, zrecv_e, ysend_s, yrecv_s, zsend_s, zrecv_s, ysend_r, yrecv_r, zsend_r, zrecv_r,
    relay_e, relay_s, relay_r, acc_e, acc_s, acc_r, pgr,
    sem,
):
    i, r = lax.axis_index("dp"), lax.axis_index("rows")
    z, y = i // 2, i % 2
    x, c = r // 2, r % 2
    yp = (i + 1 - 2 * y, r)
    cp = (i, 2 * x + 1 - c)
    xp = (i, 2 * (1 - x) + c)
    xcp = (i, 2 * (1 - x) + 1 - c)
    rest = (xp, xcp, cp)

    middle = (z + 1) // 2 == 1
    step = 1 - 2 * (z // 2)

    def on_line(places):
        return (2 * (z + places * step) + y, r)

    taken = [0]

    def new(count=1):
        taken[0] += count
        return taken[0] - count

    def copy(src, dst, send, recv, dev):
        return pltpu.make_async_remote_copy(
            src_ref=src, dst_ref=dst, send_sem=sem.at[send], recv_sem=sem.at[recv], device_id=dev, device_id_type=MESH
        )

    def got(ref, recv):
        copy(ref, ref, recv, recv, cp).wait_recv()

    def sent(ref, send):
        copy(ref, ref, send, send, cp).wait_send()

    def stored(ref, one):
        pltpu.make_async_copy(ref, ref, sem.at[one]).wait()

    def lanes(k, xx, cc_):
        return pl.ds(pl.multiple_of(512 * k + 256 * cc_ + 128 * xx, 128), 128)

    def kl(k):
        return pl.ds(128 * k, 128)

    def kind_rows(kind):
        return pl.ds(*KINDS[kind])

    def stage(src, dst, one):
        pltpu.make_async_copy(src, dst, sem.at[one]).start()

    l_wr, l_ws, l_we, l_gain = new(), new(), new(), new(6)
    l_x, l_cot = (new(), new()), (new(), new())

    @pl.when(y == c)
    def _():
        stage(w_reduce.at[pl.ds(pl.multiple_of(128 * x, 128), 128)], wr.at[z], l_wr)

    stage(w_spatial.at[:, :, pl.ds(pl.multiple_of(128 * r, 128), 128)], ws.at[:, i], l_ws)
    raw = (raw_a, raw_b, raw_c, raw_d, raw_e, raw_f)
    for n, vec in enumerate((gain_a, shift_a, gain_b, shift_b, gain_c, shift_c)):
        stage(vec, raw[n], l_gain + n)
    for k in range(4):
        stage(views.at[:, :, lanes(k, x, c)], xv.at[:, r, :, kl(k)], l_x[0])
        stage(crops.at[:, :, lanes(k, x, c)], xc4.at[r, :, :, kl(k)], l_x[1])
    for k in range(4):
        stage(w_expand.at[:, lanes(k, x, c)], we.at[i, :, kl(k)], l_we)
    for k in range(4):
        stage(cot_views.at[:, :, lanes(k, x, c)], cv.at[:, r, :, kl(k)], l_cot[0])
        stage(cot_crops.at[:, :, lanes(k, x, c)], cc4.at[r, :, :, kl(k)], l_cot[1])

    bar = pltpu.get_barrier_semaphore()
    peers = [((i + n) % 8, r) for n in range(1, 8)] + [cp, xp, xcp]
    for dev in peers:
        pl.semaphore_signal(bar, inc=1, device_id=dev, device_id_type=MESH)
    pl.semaphore_wait(bar, len(peers))

    class Share:
        def __init__(self, parts, others):
            self.parts, self.others = parts, others
            count = len(parts(0))
            self.send = new()
            self.along_z = [new(3) for _ in range(count)]
            self.along_y = [new() for _ in range(count)]

    share_r = Share(lambda k: (wr.at[k],), None)
    share_s = Share(
        lambda k: tuple(ws.at[pl.ds(3 * h, 3), 2 * k + y] for h in range(3)),
        lambda h: ws.at[pl.ds(3 * h, 3), pl.ds(0, 4)],
    )
    share_e = Share(lambda k: (we.at[2 * k + y],), lambda h: we.at[pl.ds(0, 4)])
    passed_r = new()

    inner = ((z + 1) // 2) * (2 - (z + 1) // 2)

    def line_send(share):
        for h, own in enumerate(share.parts(z)):

            def go(slot, dev, own=own):
                copy(own, own, share.send, slot, dev).start()

            go(share.along_z[h], on_line(2))
            go(share.along_z[h] + 2 - inner, on_line(1))

            @pl.when(middle)
            def _(go=go, h=h):
                go(share.along_z[h] + 1, on_line(-1))

            go(share.along_y[h], yp)

    def line_pass(share, h, send=None):
        send = share.send if send is None else send

        def take(places, slot, on=False):
            ref = share.parts(z + places * step)[h]
            got(ref, share.along_z[h] + slot)
            if on:
                copy(ref, ref, send, share.along_z[h] + 2, on_line(-1)).start()
            copy(ref, ref, send, share.along_y[h], yp).start()

        @pl.when(middle)
        def _():
            take(2, 0, True)
            take(1, 1)
            take(-1, 2)

        @pl.when(jnp.logical_not(middle))
        def _():
            take(2, 0)
            take(1, 1)
            take(3, 2)

    def line_got(share):
        for h, slot in enumerate(share.along_y):
            got(share.others(h), slot)

    def line_sent(send, for_middle, for_end):
        @pl.when(middle)
        def _():
            sent(for_middle, send)

        @pl.when(jnp.logical_not(middle))
        def _():
            sent(for_end, send)

    @pl.when(y == c)
    def _():
        stored(wr.at[z], l_wr)
        line_send(share_r)

    s_sx, s_rx = ((new(), new()), (new(), new())), ((new(), new()), (new(), new()))

    def spread_v(src, dst, s, devs):
        for dev in devs:
            for k in range(4):
                copy(src.at[:, :, lanes(k, dev[1] // 2, dev[1] % 2)], dst.at[:, r, :, kl(k)], s_sx[s][0], s_rx[s][0], dev).start()

    def spread_c(src, dst, s, devs):
        for dev in devs:
            for k in range(4):
                copy(src.at[:, :, lanes(k, dev[1] // 2, dev[1] % 2)], dst.at[r, :, :, kl(k)], s_sx[s][1], s_rx[s][1], dev).start()

    spread_v(views, xv, 0, rest)
    spread_c(crops, xc4, 0, rest)
    spread_v(cot_views, cv, 1, rest[:1])

    for n in range(6):
        stored(raw[n], l_gain + n)
    pg[i] = jnp.zeros((8, 128), F32)
    for n in range(4):
        vec = raw[n][...].reshape(1, 64).astype(F32)
        pg[i, n : n + 1, :] = jnp.concatenate([vec, vec], axis=1)
    for n in range(2):
        for m in range(2):
            pg[i, 4 + 2 * n + m : 5 + 2 * n + m, :] = raw[4 + n][128 * m : 128 * m + 128].reshape(1, 128).astype(F32)
    s_pg, r_pg = new(), new()
    for dev in peers[:7]:
        copy(pg.at[i], pg.at[i], s_pg, r_pg, dev).start()

    @pl.when(y == c)
    def _():
        line_pass(share_r, 0, passed_r)

    stored(xv.at[:, r], l_x[0])
    got(xv.at[:, pl.ds(0, 3)], s_rx[0][0])
    stored(ws.at[:, i], l_ws)
    line_send(share_s)

    @pl.when(y != c)
    def _():
        got(wr, share_r.along_y[0])

    s_cs, r_cs = new(3), new(12)
    s_xs, r_xs = new(3), new(6)
    s_ag, r_ag = new(3), new(12)

    def scatter_start(op, kind, sums):
        rows = kind_rows(kind)
        n = pl.ds(0, KINDS[kind][1])
        for s in range(4):
            part[op, s, rows, :] = sums[:, 128 * s : 128 * s + 128]
        for near, xx in enumerate((1 - x, x)):
            csend[op, kind, xx, n, :] = part[op, 2 * xx + 1 - c, rows, :].astype(BF16)
            own = csend.at[op, kind, xx, n]
            copy(own, crecv.at[op, kind, xx, n], s_cs + op, r_cs + 4 * op + 2 * kind + near, cp).start()

    def scatter_mid(op, kind):
        rows = kind_rows(kind)
        n = pl.ds(0, KINDS[kind][1])
        got(crecv.at[op, kind, 1 - x, n], r_cs + 4 * op + 2 * kind)
        far = part[op, 2 * (1 - x) + c, rows, :] + crecv[op, kind, 1 - x, n, :].astype(F32)
        xsend[op, kind, n, :] = far.astype(BF16)
        copy(xsend.at[op, kind, n], xrecv.at[op, kind, n], s_xs + op, r_xs + 2 * op + kind, xp).start()

    def scatter_end(op, kind):
        rows = kind_rows(kind)
        n = pl.ds(0, KINDS[kind][1])
        got(crecv.at[op, kind, x, n], r_cs + 4 * op + 2 * kind + 1)
        near = part[op, 2 * x + c, rows, :] + crecv[op, kind, x, n, :].astype(F32)
        got(xrecv.at[op, kind, n], r_xs + 2 * op + kind)
        return near + xrecv[op, kind, n, :].astype(F32)

    def gather_start(op, kind, buf, value):
        rows = kind_rows(kind)
        buf[r, rows, :] = value
        own = buf.at[r, rows]
        copy(own, own, s_ag + op, r_ag + 4 * op + 2 * kind, xp).start()
        copy(own, own, s_ag + op, r_ag + 4 * op + 2 * kind + 1, cp).start()

    def gather_mid(op, kind, buf):
        far = buf.at[xp[1], kind_rows(kind)]
        got(far, r_ag + 4 * op + 2 * kind)
        copy(far, far, s_ag + op, r_ag + 4 * op + 2 * kind + 1, cp).start()

    def gather_end(op, kind, buf):
        rows = kind_rows(kind)
        got(buf.at[pl.ds(0, 2), rows], r_ag + 4 * op + 2 * kind + 1)
        return jnp.concatenate([buf[s, rows, :] for s in range(4)], axis=1)

    weight_r = wr[...].reshape(512, 512)
    scatter_start(0, 0, dot(xv[...].reshape(NV, 512), weight_r))
    stored(xc4.at[r], l_x[1])
    got(xc4.at[pl.ds(0, 3)], s_rx[0][1])
    xc[...] = xc4[...].reshape(4, 64, 512)
    scatter_start(0, 1, dot(xc[...].reshape(NC, 512), weight_r))
    scatter_mid(0, 0)
    scatter_mid(0, 1)
    spread_c(cot_crops, cc4, 1, rest[:1])

    got(pg.at[pl.ds(0, 7)], r_pg)
    half = lax.broadcasted_iota(jnp.int32, (1, 128), 1) < 64
    gain1, shift1, gain2, shift2 = [
        jnp.where(half, pg[2 * r, q : q + 1, :], pg[2 * r + 1, q : q + 1, :]) for q in range(4)
    ]
    gain3 = jnp.concatenate([pg[2 * k + c, pl.ds(4 + x, 1), :] for k in range(4)], axis=1)
    shift3 = jnp.concatenate([pg[2 * k + c, pl.ds(6 + x, 1), :] for k in range(4)], axis=1)

    def norm_act(values, rows, gain, shift):
        mean = jnp.sum(values, axis=0, keepdims=True) / rows
        second = jnp.sum(values * values, axis=0, keepdims=True) / rows
        rstd = lax.rsqrt(second - mean * mean + EPSILON)
        xhat = (values - mean) * rstd
        norm = gain * xhat + shift
        sig = sigmoid(norm)
        return rstd, xhat, sig * (1.0 + norm * (1.0 - sig)), (norm * sig).astype(BF16)

    line_pass(share_s, 0)
    line_pass(share_s, 1)
    rstd1, rstd2 = [None, None], [None, None]
    for kind in range(2):
        rows = KINDS[kind][1]
        rstd1[kind], xh, sl, act = norm_act(scatter_end(0, kind), rows, gain1, shift1)
        gather_start(0, kind, act1, act)
        xhat1[kind_rows(kind), :] = xh
        slope1[kind_rows(kind), :] = sl
    spread_v(cot_views, cv, 1, rest[1:])
    spread_c(cot_crops, cc4, 1, rest[1:])
    line_pass(share_s, 2)
    stored(we.at[i], l_we)
    line_send(share_e)
    for kind in range(2):
        gather_mid(0, kind, act1)
    line_got(share_s)
    line_pass(share_e, 0)

    def weight_s():
        return jnp.concatenate([ws[t].reshape(512, 128) for t in range(9)], axis=1)

    for kind in range(2):
        rows = KINDS[kind][1]
        conv[kind_rows(kind), :] = dot(gather_end(0, kind, act1), weight_s())
        taps = [conv[kind_rows(kind), 128 * t : 128 * t + 128] for t in range(9)]
        spatial = None
        for j in range(3):
            col = taps[3 + j] + moved(taps[j], kind, 1) + moved(taps[6 + j], kind, -1)
            col = turned(col, kind, 1 - j)
            spatial = col if spatial is None else spatial + col
        rstd2[kind], xh, sl, act = norm_act(spatial, rows, gain2, shift2)
        gather_start(1, kind, act2, act)
        xhat2[kind_rows(kind), :] = xh
        slope2[kind_rows(kind), :] = sl
    pool[...] = jnp.zeros_like(pool)
    for kind in range(2):
        gather_mid(1, kind, act2)
    stored(cv.at[:, r], l_cot[0])
    stored(cc4.at[r], l_cot[1])
    got(cv.at[:, pl.ds(0, 3)], s_rx[1][0])
    got(cc4.at[pl.ds(0, 3)], s_rx[1][1])
    cc[...] = cc4[...].reshape(4, 64, 512)
    line_got(share_e)
    weight_e = we[...].reshape(512, 512)

    sum_x3, sum_d3 = [], []
    zero8 = jnp.zeros((8, 512), F32)

    def expand(kind):
        start, rows = KINDS[kind]
        ex[kind_rows(kind), :] = dot(gather_end(1, kind, act2), weight_e)

        def moments(b, acc):
            e = ex[pl.ds(pl.multiple_of(start + 32 * b, 32), 32), :].reshape(4, 8, 512)
            return acc[0] + jnp.sum(e, axis=0), acc[1] + jnp.sum(e * e, axis=0)

        tot, sq = lax.fori_loop(0, rows // 32, moments, (zero8, zero8))
        mean = jnp.sum(tot, axis=0, keepdims=True) / rows
        rstd = lax.rsqrt(jnp.sum(sq, axis=0, keepdims=True) / rows - mean * mean + EPSILON)

        def finish(b, acc):
            rs = pl.ds(pl.multiple_of(start + 16 * b, 16), 16)
            qs = pl.ds(pl.multiple_of(16 * (b % 4), 16), 16)
            xhat = (ex[rs, :] - mean) * rstd
            ex[rs, :] = xhat
            src = xv[b // 4, b % 4] if kind == 0 else xc[b // 4, qs, :]
            cot = cv[b // 4, b % 4] if kind == 0 else cc[b // 4, qs, :]
            pre = src.astype(F32) + (gain3 * xhat + shift3)
            sig = sigmoid(pre)
            activation = pre * sig
            d = cot.astype(F32) * (sig * (1.0 + pre * (1.0 - sig)))
            dpre[rs, :] = d
            if kind == 0:
                ov[b // 4, b % 4] = activation.astype(BF16)
                pool[b // 4] += activation[:8] + activation[8:]
            else:
                oc[b // 4, qs, :] = activation.astype(BF16)
                pool[8 + 2 * (b % 4)] += activation[:8]
                pool[9 + 2 * (b % 4)] += activation[8:]
            dx = d * xhat
            return acc[0] + (d[:8] + d[8:]), acc[1] + (dx[:8] + dx[8:])

        sd, sxx = lax.fori_loop(0, rows // 16, finish, (zero8, zero8))
        sd, sxx = jnp.sum(sd, axis=0, keepdims=True), jnp.sum(sxx, axis=0, keepdims=True)
        sum_d3.append(sd)
        sum_x3.append(sxx)
        scale = gain3 * rstd
        mean_d, mean_x = sd / rows, sxx / rows

        def back(b, _):
            rs = pl.ds(pl.multiple_of(start + 32 * b, 32), 32)
            dex[rs, :] = (scale * (dpre[rs, :] - mean_d - ex[rs, :] * mean_x)).astype(BF16)
            return 0

        lax.fori_loop(0, rows // 32, back, 0)

    s_out, r_out = ((new(), new()), (new(), new())), ((new(), new()), (new(), new()))
    l_out = ((new(), new()), (new(), new()))

    def hand_v(src, dst, s, devs):
        for dev in devs:
            for k in range(4):
                copy(src.at[:, dev[1], :, kl(k)], dst.at[:, :, lanes(k, x, c)], s_out[s][0], r_out[s][0], dev).start()

    def hand_c(src, dst, s, devs):
        for dev in devs:
            for k in range(4):
                copy(src.at[dev[1], :, kl(k)], dst.at[:, lanes(k, x, c)], s_out[s][1], r_out[s][1], dev).start()

    def hand_own(src_v, src_c, dst_v, dst_c, s):
        for k in range(4):
            stage(src_v.at[:, r, :, kl(k)], dst_v.at[:, :, lanes(k, x, c)], l_out[s][0])
            stage(src_c.at[r, :, kl(k)], dst_c.at[:, lanes(k, x, c)], l_out[s][1])

    def handed(src_v, src_c, dst_v, dst_c, s):
        stored(src_v.at[:, 0], l_out[s][0])
        stored(src_c.at[0], l_out[s][1])
        sent(src_v.at[:, pl.ds(0, 3)], s_out[s][0])
        sent(src_c.at[pl.ds(0, 3)], s_out[s][1])
        got(dst_v.at[:, :, pl.ds(0, 1536)], r_out[s][0])
        got(dst_c.at[:, pl.ds(0, 1536)], r_out[s][1])

    far_of = jnp.where(middle, z + 2 * step, z + 3 * step)
    mid_of = jnp.where(middle, z - step, z + 2 * step)
    order = [far_of, mid_of, z + step, z]

    class Grad:
        def __init__(self, full, ysend, yrecv, zsend, zrecv, relay, acc, both=True):
            self.full, self.ysend, self.yrecv, self.zsend, self.zrecv = full, ysend, yrecv, zsend, zrecv
            self.relay, self.acc, self.both = relay, acc, both
            self.s_y, self.r_y, self.s_z, self.r_z, self.r_relay = new(), new(4), new(), new(), new()

        def start(self):
            for k in order:
                self.ysend[k] = (self.full[k, 1 - y] if self.both else self.full[k]).astype(BF16)
                copy(self.ysend.at[k], self.yrecv.at[k], self.s_y, self.r_y + k, yp).start()

        def add(self, k):
            got(self.yrecv.at[k], self.r_y + k)
            return (self.full[k, y] if self.both else self.full[k]) + self.yrecv[k].astype(F32)

        def send(self, k, value):
            self.zsend[k] = value.astype(BF16)
            copy(self.zsend.at[k], self.zrecv.at[z], self.s_z, self.r_z, (2 * k + y, r)).start()

        def along(self):
            @pl.when(jnp.logical_not(middle))
            def _():
                k = order[0]
                self.zsend[k] = self.add(k).astype(BF16)
                copy(self.zsend.at[k], self.relay, self.s_z, self.r_relay, on_line(1)).start()

            self.send(order[1], self.add(order[1]))
            self.send(order[2], self.add(order[2]))

        def hand_on(self):
            @pl.when(middle)
            def _():
                total = self.add(order[0])
                got(self.relay, self.r_relay)
                self.send(order[0], total + self.relay[...].astype(F32))

        def total(self):
            self.acc[...] = self.add(z)

            @pl.when(middle)
            def _():
                got(self.zrecv.at[pl.ds(0, 3)], self.r_z)
                self.acc[...] += self.zrecv[z - step].astype(F32)

            @pl.when(jnp.logical_not(middle))
            def _():
                got(self.zrecv.at[pl.ds(0, 2)], self.r_z)

            return self.acc[...] + self.zrecv[z + step].astype(F32) + self.zrecv[z + 2 * step].astype(F32)

        def sent(self):
            sent(self.zsend.at[pl.ds(0, 3)], self.s_z)

    class Slices:
        def __init__(self, buf):
            self.buf, self.send, self.far, self.near = buf, new(), new(), new()

        def start(self, value):
            self.buf[r] = value.astype(BF16)
            copy(self.buf.at[r], self.buf.at[r], self.send, self.far, xp).start()
            copy(self.buf.at[r], self.buf.at[r], self.send, self.near, cp).start()

        def mid(self):
            far = self.buf.at[xp[1]]
            got(far, self.far)
            copy(far, far, self.send, self.near, cp).start()

        def end(self):
            got(self.buf.at[pl.ds(0, 2)], self.near)
            sent(self.buf.at[pl.ds(0, 3)], self.send)

    grad_e = Grad(ge, ysend_e, yrecv_e, zsend_e, zrecv_e, relay_e, acc_e)
    grad_s = [
        Grad(*(one.at[q] for one in (gs, ysend_s, yrecv_s, zsend_s, zrecv_s, relay_s, acc_s))) for q in range(3)
    ]
    grad_r = Grad(gr, ysend_r, yrecv_r, zsend_r, zrecv_r, relay_r, acc_r, False)
    slices_p, slices_e, slices_s = Slices(fin_p), Slices(fin_e), [Slices(fin_s.at[q]) for q in range(3)]

    expand(0)
    scatter_start(1, 0, dot(dex[kind_rows(0), :], weight_e, NT))
    expand(1)
    scatter_mid(1, 0)
    scatter_start(1, 1, dot(dex[kind_rows(1), :], weight_e, NT))
    ge[...] = dot(jnp.concatenate([act2[s] for s in range(4)], axis=1), dex[...], TN).reshape(4, 2, 64, 512)
    grad_e.start()
    scatter_mid(1, 1)
    hand_v(ov, out_views, 0, rest[:1])
    hand_own(ov, oc, out_views, out_crops, 0)
    hand_v(ov, out_views, 0, rest[2:])
    hand_c(oc, out_crops, 0, rest[2:])

    def norm_back(d, xhat, rstd, gain, rows):
        sd = jnp.sum(d, axis=0, keepdims=True)
        sxx = jnp.sum(d * xhat, axis=0, keepdims=True)
        return (gain * rstd) * (d - sd / rows - xhat * (sxx / rows)), sd, sxx

    sum_d2, sum_x2 = [], []
    for kind in range(2):
        rows = KINDS[kind][1]
        d = scatter_end(1, kind) * slope2[kind_rows(kind), :]
        dz_, sd, sxx = norm_back(d, xhat2[kind_rows(kind), :], rstd2[kind], gain2, rows)
        sum_d2.append(sd)
        sum_x2.append(sxx)
        dz_ = dz_.astype(BF16).astype(F32)
        for tj in range(3):
            col = turned(dz_, kind, tj - 1)
            for ti in range(3):
                t = 3 * ti + tj
                pat[kind_rows(kind), 128 * t : 128 * t + 128] = moved(col, kind, ti - 1).astype(BF16)
        scatter_start(2, kind, dot(pat[kind_rows(kind), :], weight_s(), NT))
        if kind == 1:
            scatter_mid(2, 0)
    scatter_mid(2, 1)
    hand_c(oc, out_crops, 0, rest[:1])
    full1 = jnp.concatenate([act1[s] for s in range(4)], axis=1)
    for q in range(3):
        gs[q] = dot(full1, pat[:, 384 * q : 384 * q + 384], TN).reshape(4, 2, 64, 384)
        grad_s[q].start()
    grad_e.along()
    grad_e.hand_on()

    sum_d1, sum_x1 = [], []
    for kind in range(2):
        rows = KINDS[kind][1]
        d = scatter_end(2, kind) * slope1[kind_rows(kind), :]
        dz_, sd, sxx = norm_back(d, xhat1[kind_rows(kind), :], rstd1[kind], gain1, rows)
        sum_d1.append(sd)
        sum_x1.append(sxx)
        gather_start(2, kind, dred, dz_.astype(BF16))

    rows12 = [sum_x1[0] + sum_x1[1], sum_d1[0] + sum_d1[1], sum_x2[0] + sum_x2[1], sum_d2[0] + sum_d2[1]]
    gx3, gd3 = sum_x3[0] + sum_x3[1], sum_d3[0] + sum_d3[1]
    rows3 = [g[:, 128 * k : 128 * k + 128] for g in (gx3, gd3) for k in range(4)]
    pgr[i] = jnp.concatenate(rows12 + rows3 + [jnp.zeros((4, 128), F32)], axis=0)
    s_pp, r_pp, s_ps, r_ps = new(), new(), new(), new()
    for dev in peers[:7]:
        copy(pgr.at[i], pgr.at[i], s_pp, r_pp, dev).start()
    hand_v(ov, out_views, 0, rest[1:2])
    hand_c(oc, out_crops, 0, rest[1:2])

    rows_pool[...] = jnp.zeros_like(rows_pool)
    for n in range(8):
        row = 4 * (n % 2) + n // 2
        rows_pool[row : row + 1, :] = jnp.sum(pool[n], axis=0, keepdims=True) / 64.0
        for m in range(2):
            row = 4 * (2 + 2 * (n % 2) + m) + n // 2
            rows_pool[row : row + 1, :] = jnp.sum(pool[8 + n, 4 * m : 4 * m + 4, :], axis=0, keepdims=True) / 16.0
    slices_p.start(rows_pool[...])
    grad_s[0].along()
    gather_mid(2, 0, dred)
    grad_s[1].along()
    gather_mid(2, 1, dred)
    grad_s[0].hand_on()
    full_d = [gather_end(2, kind, dred) for kind in range(2)]

    for m in range(4):
        col = dot(xv[:, :, :, 128 * m : 128 * m + 128].reshape(NV, 128), full_d[0], TN)
        gr[m] = col + dot(xc[:, :, 128 * m : 128 * m + 128].reshape(NC, 128), full_d[1], TN)

    @pl.when(y != c)
    def _():
        grad_r.start()

    gv[...] = (dpre[kind_rows(0), :] + dot(full_d[0], weight_r, NT)).astype(BF16).reshape(8, 4, 16, 512)
    hand_v(gv, grad_views, 1, rest)
    gc[...] = (dpre[kind_rows(1), :] + dot(full_d[1], weight_r, NT)).astype(BF16).reshape(4, 64, 512)
    hand_c(gc, grad_crops, 1, rest)
    hand_own(gv, gc, grad_views, grad_crops, 1)
    grad_s[2].along()
    grad_s[1].hand_on()
    slices_e.start(grad_e.total())
    slices_p.mid()
    grad_s[2].hand_on()
    slices_s[0].start(grad_s[0].total())

    @pl.when(y == c)
    def _():
        grad_r.along()

    slices_s[1].start(grad_s[1].total())
    slices_e.mid()

    @pl.when(y == c)
    def _():
        grad_r.hand_on()

    slices_s[2].start(grad_s[2].total())
    slices_s[0].mid()

    got(pgr.at[pl.ds(0, 7)], r_pp)
    total = pgr[0]
    for n in range(1, 8):
        total = total + pgr[n]
    pgs[r] = total
    for dev in rest:
        copy(pgs.at[r], pgs.at[r], s_ps, r_ps, dev).start()
    slices_s[1].mid()

    s_fr, r_fr = new(), new()

    @pl.when(y == c)
    def _():
        fin_r[x] = grad_r.total().astype(BF16)
        copy(fin_r.at[x], fin_r.at[x], s_fr, r_fr, xp).start()
        copy(fin_r.at[x], fin_r.at[x], s_fr, r_fr, cp).start()

    slices_s[2].mid()

    @pl.when(y == c)
    def _():
        far = fin_r.at[1 - x]
        got(far, r_fr)
        copy(far, far, s_fr, r_fr, cp).start()

    for one in (slices_p, slices_e, *slices_s):
        one.end()
    got(pgs.at[pl.ds(0, 3)], r_ps)
    handed(ov, oc, out_views, out_crops, 0)
    handed(gv, gc, grad_views, grad_crops, 1)
    for s, (own_v, own_c) in enumerate(((xv, xc4), (cv, cc4))):
        sent(own_v.at[:, pl.ds(0, 3)], s_sx[s][0])
        sent(own_c.at[pl.ds(0, 3)], s_sx[s][1])
    sent(pg.at[pl.ds(0, 7)], s_pg)
    sent(pgr.at[pl.ds(0, 7)], s_pp)
    sent(pgs.at[pl.ds(0, 3)], s_ps)
    line_sent(share_s.send, ws, ws.at[:, pl.ds(0, 6)])
    line_sent(share_e.send, we, we.at[pl.ds(0, 6)])
    for op in range(3):
        sent(act1.at[pl.ds(0, 2)], s_cs + op)
        sent(act1.at[0], s_xs + op)
        sent(act1.at[pl.ds(0, 3)], s_ag + op)
    for one in (grad_e, *grad_s):
        sent(one.ysend, one.s_y)
        one.sent()

    @pl.when(y != c)
    def _():
        sent(ysend_r, grad_r.s_y)
        got(fin_r, r_fr)

    @pl.when(y == c)
    def _():
        line_sent(share_r.send, wr, wr.at[pl.ds(0, 3)])
        line_sent(passed_r, wr, wr.at[pl.ds(0, 3)])
        grad_r.sent()
        sent(wr.at[pl.ds(0, 3)], s_fr)

    assert taken[0] == SEMAPHORES, taken


def store_kernel(
    out_v, out_c, pool, grad_v, grad_c, fin_e, fin_s, fin_r, sums,
    out_views, out_crops, pooled, grad_views, grad_crops, grad_reduce, grad_spatial, grad_expand,
    gain_a, shift_a, gain_b, shift_b, gain_c, shift_c,
    oc, pl_, gc, gr, gs, ge, sem,
):
    i = lax.axis_index("dp")
    z, y = i // 2, i % 2
    copies = []

    def store(src, dst):
        one = pltpu.make_async_copy(src, dst, sem.at[len(copies)])
        one.start()
        copies.append(one)

    store(out_v, out_views)
    store(grad_v, grad_views)
    for s in range(4):
        for t in range(9):
            gs[t, :, 128 * s : 128 * s + 128] = fin_s[t // 3, s, :, 128 * (t % 3) : 128 * (t % 3) + 128].astype(F32)
    store(gs, grad_spatial)
    for s in range(4):
        for k in range(4):
            lo = 512 * k + 256 * (s % 2) + 128 * (s // 2)
            ge[:, lo : lo + 128] = fin_e[s, :, 128 * k : 128 * k + 128].astype(F32)
    store(ge, grad_expand)
    gr[...] = fin_r[...].astype(F32).reshape(256, 512)
    store(gr, grad_reduce)
    oc[...] = out_c[...].reshape(16, 4, 2048)
    store(oc, out_crops)
    gc[...] = grad_c[...].reshape(16, 4, 2048)
    store(gc, grad_crops)
    for s in range(4):
        for k in range(4):
            lo = 512 * k + 256 * (s % 2) + 128 * (s // 2)
            pl_[:, :, lo : lo + 128] = pool[s, 0:24, 128 * k : 128 * k + 128].astype(F32).reshape(6, 4, 128)
    store(pl_, pooled)
    for n, out in enumerate((gain_a, shift_a, gain_b, shift_b)):
        row = sums[i // 2, n : n + 1, :]
        out[...] = jnp.where(i % 2 == 0, row[:, :64], row[:, 64:]).reshape(64)
    for n, out in enumerate((gain_c, shift_c)):
        out[...] = jnp.concatenate([sums[2 * m + y, pl.ds(4 + 4 * n + z, 1), :] for m in range(2)], axis=1).reshape(256)
    for one in copies:
        one.wait()


def fused(views, crops, w_reduce, w_spatial, w_expand, cot_views, cot_crops, *params):
    hbm, vmem = pl.BlockSpec(memory_space=pltpu.HBM), pl.BlockSpec(memory_space=pltpu.VMEM)

    def shape(dims, dtype):
        return jax.ShapeDtypeStruct(dims, dtype)

    def buf(dims, dtype=BF16):
        return pltpu.VMEM(dims, dtype)

    def dma(*dims):
        return pltpu.SemaphoreType.DMA(dims)

    held = pl.pallas_call(
        block_kernel,
        out_shape=[
            buf((8, 16, 2048)), buf((64, 2048)), buf((4, 32, 512)), buf((8, 16, 2048)), buf((64, 2048)),
            buf((4, 64, 512)), buf((3, 4, 64, 384)), buf((2, 128, 512)), buf((4, 16, 128), F32),
        ],
        in_specs=[hbm] * 13,
        out_specs=[vmem] * 9,
        scratch_shapes=[
            buf((8, 4, 16, 512)), buf((4, 16, 4, 512)), buf((4, 64, 512)),
            buf((8, 4, 16, 512)), buf((4, 16, 4, 512)), buf((4, 64, 512)),
            buf((4, 128, 512)), buf((9, 8, 64, 128)), buf((8, 64, 512)), buf((64,)), buf((64,)), buf((64,)), buf((64,)), buf((256,)), buf((256,)), buf((8, 8, 128), F32),
            buf((3, 4, N, 128), F32), buf((3, 2, 2, NV, 128)), buf((3, 2, 2, NV, 128)),
            buf((3, 2, NV, 128)), buf((3, 2, NV, 128)),
            buf((4, N, 128)), buf((4, N, 128)), buf((4, N, 128)), buf((N, 1152), F32),
            buf((N, 128), F32), buf((N, 128), F32), buf((N, 128), F32), buf((N, 128), F32),
            buf((N, 512), F32), buf((N, 512), F32), buf((N, 512)), buf((N, 1152)),
            buf((8, 4, 16, 512)), buf((4, 64, 512)), buf((8, 4, 16, 512)), buf((4, 64, 512)),
            buf((16, 8, 512), F32), buf((32, 512), F32),
            buf((4, 2, 64, 512), F32), buf((3, 4, 2, 64, 384), F32), buf((4, 128, 512), F32),
            buf((4, 64, 512)), buf((4, 64, 512)), buf((4, 64, 512)), buf((4, 64, 512)),
            buf((3, 4, 64, 384)), buf((3, 4, 64, 384)), buf((3, 4, 64, 384)), buf((3, 4, 64, 384)),
            buf((4, 128, 512)), buf((4, 128, 512)), buf((4, 128, 512)), buf((4, 128, 512)),
            buf((64, 512)), buf((3, 64, 384)), buf((128, 512)), buf((64, 512), F32), buf((3, 64, 384), F32), buf((128, 512), F32),
            buf((8, 16, 128), F32),
            dma(SEMAPHORES),
        ],
        compiler_params=pltpu.CompilerParams(collective_id=0, has_side_effects=True, vmem_limit_bytes=58 << 20),
        cost_estimate=pl.CostEstimate(flops=5_200_000_000, bytes_accessed=8_000_000, transcendentals=2_000_000),
    )(views, crops, w_reduce, w_spatial, w_expand, cot_views, cot_crops, *params)
    held = [pltpu.with_memory_space_constraint(one, pltpu.VMEM) for one in held]
    return pl.pallas_call(
        store_kernel,
        out_shape=[
            shape((8, 16, 2048), BF16), shape((16, 4, 2048), BF16), shape((6, 4, 2048), F32),
            shape((8, 16, 2048), BF16), shape((16, 4, 2048), BF16),
            shape((256, 512), F32), shape((9, 64, 512), F32), shape((64, 2048), F32),
            shape((64,), F32), shape((64,), F32), shape((64,), F32), shape((64,), F32), shape((256,), F32), shape((256,), F32),
        ],
        in_specs=[vmem] * 9,
        out_specs=[hbm] * 8 + [vmem] * 6,
        scratch_shapes=[
            buf((16, 4, 2048)), buf((6, 4, 2048), F32), buf((16, 4, 2048)),
            buf((256, 512), F32), buf((9, 64, 512), F32), buf((64, 2048), F32), dma(8),
        ],
        compiler_params=pltpu.CompilerParams(vmem_limit_bytes=16 << 20),
    )(*held)


def step(
    dp, rows, views, crops, w_reduce, gain_one, shift_one, w_spatial, gain_two, shift_two, w_expand, gain_three, shift_three,
    cot_views, cot_crops,
):
    args = (
        views, crops, w_reduce, gain_one, shift_one, w_spatial, gain_two, shift_two, w_expand, gain_three, shift_three,
        cot_views, cot_crops,
    )
    if (dp, rows) != (8, 4) or views.shape != (4, 2, 2, 8, 2048) or crops.shape != (4, 4, 1, 4, 2048):
        return body(*args)
    out_v, out_c, pooled, grad_v, grad_c, grad_r, grad_s, grad_e, ga, sa, gb, sb, gc, sc = fused(
        views.reshape(8, 16, 2048), crops.reshape(16, 4, 2048), w_reduce, w_spatial.reshape(9, 64, 512), w_expand,
        cot_views.reshape(8, 16, 2048), cot_crops.reshape(16, 4, 2048),
        gain_one, shift_one, gain_two, shift_two, gain_three, shift_three,
    )
    return (
        out_v.reshape(views.shape),
        out_c.reshape(crops.shape),
        jnp.transpose(pooled, (1, 0, 2)),
        grad_v.reshape(views.shape),
        grad_c.reshape(crops.shape),
        grad_r,
        ga,
        sa,
        grad_s.reshape(w_spatial.shape[:3] + (512,)),
        gb,
        sb,
        grad_e,
        gc,
        sc,
    )


def solution(mesh):
    return jax.shard_map(
        functools.partial(step, mesh.shape["dp"], mesh.shape["rows"]),
        mesh=mesh,
        in_specs=(
            P("dp", None, "rows", None, None),
            P("dp", None, "rows", None, None),
            P("dp", None),
            P("dp"),
            P("dp"),
            P(None, None, "dp", None),
            P("dp"),
            P("dp"),
            P("dp", None),
            P("dp"),
            P("dp"),
            P("dp", None, "rows", None, None),
            P("dp", None, "rows", None, None),
        ),
        out_specs=(
            P("dp", None, "rows", None, None),
            P("dp", None, "rows", None, None),
            P("dp", None, None),
            P("dp", None, "rows", None, None),
            P("dp", None, "rows", None, None),
            P("dp", None),
            P("dp"),
            P("dp"),
            P(None, None, "dp", None),
            P("dp"),
            P("dp"),
            P("dp", None),
            P("dp"),
            P("dp"),
        ),
        check_vma=False,
    )
```

```python
import functools

import jax
import jax.numpy as jnp
from jax import lax
from jax.experimental import pallas as pl
from jax.experimental.pallas import tpu as pltpu
from jax.sharding import PartitionSpec as P

EPSILON = 1e-05


def extended(cells, sides, width):
    for axis, dim in sides:
        count = lax.axis_size(axis)
        ends = count - 1
        head = lax.slice_in_dim(cells, 0, width, axis=dim)
        tail = lax.slice_in_dim(cells, cells.shape[dim] - width, cells.shape[dim], axis=dim)
        cells = jnp.concatenate(
            [
                lax.ppermute(tail, axis, [(i, (i + 1) % count) for i in range(ends)]),
                cells,
                lax.ppermute(head, axis, [((i + 1) % count, i) for i in range(ends)]),
            ],
            axis=dim,
        )
    return cells


def silu_slope(values):
    sigmoid_val = jax.nn.sigmoid(values)
    return sigmoid_val * (1.0 + values * (1.0 - sigmoid_val))


def standardize(reduced_pair, gain_vec, shift_vec):
    left_map = reduced_pair[0]
    right_map = reduced_pair[1]
    totals = lax.psum(
        (
            jnp.sum(left_map, 0),
            jnp.sum(left_map * left_map, 0),
            jnp.sum(right_map, 0),
            jnp.sum(right_map * right_map, 0),
        ),
        "rows",
    )
    results = []
    for member in range(2):
        values = reduced_pair[member]
        pixel_count = values.shape[0] * lax.axis_size("rows")
        channel_mean = totals[2 * member] / pixel_count
        inverse_scale = lax.rsqrt(
            totals[2 * member + 1] / pixel_count - channel_mean * channel_mean + EPSILON
        )
        centred = (values - channel_mean) * inverse_scale
        results.append((centred, inverse_scale, gain_vec * centred + shift_vec))
    return results


def unstandardize(slopes, saved, gain_vec):
    shift_left = jnp.sum(slopes[0], 0)
    gain_left = jnp.sum(slopes[0] * saved[0][0], 0)
    shift_right = jnp.sum(slopes[1], 0)
    gain_right = jnp.sum(slopes[1] * saved[1][0], 0)
    totals = lax.psum((shift_left, gain_left, shift_right, gain_right), "rows")
    results = []
    for member in range(2):
        pixel_count = slopes[member].shape[0] * lax.axis_size("rows")
        centred = saved[member][0]
        inverse_scale = saved[member][1]
        mean_slope = gain_vec * totals[2 * member] / pixel_count
        mean_cross = gain_vec * totals[2 * member + 1] / pixel_count
        results.append(
            inverse_scale * (gain_vec * slopes[member] - mean_slope - centred * mean_cross)
        )
    return (results, gain_left + gain_right, shift_left + shift_right)


def spread_rows(activity):
    return extended(activity, (("rows", 1),), 1)


def spread_grads(slopes):
    return extended(slopes, (("rows", 1),), 1)


def patches(padded, row_count, col_count, flipped):
    widened = jnp.pad(padded, ((0, 0), (0, 0), (1, 1), (0, 0)))
    tap_list = []
    for row_tap in range(3):
        for col_tap in range(3):
            row_start = 2 - row_tap if flipped else row_tap
            col_start = 2 - col_tap if flipped else col_tap
            tap_list.append(
                widened[:, row_start : row_start + row_count, col_start : col_start + col_count, :]
            )
    return jnp.concatenate(tap_list, axis=-1).reshape(-1, 9 * widened.shape[-1])


def body(
    views,
    crops,
    w_reduce,
    gain_one,
    shift_one,
    w_spatial,
    gain_two,
    shift_two,
    w_expand,
    gain_three,
    shift_three,
    cot_views,
    cot_crops,
):
    gathered = (
        lax.all_gather(w_reduce, "dp", axis=0, tiled=True),
        lax.all_gather(gain_one, "dp", axis=0, tiled=True),
        lax.all_gather(shift_one, "dp", axis=0, tiled=True),
        lax.all_gather(w_spatial, "dp", axis=2, tiled=True),
        lax.all_gather(gain_two, "dp", axis=0, tiled=True),
        lax.all_gather(shift_two, "dp", axis=0, tiled=True),
        lax.all_gather(w_expand, "dp", axis=0, tiled=True),
        lax.all_gather(gain_three, "dp", axis=0, tiled=True),
        lax.all_gather(shift_three, "dp", axis=0, tiled=True),
    )
    weight_reduce = gathered[0]
    weight_spatial = gathered[3]
    weight_expand = gathered[6]
    gain_first = gathered[1].astype(jnp.float32)
    shift_first = gathered[2].astype(jnp.float32)
    gain_second = gathered[4].astype(jnp.float32)
    shift_second = gathered[5].astype(jnp.float32)
    gain_third = gathered[7].astype(jnp.float32)
    shift_third = gathered[8].astype(jnp.float32)
    channels = views.shape[4]
    middle = weight_reduce.shape[1]
    map_shapes = [
        (views.shape[0] * views.shape[1], views.shape[2], views.shape[3]),
        (crops.shape[0] * crops.shape[1], crops.shape[2], crops.shape[3]),
    ]
    flat_inputs = [views.reshape(-1, channels), crops.reshape(-1, channels)]
    reduced = [
        jnp.dot(source, weight_reduce, preferred_element_type=jnp.float32) for source in flat_inputs
    ]
    first_norm = standardize(reduced, gain_first, shift_first)
    first_act = [jax.nn.silu(saved[2]).astype(jnp.bfloat16) for saved in first_norm]
    padded_act = [
        spread_rows(act.reshape(shape[0], shape[1], shape[2], middle))
        for act, shape in zip(first_act, map_shapes)
    ]
    patch_rows = [
        patches(padded, shape[1], shape[2], False) for padded, shape in zip(padded_act, map_shapes)
    ]
    kernel = weight_spatial.reshape(9 * middle, middle)
    spatial = [jnp.dot(patch, kernel, preferred_element_type=jnp.float32) for patch in patch_rows]
    second_norm = standardize(spatial, gain_second, shift_second)
    second_act = [jax.nn.silu(saved[2]).astype(jnp.bfloat16) for saved in second_norm]
    expanded = [
        jnp.dot(act, weight_expand, preferred_element_type=jnp.float32) for act in second_act
    ]
    third_norm = standardize(expanded, gain_third, shift_third)
    pre_list = [
        source.astype(jnp.float32) + saved[2] for source, saved in zip(flat_inputs, third_norm)
    ]
    activation = [jax.nn.silu(pre) for pre in pre_list]
    view_sums = jnp.sum(activation[0].reshape(views.shape[0], views.shape[1], -1, channels), axis=2)
    crop_sums = jnp.sum(activation[1].reshape(crops.shape[0], crops.shape[1], -1, channels), axis=2)
    pooled_sums = lax.psum((view_sums, crop_sums), "rows")
    pooled = jnp.concatenate(
        [
            pooled_sums[0] / (views.shape[3] * views.shape[3]),
            pooled_sums[1] / (crops.shape[3] * crops.shape[3]),
        ],
        axis=1,
    )
    cotangent = [
        cot_views.reshape(-1, channels).astype(jnp.float32),
        cot_crops.reshape(-1, channels).astype(jnp.float32),
    ]
    d_pre = [cot * silu_slope(pre) for cot, pre in zip(cotangent, pre_list)]
    d_expanded_f, gain_third_grad, shift_third_grad = unstandardize(d_pre, third_norm, gain_third)
    d_expanded = [grad.astype(jnp.bfloat16) for grad in d_expanded_f]
    expand_grad = jnp.einsum(
        "pm,pc->mc", second_act[0], d_expanded[0], preferred_element_type=jnp.float32
    ) + jnp.einsum("pm,pc->mc", second_act[1], d_expanded[1], preferred_element_type=jnp.float32)
    d_norm_two = [
        jnp.einsum("pc,mc->pm", grad, weight_expand, preferred_element_type=jnp.float32)
        * silu_slope(saved[2])
        for grad, saved in zip(d_expanded, second_norm)
    ]
    d_spatial_f, gain_second_grad, shift_second_grad = unstandardize(
        d_norm_two, second_norm, gain_second
    )
    d_spatial = [grad.astype(jnp.bfloat16) for grad in d_spatial_f]
    spatial_grad = (
        jnp.einsum("pk,pm->km", patch_rows[0], d_spatial[0], preferred_element_type=jnp.float32)
        + jnp.einsum("pk,pm->km", patch_rows[1], d_spatial[1], preferred_element_type=jnp.float32)
    ).reshape(3, 3, middle, middle)
    back_kernel = jnp.transpose(weight_spatial, (0, 1, 3, 2)).reshape(9 * middle, middle)
    padded_grads = [
        spread_grads(grad.reshape(shape[0], shape[1], shape[2], middle))
        for grad, shape in zip(d_spatial, map_shapes)
    ]
    d_norm_one = [
        jnp.dot(
            patches(padded, shape[1], shape[2], True),
            back_kernel,
            preferred_element_type=jnp.float32,
        )
        * silu_slope(saved[2])
        for padded, shape, saved in zip(padded_grads, map_shapes, first_norm)
    ]
    d_reduced_f, gain_first_grad, shift_first_grad = unstandardize(
        d_norm_one, first_norm, gain_first
    )
    d_reduced = [grad.astype(jnp.bfloat16) for grad in d_reduced_f]
    reduce_grad = jnp.einsum(
        "pc,pm->cm", flat_inputs[0], d_reduced[0], preferred_element_type=jnp.float32
    ) + jnp.einsum("pc,pm->cm", flat_inputs[1], d_reduced[1], preferred_element_type=jnp.float32)
    input_grads = [
        (
            pre_grad
            + jnp.einsum("pm,cm->pc", grad, weight_reduce, preferred_element_type=jnp.float32)
        ).astype(jnp.bfloat16)
        for pre_grad, grad in zip(d_pre, d_reduced)
    ]
    shares = (
        lax.psum_scatter(reduce_grad, "dp", scatter_dimension=0, tiled=True),
        lax.psum_scatter(gain_first_grad, "dp", scatter_dimension=0, tiled=True),
        lax.psum_scatter(shift_first_grad, "dp", scatter_dimension=0, tiled=True),
        lax.psum_scatter(spatial_grad, "dp", scatter_dimension=2, tiled=True),
        lax.psum_scatter(gain_second_grad, "dp", scatter_dimension=0, tiled=True),
        lax.psum_scatter(shift_second_grad, "dp", scatter_dimension=0, tiled=True),
        lax.psum_scatter(expand_grad, "dp", scatter_dimension=0, tiled=True),
        lax.psum_scatter(gain_third_grad, "dp", scatter_dimension=0, tiled=True),
        lax.psum_scatter(shift_third_grad, "dp", scatter_dimension=0, tiled=True),
    )
    summed = lax.psum(
        (
            shares[0],
            shares[1],
            shares[2],
            shares[3],
            shares[4],
            shares[5],
            shares[6],
            shares[7],
            shares[8],
        ),
        "rows",
    )
    return (
        activation[0].astype(jnp.bfloat16).reshape(views.shape),
        activation[1].astype(jnp.bfloat16).reshape(crops.shape),
        pooled,
        input_grads[0].reshape(views.shape),
        input_grads[1].reshape(crops.shape),
        summed[0],
        summed[1],
        summed[2],
        summed[3],
        summed[4],
        summed[5],
        summed[6],
        summed[7],
        summed[8],
    )


MESH = pl.DeviceIdType.MESH
SEMAPHORES = 164
F32 = jnp.float32
BF16 = jnp.bfloat16
NV = 512
NC = 256
N = NV + NC
KINDS = ((0, NV), (NV, NC))
NT = (((1,), (1,)), ((), ()))
TN = (((0,), (0,)), ((), ()))


def sigmoid(values):
    return 0.5 * jnp.tanh(0.5 * values) + 0.5


def dot(left, right, dims=(((1,), (0,)), ((), ()))):
    return lax.dot_general(left, right, dims, preferred_element_type=F32)


def moved(values, kind, step):
    rows, lanes = values.shape
    if step == 0:
        return values
    if kind == 0:
        maps = values.reshape(rows // 64, 64, lanes)
        gap = jnp.zeros((rows // 64, 8, lanes), values.dtype)
        parts = [gap, maps[:, :-8]] if step > 0 else [maps[:, 8:], gap]
        return jnp.concatenate(parts, axis=1).reshape(rows, lanes)
    gap = jnp.zeros((64, lanes), values.dtype)
    return jnp.concatenate([gap, values[:-64]] if step > 0 else [values[64:], gap], axis=0)


def turned(values, kind, step):
    if step == 0:
        return values
    rows, lanes = values.shape
    width = 8 if kind == 0 else 4
    col = lax.rem(lax.broadcasted_iota(jnp.int32, (rows, lanes), 0), width)
    edge = 0 if step > 0 else width - 1
    return jnp.where(col == edge, 0.0, pltpu.roll(values, 1 if step > 0 else rows - 1, axis=0))


def block_kernel(
    views, crops, w_reduce, w_spatial, w_expand, cot_views, cot_crops, gain_a, shift_a, gain_b, shift_b, gain_c, shift_c,
    out_views, out_crops, fin_p, grad_views, grad_crops, fin_e, fin_s, fin_r, pgs,
    xv, xc4, xc, cv, cc4, cc, xo_v, xo_c, co_v, co_c, wr, ws, we, aff, raw_a, raw_b, raw_c, raw_d, raw_e, raw_f, pg,
    part, csend, crecv, xsend, xrecv,
    act1, act2, dred, conv, xhat1, slope1, xhat2, slope2, ex, dpre, dex, pat, dpo, pool, rows_pool,
    ge, gs, gr, ysend_e, yrecv_e, zsend_e, zrecv_e, ysend_s, yrecv_s, zsend_s, zrecv_s, ysend_r, yrecv_r, zsend_r, zrecv_r,
    relay_e, relay_s, relay_r, acc_e, acc_s, acc_r, pgr,
    sem,
):
    i, r = lax.axis_index("dp"), lax.axis_index("rows")
    z, y = i // 2, i % 2
    x, c = r // 2, r % 2
    yp = (i + 1 - 2 * y, r)
    cp = (i, 2 * x + 1 - c)
    xp = (i, 2 * (1 - x) + c)
    xcp = (i, 2 * (1 - x) + 1 - c)
    rest = (xp, xcp, cp)

    middle = (z + 1) // 2 == 1
    step = 1 - 2 * (z // 2)

    def on_line(places):
        return (2 * (z + places * step) + y, r)

    taken = [0]

    def new(count=1):
        taken[0] += count
        return taken[0] - count

    def copy(src, dst, send, recv, dev):
        return pltpu.make_async_remote_copy(
            src_ref=src, dst_ref=dst, send_sem=sem.at[send], recv_sem=sem.at[recv], device_id=dev, device_id_type=MESH
        )

    def got(ref, recv):
        copy(ref, ref, recv, recv, cp).wait_recv()

    def sent(ref, send):
        copy(ref, ref, send, send, cp).wait_send()

    def stored(ref, one):
        pltpu.make_async_copy(ref, ref, sem.at[one]).wait()

    def lanes(k, xx, cc_):
        return pl.ds(pl.multiple_of(512 * k + 256 * cc_ + 128 * xx, 128), 128)

    def kl(k):
        return pl.ds(128 * k, 128)

    def kind_rows(kind):
        return pl.ds(*KINDS[kind])

    def stage(src, dst, one):
        pltpu.make_async_copy(src, dst, sem.at[one]).start()

    l_wr, l_ws, l_we, l_we2, l_gain = new(), new(), new(), new(), new(6)
    l_x, l_cot, l_own = (new(), new()), (new(), new()), new(4)

    @pl.when(y == c)
    def _():
        stage(w_reduce.at[pl.ds(pl.multiple_of(128 * x, 128), 128)], wr.at[r, z], l_wr)

    stage(w_spatial.at[:, :, pl.ds(pl.multiple_of(128 * r, 128), 128)], ws.at[:, i], l_ws)
    raw = (raw_a, raw_b, raw_c, raw_d, raw_e, raw_f)
    for n, vec in enumerate((gain_a, shift_a, gain_b, shift_b, gain_c, shift_c)):
        stage(vec, raw[n], l_gain + n)
    for k in range(4):
        stage(views.at[:, :, lanes(k, x, c)], xv.at[:, r, :, kl(k)], l_x[0])
        stage(crops.at[:, :, lanes(k, x, c)], xc4.at[r, :, :, kl(k)], l_x[1])
    for k in range(4):
        stage(w_expand.at[:, lanes(k, x, c)], we.at[r, i, :, kl(k)], l_we)
        stage(w_expand.at[:, lanes(k, 1 - x, c)], we.at[xp[1], i, :, kl(k)], l_we2)
    for k in range(4):
        stage(cot_views.at[:, :, lanes(k, x, c)], cv.at[:, r, :, kl(k)], l_cot[0])
        stage(cot_crops.at[:, :, lanes(k, x, c)], cc4.at[r, :, :, kl(k)], l_cot[1])
    for n, (src, dst) in enumerate(((views, xo_v), (crops, xo_c), (cot_views, co_v), (cot_crops, co_c))):
        stage(src, dst, l_own + n)

    bar = pltpu.get_barrier_semaphore()
    peers = [((i + n) % 8, r) for n in range(1, 8)] + [cp, xp, xcp]
    for dev in peers:
        pl.semaphore_signal(bar, inc=1, device_id=dev, device_id_type=MESH)
    pl.semaphore_wait(bar, len(peers))

    class Share:
        def __init__(self, parts, others):
            self.parts, self.others = parts, others
            count = len(parts(0))
            self.send = new()
            self.along_z = [new(3) for _ in range(count)]
            self.along_y = [new() for _ in range(count)]

    share_r = Share(lambda k: (wr.at[r, k],), None)
    share_s = Share(
        lambda k: tuple(ws.at[pl.ds(3 * h, 3), 2 * k + y] for h in range(3)),
        lambda h: ws.at[pl.ds(3 * h, 3), pl.ds(0, 4)],
    )
    share_e = Share(lambda k: (we.at[r, 2 * k + y],), lambda h: we.at[0, pl.ds(0, 4)])
    share_o = Share(lambda k: (we.at[xp[1], 2 * k + y],), lambda h: we.at[0, pl.ds(0, 4)])
    passed_r = new()

    inner = ((z + 1) // 2) * (2 - (z + 1) // 2)

    def line_send(share):
        for h, own in enumerate(share.parts(z)):

            def go(slot, dev, own=own):
                copy(own, own, share.send, slot, dev).start()

            go(share.along_z[h], on_line(2))
            go(share.along_z[h] + 2 - inner, on_line(1))

            @pl.when(middle)
            def _(go=go, h=h):
                go(share.along_z[h] + 1, on_line(-1))

            go(share.along_y[h], yp)

    def line_pass(share, h, send=None):
        send = share.send if send is None else send

        def take(places, slot, on=False):
            ref = share.parts(z + places * step)[h]
            got(ref, share.along_z[h] + slot)
            if on:
                copy(ref, ref, send, share.along_z[h] + 2, on_line(-1)).start()
            copy(ref, ref, send, share.along_y[h], yp).start()

        @pl.when(middle)
        def _():
            take(2, 0, True)
            take(1, 1)
            take(-1, 2)

        @pl.when(jnp.logical_not(middle))
        def _():
            take(2, 0)
            take(1, 1)
            take(3, 2)

    def line_got(share):
        for h, slot in enumerate(share.along_y):
            got(share.others(h), slot)

    def line_sent(send, for_middle, for_end):
        @pl.when(middle)
        def _():
            sent(for_middle, send)

        @pl.when(jnp.logical_not(middle))
        def _():
            sent(for_end, send)

    @pl.when(y == c)
    def _():
        stored(wr.at[r, z], l_wr)
        line_send(share_r)

    s_sx, s_rx = ((new(), new()), (new(), new())), ((new(), new()), (new(), new()))

    def spread_v(src, dst, s, devs):
        for dev in devs:
            for k in range(4):
                copy(src.at[:, :, lanes(k, dev[1] // 2, dev[1] % 2)], dst.at[:, r, :, kl(k)], s_sx[s][0], s_rx[s][0], dev).start()

    def spread_c(src, dst, s, devs):
        for dev in devs:
            for k in range(4):
                copy(src.at[:, :, lanes(k, dev[1] // 2, dev[1] % 2)], dst.at[r, :, :, kl(k)], s_sx[s][1], s_rx[s][1], dev).start()

    spread_v(views, xv, 0, rest)
    spread_c(crops, xc4, 0, rest)
    spread_v(cot_views, cv, 1, rest[:1])

    for n in range(6):
        stored(raw[n], l_gain + n)
    pg[i] = jnp.zeros((8, 128), F32)
    for n in range(4):
        vec = raw[n][...].reshape(1, 64).astype(F32)
        pg[i, n : n + 1, :] = jnp.concatenate([vec, vec], axis=1)
    for n in range(2):
        for m in range(2):
            pg[i, 4 + 2 * n + m : 5 + 2 * n + m, :] = raw[4 + n][128 * m : 128 * m + 128].reshape(1, 128).astype(F32)
    s_pg, r_pg = new(), new()
    for dev in peers[:7]:
        copy(pg.at[i], pg.at[i], s_pg, r_pg, dev).start()

    @pl.when(y == c)
    def _():
        line_pass(share_r, 0, passed_r)

    stored(xv.at[:, r], l_x[0])
    got(xv.at[:, pl.ds(0, 3)], s_rx[0][0])
    stored(ws.at[:, i], l_ws)
    line_send(share_s)

    @pl.when(y != c)
    def _():
        got(wr.at[r], share_r.along_y[0])

    s_cs, r_cs = new(3), new(12)
    s_xs, r_xs = new(3), new(6)
    s_ag, r_ag = new(3), new(12)

    def scatter_start(op, kind, sums):
        rows = kind_rows(kind)
        n = pl.ds(0, KINDS[kind][1])
        for s in range(4):
            part[op, s, rows, :] = sums[:, 128 * s : 128 * s + 128]
        for near, xx in enumerate((1 - x, x)):
            csend[op, kind, xx, n, :] = part[op, 2 * xx + 1 - c, rows, :].astype(BF16)
            own = csend.at[op, kind, xx, n]
            copy(own, crecv.at[op, kind, xx, n], s_cs + op, r_cs + 4 * op + 2 * kind + near, cp).start()

    def scatter_mid(op, kind):
        rows = kind_rows(kind)
        n = pl.ds(0, KINDS[kind][1])
        got(crecv.at[op, kind, 1 - x, n], r_cs + 4 * op + 2 * kind)
        far = part[op, 2 * (1 - x) + c, rows, :] + crecv[op, kind, 1 - x, n, :].astype(F32)
        xsend[op, kind, n, :] = far.astype(BF16)
        copy(xsend.at[op, kind, n], xrecv.at[op, kind, n], s_xs + op, r_xs + 2 * op + kind, xp).start()

    def scatter_end(op, kind):
        rows = kind_rows(kind)
        n = pl.ds(0, KINDS[kind][1])
        got(crecv.at[op, kind, x, n], r_cs + 4 * op + 2 * kind + 1)
        near = part[op, 2 * x + c, rows, :] + crecv[op, kind, x, n, :].astype(F32)
        got(xrecv.at[op, kind, n], r_xs + 2 * op + kind)
        return near + xrecv[op, kind, n, :].astype(F32)

    def gather_start(op, kind, buf, value):
        rows = kind_rows(kind)
        buf[r, rows, :] = value
        own = buf.at[r, rows]
        copy(own, own, s_ag + op, r_ag + 4 * op + 2 * kind, xp).start()
        copy(own, own, s_ag + op, r_ag + 4 * op + 2 * kind + 1, cp).start()

    def gather_mid(op, kind, buf):
        far = buf.at[xp[1], kind_rows(kind)]
        got(far, r_ag + 4 * op + 2 * kind)
        copy(far, far, s_ag + op, r_ag + 4 * op + 2 * kind + 1, cp).start()

    def gather_end(op, kind, buf):
        rows = kind_rows(kind)
        got(buf.at[pl.ds(0, 2), rows], r_ag + 4 * op + 2 * kind + 1)
        return jnp.concatenate([buf[s, rows, :] for s in range(4)], axis=1)

    weight_r = wr[r].reshape(512, 512)
    scatter_start(0, 0, dot(xv[...].reshape(NV, 512), weight_r))
    stored(xc4.at[r], l_x[1])
    got(xc4.at[pl.ds(0, 3)], s_rx[0][1])
    xc[...] = xc4[...].reshape(4, 64, 512)
    scatter_start(0, 1, dot(xc[...].reshape(NC, 512), weight_r))
    scatter_mid(0, 0)
    scatter_mid(0, 1)
    spread_c(cot_crops, cc4, 1, rest[:1])

    got(pg.at[pl.ds(0, 7)], r_pg)
    half = lax.broadcasted_iota(jnp.int32, (1, 128), 1) < 64
    gain1, shift1, gain2, shift2 = [
        jnp.where(half, pg[2 * r, q : q + 1, :], pg[2 * r + 1, q : q + 1, :]) for q in range(4)
    ]
    gain3 = jnp.concatenate([pg[2 * k + c, pl.ds(4 + x, 1), :] for k in range(4)], axis=1)
    shift3 = jnp.concatenate([pg[2 * k + c, pl.ds(6 + x, 1), :] for k in range(4)], axis=1)

    def norm_act(values, rows, gain, shift):
        mean = jnp.sum(values, axis=0, keepdims=True) / rows
        second = jnp.sum(values * values, axis=0, keepdims=True) / rows
        rstd = lax.rsqrt(second - mean * mean + EPSILON)
        xhat = (values - mean) * rstd
        norm = gain * xhat + shift
        sig = sigmoid(norm)
        return rstd, xhat, sig * (1.0 + norm * (1.0 - sig)), (norm * sig).astype(BF16)

    line_pass(share_s, 0)
    line_pass(share_s, 1)
    rstd1, rstd2 = [None, None], [None, None]
    for kind in range(2):
        rows = KINDS[kind][1]
        rstd1[kind], xh, sl, act = norm_act(scatter_end(0, kind), rows, gain1, shift1)
        gather_start(0, kind, act1, act)
        xhat1[kind_rows(kind), :] = xh
        slope1[kind_rows(kind), :] = sl
    spread_v(cot_views, cv, 1, rest[1:])
    spread_c(cot_crops, cc4, 1, rest[1:])
    line_pass(share_s, 2)
    stored(we.at[r, i], l_we)
    line_send(share_e)
    for kind in range(2):
        gather_mid(0, kind, act1)

    s_ow, s_xw, r_xw, r_ow = new(), new(), new(), new(2)

    def over_x(k):
        copy(wr.at[r, k], wr.at[r, k], s_xw, r_xw, xp).start()

    def between(ref, n):
        copy(ref, ref, s_ow, r_ow + n, cp).start()

    between(wr.at[r], 0)
    line_got(share_s)

    def weight_s():
        return jnp.concatenate([ws[t].reshape(512, 128) for t in range(9)], axis=1)

    for kind in range(2):
        rows = KINDS[kind][1]
        conv[kind_rows(kind), :] = dot(gather_end(0, kind, act1), weight_s())
        taps = [conv[kind_rows(kind), 128 * t : 128 * t + 128] for t in range(9)]
        spatial = None
        for j in range(3):
            col = taps[3 + j] + moved(taps[j], kind, 1) + moved(taps[6 + j], kind, -1)
            col = turned(col, kind, 1 - j)
            spatial = col if spatial is None else spatial + col
        rstd2[kind], xh, sl, act = norm_act(spatial, rows, gain2, shift2)
        gather_start(1, kind, act2, act)
        xhat2[kind_rows(kind), :] = xh
        slope2[kind_rows(kind), :] = sl
        if kind == 0:
            line_pass(share_e, 0)
            stored(we.at[r, i], l_we2)
            line_send(share_o)
    over_x(0)
    over_x(1)
    pool[...] = jnp.zeros_like(pool)
    for kind in range(2):
        gather_mid(1, kind, act2)
    stored(cv.at[:, r], l_cot[0])
    stored(cc4.at[r], l_cot[1])
    got(cv.at[:, pl.ds(0, 3)], s_rx[1][0])
    got(cc4.at[pl.ds(0, 3)], s_rx[1][1])
    cc[...] = cc4[...].reshape(4, 64, 512)
    line_got(share_e)
    between(we.at[r], 1)
    weight_e = we[r].reshape(512, 512)

    sum_x3, sum_d3 = [], []
    zero8 = jnp.zeros((8, 512), F32)

    def expand(kind):
        start, rows = KINDS[kind]
        ex[kind_rows(kind), :] = dot(gather_end(1, kind, act2), weight_e)

        def moments(b, acc):
            e = ex[pl.ds(pl.multiple_of(start + 32 * b, 32), 32), :].reshape(4, 8, 512)
            return acc[0] + jnp.sum(e, axis=0), acc[1] + jnp.sum(e * e, axis=0)

        tot, sq = lax.fori_loop(0, rows // 32, moments, (zero8, zero8))
        mean = jnp.sum(tot, axis=0, keepdims=True) / rows
        rstd = lax.rsqrt(jnp.sum(sq, axis=0, keepdims=True) / rows - mean * mean + EPSILON)

        def finish(b, acc):
            rs = pl.ds(pl.multiple_of(start + 16 * b, 16), 16)
            qs = pl.ds(pl.multiple_of(16 * (b % 4), 16), 16)
            xhat = (ex[rs, :] - mean) * rstd
            ex[rs, :] = xhat
            src = xv[b // 4, b % 4] if kind == 0 else xc[b // 4, qs, :]
            cot = cv[b // 4, b % 4] if kind == 0 else cc[b // 4, qs, :]
            pre = src.astype(F32) + (gain3 * xhat + shift3)
            sig = sigmoid(pre)
            activation = pre * sig
            d = cot.astype(F32) * (sig * (1.0 + pre * (1.0 - sig)))
            dpre[rs, :] = d
            if kind == 0:
                pool[b // 4] += activation[:8] + activation[8:]
            else:
                pool[8 + 2 * (b % 4)] += activation[:8]
                pool[9 + 2 * (b % 4)] += activation[8:]
            dx = d * xhat
            return acc[0] + (d[:8] + d[8:]), acc[1] + (dx[:8] + dx[8:])

        sd, sxx = lax.fori_loop(0, rows // 16, finish, (zero8, zero8))
        sd, sxx = jnp.sum(sd, axis=0, keepdims=True), jnp.sum(sxx, axis=0, keepdims=True)
        sum_d3.append(sd)
        sum_x3.append(sxx)
        scale = gain3 * rstd
        mean_d, mean_x = sd / rows, sxx / rows
        aff[r, 2 * kind : 2 * kind + 1, :] = scale
        aff[r, 2 * kind + 1 : 2 * kind + 2, :] = shift3 - scale * mean

        def back(b, _):
            rs = pl.ds(pl.multiple_of(start + 32 * b, 32), 32)
            dex[rs, :] = (scale * (dpre[rs, :] - mean_d - ex[rs, :] * mean_x)).astype(BF16)
            return 0

        lax.fori_loop(0, rows // 32, back, 0)

    def own_rows(buf):
        slices = []
        for s in range(4):
            rows = [buf[s, pl.ds(pl.multiple_of(64 * m + 16 * r, 16), 16), :] for m in range(8)]
            rows.append(buf[s, pl.ds(pl.multiple_of(NV + 64 * r, 64), 64), :])
            slices.append(jnp.concatenate(rows, axis=0))
        return jnp.concatenate(slices, axis=1)

    def own_blocks(values, s):
        for k in range(4):
            lo = 512 * k + 256 * (s % 2) + 128 * (s // 2)
            yield k, slice(lo, lo + 128), (values[:128, 128 * k : 128 * k + 128], values[128:, 128 * k : 128 * k + 128])

    def own_output():
        act = own_rows(act2)
        for s in range(4):
            for k, cols, blocks in own_blocks(dot(act, we[s].reshape(512, 512)), s):
                for kind, block in enumerate(blocks):
                    scale = aff[s, 2 * kind : 2 * kind + 1, 128 * k : 128 * k + 128]
                    shift = aff[s, 2 * kind + 1 : 2 * kind + 2, 128 * k : 128 * k + 128]
                    src = (xo_v if kind == 0 else xo_c)[:, :, cols].reshape(block.shape).astype(F32)
                    cot = (co_v if kind == 0 else co_c)[:, :, cols].reshape(block.shape).astype(F32)
                    pre = src + (scale * block + shift)
                    sig = sigmoid(pre)
                    if kind == 0:
                        out_views[:, :, cols] = (pre * sig).astype(BF16).reshape(8, 16, 128)
                    else:
                        out_crops[:, cols] = (pre * sig).astype(BF16)
                    dpo[128 * kind : 128 * kind + block.shape[0], cols] = cot * (sig * (1.0 + pre * (1.0 - sig)))

    def own_gradient():
        back = own_rows(dred)
        for s in range(4):
            for _, cols, blocks in own_blocks(dot(back, wr[s].reshape(512, 512), NT), s):
                grad_views[:, :, cols] = (dpo[:128, cols] + blocks[0]).astype(BF16).reshape(8, 16, 128)
                grad_crops[:, cols] = (dpo[128:, cols] + blocks[1]).astype(BF16)

    far_of = jnp.where(middle, z + 2 * step, z + 3 * step)
    mid_of = jnp.where(middle, z - step, z + 2 * step)
    order = [far_of, mid_of, z + step, z]

    class Grad:
        def __init__(self, full, ysend, yrecv, zsend, zrecv, relay, acc, both=True):
            self.full, self.ysend, self.yrecv, self.zsend, self.zrecv = full, ysend, yrecv, zsend, zrecv
            self.relay, self.acc, self.both = relay, acc, both
            self.s_y, self.r_y, self.s_z, self.r_z, self.r_relay = new(), new(4), new(), new(), new()

        def start(self):
            for k in order:
                self.ysend[k] = (self.full[k, 1 - y] if self.both else self.full[k]).astype(BF16)
                copy(self.ysend.at[k], self.yrecv.at[k], self.s_y, self.r_y + k, yp).start()

        def add(self, k):
            got(self.yrecv.at[k], self.r_y + k)
            return (self.full[k, y] if self.both else self.full[k]) + self.yrecv[k].astype(F32)

        def send(self, k, value):
            self.zsend[k] = value.astype(BF16)
            copy(self.zsend.at[k], self.zrecv.at[z], self.s_z, self.r_z, (2 * k + y, r)).start()

        def along(self):
            @pl.when(jnp.logical_not(middle))
            def _():
                k = order[0]
                self.zsend[k] = self.add(k).astype(BF16)
                copy(self.zsend.at[k], self.relay, self.s_z, self.r_relay, on_line(1)).start()

            self.send(order[1], self.add(order[1]))
            self.send(order[2], self.add(order[2]))

        def hand_on(self):
            @pl.when(middle)
            def _():
                total = self.add(order[0])
                got(self.relay, self.r_relay)
                self.send(order[0], total + self.relay[...].astype(F32))

        def total(self):
            self.acc[...] = self.add(z)

            @pl.when(middle)
            def _():
                got(self.zrecv.at[pl.ds(0, 3)], self.r_z)
                self.acc[...] += self.zrecv[z - step].astype(F32)

            @pl.when(jnp.logical_not(middle))
            def _():
                got(self.zrecv.at[pl.ds(0, 2)], self.r_z)

            return self.acc[...] + self.zrecv[z + step].astype(F32) + self.zrecv[z + 2 * step].astype(F32)

        def sent(self):
            sent(self.zsend.at[pl.ds(0, 3)], self.s_z)

    class Slices:
        def __init__(self, buf):
            self.buf, self.send, self.far, self.near = buf, new(), new(), new()

        def start(self, value):
            self.buf[r] = value.astype(BF16)
            copy(self.buf.at[r], self.buf.at[r], self.send, self.far, xp).start()
            copy(self.buf.at[r], self.buf.at[r], self.send, self.near, cp).start()

        def mid(self):
            far = self.buf.at[xp[1]]
            got(far, self.far)
            copy(far, far, self.send, self.near, cp).start()

        def end(self):
            got(self.buf.at[pl.ds(0, 2)], self.near)
            sent(self.buf.at[pl.ds(0, 3)], self.send)

    grad_e = Grad(ge, ysend_e, yrecv_e, zsend_e, zrecv_e, relay_e, acc_e)
    grad_s = [
        Grad(*(one.at[q] for one in (gs, ysend_s, yrecv_s, zsend_s, zrecv_s, relay_s, acc_s))) for q in range(3)
    ]
    grad_r = Grad(gr, ysend_r, yrecv_r, zsend_r, zrecv_r, relay_r, acc_r, False)
    slices_p, slices_e, slices_s = Slices(fin_p), Slices(fin_e), [Slices(fin_s.at[q]) for q in range(3)]

    expand(0)
    scatter_start(1, 0, dot(dex[kind_rows(0), :], weight_e, NT))
    line_pass(share_o, 0)
    expand(1)
    scatter_mid(1, 0)
    scatter_start(1, 1, dot(dex[kind_rows(1), :], weight_e, NT))
    ge[...] = dot(jnp.concatenate([act2[s] for s in range(4)], axis=1), dex[...], TN).reshape(4, 2, 64, 512)
    grad_e.start()
    scatter_mid(1, 1)
    s_af, r_af = new(), new()
    for dev in rest:
        copy(aff.at[r], aff.at[r], s_af, r_af, dev).start()
    over_x(2)

    def norm_back(d, xhat, rstd, gain, rows):
        sd = jnp.sum(d, axis=0, keepdims=True)
        sxx = jnp.sum(d * xhat, axis=0, keepdims=True)
        return (gain * rstd) * (d - sd / rows - xhat * (sxx / rows)), sd, sxx

    sum_d2, sum_x2 = [], []
    for kind in range(2):
        rows = KINDS[kind][1]
        d = scatter_end(1, kind) * slope2[kind_rows(kind), :]
        dz_, sd, sxx = norm_back(d, xhat2[kind_rows(kind), :], rstd2[kind], gain2, rows)
        sum_d2.append(sd)
        sum_x2.append(sxx)
        dz_ = dz_.astype(BF16).astype(F32)
        for tj in range(3):
            col = turned(dz_, kind, tj - 1)
            for ti in range(3):
                t = 3 * ti + tj
                pat[kind_rows(kind), 128 * t : 128 * t + 128] = moved(col, kind, ti - 1).astype(BF16)
        scatter_start(2, kind, dot(pat[kind_rows(kind), :], weight_s(), NT))
        if kind == 1:
            scatter_mid(2, 0)
    scatter_mid(2, 1)
    full1 = jnp.concatenate([act1[s] for s in range(4)], axis=1)
    for q in range(3):
        gs[q] = dot(full1, pat[:, 384 * q : 384 * q + 384], TN).reshape(4, 2, 64, 384)
        grad_s[q].start()
    grad_e.along()
    line_got(share_o)
    between(we.at[xp[1]], 1)

    sum_d1, sum_x1 = [], []
    for kind in range(2):
        rows = KINDS[kind][1]
        d = scatter_end(2, kind) * slope1[kind_rows(kind), :]
        dz_, sd, sxx = norm_back(d, xhat1[kind_rows(kind), :], rstd1[kind], gain1, rows)
        sum_d1.append(sd)
        sum_x1.append(sxx)
        gather_start(2, kind, dred, dz_.astype(BF16))

    rows12 = [sum_x1[0] + sum_x1[1], sum_d1[0] + sum_d1[1], sum_x2[0] + sum_x2[1], sum_d2[0] + sum_d2[1]]
    gx3, gd3 = sum_x3[0] + sum_x3[1], sum_d3[0] + sum_d3[1]
    rows3 = [g[:, 128 * k : 128 * k + 128] for g in (gx3, gd3) for k in range(4)]
    pgr[i] = jnp.concatenate(rows12 + rows3 + [jnp.zeros((4, 128), F32)], axis=0)
    s_pp, r_pp, s_ps, r_ps = new(), new(), new(), new()
    for dev in peers[:7]:
        copy(pgr.at[i], pgr.at[i], s_pp, r_pp, dev).start()
    over_x(3)
    grad_e.hand_on()

    rows_pool[...] = jnp.zeros_like(rows_pool)
    for n in range(8):
        row = 4 * (n % 2) + n // 2
        rows_pool[row : row + 1, :] = jnp.sum(pool[n], axis=0, keepdims=True) / 64.0
        for m in range(2):
            row = 4 * (2 + 2 * (n % 2) + m) + n // 2
            rows_pool[row : row + 1, :] = jnp.sum(pool[8 + n, 4 * m : 4 * m + 4, :], axis=0, keepdims=True) / 16.0
    slices_p.start(rows_pool[...])
    grad_s[0].along()
    gather_mid(2, 0, dred)
    grad_s[1].along()
    gather_mid(2, 1, dred)
    grad_s[0].hand_on()
    full_d = [gather_end(2, kind, dred) for kind in range(2)]

    for m in range(4):
        col = dot(xv[:, :, :, 128 * m : 128 * m + 128].reshape(NV, 128), full_d[0], TN)
        gr[m] = col + dot(xc[:, :, 128 * m : 128 * m + 128].reshape(NC, 128), full_d[1], TN)

    @pl.when(y != c)
    def _():
        grad_r.start()

    got(wr.at[0], r_xw)
    between(wr.at[xp[1]], 0)
    for n, ref in enumerate((xo_v, xo_c, co_v, co_c)):
        stored(ref, l_own + n)
    got(aff.at[pl.ds(0, 3)], r_af)
    got(we.at[pl.ds(0, 2)], r_ow + 1)
    own_output()
    grad_s[1].hand_on()
    grad_s[2].along()
    slices_e.start(grad_e.total())
    slices_s[0].start(grad_s[0].total())
    got(wr.at[pl.ds(0, 2)], r_ow)
    own_gradient()

    @pl.when(y == c)
    def _():
        grad_r.along()

    grad_s[2].hand_on()
    slices_s[1].start(grad_s[1].total())
    slices_p.mid()
    slices_e.mid()

    @pl.when(y == c)
    def _():
        grad_r.hand_on()

    slices_s[0].mid()
    slices_s[2].start(grad_s[2].total())

    got(pgr.at[pl.ds(0, 7)], r_pp)
    total = pgr[0]
    for n in range(1, 8):
        total = total + pgr[n]
    pgs[r] = total
    for dev in rest:
        copy(pgs.at[r], pgs.at[r], s_ps, r_ps, dev).start()
    slices_s[1].mid()

    s_fr, r_fr = new(), new()

    @pl.when(y == c)
    def _():
        fin_r[x] = grad_r.total().astype(BF16)
        copy(fin_r.at[x], fin_r.at[x], s_fr, r_fr, xp).start()
        copy(fin_r.at[x], fin_r.at[x], s_fr, r_fr, cp).start()

    slices_s[2].mid()

    @pl.when(y == c)
    def _():
        far = fin_r.at[1 - x]
        got(far, r_fr)
        copy(far, far, s_fr, r_fr, cp).start()

    for one in (slices_p, slices_e, *slices_s):
        one.end()
    got(pgs.at[pl.ds(0, 3)], r_ps)
    sent(aff.at[pl.ds(0, 3)], s_af)
    sent(we, s_ow)
    sent(wr.at[0], s_xw)
    for s, (own_v, own_c) in enumerate(((xv, xc4), (cv, cc4))):
        sent(own_v.at[:, pl.ds(0, 3)], s_sx[s][0])
        sent(own_c.at[pl.ds(0, 3)], s_sx[s][1])
    sent(pg.at[pl.ds(0, 7)], s_pg)
    sent(pgr.at[pl.ds(0, 7)], s_pp)
    sent(pgs.at[pl.ds(0, 3)], s_ps)
    line_sent(share_s.send, ws, ws.at[:, pl.ds(0, 6)])
    line_sent(share_e.send, we.at[0], we.at[0, pl.ds(0, 6)])
    line_sent(share_o.send, we.at[0], we.at[0, pl.ds(0, 6)])
    for op in range(3):
        sent(act1.at[pl.ds(0, 2)], s_cs + op)
        sent(act1.at[0], s_xs + op)
        sent(act1.at[pl.ds(0, 3)], s_ag + op)
    for one in (grad_e, *grad_s):
        sent(one.ysend, one.s_y)
        one.sent()

    @pl.when(y != c)
    def _():
        sent(ysend_r, grad_r.s_y)
        got(fin_r, r_fr)

    @pl.when(y == c)
    def _():
        line_sent(share_r.send, wr.at[0], wr.at[0, pl.ds(0, 3)])
        line_sent(passed_r, wr.at[0], wr.at[0, pl.ds(0, 3)])
        grad_r.sent()
        sent(wr.at[0, pl.ds(0, 3)], s_fr)

    assert taken[0] == SEMAPHORES, taken


def store_kernel(
    out_v, out_c, pool, grad_v, grad_c, fin_e, fin_s, fin_r, sums,
    out_views, out_crops, pooled, grad_views, grad_crops, grad_reduce, grad_spatial, grad_expand,
    gain_a, shift_a, gain_b, shift_b, gain_c, shift_c,
    oc, pl_, gc, gr, gs, ge, sem,
):
    i = lax.axis_index("dp")
    z, y = i // 2, i % 2
    copies = []

    def store(src, dst):
        one = pltpu.make_async_copy(src, dst, sem.at[len(copies)])
        one.start()
        copies.append(one)

    store(out_v, out_views)
    store(grad_v, grad_views)
    for s in range(4):
        for t in range(9):
            gs[t, :, 128 * s : 128 * s + 128] = fin_s[t // 3, s, :, 128 * (t % 3) : 128 * (t % 3) + 128].astype(F32)
    store(gs, grad_spatial)
    for s in range(4):
        for k in range(4):
            lo = 512 * k + 256 * (s % 2) + 128 * (s // 2)
            ge[:, lo : lo + 128] = fin_e[s, :, 128 * k : 128 * k + 128].astype(F32)
    store(ge, grad_expand)
    gr[...] = fin_r[...].astype(F32).reshape(256, 512)
    store(gr, grad_reduce)
    oc[...] = out_c[...].reshape(16, 4, 2048)
    store(oc, out_crops)
    gc[...] = grad_c[...].reshape(16, 4, 2048)
    store(gc, grad_crops)
    for s in range(4):
        for k in range(4):
            lo = 512 * k + 256 * (s % 2) + 128 * (s // 2)
            pl_[:, :, lo : lo + 128] = pool[s, 0:24, 128 * k : 128 * k + 128].astype(F32).reshape(6, 4, 128)
    store(pl_, pooled)
    for n, out in enumerate((gain_a, shift_a, gain_b, shift_b)):
        row = sums[i // 2, n : n + 1, :]
        out[...] = jnp.where(i % 2 == 0, row[:, :64], row[:, 64:]).reshape(64)
    for n, out in enumerate((gain_c, shift_c)):
        out[...] = jnp.concatenate([sums[2 * m + y, pl.ds(4 + 4 * n + z, 1), :] for m in range(2)], axis=1).reshape(256)
    for one in copies:
        one.wait()


def fused(views, crops, w_reduce, w_spatial, w_expand, cot_views, cot_crops, *params):
    hbm, vmem = pl.BlockSpec(memory_space=pltpu.HBM), pl.BlockSpec(memory_space=pltpu.VMEM)

    def shape(dims, dtype):
        return jax.ShapeDtypeStruct(dims, dtype)

    def buf(dims, dtype=BF16):
        return pltpu.VMEM(dims, dtype)

    def dma(*dims):
        return pltpu.SemaphoreType.DMA(dims)

    held = pl.pallas_call(
        block_kernel,
        out_shape=[
            buf((8, 16, 2048)), buf((64, 2048)), buf((4, 32, 512)), buf((8, 16, 2048)), buf((64, 2048)),
            buf((4, 64, 512)), buf((3, 4, 64, 384)), buf((2, 128, 512)), buf((4, 16, 128), F32),
        ],
        in_specs=[hbm] * 13,
        out_specs=[vmem] * 9,
        scratch_shapes=[
            buf((8, 4, 16, 512)), buf((4, 16, 4, 512)), buf((4, 64, 512)),
            buf((8, 4, 16, 512)), buf((4, 16, 4, 512)), buf((4, 64, 512)),
            buf((8, 16, 2048)), buf((16, 4, 2048)), buf((8, 16, 2048)), buf((16, 4, 2048)),
            buf((4, 4, 128, 512)), buf((9, 8, 64, 128)), buf((4, 8, 64, 512)), buf((4, 8, 512), F32), buf((64,)), buf((64,)), buf((64,)), buf((64,)), buf((256,)), buf((256,)), buf((8, 8, 128), F32),
            buf((3, 4, N, 128), F32), buf((3, 2, 2, NV, 128)), buf((3, 2, 2, NV, 128)),
            buf((3, 2, NV, 128)), buf((3, 2, NV, 128)),
            buf((4, N, 128)), buf((4, N, 128)), buf((4, N, 128)), buf((N, 1152), F32),
            buf((N, 128), F32), buf((N, 128), F32), buf((N, 128), F32), buf((N, 128), F32),
            buf((N, 512), F32), buf((N, 512), F32), buf((N, 512)), buf((N, 1152)),
            buf((192, 2048), F32), buf((16, 8, 512), F32), buf((32, 512), F32),
            buf((4, 2, 64, 512), F32), buf((3, 4, 2, 64, 384), F32), buf((4, 128, 512), F32),
            buf((4, 64, 512)), buf((4, 64, 512)), buf((4, 64, 512)), buf((4, 64, 512)),
            buf((3, 4, 64, 384)), buf((3, 4, 64, 384)), buf((3, 4, 64, 384)), buf((3, 4, 64, 384)),
            buf((4, 128, 512)), buf((4, 128, 512)), buf((4, 128, 512)), buf((4, 128, 512)),
            buf((64, 512)), buf((3, 64, 384)), buf((128, 512)), buf((64, 512), F32), buf((3, 64, 384), F32), buf((128, 512), F32),
            buf((8, 16, 128), F32),
            dma(SEMAPHORES),
        ],
        compiler_params=pltpu.CompilerParams(collective_id=0, has_side_effects=True, vmem_limit_bytes=58 << 20),
        cost_estimate=pl.CostEstimate(flops=5_200_000_000, bytes_accessed=8_000_000, transcendentals=2_000_000),
    )(views, crops, w_reduce, w_spatial, w_expand, cot_views, cot_crops, *params)
    held = [pltpu.with_memory_space_constraint(one, pltpu.VMEM) for one in held]
    return pl.pallas_call(
        store_kernel,
        out_shape=[
            shape((8, 16, 2048), BF16), shape((16, 4, 2048), BF16), shape((6, 4, 2048), F32),
            shape((8, 16, 2048), BF16), shape((16, 4, 2048), BF16),
            shape((256, 512), F32), shape((9, 64, 512), F32), shape((64, 2048), F32),
            shape((64,), F32), shape((64,), F32), shape((64,), F32), shape((64,), F32), shape((256,), F32), shape((256,), F32),
        ],
        in_specs=[vmem] * 9,
        out_specs=[hbm] * 8 + [vmem] * 6,
        scratch_shapes=[
            buf((16, 4, 2048)), buf((6, 4, 2048), F32), buf((16, 4, 2048)),
            buf((256, 512), F32), buf((9, 64, 512), F32), buf((64, 2048), F32), dma(8),
        ],
        compiler_params=pltpu.CompilerParams(vmem_limit_bytes=16 << 20),
    )(*held)


def step(
    dp, rows, views, crops, w_reduce, gain_one, shift_one, w_spatial, gain_two, shift_two, w_expand, gain_three, shift_three,
    cot_views, cot_crops,
):
    args = (
        views, crops, w_reduce, gain_one, shift_one, w_spatial, gain_two, shift_two, w_expand, gain_three, shift_three,
        cot_views, cot_crops,
    )
    if (dp, rows) != (8, 4) or views.shape != (4, 2, 2, 8, 2048) or crops.shape != (4, 4, 1, 4, 2048):
        return body(*args)
    out_v, out_c, pooled, grad_v, grad_c, grad_r, grad_s, grad_e, ga, sa, gb, sb, gc, sc = fused(
        views.reshape(8, 16, 2048), crops.reshape(16, 4, 2048), w_reduce, w_spatial.reshape(9, 64, 512), w_expand,
        cot_views.reshape(8, 16, 2048), cot_crops.reshape(16, 4, 2048),
        gain_one, shift_one, gain_two, shift_two, gain_three, shift_three,
    )
    return (
        out_v.reshape(views.shape),
        out_c.reshape(crops.shape),
        jnp.transpose(pooled, (1, 0, 2)),
        grad_v.reshape(views.shape),
        grad_c.reshape(crops.shape),
        grad_r,
        ga,
        sa,
        grad_s.reshape(w_spatial.shape[:3] + (512,)),
        gb,
        sb,
        grad_e,
        gc,
        sc,
    )


def solution(mesh):
    return jax.shard_map(
        functools.partial(step, mesh.shape["dp"], mesh.shape["rows"]),
        mesh=mesh,
        in_specs=(
            P("dp", None, "rows", None, None),
            P("dp", None, "rows", None, None),
            P("dp", None),
            P("dp"),
            P("dp"),
            P(None, None, "dp", None),
            P("dp"),
            P("dp"),
            P("dp", None),
            P("dp"),
            P("dp"),
            P("dp", None, "rows", None, None),
            P("dp", None, "rows", None, None),
        ),
        out_specs=(
            P("dp", None, "rows", None, None),
            P("dp", None, "rows", None, None),
            P("dp", None, None),
            P("dp", None, "rows", None, None),
            P("dp", None, "rows", None, None),
            P("dp", None),
            P("dp"),
            P("dp"),
            P(None, None, "dp", None),
            P("dp"),
            P("dp"),
            P("dp", None),
            P("dp"),
            P("dp"),
        ),
        check_vma=False,
    )
```

```python
import functools

import jax
import jax.numpy as jnp
from jax import lax
from jax.experimental import pallas as pl
from jax.experimental.pallas import tpu as pltpu
from jax.sharding import PartitionSpec as P

EPSILON = 1e-05


def extended(cells, sides, width):
    for axis, dim in sides:
        count = lax.axis_size(axis)
        ends = count - 1
        head = lax.slice_in_dim(cells, 0, width, axis=dim)
        tail = lax.slice_in_dim(cells, cells.shape[dim] - width, cells.shape[dim], axis=dim)
        cells = jnp.concatenate(
            [
                lax.ppermute(tail, axis, [(i, (i + 1) % count) for i in range(ends)]),
                cells,
                lax.ppermute(head, axis, [((i + 1) % count, i) for i in range(ends)]),
            ],
            axis=dim,
        )
    return cells


def silu_slope(values):
    sigmoid_val = jax.nn.sigmoid(values)
    return sigmoid_val * (1.0 + values * (1.0 - sigmoid_val))


def standardize(reduced_pair, gain_vec, shift_vec):
    left_map = reduced_pair[0]
    right_map = reduced_pair[1]
    totals = lax.psum(
        (
            jnp.sum(left_map, 0),
            jnp.sum(left_map * left_map, 0),
            jnp.sum(right_map, 0),
            jnp.sum(right_map * right_map, 0),
        ),
        "rows",
    )
    results = []
    for member in range(2):
        values = reduced_pair[member]
        pixel_count = values.shape[0] * lax.axis_size("rows")
        channel_mean = totals[2 * member] / pixel_count
        inverse_scale = lax.rsqrt(
            totals[2 * member + 1] / pixel_count - channel_mean * channel_mean + EPSILON
        )
        centred = (values - channel_mean) * inverse_scale
        results.append((centred, inverse_scale, gain_vec * centred + shift_vec))
    return results


def unstandardize(slopes, saved, gain_vec):
    shift_left = jnp.sum(slopes[0], 0)
    gain_left = jnp.sum(slopes[0] * saved[0][0], 0)
    shift_right = jnp.sum(slopes[1], 0)
    gain_right = jnp.sum(slopes[1] * saved[1][0], 0)
    totals = lax.psum((shift_left, gain_left, shift_right, gain_right), "rows")
    results = []
    for member in range(2):
        pixel_count = slopes[member].shape[0] * lax.axis_size("rows")
        centred = saved[member][0]
        inverse_scale = saved[member][1]
        mean_slope = gain_vec * totals[2 * member] / pixel_count
        mean_cross = gain_vec * totals[2 * member + 1] / pixel_count
        results.append(
            inverse_scale * (gain_vec * slopes[member] - mean_slope - centred * mean_cross)
        )
    return (results, gain_left + gain_right, shift_left + shift_right)


def spread_rows(activity):
    return extended(activity, (("rows", 1),), 1)


def spread_grads(slopes):
    return extended(slopes, (("rows", 1),), 1)


def patches(padded, row_count, col_count, flipped):
    widened = jnp.pad(padded, ((0, 0), (0, 0), (1, 1), (0, 0)))
    tap_list = []
    for row_tap in range(3):
        for col_tap in range(3):
            row_start = 2 - row_tap if flipped else row_tap
            col_start = 2 - col_tap if flipped else col_tap
            tap_list.append(
                widened[:, row_start : row_start + row_count, col_start : col_start + col_count, :]
            )
    return jnp.concatenate(tap_list, axis=-1).reshape(-1, 9 * widened.shape[-1])


def body(
    views,
    crops,
    w_reduce,
    gain_one,
    shift_one,
    w_spatial,
    gain_two,
    shift_two,
    w_expand,
    gain_three,
    shift_three,
    cot_views,
    cot_crops,
):
    gathered = (
        lax.all_gather(w_reduce, "dp", axis=0, tiled=True),
        lax.all_gather(gain_one, "dp", axis=0, tiled=True),
        lax.all_gather(shift_one, "dp", axis=0, tiled=True),
        lax.all_gather(w_spatial, "dp", axis=2, tiled=True),
        lax.all_gather(gain_two, "dp", axis=0, tiled=True),
        lax.all_gather(shift_two, "dp", axis=0, tiled=True),
        lax.all_gather(w_expand, "dp", axis=0, tiled=True),
        lax.all_gather(gain_three, "dp", axis=0, tiled=True),
        lax.all_gather(shift_three, "dp", axis=0, tiled=True),
    )
    weight_reduce = gathered[0]
    weight_spatial = gathered[3]
    weight_expand = gathered[6]
    gain_first = gathered[1].astype(jnp.float32)
    shift_first = gathered[2].astype(jnp.float32)
    gain_second = gathered[4].astype(jnp.float32)
    shift_second = gathered[5].astype(jnp.float32)
    gain_third = gathered[7].astype(jnp.float32)
    shift_third = gathered[8].astype(jnp.float32)
    channels = views.shape[4]
    middle = weight_reduce.shape[1]
    map_shapes = [
        (views.shape[0] * views.shape[1], views.shape[2], views.shape[3]),
        (crops.shape[0] * crops.shape[1], crops.shape[2], crops.shape[3]),
    ]
    flat_inputs = [views.reshape(-1, channels), crops.reshape(-1, channels)]
    reduced = [
        jnp.dot(source, weight_reduce, preferred_element_type=jnp.float32) for source in flat_inputs
    ]
    first_norm = standardize(reduced, gain_first, shift_first)
    first_act = [jax.nn.silu(saved[2]).astype(jnp.bfloat16) for saved in first_norm]
    padded_act = [
        spread_rows(act.reshape(shape[0], shape[1], shape[2], middle))
        for act, shape in zip(first_act, map_shapes)
    ]
    patch_rows = [
        patches(padded, shape[1], shape[2], False) for padded, shape in zip(padded_act, map_shapes)
    ]
    kernel = weight_spatial.reshape(9 * middle, middle)
    spatial = [jnp.dot(patch, kernel, preferred_element_type=jnp.float32) for patch in patch_rows]
    second_norm = standardize(spatial, gain_second, shift_second)
    second_act = [jax.nn.silu(saved[2]).astype(jnp.bfloat16) for saved in second_norm]
    expanded = [
        jnp.dot(act, weight_expand, preferred_element_type=jnp.float32) for act in second_act
    ]
    third_norm = standardize(expanded, gain_third, shift_third)
    pre_list = [
        source.astype(jnp.float32) + saved[2] for source, saved in zip(flat_inputs, third_norm)
    ]
    activation = [jax.nn.silu(pre) for pre in pre_list]
    view_sums = jnp.sum(activation[0].reshape(views.shape[0], views.shape[1], -1, channels), axis=2)
    crop_sums = jnp.sum(activation[1].reshape(crops.shape[0], crops.shape[1], -1, channels), axis=2)
    pooled_sums = lax.psum((view_sums, crop_sums), "rows")
    pooled = jnp.concatenate(
        [
            pooled_sums[0] / (views.shape[3] * views.shape[3]),
            pooled_sums[1] / (crops.shape[3] * crops.shape[3]),
        ],
        axis=1,
    )
    cotangent = [
        cot_views.reshape(-1, channels).astype(jnp.float32),
        cot_crops.reshape(-1, channels).astype(jnp.float32),
    ]
    d_pre = [cot * silu_slope(pre) for cot, pre in zip(cotangent, pre_list)]
    d_expanded_f, gain_third_grad, shift_third_grad = unstandardize(d_pre, third_norm, gain_third)
    d_expanded = [grad.astype(jnp.bfloat16) for grad in d_expanded_f]
    expand_grad = jnp.einsum(
        "pm,pc->mc", second_act[0], d_expanded[0], preferred_element_type=jnp.float32
    ) + jnp.einsum("pm,pc->mc", second_act[1], d_expanded[1], preferred_element_type=jnp.float32)
    d_norm_two = [
        jnp.einsum("pc,mc->pm", grad, weight_expand, preferred_element_type=jnp.float32)
        * silu_slope(saved[2])
        for grad, saved in zip(d_expanded, second_norm)
    ]
    d_spatial_f, gain_second_grad, shift_second_grad = unstandardize(
        d_norm_two, second_norm, gain_second
    )
    d_spatial = [grad.astype(jnp.bfloat16) for grad in d_spatial_f]
    spatial_grad = (
        jnp.einsum("pk,pm->km", patch_rows[0], d_spatial[0], preferred_element_type=jnp.float32)
        + jnp.einsum("pk,pm->km", patch_rows[1], d_spatial[1], preferred_element_type=jnp.float32)
    ).reshape(3, 3, middle, middle)
    back_kernel = jnp.transpose(weight_spatial, (0, 1, 3, 2)).reshape(9 * middle, middle)
    padded_grads = [
        spread_grads(grad.reshape(shape[0], shape[1], shape[2], middle))
        for grad, shape in zip(d_spatial, map_shapes)
    ]
    d_norm_one = [
        jnp.dot(
            patches(padded, shape[1], shape[2], True),
            back_kernel,
            preferred_element_type=jnp.float32,
        )
        * silu_slope(saved[2])
        for padded, shape, saved in zip(padded_grads, map_shapes, first_norm)
    ]
    d_reduced_f, gain_first_grad, shift_first_grad = unstandardize(
        d_norm_one, first_norm, gain_first
    )
    d_reduced = [grad.astype(jnp.bfloat16) for grad in d_reduced_f]
    reduce_grad = jnp.einsum(
        "pc,pm->cm", flat_inputs[0], d_reduced[0], preferred_element_type=jnp.float32
    ) + jnp.einsum("pc,pm->cm", flat_inputs[1], d_reduced[1], preferred_element_type=jnp.float32)
    input_grads = [
        (
            pre_grad
            + jnp.einsum("pm,cm->pc", grad, weight_reduce, preferred_element_type=jnp.float32)
        ).astype(jnp.bfloat16)
        for pre_grad, grad in zip(d_pre, d_reduced)
    ]
    shares = (
        lax.psum_scatter(reduce_grad, "dp", scatter_dimension=0, tiled=True),
        lax.psum_scatter(gain_first_grad, "dp", scatter_dimension=0, tiled=True),
        lax.psum_scatter(shift_first_grad, "dp", scatter_dimension=0, tiled=True),
        lax.psum_scatter(spatial_grad, "dp", scatter_dimension=2, tiled=True),
        lax.psum_scatter(gain_second_grad, "dp", scatter_dimension=0, tiled=True),
        lax.psum_scatter(shift_second_grad, "dp", scatter_dimension=0, tiled=True),
        lax.psum_scatter(expand_grad, "dp", scatter_dimension=0, tiled=True),
        lax.psum_scatter(gain_third_grad, "dp", scatter_dimension=0, tiled=True),
        lax.psum_scatter(shift_third_grad, "dp", scatter_dimension=0, tiled=True),
    )
    summed = lax.psum(
        (
            shares[0],
            shares[1],
            shares[2],
            shares[3],
            shares[4],
            shares[5],
            shares[6],
            shares[7],
            shares[8],
        ),
        "rows",
    )
    return (
        activation[0].astype(jnp.bfloat16).reshape(views.shape),
        activation[1].astype(jnp.bfloat16).reshape(crops.shape),
        pooled,
        input_grads[0].reshape(views.shape),
        input_grads[1].reshape(crops.shape),
        summed[0],
        summed[1],
        summed[2],
        summed[3],
        summed[4],
        summed[5],
        summed[6],
        summed[7],
        summed[8],
    )


MESH = pl.DeviceIdType.MESH
SEMAPHORES = 167
F32 = jnp.float32
BF16 = jnp.bfloat16
NV = 512
NC = 256
N = NV + NC
KINDS = ((0, NV), (NV, NC))
NT = (((1,), (1,)), ((), ()))
TN = (((0,), (0,)), ((), ()))


def sigmoid(values):
    return 0.5 * jnp.tanh(0.5 * values) + 0.5


def dot(left, right, dims=(((1,), (0,)), ((), ()))):
    return lax.dot_general(left, right, dims, preferred_element_type=F32)


def moved(values, kind, step):
    rows, lanes = values.shape
    if step == 0:
        return values
    if kind == 0:
        maps = values.reshape(rows // 64, 64, lanes)
        gap = jnp.zeros((rows // 64, 8, lanes), values.dtype)
        parts = [gap, maps[:, :-8]] if step > 0 else [maps[:, 8:], gap]
        return jnp.concatenate(parts, axis=1).reshape(rows, lanes)
    gap = jnp.zeros((64, lanes), values.dtype)
    return jnp.concatenate([gap, values[:-64]] if step > 0 else [values[64:], gap], axis=0)


def turned(values, kind, step):
    if step == 0:
        return values
    rows, lanes = values.shape
    width = 8 if kind == 0 else 4
    col = lax.rem(lax.broadcasted_iota(jnp.int32, (rows, lanes), 0), width)
    edge = 0 if step > 0 else width - 1
    return jnp.where(col == edge, 0.0, pltpu.roll(values, 1 if step > 0 else rows - 1, axis=0))


def block_kernel(
    views, crops, w_reduce, w_spatial, w_expand, cot_views, cot_crops, gain_a, shift_a, gain_b, shift_b, gain_c, shift_c,
    out_views, out_crops, fin_p, grad_views, grad_crops, fin_e, fin_s, fin_r, pgs,
    xv, xc4, xc, cv, cc4, cc, xo_v, xo_c, co_v, co_c, wr, ws, we, aff, raw_a, raw_b, raw_c, raw_d, raw_e, raw_f, pg,
    part, csend, crecv, xsend, xrecv,
    act1, act2, dred, conv, xhat1, slope1, xhat2, slope2, ex, dpre, dex, pat, dpo, pool, rows_pool,
    ge, gs, gr, ysend_e, yrecv_e, zsend_e, zrecv_e, ysend_s, yrecv_s, zsend_s, zrecv_s, ysend_r, yrecv_r, zsend_r, zrecv_r,
    acc_e, acc_s, acc_r, pgr,
    sem,
):
    i, r = lax.axis_index("dp"), lax.axis_index("rows")
    z, y = i // 2, i % 2
    x, c = r // 2, r % 2
    yp = (i + 1 - 2 * y, r)
    cp = (i, 2 * x + 1 - c)
    xp = (i, 2 * (1 - x) + c)
    xcp = (i, 2 * (1 - x) + 1 - c)
    rest = (xp, xcp, cp)

    middle = (z + 1) // 2 == 1
    step = 1 - 2 * (z // 2)

    def on_line(places):
        return (2 * (z + places * step) + y, r)

    taken = [0]

    def new(count=1):
        taken[0] += count
        return taken[0] - count

    def copy(src, dst, send, recv, dev):
        return pltpu.make_async_remote_copy(
            src_ref=src, dst_ref=dst, send_sem=sem.at[send], recv_sem=sem.at[recv], device_id=dev, device_id_type=MESH
        )

    def got(ref, recv):
        copy(ref, ref, recv, recv, cp).wait_recv()

    def sent(ref, send):
        copy(ref, ref, send, send, cp).wait_send()

    def stored(ref, one):
        pltpu.make_async_copy(ref, ref, sem.at[one]).wait()

    def lanes(k, xx, cc_):
        return pl.ds(pl.multiple_of(512 * k + 256 * cc_ + 128 * xx, 128), 128)

    def kl(k):
        return pl.ds(128 * k, 128)

    def kind_rows(kind):
        return pl.ds(*KINDS[kind])

    def stage(src, dst, one):
        pltpu.make_async_copy(src, dst, sem.at[one]).start()

    l_wr, l_ws, l_we, l_we2, l_gain = new(), new(), new(), new(), new(6)
    l_x, l_cot, l_own = (new(), new()), (new(), new()), new(4)

    @pl.when(y == c)
    def _():
        stage(w_reduce.at[pl.ds(pl.multiple_of(128 * x, 128), 128)], wr.at[r, z], l_wr)

    stage(w_spatial.at[:, :, pl.ds(pl.multiple_of(128 * r, 128), 128)], ws.at[:, i], l_ws)
    raw = (raw_a, raw_b, raw_c, raw_d, raw_e, raw_f)
    for n, vec in enumerate((gain_a, shift_a, gain_b, shift_b, gain_c, shift_c)):
        stage(vec, raw[n], l_gain + n)
    for k in range(4):
        stage(views.at[:, :, lanes(k, x, c)], xv.at[:, r, :, kl(k)], l_x[0])
        stage(crops.at[:, :, lanes(k, x, c)], xc4.at[r, :, :, kl(k)], l_x[1])
    for k in range(4):
        stage(w_expand.at[:, lanes(k, x, c)], we.at[r, i, :, kl(k)], l_we)
        stage(w_expand.at[:, lanes(k, 1 - x, c)], we.at[xp[1], i, :, kl(k)], l_we2)
    for k in range(4):
        stage(cot_views.at[:, :, lanes(k, x, c)], cv.at[:, r, :, kl(k)], l_cot[0])
        stage(cot_crops.at[:, :, lanes(k, x, c)], cc4.at[r, :, :, kl(k)], l_cot[1])
    for n, (src, dst) in enumerate(((views, xo_v), (crops, xo_c), (cot_views, co_v), (cot_crops, co_c))):
        stage(src, dst, l_own + n)

    bar = pltpu.get_barrier_semaphore()
    peers = [((i + n) % 8, r) for n in range(1, 8)] + [cp, xp, xcp]
    for dev in peers:
        pl.semaphore_signal(bar, inc=1, device_id=dev, device_id_type=MESH)
    pl.semaphore_wait(bar, len(peers))

    class Share:
        def __init__(self, parts, others):
            self.parts, self.others = parts, others
            count = len(parts(0))
            self.send, self.passed = new(), new()
            self.along_z = [new(3) for _ in range(count)]
            self.along_y = [new() for _ in range(count)]

    share_r = Share(lambda k: (wr.at[r, k],), None)
    share_s = Share(
        lambda k: tuple(ws.at[pl.ds(3 * h, 3), 2 * k + y] for h in range(3)),
        lambda h: ws.at[pl.ds(3 * h, 3), pl.ds(0, 4)],
    )
    share_e = Share(lambda k: (we.at[r, 2 * k + y],), lambda h: we.at[0, pl.ds(0, 4)])
    share_o = Share(lambda k: (we.at[xp[1], 2 * k + y],), lambda h: we.at[0, pl.ds(0, 4)])

    inner = ((z + 1) // 2) * (2 - (z + 1) // 2)

    def line_send(share, direct=False):
        for h, own in enumerate(share.parts(z)):

            def go(slot, dev, own=own):
                copy(own, own, share.send, slot, dev).start()

            go(share.along_z[h], on_line(2))
            go(share.along_z[h] + 2 - inner, on_line(1))

            @pl.when(middle)
            def _(go=go, h=h):
                go(share.along_z[h] + 1, on_line(-1))

            if direct:

                @pl.when(jnp.logical_not(middle))
                def _(go=go, h=h):
                    go(share.along_z[h] + 2, on_line(3))

    def line_over(share):
        for h, own in enumerate(share.parts(z)):
            copy(own, own, share.send, share.along_y[h], yp).start()

    def line_pass(share, h, send=None, which=(0, 1, 2)):
        relayed = send is None
        send = share.send if relayed else send

        def take(places, slot, on=False):
            if slot not in which:
                return
            ref = share.parts(z + places * step)[h]
            got(ref, share.along_z[h] + slot)
            if on:
                copy(ref, ref, send, share.along_z[h] + 2, on_line(-1)).start()
            copy(ref, ref, send, share.along_y[h], yp).start()

        @pl.when(middle)
        def _():
            take(2, 0, relayed)
            take(1, 1)
            take(-1, 2)

        @pl.when(jnp.logical_not(middle))
        def _():
            take(2, 0)
            take(1, 1)
            take(3, 2)

    def line_got(share):
        for h, slot in enumerate(share.along_y):
            got(share.others(h), slot)

    def line_sent(send, for_middle, for_end):
        @pl.when(middle)
        def _():
            sent(for_middle, send)

        @pl.when(jnp.logical_not(middle))
        def _():
            sent(for_end, send)

    @pl.when(y == c)
    def _():
        stored(wr.at[r, z], l_wr)
        line_send(share_r, True)
        line_over(share_r)

    s_sx, s_rx = ((new(), new()), (new(), new())), ((new(), new()), (new(), new()))

    def spread_v(src, dst, s, devs):
        for dev in devs:
            for k in range(4):
                copy(src.at[:, :, lanes(k, dev[1] // 2, dev[1] % 2)], dst.at[:, r, :, kl(k)], s_sx[s][0], s_rx[s][0], dev).start()

    def spread_c(src, dst, s, devs):
        for dev in devs:
            for k in range(4):
                copy(src.at[:, :, lanes(k, dev[1] // 2, dev[1] % 2)], dst.at[r, :, :, kl(k)], s_sx[s][1], s_rx[s][1], dev).start()

    spread_v(views, xv, 0, rest)
    spread_c(crops, xc4, 0, rest)
    spread_v(cot_views, cv, 1, rest[:1])
    spread_c(cot_crops, cc4, 1, rest[:1])
    stored(ws.at[:, i], l_ws)
    line_over(share_s)

    for n in range(6):
        stored(raw[n], l_gain + n)
    pg[i] = jnp.zeros((8, 128), F32)
    for n in range(4):
        vec = raw[n][...].reshape(1, 64).astype(F32)
        pg[i, n : n + 1, :] = jnp.concatenate([vec, vec], axis=1)
    for n in range(2):
        for m in range(2):
            pg[i, 4 + 2 * n + m : 5 + 2 * n + m, :] = raw[4 + n][128 * m : 128 * m + 128].reshape(1, 128).astype(F32)
    s_pg, r_pg = new(), new()
    for dev in peers[:7]:
        copy(pg.at[i], pg.at[i], s_pg, r_pg, dev).start()

    @pl.when(y == c)
    def _():
        line_pass(share_r, 0, share_r.passed)

    got(pg.at[pl.ds(0, 7)], r_pg)
    line_send(share_s)
    stored(xv.at[:, r], l_x[0])
    got(xv.at[:, pl.ds(0, 3)], s_rx[0][0])

    @pl.when(y != c)
    def _():
        got(wr.at[r], share_r.along_y[0])

    s_cs, r_cs = new(3), new(12)
    s_xs, r_xs = new(3), new(6)
    s_ag, r_ag = new(3), new(8)

    def scatter_start(op, kind, sums):
        rows = kind_rows(kind)
        n = pl.ds(0, KINDS[kind][1])
        for s in range(4):
            part[op, s, rows, :] = sums[:, 128 * s : 128 * s + 128]
        for near, xx in enumerate((1 - x, x)):
            csend[op, kind, xx, n, :] = part[op, 2 * xx + 1 - c, rows, :].astype(BF16)
            own = csend.at[op, kind, xx, n]
            copy(own, crecv.at[op, kind, xx, n], s_cs + op, r_cs + 4 * op + 2 * kind + near, cp).start()

    def scatter_mid(op, kind):
        rows = kind_rows(kind)
        n = pl.ds(0, KINDS[kind][1])
        got(crecv.at[op, kind, 1 - x, n], r_cs + 4 * op + 2 * kind)
        far = part[op, 2 * (1 - x) + c, rows, :] + crecv[op, kind, 1 - x, n, :].astype(F32)
        xsend[op, kind, 0, n, :] = far.astype(BF16)
        copy(xsend.at[op, kind, 0, n], xrecv.at[op, kind, 0, n], s_xs + op, r_xs + 2 * op + kind, xp).start()

    def scatter_end(op, kind):
        rows = kind_rows(kind)
        n = pl.ds(0, KINDS[kind][1])
        got(crecv.at[op, kind, x, n], r_cs + 4 * op + 2 * kind + 1)
        near = part[op, 2 * x + c, rows, :] + crecv[op, kind, x, n, :].astype(F32)
        got(xrecv.at[op, kind, 0, n], r_xs + 2 * op + kind)
        return near + xrecv[op, kind, 0, n, :].astype(F32)

    def gather_start(kind, buf, value):
        rows = kind_rows(kind)
        buf[r, rows, :] = value
        own = buf.at[r, rows]
        copy(own, own, s_ag + 1, r_ag + 6 + kind, xp).start()
        copy(own, own, s_ag + 1, r_ag + 2 + kind, cp).start()

    def gather_mid(kind, buf):
        far = buf.at[xp[1], kind_rows(kind)]
        got(far, r_ag + 6 + kind)
        copy(far, far, s_ag + 1, r_ag + 2 + kind, cp).start()

    def gather_end(op, kind, buf):
        rows = kind_rows(kind)
        got(buf.at[pl.ds(0, 2), rows], r_ag + 2 * op + kind)
        return jnp.concatenate([buf[s, rows, :] for s in range(4)], axis=1)

    def both_mid(op, kind):
        rows = kind_rows(kind)
        n = pl.ds(0, KINDS[kind][1])
        for near, xx in enumerate((1 - x, x)):
            got(crecv.at[op, kind, xx, n], r_cs + 4 * op + 2 * kind + near)
        for xx in range(2):
            total = part[op, 2 * xx + c, rows, :] + crecv[op, kind, xx, n, :].astype(F32)
            part[op, 2 * xx + c, rows, :] = total
            xsend[op, kind, xx, n, :] = total.astype(BF16)
        both = xsend.at[op, kind, :, n]
        copy(both, xrecv.at[op, kind, :, n], s_xs + op, r_xs + 2 * op + kind, xp).start()

    def both_end(op, kind):
        rows = kind_rows(kind)
        n = pl.ds(0, KINDS[kind][1])
        got(xrecv.at[op, kind, :, n], r_xs + 2 * op + kind)
        return jnp.concatenate(
            [part[op, 2 * xx + c, rows, :] + xrecv[op, kind, xx, n, :].astype(F32) for xx in range(2)], axis=1
        )

    def both_out(op, kind, buf, value):
        rows = kind_rows(kind)
        for xx in range(2):
            buf[2 * xx + c, rows, :] = value[:, 128 * xx : 128 * xx + 128]
            own = buf.at[2 * xx + c, rows]
            copy(own, own, s_ag + op, r_ag + 2 * op + kind, cp).start()

    weight_r = wr[r].reshape(512, 512)
    scatter_start(0, 0, dot(xv[...].reshape(NV, 512), weight_r))
    stored(xc4.at[r], l_x[1])
    got(xc4.at[pl.ds(0, 3)], s_rx[0][1])
    xc[...] = xc4[...].reshape(4, 64, 512)
    scatter_start(0, 1, dot(xc[...].reshape(NC, 512), weight_r))
    line_pass(share_s, 0, None, (0, 1))
    both_mid(0, 0)
    both_mid(0, 1)

    half = lax.broadcasted_iota(jnp.int32, (1, 128), 1) < 64

    def slice_of(s, q):
        return jnp.where(half, pg[2 * s, q : q + 1, :], pg[2 * s + 1, q : q + 1, :])

    gain1, shift1 = [jnp.concatenate([slice_of(c, q), slice_of(2 + c, q)], axis=1) for q in range(2)]
    gain2, shift2 = slice_of(r, 2), slice_of(r, 3)
    gain3 = jnp.concatenate([pg[2 * k + c, pl.ds(4 + x, 1), :] for k in range(4)], axis=1)
    shift3 = jnp.concatenate([pg[2 * k + c, pl.ds(6 + x, 1), :] for k in range(4)], axis=1)

    def norm_act(values, rows, gain, shift):
        mean = jnp.sum(values, axis=0, keepdims=True) / rows
        second = jnp.sum(values * values, axis=0, keepdims=True) / rows
        rstd = lax.rsqrt(second - mean * mean + EPSILON)
        xhat = (values - mean) * rstd
        norm = gain * xhat + shift
        sig = sigmoid(norm)
        return rstd, xhat, sig * (1.0 + norm * (1.0 - sig)), (norm * sig).astype(BF16)

    for h, which in ((1, (0, 1)), (0, (2,)), (2, (0, 1)), (1, (2,)), (2, (2,))):
        line_pass(share_s, h, None, which)
    stored(we.at[r, i], l_we)
    stored(we.at[r, i], l_we2)
    for share in (share_e, share_o):
        line_send(share, True)
        line_over(share)
    rstd1, rstd2 = [None, None], [None, None]
    for kind in range(2):
        rows = KINDS[kind][1]
        rstd1[kind], xh, sl, act = norm_act(both_end(0, kind), rows, gain1, shift1)
        both_out(0, kind, act1, act)
        xhat1[kind_rows(kind), :] = xh
        slope1[kind_rows(kind), :] = sl
        if kind == 0:
            spread_v(cot_views, cv, 1, rest[1:])

    s_ow, s_xw, r_xw, r_ow = new(), new(), new(), new(2)

    def over_x(k):
        copy(wr.at[r, k], wr.at[r, k], s_xw, r_xw, xp).start()

    def between(ref, n):
        copy(ref, ref, s_ow, r_ow + n, cp).start()

    between(wr.at[r], 0)
    line_pass(share_e, 0, share_e.passed, (0,))
    line_got(share_s)
    line_pass(share_e, 0, share_e.passed, (1,))

    def weight_s():
        return jnp.concatenate([ws[t].reshape(512, 128) for t in range(9)], axis=1)

    for kind in range(2):
        rows = KINDS[kind][1]
        conv[kind_rows(kind), :] = dot(gather_end(0, kind, act1), weight_s())
        taps = [conv[kind_rows(kind), 128 * t : 128 * t + 128] for t in range(9)]
        spatial = None
        for j in range(3):
            col = taps[3 + j] + moved(taps[j], kind, 1) + moved(taps[6 + j], kind, -1)
            col = turned(col, kind, 1 - j)
            spatial = col if spatial is None else spatial + col
        rstd2[kind], xh, sl, act = norm_act(spatial, rows, gain2, shift2)
        gather_start(kind, act2, act)
        xhat2[kind_rows(kind), :] = xh
        slope2[kind_rows(kind), :] = sl
        if kind == 0:
            line_pass(share_e, 0, share_e.passed, (2,))
    spread_c(cot_crops, cc4, 1, rest[1:])
    over_x(0)
    over_x(1)
    pool[...] = jnp.zeros_like(pool)
    gather_mid(0, act2)
    stored(cv.at[:, r], l_cot[0])
    got(cv.at[:, pl.ds(0, 3)], s_rx[1][0])
    line_got(share_e)
    line_pass(share_o, 0, share_o.passed)
    between(we.at[r], 1)
    weight_e = we[r].reshape(512, 512)

    sum_x3, sum_d3 = [], []
    zero8 = jnp.zeros((8, 512), F32)

    def expand(kind):
        start, rows = KINDS[kind]
        ex[kind_rows(kind), :] = dot(gather_end(1, kind, act2), weight_e)

        def moments(b, acc):
            e = ex[pl.ds(pl.multiple_of(start + 32 * b, 32), 32), :].reshape(4, 8, 512)
            return acc[0] + jnp.sum(e, axis=0), acc[1] + jnp.sum(e * e, axis=0)

        tot, sq = lax.fori_loop(0, rows // 32, moments, (zero8, zero8))
        if kind == 0:
            gather_mid(1, act2)
        mean = jnp.sum(tot, axis=0, keepdims=True) / rows
        rstd = lax.rsqrt(jnp.sum(sq, axis=0, keepdims=True) / rows - mean * mean + EPSILON)

        def finish(b, acc):
            rs = pl.ds(pl.multiple_of(start + 16 * b, 16), 16)
            qs = pl.ds(pl.multiple_of(16 * (b % 4), 16), 16)
            xhat = (ex[rs, :] - mean) * rstd
            ex[rs, :] = xhat
            src = xv[b // 4, b % 4] if kind == 0 else xc[b // 4, qs, :]
            cot = cv[b // 4, b % 4] if kind == 0 else cc[b // 4, qs, :]
            pre = src.astype(F32) + (gain3 * xhat + shift3)
            sig = sigmoid(pre)
            activation = pre * sig
            d = cot.astype(F32) * (sig * (1.0 + pre * (1.0 - sig)))
            dpre[rs, :] = d
            if kind == 0:
                pool[b // 4] += activation[:8] + activation[8:]
            else:
                pool[8 + 2 * (b % 4)] += activation[:8]
                pool[9 + 2 * (b % 4)] += activation[8:]
            dx = d * xhat
            return acc[0] + (d[:8] + d[8:]), acc[1] + (dx[:8] + dx[8:])

        sd, sxx = lax.fori_loop(0, rows // 16, finish, (zero8, zero8))
        sd, sxx = jnp.sum(sd, axis=0, keepdims=True), jnp.sum(sxx, axis=0, keepdims=True)
        sum_d3.append(sd)
        sum_x3.append(sxx)
        scale = gain3 * rstd
        mean_d, mean_x = sd / rows, sxx / rows
        aff[r, 2 * kind : 2 * kind + 1, :] = scale
        aff[r, 2 * kind + 1 : 2 * kind + 2, :] = shift3 - scale * mean

        def back(b, _):
            rs = pl.ds(pl.multiple_of(start + 32 * b, 32), 32)
            dex[rs, :] = (scale * (dpre[rs, :] - mean_d - ex[rs, :] * mean_x)).astype(BF16)
            return 0

        lax.fori_loop(0, rows // 32, back, 0)

    def own_rows(buf):
        slices = []
        for s in range(4):
            rows = [buf[s, pl.ds(pl.multiple_of(64 * m + 16 * r, 16), 16), :] for m in range(8)]
            rows.append(buf[s, pl.ds(pl.multiple_of(NV + 64 * r, 64), 64), :])
            slices.append(jnp.concatenate(rows, axis=0))
        return jnp.concatenate(slices, axis=1)

    def own_blocks(values, s):
        for k in range(4):
            lo = 512 * k + 256 * (s % 2) + 128 * (s // 2)
            yield k, slice(lo, lo + 128), (values[:128, 128 * k : 128 * k + 128], values[128:, 128 * k : 128 * k + 128])

    def own_output():
        act = own_rows(act2)
        for s in range(4):
            for k, cols, blocks in own_blocks(dot(act, we[s].reshape(512, 512)), s):
                for kind, block in enumerate(blocks):
                    scale = aff[s, 2 * kind : 2 * kind + 1, 128 * k : 128 * k + 128]
                    shift = aff[s, 2 * kind + 1 : 2 * kind + 2, 128 * k : 128 * k + 128]
                    src = (xo_v if kind == 0 else xo_c)[:, :, cols].reshape(block.shape).astype(F32)
                    cot = (co_v if kind == 0 else co_c)[:, :, cols].reshape(block.shape).astype(F32)
                    pre = src + (scale * block + shift)
                    sig = sigmoid(pre)
                    if kind == 0:
                        out_views[:, :, cols] = (pre * sig).astype(BF16).reshape(8, 16, 128)
                    else:
                        out_crops[:, cols] = (pre * sig).astype(BF16)
                    dpo[128 * kind : 128 * kind + block.shape[0], cols] = cot * (sig * (1.0 + pre * (1.0 - sig)))

    def own_gradient():
        back = own_rows(dred)
        for s in range(4):
            for _, cols, blocks in own_blocks(dot(back, wr[s].reshape(512, 512), NT), s):
                grad_views[:, :, cols] = (dpo[:128, cols] + blocks[0]).astype(BF16).reshape(8, 16, 128)
                grad_crops[:, cols] = (dpo[128:, cols] + blocks[1]).astype(BF16)

    far_of = jnp.where(middle, z + 2 * step, z + 3 * step)
    mid_of = jnp.where(middle, z - step, z + 2 * step)
    order = [far_of, mid_of, z + step, z]

    class Grad:
        def __init__(self, full, ysend, yrecv, zsend, zrecv, acc, both=True):
            self.full, self.ysend, self.yrecv, self.zsend, self.zrecv = full, ysend, yrecv, zsend, zrecv
            self.acc, self.both = acc, both
            self.s_y, self.r_y, self.s_z, self.r_z = new(), new(4), new(), new()

        def start(self):
            for k in order:
                self.ysend[k] = (self.full[k, 1 - y] if self.both else self.full[k]).astype(BF16)
                copy(self.ysend.at[k], self.yrecv.at[k], self.s_y, self.r_y + k, yp).start()

        def add(self, k):
            got(self.yrecv.at[k], self.r_y + k)
            return (self.full[k, y] if self.both else self.full[k]) + self.yrecv[k].astype(F32)

        def send(self, k, value):
            self.zsend[k] = value.astype(BF16)
            copy(self.zsend.at[k], self.zrecv.at[z], self.s_z, self.r_z, (2 * k + y, r)).start()

        def along(self):
            for k in order[:3]:
                self.send(k, self.add(k))

        def total(self):
            self.acc[...] = self.add(z)
            got(self.zrecv.at[pl.ds(0, 3)], self.r_z)
            self.acc[...] += self.zrecv[order[0]].astype(F32) + self.zrecv[order[1]].astype(F32)
            return self.acc[...] + self.zrecv[order[2]].astype(F32)

        def sent(self):
            sent(self.zsend.at[pl.ds(0, 3)], self.s_z)

    class Slices:
        def __init__(self, buf):
            self.buf, self.send, self.far, self.near = buf, new(), new(), new()

        def start(self, value):
            self.buf[r] = value.astype(BF16)
            copy(self.buf.at[r], self.buf.at[r], self.send, self.far, xp).start()
            copy(self.buf.at[r], self.buf.at[r], self.send, self.near, cp).start()

        def mid(self):
            far = self.buf.at[xp[1]]
            got(far, self.far)
            copy(far, far, self.send, self.near, cp).start()

        def end(self):
            got(self.buf.at[pl.ds(0, 2)], self.near)
            sent(self.buf.at[pl.ds(0, 3)], self.send)

    grad_e = Grad(ge, ysend_e, yrecv_e, zsend_e, zrecv_e, acc_e)
    grad_s = [
        Grad(*(one.at[q] for one in (gs, ysend_s, yrecv_s, zsend_s, zrecv_s, acc_s))) for q in range(3)
    ]
    grad_r = [Grad(*(one.at[q] for one in (gr, ysend_r, yrecv_r, zsend_r, zrecv_r, acc_r)), both=False) for q in range(2)]
    slices_p, slices_e, slices_s = Slices(fin_p), Slices(fin_e), [Slices(fin_s.at[q]) for q in range(3)]

    expand(0)
    scatter_start(1, 0, dot(dex[kind_rows(0), :], weight_e, NT))
    stored(cc4.at[r], l_cot[1])
    got(cc4.at[pl.ds(0, 3)], s_rx[1][1])
    cc[...] = cc4[...].reshape(4, 64, 512)
    expand(1)
    scatter_mid(1, 0)
    scatter_start(1, 1, dot(dex[kind_rows(1), :], weight_e, NT))
    ge[...] = dot(jnp.concatenate([act2[s] for s in range(4)], axis=1), dex[...], TN).reshape(4, 2, 64, 512)
    grad_e.start()
    scatter_mid(1, 1)
    s_af, r_af = new(), new()
    for dev in rest:
        copy(aff.at[r], aff.at[r], s_af, r_af, dev).start()

    def norm_back(d, xhat, rstd, gain, rows):
        sd = jnp.sum(d, axis=0, keepdims=True)
        sxx = jnp.sum(d * xhat, axis=0, keepdims=True)
        return (gain * rstd) * (d - sd / rows - xhat * (sxx / rows)), sd, sxx

    sum_d2, sum_x2 = [], []
    for kind in range(2):
        rows = KINDS[kind][1]
        d = scatter_end(1, kind) * slope2[kind_rows(kind), :]
        dz_, sd, sxx = norm_back(d, xhat2[kind_rows(kind), :], rstd2[kind], gain2, rows)
        sum_d2.append(sd)
        sum_x2.append(sxx)
        dz_ = dz_.astype(BF16).astype(F32)
        for tj in range(3):
            col = turned(dz_, kind, tj - 1)
            for ti in range(3):
                t = 3 * ti + tj
                pat[kind_rows(kind), 128 * t : 128 * t + 128] = moved(col, kind, ti - 1).astype(BF16)
        if kind == 1:
            both_mid(2, 0)
        scatter_start(2, kind, dot(pat[kind_rows(kind), :], weight_s(), NT))
    full1 = jnp.concatenate([act1[s] for s in range(4)], axis=1)
    grad_e.along()
    for q in range(3):
        gs[q] = dot(full1, pat[:, 384 * q : 384 * q + 384], TN).reshape(4, 2, 64, 384)
        grad_s[q].start()
    both_mid(2, 1)
    over_x(2)
    over_x(3)
    line_got(share_o)
    between(we.at[xp[1]], 1)
    grad_s[0].along()

    sum_d1, sum_x1 = [], []
    for kind in range(2):
        rows = KINDS[kind][1]
        d = both_end(2, kind) * slope1[kind_rows(kind), :]
        dz_, sd, sxx = norm_back(d, xhat1[kind_rows(kind), :], rstd1[kind], gain1, rows)
        sum_d1.append(sd)
        sum_x1.append(sxx)
        both_out(2, kind, dred, dz_.astype(BF16))

    gx1, gd1 = sum_x1[0] + sum_x1[1], sum_d1[0] + sum_d1[1]
    rows12 = [jnp.where(x == 0, g[:, :128], g[:, 128:]) for g in (gx1, gd1)]
    rows12 += [sum_x2[0] + sum_x2[1], sum_d2[0] + sum_d2[1]]
    gx3, gd3 = sum_x3[0] + sum_x3[1], sum_d3[0] + sum_d3[1]
    rows3 = [g[:, 128 * k : 128 * k + 128] for g in (gx3, gd3) for k in range(4)]
    pgr[i] = jnp.concatenate(rows12 + rows3 + [jnp.zeros((4, 128), F32)], axis=0)
    s_pp, r_pp, s_ps, r_ps = new(), new(), new(), new()
    for dev in peers[:7]:
        copy(pgr.at[i], pgr.at[i], s_pp, r_pp, dev).start()

    rows_pool[...] = jnp.zeros_like(rows_pool)
    for n in range(8):
        row = 4 * (n % 2) + n // 2
        rows_pool[row : row + 1, :] = jnp.sum(pool[n], axis=0, keepdims=True) / 64.0
        for m in range(2):
            row = 4 * (2 + 2 * (n % 2) + m) + n // 2
            rows_pool[row : row + 1, :] = jnp.sum(pool[8 + n, 4 * m : 4 * m + 4, :], axis=0, keepdims=True) / 16.0
    slices_p.start(rows_pool[...])
    grad_s[1].along()
    full_d = [gather_end(2, kind, dred) for kind in range(2)]

    for m in range(4):
        col = dot(xv[:, :, :, 128 * m : 128 * m + 128].reshape(NV, 128), full_d[0], TN)
        col = col + dot(xc[:, :, 128 * m : 128 * m + 128].reshape(NC, 128), full_d[1], TN)
        for q in range(2):
            gr[q, m] = col[:, 256 * q : 256 * q + 256]

    @pl.when(y != c)
    def _():
        for one in grad_r:
            one.start()

    for n, ref in enumerate((xo_v, xo_c, co_v, co_c)):
        stored(ref, l_own + n)
    got(aff.at[pl.ds(0, 3)], r_af)
    got(we.at[pl.ds(0, 2)], r_ow + 1)
    own_output()
    grad_s[2].along()
    slices_s[0].start(grad_s[0].total())
    slices_e.start(grad_e.total())
    got(wr.at[0], r_xw)
    between(wr.at[xp[1]], 0)

    @pl.when(y == c)
    def _():
        grad_r[0].along()
        grad_r[1].along()


    slices_s[1].start(grad_s[1].total())
    got(wr.at[pl.ds(0, 2)], r_ow)
    own_gradient()
    slices_p.mid()
    slices_e.mid()
    slices_s[0].mid()

    got(pgr.at[pl.ds(0, 7)], r_pp)
    total = pgr[0]
    for n in range(1, 8):
        total = total + pgr[n]
    pgs[r] = total
    for dev in rest:
        copy(pgs.at[r], pgs.at[r], s_ps, r_ps, dev).start()
    slices_s[2].start(grad_s[2].total())
    slices_s[1].mid()

    s_fr, r_fr = new(2), new(2)
    for q in range(2):

        @pl.when(y == c)
        def _(q=q):
            fin_r[q, x] = grad_r[q].total().astype(BF16)
            copy(fin_r.at[q, x], fin_r.at[q, x], s_fr + q, r_fr + q, xp).start()
            copy(fin_r.at[q, x], fin_r.at[q, x], s_fr + q, r_fr + q, cp).start()

    slices_s[2].mid()
    for q in range(2):

        @pl.when(y == c)
        def _(q=q):
            far = fin_r.at[q, 1 - x]
            got(far, r_fr + q)
            copy(far, far, s_fr + q, r_fr + q, cp).start()

    for one in (slices_p, slices_e, *slices_s):
        one.end()
    got(pgs.at[pl.ds(0, 3)], r_ps)
    sent(aff.at[pl.ds(0, 3)], s_af)
    sent(we, s_ow)
    sent(wr.at[0], s_xw)
    for s, (own_v, own_c) in enumerate(((xv, xc4), (cv, cc4))):
        sent(own_v.at[:, pl.ds(0, 3)], s_sx[s][0])
        sent(own_c.at[pl.ds(0, 3)], s_sx[s][1])
    sent(pg.at[pl.ds(0, 7)], s_pg)
    sent(pgr.at[pl.ds(0, 7)], s_pp)
    sent(pgs.at[pl.ds(0, 3)], s_ps)
    line_sent(share_s.send, ws, ws.at[:, pl.ds(0, 6)])
    for share in (share_e, share_o):
        sent(we.at[0, pl.ds(0, 4)], share.send)
        sent(we.at[0, pl.ds(0, 3)], share.passed)
    for op in range(3):
        sent(act1.at[pl.ds(0, 2)], s_cs + op)
        sent(act1.at[pl.ds(0, 1 if op == 1 else 2)], s_xs + op)
        sent(act1.at[pl.ds(0, 3 if op == 1 else 2)], s_ag + op)
    for one in (grad_e, *grad_s):
        sent(one.ysend, one.s_y)
        one.sent()

    @pl.when(y != c)
    def _():
        for q, one in enumerate(grad_r):
            sent(one.ysend, one.s_y)
            got(fin_r.at[q], r_fr + q)

    @pl.when(y == c)
    def _():
        sent(wr.at[0], share_r.send)
        sent(wr.at[0, pl.ds(0, 3)], share_r.passed)
        for q, one in enumerate(grad_r):
            one.sent()
            sent(one.zsend.at[pl.ds(0, 3)], s_fr + q)

    assert taken[0] == SEMAPHORES, taken


def store_kernel(
    out_v, out_c, pool, grad_v, grad_c, fin_e, fin_s, fin_r, sums,
    out_views, out_crops, pooled, grad_views, grad_crops, grad_reduce, grad_spatial, grad_expand,
    gain_a, shift_a, gain_b, shift_b, gain_c, shift_c,
    oc, pl_, gc, gr, gs, ge, sem,
):
    i = lax.axis_index("dp")
    z, y = i // 2, i % 2
    copies = []

    def store(src, dst):
        one = pltpu.make_async_copy(src, dst, sem.at[len(copies)])
        one.start()
        copies.append(one)

    store(out_v, out_views)
    store(grad_v, grad_views)
    for s in range(4):
        for t in range(9):
            gs[t, :, 128 * s : 128 * s + 128] = fin_s[t // 3, s, :, 128 * (t % 3) : 128 * (t % 3) + 128].astype(F32)
    store(gs, grad_spatial)
    for s in range(4):
        for k in range(4):
            lo = 512 * k + 256 * (s % 2) + 128 * (s // 2)
            ge[:, lo : lo + 128] = fin_e[s, :, 128 * k : 128 * k + 128].astype(F32)
    store(ge, grad_expand)
    for n in range(2):
        gr[:, 256 * n : 256 * n + 256] = fin_r[n].astype(F32).reshape(256, 256)
    store(gr, grad_reduce)
    oc[...] = out_c[...].reshape(16, 4, 2048)
    store(oc, out_crops)
    gc[...] = grad_c[...].reshape(16, 4, 2048)
    store(gc, grad_crops)
    for s in range(4):
        for k in range(4):
            lo = 512 * k + 256 * (s % 2) + 128 * (s // 2)
            pl_[:, :, lo : lo + 128] = pool[s, 0:24, 128 * k : 128 * k + 128].astype(F32).reshape(6, 4, 128)
    store(pl_, pooled)
    for n, out in enumerate((gain_a, shift_a, gain_b, shift_b)):
        row = sums[i // 2, n : n + 1, :]
        out[...] = jnp.where(i % 2 == 0, row[:, :64], row[:, 64:]).reshape(64)
    for n, out in enumerate((gain_c, shift_c)):
        out[...] = jnp.concatenate([sums[2 * m + y, pl.ds(4 + 4 * n + z, 1), :] for m in range(2)], axis=1).reshape(256)
    for one in copies:
        one.wait()


def fused(views, crops, w_reduce, w_spatial, w_expand, cot_views, cot_crops, *params):
    hbm, vmem = pl.BlockSpec(memory_space=pltpu.HBM), pl.BlockSpec(memory_space=pltpu.VMEM)

    def shape(dims, dtype):
        return jax.ShapeDtypeStruct(dims, dtype)

    def buf(dims, dtype=BF16):
        return pltpu.VMEM(dims, dtype)

    def dma(*dims):
        return pltpu.SemaphoreType.DMA(dims)

    held = pl.pallas_call(
        block_kernel,
        out_shape=[
            buf((8, 16, 2048)), buf((64, 2048)), buf((4, 32, 512)), buf((8, 16, 2048)), buf((64, 2048)),
            buf((4, 64, 512)), buf((3, 4, 64, 384)), buf((2, 2, 128, 256)), buf((4, 16, 128), F32),
        ],
        in_specs=[hbm] * 13,
        out_specs=[vmem] * 9,
        scratch_shapes=[
            buf((8, 4, 16, 512)), buf((4, 16, 4, 512)), buf((4, 64, 512)),
            buf((8, 4, 16, 512)), buf((4, 16, 4, 512)), buf((4, 64, 512)),
            buf((8, 16, 2048)), buf((16, 4, 2048)), buf((8, 16, 2048)), buf((16, 4, 2048)),
            buf((4, 4, 128, 512)), buf((9, 8, 64, 128)), buf((4, 8, 64, 512)), buf((4, 8, 512), F32), buf((64,)), buf((64,)), buf((64,)), buf((64,)), buf((256,)), buf((256,)), buf((8, 8, 128), F32),
            buf((3, 4, N, 128), F32), buf((3, 2, 2, NV, 128)), buf((3, 2, 2, NV, 128)),
            buf((3, 2, 2, NV, 128)), buf((3, 2, 2, NV, 128)),
            buf((4, N, 128)), buf((4, N, 128)), buf((4, N, 128)), buf((N, 1152), F32),
            buf((N, 256), F32), buf((N, 256), F32), buf((N, 128), F32), buf((N, 128), F32),
            buf((N, 512), F32), buf((N, 512), F32), buf((N, 512)), buf((N, 1152)),
            buf((192, 2048), F32), buf((16, 8, 512), F32), buf((32, 512), F32),
            buf((4, 2, 64, 512), F32), buf((3, 4, 2, 64, 384), F32), buf((2, 4, 128, 256), F32),
            buf((4, 64, 512)), buf((4, 64, 512)), buf((4, 64, 512)), buf((4, 64, 512)),
            buf((3, 4, 64, 384)), buf((3, 4, 64, 384)), buf((3, 4, 64, 384)), buf((3, 4, 64, 384)),
            buf((2, 4, 128, 256)), buf((2, 4, 128, 256)), buf((2, 4, 128, 256)), buf((2, 4, 128, 256)),
            buf((64, 512), F32), buf((3, 64, 384), F32), buf((2, 128, 256), F32),
            buf((8, 16, 128), F32),
            dma(SEMAPHORES),
        ],
        compiler_params=pltpu.CompilerParams(collective_id=0, has_side_effects=True, vmem_limit_bytes=58 << 20),
        cost_estimate=pl.CostEstimate(flops=5_200_000_000, bytes_accessed=8_000_000, transcendentals=2_000_000),
    )(views, crops, w_reduce, w_spatial, w_expand, cot_views, cot_crops, *params)
    held = [pltpu.with_memory_space_constraint(one, pltpu.VMEM) for one in held]
    return pl.pallas_call(
        store_kernel,
        out_shape=[
            shape((8, 16, 2048), BF16), shape((16, 4, 2048), BF16), shape((6, 4, 2048), F32),
            shape((8, 16, 2048), BF16), shape((16, 4, 2048), BF16),
            shape((256, 512), F32), shape((9, 64, 512), F32), shape((64, 2048), F32),
            shape((64,), F32), shape((64,), F32), shape((64,), F32), shape((64,), F32), shape((256,), F32), shape((256,), F32),
        ],
        in_specs=[vmem] * 9,
        out_specs=[hbm] * 8 + [vmem] * 6,
        scratch_shapes=[
            buf((16, 4, 2048)), buf((6, 4, 2048), F32), buf((16, 4, 2048)),
            buf((256, 512), F32), buf((9, 64, 512), F32), buf((64, 2048), F32), dma(8),
        ],
        compiler_params=pltpu.CompilerParams(vmem_limit_bytes=16 << 20),
    )(*held)


def step(
    dp, rows, views, crops, w_reduce, gain_one, shift_one, w_spatial, gain_two, shift_two, w_expand, gain_three, shift_three,
    cot_views, cot_crops,
):
    args = (
        views, crops, w_reduce, gain_one, shift_one, w_spatial, gain_two, shift_two, w_expand, gain_three, shift_three,
        cot_views, cot_crops,
    )
    if (dp, rows) != (8, 4) or views.shape != (4, 2, 2, 8, 2048) or crops.shape != (4, 4, 1, 4, 2048):
        return body(*args)
    out_v, out_c, pooled, grad_v, grad_c, grad_r, grad_s, grad_e, ga, sa, gb, sb, gc, sc = fused(
        views.reshape(8, 16, 2048), crops.reshape(16, 4, 2048), w_reduce, w_spatial.reshape(9, 64, 512), w_expand,
        cot_views.reshape(8, 16, 2048), cot_crops.reshape(16, 4, 2048),
        gain_one, shift_one, gain_two, shift_two, gain_three, shift_three,
    )
    return (
        out_v.reshape(views.shape),
        out_c.reshape(crops.shape),
        jnp.transpose(pooled, (1, 0, 2)),
        grad_v.reshape(views.shape),
        grad_c.reshape(crops.shape),
        grad_r,
        ga,
        sa,
        grad_s.reshape(w_spatial.shape[:3] + (512,)),
        gb,
        sb,
        grad_e,
        gc,
        sc,
    )


def solution(mesh):
    return jax.shard_map(
        functools.partial(step, mesh.shape["dp"], mesh.shape["rows"]),
        mesh=mesh,
        in_specs=(
            P("dp", None, "rows", None, None),
            P("dp", None, "rows", None, None),
            P("dp", None),
            P("dp"),
            P("dp"),
            P(None, None, "dp", None),
            P("dp"),
            P("dp"),
            P("dp", None),
            P("dp"),
            P("dp"),
            P("dp", None, "rows", None, None),
            P("dp", None, "rows", None, None),
        ),
        out_specs=(
            P("dp", None, "rows", None, None),
            P("dp", None, "rows", None, None),
            P("dp", None, None),
            P("dp", None, "rows", None, None),
            P("dp", None, "rows", None, None),
            P("dp", None),
            P("dp"),
            P("dp"),
            P(None, None, "dp", None),
            P("dp"),
            P("dp"),
            P("dp", None),
            P("dp"),
            P("dp"),
        ),
        check_vma=False,
    )
```

```python
import functools

import jax
import jax.numpy as jnp
from jax import lax
from jax.experimental import pallas as pl
from jax.experimental.pallas import tpu as pltpu
from jax.sharding import PartitionSpec as P

EPSILON = 1e-05


def extended(cells, sides, width):
    for axis, dim in sides:
        count = lax.axis_size(axis)
        ends = count - 1
        head = lax.slice_in_dim(cells, 0, width, axis=dim)
        tail = lax.slice_in_dim(cells, cells.shape[dim] - width, cells.shape[dim], axis=dim)
        cells = jnp.concatenate(
            [
                lax.ppermute(tail, axis, [(i, (i + 1) % count) for i in range(ends)]),
                cells,
                lax.ppermute(head, axis, [((i + 1) % count, i) for i in range(ends)]),
            ],
            axis=dim,
        )
    return cells


def silu_slope(values):
    sigmoid_val = jax.nn.sigmoid(values)
    return sigmoid_val * (1.0 + values * (1.0 - sigmoid_val))


def standardize(reduced_pair, gain_vec, shift_vec):
    left_map = reduced_pair[0]
    right_map = reduced_pair[1]
    totals = lax.psum(
        (
            jnp.sum(left_map, 0),
            jnp.sum(left_map * left_map, 0),
            jnp.sum(right_map, 0),
            jnp.sum(right_map * right_map, 0),
        ),
        "rows",
    )
    results = []
    for member in range(2):
        values = reduced_pair[member]
        pixel_count = values.shape[0] * lax.axis_size("rows")
        channel_mean = totals[2 * member] / pixel_count
        inverse_scale = lax.rsqrt(
            totals[2 * member + 1] / pixel_count - channel_mean * channel_mean + EPSILON
        )
        centred = (values - channel_mean) * inverse_scale
        results.append((centred, inverse_scale, gain_vec * centred + shift_vec))
    return results


def unstandardize(slopes, saved, gain_vec):
    shift_left = jnp.sum(slopes[0], 0)
    gain_left = jnp.sum(slopes[0] * saved[0][0], 0)
    shift_right = jnp.sum(slopes[1], 0)
    gain_right = jnp.sum(slopes[1] * saved[1][0], 0)
    totals = lax.psum((shift_left, gain_left, shift_right, gain_right), "rows")
    results = []
    for member in range(2):
        pixel_count = slopes[member].shape[0] * lax.axis_size("rows")
        centred = saved[member][0]
        inverse_scale = saved[member][1]
        mean_slope = gain_vec * totals[2 * member] / pixel_count
        mean_cross = gain_vec * totals[2 * member + 1] / pixel_count
        results.append(
            inverse_scale * (gain_vec * slopes[member] - mean_slope - centred * mean_cross)
        )
    return (results, gain_left + gain_right, shift_left + shift_right)


def spread_rows(activity):
    return extended(activity, (("rows", 1),), 1)


def spread_grads(slopes):
    return extended(slopes, (("rows", 1),), 1)


def patches(padded, row_count, col_count, flipped):
    widened = jnp.pad(padded, ((0, 0), (0, 0), (1, 1), (0, 0)))
    tap_list = []
    for row_tap in range(3):
        for col_tap in range(3):
            row_start = 2 - row_tap if flipped else row_tap
            col_start = 2 - col_tap if flipped else col_tap
            tap_list.append(
                widened[:, row_start : row_start + row_count, col_start : col_start + col_count, :]
            )
    return jnp.concatenate(tap_list, axis=-1).reshape(-1, 9 * widened.shape[-1])


def body(
    views,
    crops,
    w_reduce,
    gain_one,
    shift_one,
    w_spatial,
    gain_two,
    shift_two,
    w_expand,
    gain_three,
    shift_three,
    cot_views,
    cot_crops,
):
    gathered = (
        lax.all_gather(w_reduce, "dp", axis=0, tiled=True),
        lax.all_gather(gain_one, "dp", axis=0, tiled=True),
        lax.all_gather(shift_one, "dp", axis=0, tiled=True),
        lax.all_gather(w_spatial, "dp", axis=2, tiled=True),
        lax.all_gather(gain_two, "dp", axis=0, tiled=True),
        lax.all_gather(shift_two, "dp", axis=0, tiled=True),
        lax.all_gather(w_expand, "dp", axis=0, tiled=True),
        lax.all_gather(gain_three, "dp", axis=0, tiled=True),
        lax.all_gather(shift_three, "dp", axis=0, tiled=True),
    )
    weight_reduce = gathered[0]
    weight_spatial = gathered[3]
    weight_expand = gathered[6]
    gain_first = gathered[1].astype(jnp.float32)
    shift_first = gathered[2].astype(jnp.float32)
    gain_second = gathered[4].astype(jnp.float32)
    shift_second = gathered[5].astype(jnp.float32)
    gain_third = gathered[7].astype(jnp.float32)
    shift_third = gathered[8].astype(jnp.float32)
    channels = views.shape[4]
    middle = weight_reduce.shape[1]
    map_shapes = [
        (views.shape[0] * views.shape[1], views.shape[2], views.shape[3]),
        (crops.shape[0] * crops.shape[1], crops.shape[2], crops.shape[3]),
    ]
    flat_inputs = [views.reshape(-1, channels), crops.reshape(-1, channels)]
    reduced = [
        jnp.dot(source, weight_reduce, preferred_element_type=jnp.float32) for source in flat_inputs
    ]
    first_norm = standardize(reduced, gain_first, shift_first)
    first_act = [jax.nn.silu(saved[2]).astype(jnp.bfloat16) for saved in first_norm]
    padded_act = [
        spread_rows(act.reshape(shape[0], shape[1], shape[2], middle))
        for act, shape in zip(first_act, map_shapes)
    ]
    patch_rows = [
        patches(padded, shape[1], shape[2], False) for padded, shape in zip(padded_act, map_shapes)
    ]
    kernel = weight_spatial.reshape(9 * middle, middle)
    spatial = [jnp.dot(patch, kernel, preferred_element_type=jnp.float32) for patch in patch_rows]
    second_norm = standardize(spatial, gain_second, shift_second)
    second_act = [jax.nn.silu(saved[2]).astype(jnp.bfloat16) for saved in second_norm]
    expanded = [
        jnp.dot(act, weight_expand, preferred_element_type=jnp.float32) for act in second_act
    ]
    third_norm = standardize(expanded, gain_third, shift_third)
    pre_list = [
        source.astype(jnp.float32) + saved[2] for source, saved in zip(flat_inputs, third_norm)
    ]
    activation = [jax.nn.silu(pre) for pre in pre_list]
    view_sums = jnp.sum(activation[0].reshape(views.shape[0], views.shape[1], -1, channels), axis=2)
    crop_sums = jnp.sum(activation[1].reshape(crops.shape[0], crops.shape[1], -1, channels), axis=2)
    pooled_sums = lax.psum((view_sums, crop_sums), "rows")
    pooled = jnp.concatenate(
        [
            pooled_sums[0] / (views.shape[3] * views.shape[3]),
            pooled_sums[1] / (crops.shape[3] * crops.shape[3]),
        ],
        axis=1,
    )
    cotangent = [
        cot_views.reshape(-1, channels).astype(jnp.float32),
        cot_crops.reshape(-1, channels).astype(jnp.float32),
    ]
    d_pre = [cot * silu_slope(pre) for cot, pre in zip(cotangent, pre_list)]
    d_expanded_f, gain_third_grad, shift_third_grad = unstandardize(d_pre, third_norm, gain_third)
    d_expanded = [grad.astype(jnp.bfloat16) for grad in d_expanded_f]
    expand_grad = jnp.einsum(
        "pm,pc->mc", second_act[0], d_expanded[0], preferred_element_type=jnp.float32
    ) + jnp.einsum("pm,pc->mc", second_act[1], d_expanded[1], preferred_element_type=jnp.float32)
    d_norm_two = [
        jnp.einsum("pc,mc->pm", grad, weight_expand, preferred_element_type=jnp.float32)
        * silu_slope(saved[2])
        for grad, saved in zip(d_expanded, second_norm)
    ]
    d_spatial_f, gain_second_grad, shift_second_grad = unstandardize(
        d_norm_two, second_norm, gain_second
    )
    d_spatial = [grad.astype(jnp.bfloat16) for grad in d_spatial_f]
    spatial_grad = (
        jnp.einsum("pk,pm->km", patch_rows[0], d_spatial[0], preferred_element_type=jnp.float32)
        + jnp.einsum("pk,pm->km", patch_rows[1], d_spatial[1], preferred_element_type=jnp.float32)
    ).reshape(3, 3, middle, middle)
    back_kernel = jnp.transpose(weight_spatial, (0, 1, 3, 2)).reshape(9 * middle, middle)
    padded_grads = [
        spread_grads(grad.reshape(shape[0], shape[1], shape[2], middle))
        for grad, shape in zip(d_spatial, map_shapes)
    ]
    d_norm_one = [
        jnp.dot(
            patches(padded, shape[1], shape[2], True),
            back_kernel,
            preferred_element_type=jnp.float32,
        )
        * silu_slope(saved[2])
        for padded, shape, saved in zip(padded_grads, map_shapes, first_norm)
    ]
    d_reduced_f, gain_first_grad, shift_first_grad = unstandardize(
        d_norm_one, first_norm, gain_first
    )
    d_reduced = [grad.astype(jnp.bfloat16) for grad in d_reduced_f]
    reduce_grad = jnp.einsum(
        "pc,pm->cm", flat_inputs[0], d_reduced[0], preferred_element_type=jnp.float32
    ) + jnp.einsum("pc,pm->cm", flat_inputs[1], d_reduced[1], preferred_element_type=jnp.float32)
    input_grads = [
        (
            pre_grad
            + jnp.einsum("pm,cm->pc", grad, weight_reduce, preferred_element_type=jnp.float32)
        ).astype(jnp.bfloat16)
        for pre_grad, grad in zip(d_pre, d_reduced)
    ]
    shares = (
        lax.psum_scatter(reduce_grad, "dp", scatter_dimension=0, tiled=True),
        lax.psum_scatter(gain_first_grad, "dp", scatter_dimension=0, tiled=True),
        lax.psum_scatter(shift_first_grad, "dp", scatter_dimension=0, tiled=True),
        lax.psum_scatter(spatial_grad, "dp", scatter_dimension=2, tiled=True),
        lax.psum_scatter(gain_second_grad, "dp", scatter_dimension=0, tiled=True),
        lax.psum_scatter(shift_second_grad, "dp", scatter_dimension=0, tiled=True),
        lax.psum_scatter(expand_grad, "dp", scatter_dimension=0, tiled=True),
        lax.psum_scatter(gain_third_grad, "dp", scatter_dimension=0, tiled=True),
        lax.psum_scatter(shift_third_grad, "dp", scatter_dimension=0, tiled=True),
    )
    summed = lax.psum(
        (
            shares[0],
            shares[1],
            shares[2],
            shares[3],
            shares[4],
            shares[5],
            shares[6],
            shares[7],
            shares[8],
        ),
        "rows",
    )
    return (
        activation[0].astype(jnp.bfloat16).reshape(views.shape),
        activation[1].astype(jnp.bfloat16).reshape(crops.shape),
        pooled,
        input_grads[0].reshape(views.shape),
        input_grads[1].reshape(crops.shape),
        summed[0],
        summed[1],
        summed[2],
        summed[3],
        summed[4],
        summed[5],
        summed[6],
        summed[7],
        summed[8],
    )


MESH = pl.DeviceIdType.MESH
SEMAPHORES = 174
F32 = jnp.float32
BF16 = jnp.bfloat16
NV = 512
NC = 256
N = NV + NC
KINDS = ((0, NV), (NV, NC))
NT = (((1,), (1,)), ((), ()))
TN = (((0,), (0,)), ((), ()))


def sigmoid(values):
    return 0.5 * jnp.tanh(0.5 * values) + 0.5


def dot(left, right, dims=(((1,), (0,)), ((), ()))):
    return lax.dot_general(left, right, dims, preferred_element_type=F32)


def moved(values, kind, step):
    rows, lanes = values.shape
    if step == 0:
        return values
    if kind == 0:
        maps = values.reshape(rows // 64, 64, lanes)
        gap = jnp.zeros((rows // 64, 8, lanes), values.dtype)
        parts = [gap, maps[:, :-8]] if step > 0 else [maps[:, 8:], gap]
        return jnp.concatenate(parts, axis=1).reshape(rows, lanes)
    gap = jnp.zeros((64, lanes), values.dtype)
    return jnp.concatenate([gap, values[:-64]] if step > 0 else [values[64:], gap], axis=0)


def turned(values, kind, step):
    if step == 0:
        return values
    rows, lanes = values.shape
    width = 8 if kind == 0 else 4
    col = lax.rem(lax.broadcasted_iota(jnp.int32, (rows, lanes), 0), width)
    edge = 0 if step > 0 else width - 1
    return jnp.where(col == edge, 0.0, pltpu.roll(values, 1 if step > 0 else rows - 1, axis=0))


def block_kernel(
    views, crops, w_reduce, w_spatial, w_expand, cot_views, cot_crops, gain_a, shift_a, gain_b, shift_b, gain_c, shift_c,
    out_views, out_crops, fin_p, grad_views, grad_crops, fin_e, fin_s, fin_r, pgs,
    xv, xc4, xc, cv, cc4, cc, xo_v, xo_c, co_v, co_c, wr, ws, we, aff, raw_a, raw_b, raw_c, raw_d, raw_e, raw_f, pg,
    part, csend, crecv, xsend, xrecv,
    act1, act2, dred, conv, xhat1, slope1, xhat2, slope2, ex, dpre, dex, pat, dpo, pool, rows_pool,
    ge, gs, gr, ysend_e, yrecv_e, zsend_e, zrecv_e, ysend_s, yrecv_s, zsend_s, zrecv_s, ysend_r, yrecv_r, zsend_r, zrecv_r,
    relay_e, relay_s, acc_e, acc_s, acc_r, pgr,
    sem,
):
    i, r = lax.axis_index("dp"), lax.axis_index("rows")
    z, y = i // 2, i % 2
    x, c = r // 2, r % 2
    yp = (i + 1 - 2 * y, r)
    cp = (i, 2 * x + 1 - c)
    xp = (i, 2 * (1 - x) + c)
    xcp = (i, 2 * (1 - x) + 1 - c)
    rest = (xp, xcp, cp)

    middle = (z + 1) // 2 == 1
    step = 1 - 2 * (z // 2)

    def on_line(places):
        return (2 * (z + places * step) + y, r)

    taken = [0]

    def new(count=1):
        taken[0] += count
        return taken[0] - count

    def copy(src, dst, send, recv, dev):
        return pltpu.make_async_remote_copy(
            src_ref=src, dst_ref=dst, send_sem=sem.at[send], recv_sem=sem.at[recv], device_id=dev, device_id_type=MESH
        )

    def got(ref, recv):
        copy(ref, ref, recv, recv, cp).wait_recv()

    def sent(ref, send):
        copy(ref, ref, send, send, cp).wait_send()

    def stored(ref, one):
        pltpu.make_async_copy(ref, ref, sem.at[one]).wait()

    def lanes(k, xx, cc_):
        return pl.ds(pl.multiple_of(512 * k + 256 * cc_ + 128 * xx, 128), 128)

    def kl(k):
        return pl.ds(128 * k, 128)

    def kind_rows(kind):
        return pl.ds(*KINDS[kind])

    def stage(src, dst, one):
        pltpu.make_async_copy(src, dst, sem.at[one]).start()

    l_wr, l_ws, l_we, l_we2, l_gain = new(), new(), new(), new(), new(6)
    l_x, l_cot, l_own = (new(), new()), (new(), new()), new(4)

    @pl.when(y == c)
    def _():
        stage(w_reduce.at[pl.ds(pl.multiple_of(128 * x, 128), 128)], wr.at[r, z], l_wr)

    stage(w_spatial.at[:, :, pl.ds(pl.multiple_of(128 * r, 128), 128)], ws.at[:, i], l_ws)
    raw = (raw_a, raw_b, raw_c, raw_d, raw_e, raw_f)
    for n, vec in enumerate((gain_a, shift_a, gain_b, shift_b, gain_c, shift_c)):
        stage(vec, raw[n], l_gain + n)
    for k in range(4):
        stage(views.at[:, :, lanes(k, x, c)], xv.at[:, r, :, kl(k)], l_x[0])
        stage(crops.at[:, :, lanes(k, x, c)], xc4.at[r, :, :, kl(k)], l_x[1])
    for k in range(4):
        stage(w_expand.at[:, lanes(k, x, c)], we.at[r, i, :, kl(k)], l_we)
        stage(w_expand.at[:, lanes(k, 1 - x, c)], we.at[xp[1], i, :, kl(k)], l_we2)
    for k in range(4):
        stage(cot_views.at[:, :, lanes(k, x, c)], cv.at[:, r, :, kl(k)], l_cot[0])
        stage(cot_crops.at[:, :, lanes(k, x, c)], cc4.at[r, :, :, kl(k)], l_cot[1])
    for n, (src, dst) in enumerate(((views, xo_v), (crops, xo_c), (cot_views, co_v), (cot_crops, co_c))):
        stage(src, dst, l_own + n)

    bar = pltpu.get_barrier_semaphore()
    peers = [((i + n) % 8, r) for n in range(1, 8)] + [cp, xp, xcp]
    for dev in peers:
        pl.semaphore_signal(bar, inc=1, device_id=dev, device_id_type=MESH)
    pl.semaphore_wait(bar, len(peers))

    class Share:
        def __init__(self, parts, others):
            self.parts, self.others = parts, others
            count = len(parts(0))
            self.send, self.passed = new(), new()
            self.along_z = [new(3) for _ in range(count)]
            self.along_y = [new() for _ in range(count)]

    share_r = Share(lambda k: (wr.at[r, k],), None)
    share_s = Share(
        lambda k: tuple(ws.at[pl.ds(3 * h, 3), 2 * k + y] for h in range(3)),
        lambda h: ws.at[pl.ds(3 * h, 3), pl.ds(0, 4)],
    )
    share_e = Share(lambda k: (we.at[r, 2 * k + y],), lambda h: we.at[0, pl.ds(0, 4)])
    share_o = Share(lambda k: (we.at[xp[1], 2 * k + y],), lambda h: we.at[0, pl.ds(0, 4)])

    inner = ((z + 1) // 2) * (2 - (z + 1) // 2)

    def line_send(share, direct=False):
        for h, own in enumerate(share.parts(z)):

            def go(slot, dev, own=own):
                copy(own, own, share.send, slot, dev).start()

            go(share.along_z[h], on_line(2))
            go(share.along_z[h] + 2 - inner, on_line(1))

            @pl.when(middle)
            def _(go=go, h=h):
                go(share.along_z[h] + 1, on_line(-1))

            if direct:

                @pl.when(jnp.logical_not(middle))
                def _(go=go, h=h):
                    go(share.along_z[h] + 2, on_line(3))

    def line_over(share):
        for h, own in enumerate(share.parts(z)):
            copy(own, own, share.send, share.along_y[h], yp).start()

    def line_pass(share, h, send=None, which=(0, 1, 2)):
        relayed = send is None
        send = share.send if relayed else send

        def take(places, slot, on=False):
            if slot not in which:
                return
            ref = share.parts(z + places * step)[h]
            got(ref, share.along_z[h] + slot)
            if on:
                copy(ref, ref, send, share.along_z[h] + 2, on_line(-1)).start()
            copy(ref, ref, send, share.along_y[h], yp).start()

        @pl.when(middle)
        def _():
            take(2, 0, relayed)
            take(1, 1)
            take(-1, 2)

        @pl.when(jnp.logical_not(middle))
        def _():
            take(2, 0)
            take(1, 1)
            take(3, 2)

    def line_got(share):
        for h, slot in enumerate(share.along_y):
            got(share.others(h), slot)

    def line_sent(send, for_middle, for_end):
        @pl.when(middle)
        def _():
            sent(for_middle, send)

        @pl.when(jnp.logical_not(middle))
        def _():
            sent(for_end, send)

    @pl.when(y == c)
    def _():
        stored(wr.at[r, z], l_wr)
        line_send(share_r, True)
        line_over(share_r)

    s_sx, s_rx = ((new(), new()), (new(), new())), ((new(), new()), (new(), new()))

    def spread_v(src, dst, s, devs):
        for dev in devs:
            for k in range(4):
                copy(src.at[:, :, lanes(k, dev[1] // 2, dev[1] % 2)], dst.at[:, r, :, kl(k)], s_sx[s][0], s_rx[s][0], dev).start()

    def spread_c(src, dst, s, devs):
        for dev in devs:
            for k in range(4):
                copy(src.at[:, :, lanes(k, dev[1] // 2, dev[1] % 2)], dst.at[r, :, :, kl(k)], s_sx[s][1], s_rx[s][1], dev).start()

    spread_v(views, xv, 0, rest)
    spread_c(crops, xc4, 0, rest)
    spread_v(cot_views, cv, 1, rest[:1])
    spread_c(cot_crops, cc4, 1, rest[:1])
    stored(ws.at[:, i], l_ws)
    line_over(share_s)

    for n in range(6):
        stored(raw[n], l_gain + n)
    pg[i] = jnp.zeros((8, 128), F32)
    for n in range(4):
        vec = raw[n][...].reshape(1, 64).astype(F32)
        pg[i, n : n + 1, :] = jnp.concatenate([vec, vec], axis=1)
    for n in range(2):
        for m in range(2):
            pg[i, 4 + 2 * n + m : 5 + 2 * n + m, :] = raw[4 + n][128 * m : 128 * m + 128].reshape(1, 128).astype(F32)
    s_pg, r_pg = new(), new()
    for dev in peers[:7]:
        copy(pg.at[i], pg.at[i], s_pg, r_pg, dev).start()

    @pl.when(y == c)
    def _():
        line_pass(share_r, 0, share_r.passed)

    got(pg.at[pl.ds(0, 7)], r_pg)
    line_send(share_s)
    stored(xv.at[:, r], l_x[0])
    got(xv.at[:, pl.ds(0, 3)], s_rx[0][0])

    @pl.when(y != c)
    def _():
        got(wr.at[r], share_r.along_y[0])

    s_cs, r_cs = new(3), new(12)
    s_xs, r_xs = new(3), new(12)
    s_ag, r_ag = new(3), new(8)

    def scatter_start(op, kind, sums):
        rows = kind_rows(kind)
        n = pl.ds(0, KINDS[kind][1])
        if op == 0:
            sums = sums - jnp.sum(sums, axis=0, keepdims=True) / KINDS[kind][1]
        for s in range(4):
            part[op, s, rows, :] = sums[:, 128 * s : 128 * s + 128]
        for near, xx in enumerate((1 - x, x)):
            csend[op, kind, xx, n, :] = part[op, 2 * xx + 1 - c, rows, :].astype(BF16)
            own = csend.at[op, kind, xx, n]
            copy(own, crecv.at[op, kind, xx, n], s_cs + op, r_cs + 4 * op + 2 * kind + near, cp).start()

    def scatter_mid(op, kind):
        rows = kind_rows(kind)
        n = pl.ds(0, KINDS[kind][1])
        got(crecv.at[op, kind, 1 - x, n], r_cs + 4 * op + 2 * kind)
        far = part[op, 2 * (1 - x) + c, rows, :] + crecv[op, kind, 1 - x, n, :].astype(F32)
        xsend[op, kind, 0, n, :] = far.astype(BF16)
        copy(xsend.at[op, kind, 0, n], xrecv.at[op, kind, 0, n], s_xs + op, r_xs + 4 * op + 2 * kind, xp).start()

    def scatter_end(op, kind):
        rows = kind_rows(kind)
        n = pl.ds(0, KINDS[kind][1])
        got(crecv.at[op, kind, x, n], r_cs + 4 * op + 2 * kind + 1)
        near = part[op, 2 * x + c, rows, :] + crecv[op, kind, x, n, :].astype(F32)
        got(xrecv.at[op, kind, 0, n], r_xs + 4 * op + 2 * kind)
        return near + xrecv[op, kind, 0, n, :].astype(F32)

    def gather_start(kind, buf, value):
        rows = kind_rows(kind)
        buf[r, rows, :] = value
        own = buf.at[r, rows]
        copy(own, own, s_ag + 1, r_ag + 6 + kind, xp).start()
        copy(own, own, s_ag + 1, r_ag + 2 + kind, cp).start()

    def gather_mid(kind, buf):
        far = buf.at[xp[1], kind_rows(kind)]
        got(far, r_ag + 6 + kind)
        copy(far, far, s_ag + 1, r_ag + 2 + kind, cp).start()

    def gather_end(op, kind, buf):
        rows = kind_rows(kind)
        got(buf.at[pl.ds(0, 2), rows], r_ag + 2 * op + kind)
        return jnp.concatenate([buf[s, rows, :] for s in range(4)], axis=1)

    def both_mid(op, kind):
        rows = kind_rows(kind)
        n = pl.ds(0, KINDS[kind][1])
        for near, xx in enumerate((1 - x, x)):
            got(crecv.at[op, kind, xx, n], r_cs + 4 * op + 2 * kind + near)
        for xx in range(2):
            total = part[op, 2 * xx + c, rows, :] + crecv[op, kind, xx, n, :].astype(F32)
            part[op, 2 * xx + c, rows, :] = total
            xsend[op, kind, xx, n, :] = total.astype(BF16)
            one = xsend.at[op, kind, xx, n]
            copy(one, xrecv.at[op, kind, xx, n], s_xs + op, r_xs + 4 * op + 2 * kind + xx, xp).start()

    def both_end(op, kind, xx):
        n = pl.ds(0, KINDS[kind][1])
        got(xrecv.at[op, kind, xx, n], r_xs + 4 * op + 2 * kind + xx)
        return part[op, 2 * xx + c, kind_rows(kind), :] + xrecv[op, kind, xx, n, :].astype(F32)

    def both_out(op, kind, xx, buf, value):
        rows = kind_rows(kind)
        buf[2 * xx + c, rows, :] = value
        own = buf.at[2 * xx + c, rows]
        copy(own, own, s_ag + op, r_ag + 2 * op + kind, cp).start()

    weight_r = wr[r].reshape(512, 512)
    scatter_start(0, 0, dot(xv[...].reshape(NV, 512), weight_r))
    stored(xc4.at[r], l_x[1])
    got(xc4.at[pl.ds(0, 3)], s_rx[0][1])
    xc[...] = xc4[...].reshape(4, 64, 512)
    scatter_start(0, 1, dot(xc[...].reshape(NC, 512), weight_r))
    line_pass(share_s, 0, None, (0, 1))
    both_mid(0, 0)
    both_mid(0, 1)

    half = lax.broadcasted_iota(jnp.int32, (1, 128), 1) < 64

    def slice_of(s, q):
        return jnp.where(half, pg[2 * s, q : q + 1, :], pg[2 * s + 1, q : q + 1, :])

    gain1, shift1 = [[slice_of(2 * xx + c, q) for xx in range(2)] for q in range(2)]
    gain2, shift2 = slice_of(r, 2), slice_of(r, 3)
    gain3 = jnp.concatenate([pg[2 * k + c, pl.ds(4 + x, 1), :] for k in range(4)], axis=1)
    shift3 = jnp.concatenate([pg[2 * k + c, pl.ds(6 + x, 1), :] for k in range(4)], axis=1)

    def norm_act(values, rows, gain, shift):
        mean = jnp.sum(values, axis=0, keepdims=True) / rows
        second = jnp.sum(values * values, axis=0, keepdims=True) / rows
        rstd = lax.rsqrt(second - mean * mean + EPSILON)
        xhat = (values - mean) * rstd
        norm = gain * xhat + shift
        sig = sigmoid(norm)
        return rstd, xhat, sig * (1.0 + norm * (1.0 - sig)), (norm * sig).astype(BF16)

    for h, which in ((1, (0, 1)), (0, (2,)), (2, (0, 1)), (1, (2,)), (2, (2,))):
        line_pass(share_s, h, None, which)
    stored(we.at[r, i], l_we)
    stored(we.at[r, i], l_we2)
    for share in (share_e, share_o):
        line_send(share, True)
        line_over(share)
    rstd1, rstd2 = [[None, None], [None, None]], [None, None]
    for kind in range(2):
        rows = KINDS[kind][1]
        for xx in range(2):
            rstd1[kind][xx], xh, sl, act = norm_act(both_end(0, kind, xx), rows, gain1[xx], shift1[xx])
            both_out(0, kind, xx, act1, act)
            xhat1[xx, kind_rows(kind), :] = xh
            slope1[xx, kind_rows(kind), :] = sl
        if kind == 0:
            spread_v(cot_views, cv, 1, rest[1:])

    s_ow, s_xw, r_xw, r_ow = new(), new(), new(), new(2)

    def over_x(k):
        copy(wr.at[r, k], wr.at[r, k], s_xw, r_xw, xp).start()

    def between(ref, n):
        copy(ref, ref, s_ow, r_ow + n, cp).start()

    between(wr.at[r], 0)
    line_pass(share_e, 0, share_e.passed, (0,))
    line_got(share_s)
    line_pass(share_e, 0, share_e.passed, (1,))

    def weight_s():
        return jnp.concatenate([ws[t].reshape(512, 128) for t in range(9)], axis=1)

    for kind in range(2):
        rows = KINDS[kind][1]
        conv[kind_rows(kind), :] = dot(gather_end(0, kind, act1), weight_s())
        taps = [conv[kind_rows(kind), 128 * t : 128 * t + 128] for t in range(9)]
        spatial = None
        for j in range(3):
            col = taps[3 + j] + moved(taps[j], kind, 1) + moved(taps[6 + j], kind, -1)
            col = turned(col, kind, 1 - j)
            spatial = col if spatial is None else spatial + col
        rstd2[kind], xh, sl, act = norm_act(spatial, rows, gain2, shift2)
        gather_start(kind, act2, act)
        xhat2[kind_rows(kind), :] = xh
        slope2[kind_rows(kind), :] = sl
        if kind == 0:
            line_pass(share_e, 0, share_e.passed, (2,))
    spread_c(cot_crops, cc4, 1, rest[1:])
    over_x(0)
    over_x(1)
    pool[...] = jnp.zeros_like(pool)
    gather_mid(0, act2)
    stored(cv.at[:, r], l_cot[0])
    got(cv.at[:, pl.ds(0, 3)], s_rx[1][0])
    line_got(share_e)
    line_pass(share_o, 0, share_o.passed)
    between(we.at[r], 1)
    weight_e = we[r].reshape(512, 512)

    sum_x3, sum_d3 = [], []
    zero8 = jnp.zeros((8, 512), F32)

    def expand(kind):
        start, rows = KINDS[kind]
        ex[kind_rows(kind), :] = dot(gather_end(1, kind, act2), weight_e)

        def moments(b, acc):
            e = ex[pl.ds(pl.multiple_of(start + 32 * b, 32), 32), :].reshape(4, 8, 512)
            return acc[0] + jnp.sum(e, axis=0), acc[1] + jnp.sum(e * e, axis=0)

        tot, sq = lax.fori_loop(0, rows // 32, moments, (zero8, zero8))
        if kind == 0:
            gather_mid(1, act2)
        mean = jnp.sum(tot, axis=0, keepdims=True) / rows
        rstd = lax.rsqrt(jnp.sum(sq, axis=0, keepdims=True) / rows - mean * mean + EPSILON)

        def finish(b, acc):
            rs = pl.ds(pl.multiple_of(start + 16 * b, 16), 16)
            qs = pl.ds(pl.multiple_of(16 * (b % 4), 16), 16)
            xhat = (ex[rs, :] - mean) * rstd
            ex[rs, :] = xhat
            src = xv[b // 4, b % 4] if kind == 0 else xc[b // 4, qs, :]
            cot = cv[b // 4, b % 4] if kind == 0 else cc[b // 4, qs, :]
            pre = src.astype(F32) + (gain3 * xhat + shift3)
            sig = sigmoid(pre)
            activation = pre * sig
            d = cot.astype(F32) * (sig * (1.0 + pre * (1.0 - sig)))
            dpre[rs, :] = d
            if kind == 0:
                pool[b // 4] += activation[:8] + activation[8:]
            else:
                pool[8 + 2 * (b % 4)] += activation[:8]
                pool[9 + 2 * (b % 4)] += activation[8:]
            dx = d * xhat
            return acc[0] + (d[:8] + d[8:]), acc[1] + (dx[:8] + dx[8:])

        sd, sxx = lax.fori_loop(0, rows // 16, finish, (zero8, zero8), unroll=2)
        sd, sxx = jnp.sum(sd, axis=0, keepdims=True), jnp.sum(sxx, axis=0, keepdims=True)
        sum_d3.append(sd)
        sum_x3.append(sxx)
        scale = gain3 * rstd
        mean_d, mean_x = sd / rows, sxx / rows
        aff[r, 2 * kind : 2 * kind + 1, :] = scale
        aff[r, 2 * kind + 1 : 2 * kind + 2, :] = shift3 - scale * mean

        def back(b, _):
            rs = pl.ds(pl.multiple_of(start + 32 * b, 32), 32)
            dex[rs, :] = (scale * (dpre[rs, :] - mean_d - ex[rs, :] * mean_x)).astype(BF16)
            return 0

        lax.fori_loop(0, rows // 32, back, 0)

    def own_rows(buf):
        slices = []
        for s in range(4):
            rows = [buf[s, pl.ds(pl.multiple_of(64 * m + 16 * r, 16), 16), :] for m in range(8)]
            rows.append(buf[s, pl.ds(pl.multiple_of(NV + 64 * r, 64), 64), :])
            slices.append(jnp.concatenate(rows, axis=0))
        return jnp.concatenate(slices, axis=1)

    def own_blocks(values, s):
        for k in range(4):
            lo = 512 * k + 256 * (s % 2) + 128 * (s // 2)
            yield k, slice(lo, lo + 128), (values[:128, 128 * k : 128 * k + 128], values[128:, 128 * k : 128 * k + 128])

    def own_output():
        act = own_rows(act2)
        for s in range(4):
            for k, cols, blocks in own_blocks(dot(act, we[s].reshape(512, 512)), s):
                for kind, block in enumerate(blocks):
                    scale = aff[s, 2 * kind : 2 * kind + 1, 128 * k : 128 * k + 128]
                    shift = aff[s, 2 * kind + 1 : 2 * kind + 2, 128 * k : 128 * k + 128]
                    src = (xo_v if kind == 0 else xo_c)[:, :, cols].reshape(block.shape).astype(F32)
                    cot = (co_v if kind == 0 else co_c)[:, :, cols].reshape(block.shape).astype(F32)
                    pre = src + (scale * block + shift)
                    sig = sigmoid(pre)
                    if kind == 0:
                        out_views[:, :, cols] = (pre * sig).astype(BF16).reshape(8, 16, 128)
                    else:
                        out_crops[:, cols] = (pre * sig).astype(BF16)
                    dpo[128 * kind : 128 * kind + block.shape[0], cols] = cot * (sig * (1.0 + pre * (1.0 - sig)))

    def own_gradient():
        back = own_rows(dred)
        for s in range(4):
            for _, cols, blocks in own_blocks(dot(back, wr[s].reshape(512, 512), NT), s):
                grad_views[:, :, cols] = (dpo[:128, cols] + blocks[0]).astype(BF16).reshape(8, 16, 128)
                grad_crops[:, cols] = (dpo[128:, cols] + blocks[1]).astype(BF16)

    far_of = jnp.where(middle, z + 2 * step, z + 3 * step)
    mid_of = jnp.where(middle, z - step, z + 2 * step)
    order = [far_of, mid_of, z + step, z]

    class Grad:
        def __init__(self, full, ysend, yrecv, zsend, zrecv, acc, relay=None, both=True):
            self.full, self.ysend, self.yrecv, self.zsend, self.zrecv = full, ysend, yrecv, zsend, zrecv
            self.acc, self.relay, self.both = acc, relay, both
            self.s_y, self.r_y, self.s_z, self.r_z, self.r_relay = new(), new(4), new(), new(), new()

        def start(self):
            for k in order:
                self.ysend[k] = (self.full[k, 1 - y] if self.both else self.full[k]).astype(BF16)
                copy(self.ysend.at[k], self.yrecv.at[k], self.s_y, self.r_y + k, yp).start()

        def add(self, k):
            got(self.yrecv.at[k], self.r_y + k)
            return (self.full[k, y] if self.both else self.full[k]) + self.yrecv[k].astype(F32)

        def send(self, k, value):
            self.zsend[k] = value.astype(BF16)
            copy(self.zsend.at[k], self.zrecv.at[z], self.s_z, self.r_z, (2 * k + y, r)).start()

        def along(self):
            if self.relay is None:
                self.send(order[0], self.add(order[0]))
            else:

                @pl.when(jnp.logical_not(middle))
                def _():
                    self.zsend[order[0]] = self.add(order[0]).astype(BF16)
                    copy(self.zsend.at[order[0]], self.relay, self.s_z, self.r_relay, on_line(1)).start()

            self.send(order[1], self.add(order[1]))
            self.send(order[2], self.add(order[2]))

        def hand_on(self):
            @pl.when(middle)
            def _():
                total = self.add(order[0])
                got(self.relay, self.r_relay)
                self.send(order[0], total + self.relay[...].astype(F32))

        def total(self):
            self.acc[...] = self.add(z)
            if self.relay is None:
                got(self.zrecv.at[pl.ds(0, 3)], self.r_z)
                self.acc[...] += self.zrecv[order[0]].astype(F32) + self.zrecv[order[1]].astype(F32)
                return self.acc[...] + self.zrecv[order[2]].astype(F32)

            @pl.when(middle)
            def _():
                got(self.zrecv.at[pl.ds(0, 3)], self.r_z)
                self.acc[...] += self.zrecv[z - step].astype(F32)

            @pl.when(jnp.logical_not(middle))
            def _():
                got(self.zrecv.at[pl.ds(0, 2)], self.r_z)

            return self.acc[...] + self.zrecv[z + step].astype(F32) + self.zrecv[z + 2 * step].astype(F32)

        def sent(self):
            sent(self.zsend.at[pl.ds(0, 3)], self.s_z)

    class Slices:
        def __init__(self, buf):
            self.buf, self.send, self.come = buf, new(), new()

        def start(self, value):
            self.buf[r] = value.astype(BF16)
            for dev in rest:
                copy(self.buf.at[r], self.buf.at[r], self.send, self.come, dev).start()

        def end(self):
            got(self.buf.at[pl.ds(0, 3)], self.come)
            sent(self.buf.at[pl.ds(0, 3)], self.send)

    grad_e = Grad(ge, ysend_e, yrecv_e, zsend_e, zrecv_e, acc_e, relay_e)
    grad_s = [
        Grad(*(one.at[q] for one in (gs, ysend_s, yrecv_s, zsend_s, zrecv_s, acc_s, relay_s))) for q in range(3)
    ]
    grad_r = [Grad(*(one.at[q] for one in (gr, ysend_r, yrecv_r, zsend_r, zrecv_r, acc_r)), both=False) for q in range(2)]
    slices_p, slices_e, slices_s = Slices(fin_p), Slices(fin_e), [Slices(fin_s.at[q]) for q in range(3)]

    expand(0)
    scatter_start(1, 0, dot(dex[kind_rows(0), :], weight_e, NT))
    stored(cc4.at[r], l_cot[1])
    got(cc4.at[pl.ds(0, 3)], s_rx[1][1])
    cc[...] = cc4[...].reshape(4, 64, 512)
    expand(1)
    scatter_mid(1, 0)
    scatter_start(1, 1, dot(dex[kind_rows(1), :], weight_e, NT))
    ge[...] = dot(jnp.concatenate([act2[s] for s in range(4)], axis=1), dex[...], TN).reshape(4, 2, 64, 512)
    grad_e.start()
    scatter_mid(1, 1)
    s_af, r_af = new(), new()
    for dev in rest:
        copy(aff.at[r], aff.at[r], s_af, r_af, dev).start()

    def norm_back(d, xhat, rstd, gain, rows):
        sd = jnp.sum(d, axis=0, keepdims=True)
        sxx = jnp.sum(d * xhat, axis=0, keepdims=True)
        return (gain * rstd) * (d - sd / rows - xhat * (sxx / rows)), sd, sxx

    def weight_grad(q):
        full = jnp.concatenate([act1[s] for s in range(4)], axis=1)
        gs[q] = dot(full, pat[:, 384 * q : 384 * q + 384], TN).reshape(4, 2, 64, 384)
        grad_s[q].start()

    sum_d2, sum_x2 = [], []
    for kind in range(2):
        rows = KINDS[kind][1]
        d = scatter_end(1, kind) * slope2[kind_rows(kind), :]
        dz_, sd, sxx = norm_back(d, xhat2[kind_rows(kind), :], rstd2[kind], gain2, rows)
        sum_d2.append(sd)
        sum_x2.append(sxx)
        dz_ = dz_.astype(BF16).astype(F32)
        for tj in range(3):
            col = turned(dz_, kind, tj - 1)
            for ti in range(3):
                t = 3 * ti + tj
                pat[kind_rows(kind), 128 * t : 128 * t + 128] = moved(col, kind, ti - 1).astype(BF16)
        if kind == 1:
            weight_grad(0)
            both_mid(2, 0)
        scatter_start(2, kind, dot(pat[kind_rows(kind), :], weight_s(), NT))
    grad_e.along()
    weight_grad(1)
    weight_grad(2)
    both_mid(2, 1)
    over_x(2)
    over_x(3)
    line_got(share_o)
    between(we.at[xp[1]], 1)
    grad_s[0].along()
    grad_e.hand_on()
    grad_s[0].hand_on()

    sum_1 = [[0.0, 0.0], [0.0, 0.0]]
    for kind in range(2):
        rows = KINDS[kind][1]
        for xx in range(2):
            d = both_end(2, kind, xx) * slope1[xx, kind_rows(kind), :]
            dz_, sd, sxx = norm_back(d, xhat1[xx, kind_rows(kind), :], rstd1[kind][xx], gain1[xx], rows)
            sum_1[xx][0] += sxx
            sum_1[xx][1] += sd
            both_out(2, kind, xx, dred, dz_.astype(BF16))
        if kind == 0:
            grad_s[1].along()

    rows12 = [jnp.where(x == 0, sum_1[0][n], sum_1[1][n]) for n in range(2)]
    rows12 += [sum_x2[0] + sum_x2[1], sum_d2[0] + sum_d2[1]]
    gx3, gd3 = sum_x3[0] + sum_x3[1], sum_d3[0] + sum_d3[1]
    rows3 = [g[:, 128 * k : 128 * k + 128] for g in (gx3, gd3) for k in range(4)]
    pgr[i] = jnp.concatenate(rows12 + rows3 + [jnp.zeros((4, 128), F32)], axis=0)
    s_pp, r_pp, s_ps, r_ps = new(), new(), new(), new()
    for dev in peers[:7]:
        copy(pgr.at[i], pgr.at[i], s_pp, r_pp, dev).start()

    rows_pool[...] = jnp.zeros_like(rows_pool)
    for n in range(8):
        row = 4 * (n % 2) + n // 2
        rows_pool[row : row + 1, :] = jnp.sum(pool[n], axis=0, keepdims=True) / 64.0
        for m in range(2):
            row = 4 * (2 + 2 * (n % 2) + m) + n // 2
            rows_pool[row : row + 1, :] = jnp.sum(pool[8 + n, 4 * m : 4 * m + 4, :], axis=0, keepdims=True) / 16.0
    slices_p.start(rows_pool[...])
    grad_s[1].hand_on()
    full_d = [gather_end(2, kind, dred) for kind in range(2)]

    for m in range(4):
        col = dot(xv[:, :, :, 128 * m : 128 * m + 128].reshape(NV, 128), full_d[0], TN)
        col = col + dot(xc[:, :, 128 * m : 128 * m + 128].reshape(NC, 128), full_d[1], TN)
        for q in range(2):
            gr[q, m] = col[:, 256 * q : 256 * q + 256]

    @pl.when(y != c)
    def _():
        for one in grad_r:
            one.start()

    for n, ref in enumerate((xo_v, xo_c, co_v, co_c)):
        stored(ref, l_own + n)
    got(aff.at[pl.ds(0, 3)], r_af)
    got(we.at[pl.ds(0, 2)], r_ow + 1)
    own_output()
    grad_s[2].along()
    slices_s[0].start(grad_s[0].total())
    slices_e.start(grad_e.total())
    got(wr.at[0], r_xw)
    grad_s[2].hand_on()
    between(wr.at[xp[1]], 0)

    @pl.when(y == c)
    def _():
        grad_r[0].along()
        grad_r[1].along()


    slices_s[1].start(grad_s[1].total())
    got(wr.at[pl.ds(0, 2)], r_ow)
    own_gradient()

    got(pgr.at[pl.ds(0, 7)], r_pp)
    total = pgr[0]
    for n in range(1, 8):
        total = total + pgr[n]
    pgs[r] = total
    for dev in rest:
        copy(pgs.at[r], pgs.at[r], s_ps, r_ps, dev).start()
    slices_s[2].start(grad_s[2].total())

    s_fr, r_fr = new(2), new(2)
    for q in range(2):

        @pl.when(y == c)
        def _(q=q):
            fin_r[q, x] = grad_r[q].total().astype(BF16)
            for dev in rest:
                copy(fin_r.at[q, x], fin_r.at[q, x], s_fr + q, r_fr + q, dev).start()

    for one in (slices_p, slices_e, *slices_s):
        one.end()
    got(pgs.at[pl.ds(0, 3)], r_ps)
    sent(aff.at[pl.ds(0, 3)], s_af)
    sent(we, s_ow)
    sent(wr.at[0], s_xw)
    for s, (own_v, own_c) in enumerate(((xv, xc4), (cv, cc4))):
        sent(own_v.at[:, pl.ds(0, 3)], s_sx[s][0])
        sent(own_c.at[pl.ds(0, 3)], s_sx[s][1])
    sent(pg.at[pl.ds(0, 7)], s_pg)
    sent(pgr.at[pl.ds(0, 7)], s_pp)
    sent(pgs.at[pl.ds(0, 3)], s_ps)
    line_sent(share_s.send, ws, ws.at[:, pl.ds(0, 6)])
    for share in (share_e, share_o):
        sent(we.at[0, pl.ds(0, 4)], share.send)
        sent(we.at[0, pl.ds(0, 3)], share.passed)
    for op in range(3):
        sent(act1.at[pl.ds(0, 2)], s_cs + op)
        sent(act1.at[pl.ds(0, 1 if op == 1 else 2)], s_xs + op)
        sent(act1.at[pl.ds(0, 3 if op == 1 else 2)], s_ag + op)
    for one in (grad_e, *grad_s):
        sent(one.ysend, one.s_y)
        one.sent()

    @pl.when(y != c)
    def _():
        for q, one in enumerate(grad_r):
            sent(one.ysend, one.s_y)
            got(fin_r.at[q], r_fr + q)

    @pl.when(y == c)
    def _():
        sent(wr.at[0], share_r.send)
        sent(wr.at[0, pl.ds(0, 3)], share_r.passed)
        for q, one in enumerate(grad_r):
            one.sent()
            sent(one.zsend.at[pl.ds(0, 3)], s_fr + q)
            got(fin_r.at[q, 1 - x], r_fr + q)

    assert taken[0] == SEMAPHORES, taken


def store_kernel(
    out_v, out_c, pool, grad_v, grad_c, fin_e, fin_s, fin_r, sums,
    out_views, out_crops, pooled, grad_views, grad_crops, grad_reduce, grad_spatial, grad_expand,
    gain_a, shift_a, gain_b, shift_b, gain_c, shift_c,
    oc, pl_, gc, gr, gs, ge, sem,
):
    i = lax.axis_index("dp")
    z, y = i // 2, i % 2
    copies = []

    def store(src, dst):
        one = pltpu.make_async_copy(src, dst, sem.at[len(copies)])
        one.start()
        copies.append(one)

    store(out_v, out_views)
    store(grad_v, grad_views)
    for s in range(4):
        for t in range(9):
            gs[t, :, 128 * s : 128 * s + 128] = fin_s[t // 3, s, :, 128 * (t % 3) : 128 * (t % 3) + 128].astype(F32)
    store(gs, grad_spatial)
    for s in range(4):
        for k in range(4):
            lo = 512 * k + 256 * (s % 2) + 128 * (s // 2)
            ge[:, lo : lo + 128] = fin_e[s, :, 128 * k : 128 * k + 128].astype(F32)
    store(ge, grad_expand)
    for n in range(2):
        gr[:, 256 * n : 256 * n + 256] = fin_r[n].astype(F32).reshape(256, 256)
    store(gr, grad_reduce)
    oc[...] = out_c[...].reshape(16, 4, 2048)
    store(oc, out_crops)
    gc[...] = grad_c[...].reshape(16, 4, 2048)
    store(gc, grad_crops)
    for s in range(4):
        for k in range(4):
            lo = 512 * k + 256 * (s % 2) + 128 * (s // 2)
            pl_[:, :, lo : lo + 128] = pool[s, 0:24, 128 * k : 128 * k + 128].astype(F32).reshape(6, 4, 128)
    store(pl_, pooled)
    for n, out in enumerate((gain_a, shift_a, gain_b, shift_b)):
        row = sums[i // 2, n : n + 1, :]
        out[...] = jnp.where(i % 2 == 0, row[:, :64], row[:, 64:]).reshape(64)
    for n, out in enumerate((gain_c, shift_c)):
        out[...] = jnp.concatenate([sums[2 * m + y, pl.ds(4 + 4 * n + z, 1), :] for m in range(2)], axis=1).reshape(256)
    for one in copies:
        one.wait()


def fused(views, crops, w_reduce, w_spatial, w_expand, cot_views, cot_crops, *params):
    hbm, vmem = pl.BlockSpec(memory_space=pltpu.HBM), pl.BlockSpec(memory_space=pltpu.VMEM)

    def shape(dims, dtype):
        return jax.ShapeDtypeStruct(dims, dtype)

    def buf(dims, dtype=BF16):
        return pltpu.VMEM(dims, dtype)

    def dma(*dims):
        return pltpu.SemaphoreType.DMA(dims)

    held = pl.pallas_call(
        block_kernel,
        out_shape=[
            buf((8, 16, 2048)), buf((64, 2048)), buf((4, 32, 512)), buf((8, 16, 2048)), buf((64, 2048)),
            buf((4, 64, 512)), buf((3, 4, 64, 384)), buf((2, 2, 128, 256)), buf((4, 16, 128), F32),
        ],
        in_specs=[hbm] * 13,
        out_specs=[vmem] * 9,
        scratch_shapes=[
            buf((8, 4, 16, 512)), buf((4, 16, 4, 512)), buf((4, 64, 512)),
            buf((8, 4, 16, 512)), buf((4, 16, 4, 512)), buf((4, 64, 512)),
            buf((8, 16, 2048)), buf((16, 4, 2048)), buf((8, 16, 2048)), buf((16, 4, 2048)),
            buf((4, 4, 128, 512)), buf((9, 8, 64, 128)), buf((4, 8, 64, 512)), buf((4, 8, 512), F32), buf((64,)), buf((64,)), buf((64,)), buf((64,)), buf((256,)), buf((256,)), buf((8, 8, 128), F32),
            buf((3, 4, N, 128), F32), buf((3, 2, 2, NV, 128)), buf((3, 2, 2, NV, 128)),
            buf((3, 2, 2, NV, 128)), buf((3, 2, 2, NV, 128)),
            buf((4, N, 128)), buf((4, N, 128)), buf((4, N, 128)), buf((N, 1152), F32),
            buf((2, N, 128), F32), buf((2, N, 128), F32), buf((N, 128), F32), buf((N, 128), F32),
            buf((N, 512), F32), buf((N, 512), F32), buf((N, 512)), buf((N, 1152)),
            buf((192, 2048), F32), buf((16, 8, 512), F32), buf((32, 512), F32),
            buf((4, 2, 64, 512), F32), buf((3, 4, 2, 64, 384), F32), buf((2, 4, 128, 256), F32),
            buf((4, 64, 512)), buf((4, 64, 512)), buf((4, 64, 512)), buf((4, 64, 512)),
            buf((3, 4, 64, 384)), buf((3, 4, 64, 384)), buf((3, 4, 64, 384)), buf((3, 4, 64, 384)),
            buf((2, 4, 128, 256)), buf((2, 4, 128, 256)), buf((2, 4, 128, 256)), buf((2, 4, 128, 256)),
            buf((64, 512)), buf((3, 64, 384)), buf((64, 512), F32), buf((3, 64, 384), F32), buf((2, 128, 256), F32),
            buf((8, 16, 128), F32),
            dma(SEMAPHORES),
        ],
        compiler_params=pltpu.CompilerParams(collective_id=0, has_side_effects=True, vmem_limit_bytes=58 << 20),
        cost_estimate=pl.CostEstimate(flops=5_200_000_000, bytes_accessed=8_000_000, transcendentals=2_000_000),
    )(views, crops, w_reduce, w_spatial, w_expand, cot_views, cot_crops, *params)
    held = [pltpu.with_memory_space_constraint(one, pltpu.VMEM) for one in held]
    return pl.pallas_call(
        store_kernel,
        out_shape=[
            shape((8, 16, 2048), BF16), shape((16, 4, 2048), BF16), shape((6, 4, 2048), F32),
            shape((8, 16, 2048), BF16), shape((16, 4, 2048), BF16),
            shape((256, 512), F32), shape((9, 64, 512), F32), shape((64, 2048), F32),
            shape((64,), F32), shape((64,), F32), shape((64,), F32), shape((64,), F32), shape((256,), F32), shape((256,), F32),
        ],
        in_specs=[vmem] * 9,
        out_specs=[hbm] * 8 + [vmem] * 6,
        scratch_shapes=[
            buf((16, 4, 2048)), buf((6, 4, 2048), F32), buf((16, 4, 2048)),
            buf((256, 512), F32), buf((9, 64, 512), F32), buf((64, 2048), F32), dma(8),
        ],
        compiler_params=pltpu.CompilerParams(vmem_limit_bytes=16 << 20),
    )(*held)


def step(
    dp, rows, views, crops, w_reduce, gain_one, shift_one, w_spatial, gain_two, shift_two, w_expand, gain_three, shift_three,
    cot_views, cot_crops,
):
    args = (
        views, crops, w_reduce, gain_one, shift_one, w_spatial, gain_two, shift_two, w_expand, gain_three, shift_three,
        cot_views, cot_crops,
    )
    if (dp, rows) != (8, 4) or views.shape != (4, 2, 2, 8, 2048) or crops.shape != (4, 4, 1, 4, 2048):
        return body(*args)
    out_v, out_c, pooled, grad_v, grad_c, grad_r, grad_s, grad_e, ga, sa, gb, sb, gc, sc = fused(
        views.reshape(8, 16, 2048), crops.reshape(16, 4, 2048), w_reduce, w_spatial.reshape(9, 64, 512), w_expand,
        cot_views.reshape(8, 16, 2048), cot_crops.reshape(16, 4, 2048),
        gain_one, shift_one, gain_two, shift_two, gain_three, shift_three,
    )
    return (
        out_v.reshape(views.shape),
        out_c.reshape(crops.shape),
        jnp.transpose(pooled, (1, 0, 2)),
        grad_v.reshape(views.shape),
        grad_c.reshape(crops.shape),
        grad_r,
        ga,
        sa,
        grad_s.reshape(w_spatial.shape[:3] + (512,)),
        gb,
        sb,
        grad_e,
        gc,
        sc,
    )


def solution(mesh):
    return jax.shard_map(
        functools.partial(step, mesh.shape["dp"], mesh.shape["rows"]),
        mesh=mesh,
        in_specs=(
            P("dp", None, "rows", None, None),
            P("dp", None, "rows", None, None),
            P("dp", None),
            P("dp"),
            P("dp"),
            P(None, None, "dp", None),
            P("dp"),
            P("dp"),
            P("dp", None),
            P("dp"),
            P("dp"),
            P("dp", None, "rows", None, None),
            P("dp", None, "rows", None, None),
        ),
        out_specs=(
            P("dp", None, "rows", None, None),
            P("dp", None, "rows", None, None),
            P("dp", None, None),
            P("dp", None, "rows", None, None),
            P("dp", None, "rows", None, None),
            P("dp", None),
            P("dp"),
            P("dp"),
            P(None, None, "dp", None),
            P("dp"),
            P("dp"),
            P("dp", None),
            P("dp"),
            P("dp"),
        ),
        check_vma=False,
    )
```

```python
import functools

import jax
import jax.numpy as jnp
from jax import lax
from jax.experimental import pallas as pl
from jax.experimental.pallas import tpu as pltpu
from jax.sharding import PartitionSpec as P

EPSILON = 1e-05


def extended(cells, sides, width):
    for axis, dim in sides:
        count = lax.axis_size(axis)
        ends = count - 1
        head = lax.slice_in_dim(cells, 0, width, axis=dim)
        tail = lax.slice_in_dim(cells, cells.shape[dim] - width, cells.shape[dim], axis=dim)
        cells = jnp.concatenate(
            [
                lax.ppermute(tail, axis, [(i, (i + 1) % count) for i in range(ends)]),
                cells,
                lax.ppermute(head, axis, [((i + 1) % count, i) for i in range(ends)]),
            ],
            axis=dim,
        )
    return cells


def silu_slope(values):
    sigmoid_val = jax.nn.sigmoid(values)
    return sigmoid_val * (1.0 + values * (1.0 - sigmoid_val))


def standardize(reduced_pair, gain_vec, shift_vec):
    left_map = reduced_pair[0]
    right_map = reduced_pair[1]
    totals = lax.psum(
        (
            jnp.sum(left_map, 0),
            jnp.sum(left_map * left_map, 0),
            jnp.sum(right_map, 0),
            jnp.sum(right_map * right_map, 0),
        ),
        "rows",
    )
    results = []
    for member in range(2):
        values = reduced_pair[member]
        pixel_count = values.shape[0] * lax.axis_size("rows")
        channel_mean = totals[2 * member] / pixel_count
        inverse_scale = lax.rsqrt(
            totals[2 * member + 1] / pixel_count - channel_mean * channel_mean + EPSILON
        )
        centred = (values - channel_mean) * inverse_scale
        results.append((centred, inverse_scale, gain_vec * centred + shift_vec))
    return results


def unstandardize(slopes, saved, gain_vec):
    shift_left = jnp.sum(slopes[0], 0)
    gain_left = jnp.sum(slopes[0] * saved[0][0], 0)
    shift_right = jnp.sum(slopes[1], 0)
    gain_right = jnp.sum(slopes[1] * saved[1][0], 0)
    totals = lax.psum((shift_left, gain_left, shift_right, gain_right), "rows")
    results = []
    for member in range(2):
        pixel_count = slopes[member].shape[0] * lax.axis_size("rows")
        centred = saved[member][0]
        inverse_scale = saved[member][1]
        mean_slope = gain_vec * totals[2 * member] / pixel_count
        mean_cross = gain_vec * totals[2 * member + 1] / pixel_count
        results.append(
            inverse_scale * (gain_vec * slopes[member] - mean_slope - centred * mean_cross)
        )
    return (results, gain_left + gain_right, shift_left + shift_right)


def spread_rows(activity):
    return extended(activity, (("rows", 1),), 1)


def spread_grads(slopes):
    return extended(slopes, (("rows", 1),), 1)


def patches(padded, row_count, col_count, flipped):
    widened = jnp.pad(padded, ((0, 0), (0, 0), (1, 1), (0, 0)))
    tap_list = []
    for row_tap in range(3):
        for col_tap in range(3):
            row_start = 2 - row_tap if flipped else row_tap
            col_start = 2 - col_tap if flipped else col_tap
            tap_list.append(
                widened[:, row_start : row_start + row_count, col_start : col_start + col_count, :]
            )
    return jnp.concatenate(tap_list, axis=-1).reshape(-1, 9 * widened.shape[-1])


def body(
    views,
    crops,
    w_reduce,
    gain_one,
    shift_one,
    w_spatial,
    gain_two,
    shift_two,
    w_expand,
    gain_three,
    shift_three,
    cot_views,
    cot_crops,
):
    gathered = (
        lax.all_gather(w_reduce, "dp", axis=0, tiled=True),
        lax.all_gather(gain_one, "dp", axis=0, tiled=True),
        lax.all_gather(shift_one, "dp", axis=0, tiled=True),
        lax.all_gather(w_spatial, "dp", axis=2, tiled=True),
        lax.all_gather(gain_two, "dp", axis=0, tiled=True),
        lax.all_gather(shift_two, "dp", axis=0, tiled=True),
        lax.all_gather(w_expand, "dp", axis=0, tiled=True),
        lax.all_gather(gain_three, "dp", axis=0, tiled=True),
        lax.all_gather(shift_three, "dp", axis=0, tiled=True),
    )
    weight_reduce = gathered[0]
    weight_spatial = gathered[3]
    weight_expand = gathered[6]
    gain_first = gathered[1].astype(jnp.float32)
    shift_first = gathered[2].astype(jnp.float32)
    gain_second = gathered[4].astype(jnp.float32)
    shift_second = gathered[5].astype(jnp.float32)
    gain_third = gathered[7].astype(jnp.float32)
    shift_third = gathered[8].astype(jnp.float32)
    channels = views.shape[4]
    middle = weight_reduce.shape[1]
    map_shapes = [
        (views.shape[0] * views.shape[1], views.shape[2], views.shape[3]),
        (crops.shape[0] * crops.shape[1], crops.shape[2], crops.shape[3]),
    ]
    flat_inputs = [views.reshape(-1, channels), crops.reshape(-1, channels)]
    reduced = [
        jnp.dot(source, weight_reduce, preferred_element_type=jnp.float32) for source in flat_inputs
    ]
    first_norm = standardize(reduced, gain_first, shift_first)
    first_act = [jax.nn.silu(saved[2]).astype(jnp.bfloat16) for saved in first_norm]
    padded_act = [
        spread_rows(act.reshape(shape[0], shape[1], shape[2], middle))
        for act, shape in zip(first_act, map_shapes)
    ]
    patch_rows = [
        patches(padded, shape[1], shape[2], False) for padded, shape in zip(padded_act, map_shapes)
    ]
    kernel = weight_spatial.reshape(9 * middle, middle)
    spatial = [jnp.dot(patch, kernel, preferred_element_type=jnp.float32) for patch in patch_rows]
    second_norm = standardize(spatial, gain_second, shift_second)
    second_act = [jax.nn.silu(saved[2]).astype(jnp.bfloat16) for saved in second_norm]
    expanded = [
        jnp.dot(act, weight_expand, preferred_element_type=jnp.float32) for act in second_act
    ]
    third_norm = standardize(expanded, gain_third, shift_third)
    pre_list = [
        source.astype(jnp.float32) + saved[2] for source, saved in zip(flat_inputs, third_norm)
    ]
    activation = [jax.nn.silu(pre) for pre in pre_list]
    view_sums = jnp.sum(activation[0].reshape(views.shape[0], views.shape[1], -1, channels), axis=2)
    crop_sums = jnp.sum(activation[1].reshape(crops.shape[0], crops.shape[1], -1, channels), axis=2)
    pooled_sums = lax.psum((view_sums, crop_sums), "rows")
    pooled = jnp.concatenate(
        [
            pooled_sums[0] / (views.shape[3] * views.shape[3]),
            pooled_sums[1] / (crops.shape[3] * crops.shape[3]),
        ],
        axis=1,
    )
    cotangent = [
        cot_views.reshape(-1, channels).astype(jnp.float32),
        cot_crops.reshape(-1, channels).astype(jnp.float32),
    ]
    d_pre = [cot * silu_slope(pre) for cot, pre in zip(cotangent, pre_list)]
    d_expanded_f, gain_third_grad, shift_third_grad = unstandardize(d_pre, third_norm, gain_third)
    d_expanded = [grad.astype(jnp.bfloat16) for grad in d_expanded_f]
    expand_grad = jnp.einsum(
        "pm,pc->mc", second_act[0], d_expanded[0], preferred_element_type=jnp.float32
    ) + jnp.einsum("pm,pc->mc", second_act[1], d_expanded[1], preferred_element_type=jnp.float32)
    d_norm_two = [
        jnp.einsum("pc,mc->pm", grad, weight_expand, preferred_element_type=jnp.float32)
        * silu_slope(saved[2])
        for grad, saved in zip(d_expanded, second_norm)
    ]
    d_spatial_f, gain_second_grad, shift_second_grad = unstandardize(
        d_norm_two, second_norm, gain_second
    )
    d_spatial = [grad.astype(jnp.bfloat16) for grad in d_spatial_f]
    spatial_grad = (
        jnp.einsum("pk,pm->km", patch_rows[0], d_spatial[0], preferred_element_type=jnp.float32)
        + jnp.einsum("pk,pm->km", patch_rows[1], d_spatial[1], preferred_element_type=jnp.float32)
    ).reshape(3, 3, middle, middle)
    back_kernel = jnp.transpose(weight_spatial, (0, 1, 3, 2)).reshape(9 * middle, middle)
    padded_grads = [
        spread_grads(grad.reshape(shape[0], shape[1], shape[2], middle))
        for grad, shape in zip(d_spatial, map_shapes)
    ]
    d_norm_one = [
        jnp.dot(
            patches(padded, shape[1], shape[2], True),
            back_kernel,
            preferred_element_type=jnp.float32,
        )
        * silu_slope(saved[2])
        for padded, shape, saved in zip(padded_grads, map_shapes, first_norm)
    ]
    d_reduced_f, gain_first_grad, shift_first_grad = unstandardize(
        d_norm_one, first_norm, gain_first
    )
    d_reduced = [grad.astype(jnp.bfloat16) for grad in d_reduced_f]
    reduce_grad = jnp.einsum(
        "pc,pm->cm", flat_inputs[0], d_reduced[0], preferred_element_type=jnp.float32
    ) + jnp.einsum("pc,pm->cm", flat_inputs[1], d_reduced[1], preferred_element_type=jnp.float32)
    input_grads = [
        (
            pre_grad
            + jnp.einsum("pm,cm->pc", grad, weight_reduce, preferred_element_type=jnp.float32)
        ).astype(jnp.bfloat16)
        for pre_grad, grad in zip(d_pre, d_reduced)
    ]
    shares = (
        lax.psum_scatter(reduce_grad, "dp", scatter_dimension=0, tiled=True),
        lax.psum_scatter(gain_first_grad, "dp", scatter_dimension=0, tiled=True),
        lax.psum_scatter(shift_first_grad, "dp", scatter_dimension=0, tiled=True),
        lax.psum_scatter(spatial_grad, "dp", scatter_dimension=2, tiled=True),
        lax.psum_scatter(gain_second_grad, "dp", scatter_dimension=0, tiled=True),
        lax.psum_scatter(shift_second_grad, "dp", scatter_dimension=0, tiled=True),
        lax.psum_scatter(expand_grad, "dp", scatter_dimension=0, tiled=True),
        lax.psum_scatter(gain_third_grad, "dp", scatter_dimension=0, tiled=True),
        lax.psum_scatter(shift_third_grad, "dp", scatter_dimension=0, tiled=True),
    )
    summed = lax.psum(
        (
            shares[0],
            shares[1],
            shares[2],
            shares[3],
            shares[4],
            shares[5],
            shares[6],
            shares[7],
            shares[8],
        ),
        "rows",
    )
    return (
        activation[0].astype(jnp.bfloat16).reshape(views.shape),
        activation[1].astype(jnp.bfloat16).reshape(crops.shape),
        pooled,
        input_grads[0].reshape(views.shape),
        input_grads[1].reshape(crops.shape),
        summed[0],
        summed[1],
        summed[2],
        summed[3],
        summed[4],
        summed[5],
        summed[6],
        summed[7],
        summed[8],
    )


MESH = pl.DeviceIdType.MESH
SEMAPHORES = 179
F32 = jnp.float32
BF16 = jnp.bfloat16
NV = 512
NC = 256
N = NV + NC
KINDS = ((0, NV), (NV, NC))
NT = (((1,), (1,)), ((), ()))
TN = (((0,), (0,)), ((), ()))


def sigmoid(values):
    return 0.5 * jnp.tanh(0.5 * values) + 0.5


def dot(left, right, dims=(((1,), (0,)), ((), ()))):
    return lax.dot_general(left, right, dims, preferred_element_type=F32)


def moved(values, kind, step):
    rows, lanes = values.shape
    if step == 0:
        return values
    if kind == 0:
        maps = values.reshape(rows // 64, 64, lanes)
        gap = jnp.zeros((rows // 64, 8, lanes), values.dtype)
        parts = [gap, maps[:, :-8]] if step > 0 else [maps[:, 8:], gap]
        return jnp.concatenate(parts, axis=1).reshape(rows, lanes)
    gap = jnp.zeros((64, lanes), values.dtype)
    return jnp.concatenate([gap, values[:-64]] if step > 0 else [values[64:], gap], axis=0)


def turned(values, kind, step):
    if step == 0:
        return values
    rows, lanes = values.shape
    width = 8 if kind == 0 else 4
    col = lax.rem(lax.broadcasted_iota(jnp.int32, (rows, lanes), 0), width)
    edge = 0 if step > 0 else width - 1
    return jnp.where(col == edge, 0.0, pltpu.roll(values, 1 if step > 0 else rows - 1, axis=0))


def block_kernel(
    views, crops, w_reduce, w_spatial, w_expand, cot_views, cot_crops, gain_a, shift_a, gain_b, shift_b, gain_c, shift_c,
    out_views, out_crops, fin_p, grad_views, grad_crops, fin_e, fin_s, fin_r, pgs,
    xv, xc4, xc, cv, cc4, cc, xo_v, xo_c, co_v, co_c, wr, ws, we, aff, raw_a, raw_b, raw_c, raw_d, raw_e, raw_f, pg,
    part, csend, crecv, xsend, xrecv,
    act1, act2, dred, conv, xhat1, slope1, xhat2, slope2, ex, dpre, dex, pat, dpo, pool, rows_pool,
    ge, gs, gr, ysend_e, yrecv_e, zsend_e, zrecv_e, ysend_s, yrecv_s, zsend_s, zrecv_s, ysend_r, yrecv_r, zsend_r, zrecv_r,
    relay_e, relay_s, acc_e, acc_s, acc_r, pgr,
    sem,
):
    i, r = lax.axis_index("dp"), lax.axis_index("rows")
    z, y = i // 2, i % 2
    x, c = r // 2, r % 2
    yp = (i + 1 - 2 * y, r)
    cp = (i, 2 * x + 1 - c)
    xp = (i, 2 * (1 - x) + c)
    xcp = (i, 2 * (1 - x) + 1 - c)
    rest = (xp, xcp, cp)

    middle = (z + 1) // 2 == 1
    step = 1 - 2 * (z // 2)

    def on_line(places):
        return (2 * (z + places * step) + y, r)

    taken = [0]

    def new(count=1):
        taken[0] += count
        return taken[0] - count

    def copy(src, dst, send, recv, dev):
        return pltpu.make_async_remote_copy(
            src_ref=src, dst_ref=dst, send_sem=sem.at[send], recv_sem=sem.at[recv], device_id=dev, device_id_type=MESH
        )

    def got(ref, recv):
        copy(ref, ref, recv, recv, cp).wait_recv()

    def sent(ref, send):
        copy(ref, ref, send, send, cp).wait_send()

    def stored(ref, one):
        pltpu.make_async_copy(ref, ref, sem.at[one]).wait()

    def lanes(k, xx, cc_):
        return pl.ds(pl.multiple_of(512 * k + 256 * cc_ + 128 * xx, 128), 128)

    def kl(k):
        return pl.ds(128 * k, 128)

    def kind_rows(kind):
        return pl.ds(*KINDS[kind])

    def stage(src, dst, one):
        pltpu.make_async_copy(src, dst, sem.at[one]).start()

    l_wr, l_ws, l_we, l_we2, l_gain = new(), new(), new(), new(), new(6)
    l_x, l_cot, l_own = (new(), new()), (new(), new()), new(4)

    @pl.when(y == c)
    def _():
        stage(w_reduce.at[pl.ds(pl.multiple_of(128 * x, 128), 128)], wr.at[r, z], l_wr)

    stage(w_spatial.at[:, :, pl.ds(pl.multiple_of(128 * r, 128), 128)], ws.at[:, i], l_ws)
    raw = (raw_a, raw_b, raw_c, raw_d, raw_e, raw_f)
    for n, vec in enumerate((gain_a, shift_a, gain_b, shift_b, gain_c, shift_c)):
        stage(vec, raw[n], l_gain + n)
    for k in range(4):
        stage(views.at[:, :, lanes(k, x, c)], xv.at[:, r, :, kl(k)], l_x[0])
        stage(crops.at[:, :, lanes(k, x, c)], xc4.at[r, :, :, kl(k)], l_x[1])
    for k in range(4):
        stage(w_expand.at[:, lanes(k, x, c)], we.at[r, i, :, kl(k)], l_we)
        stage(w_expand.at[:, lanes(k, 1 - x, c)], we.at[xp[1], i, :, kl(k)], l_we2)
    for k in range(4):
        stage(cot_views.at[:, :, lanes(k, x, c)], cv.at[:, r, :, kl(k)], l_cot[0])
        stage(cot_crops.at[:, :, lanes(k, x, c)], cc4.at[r, :, :, kl(k)], l_cot[1])
    for n, (src, dst) in enumerate(((views, xo_v), (crops, xo_c), (cot_views, co_v), (cot_crops, co_c))):
        stage(src, dst, l_own + n)

    bar = pltpu.get_barrier_semaphore()
    peers = [((i + n) % 8, r) for n in range(1, 8)] + [cp, xp, xcp]
    for dev in peers:
        pl.semaphore_signal(bar, inc=1, device_id=dev, device_id_type=MESH)
    pl.semaphore_wait(bar, len(peers))

    class Share:
        def __init__(self, parts, others):
            self.parts, self.others = parts, others
            count = len(parts(0))
            self.send, self.passed = new(), new()
            self.along_z = [new(3) for _ in range(count)]
            self.along_y = [new() for _ in range(count)]

    share_r = Share(lambda k: (wr.at[r, k],), None)
    share_s = Share(
        lambda k: tuple(ws.at[pl.ds(3 * h, 3), 2 * k + y] for h in range(3)),
        lambda h: ws.at[pl.ds(3 * h, 3), pl.ds(0, 4)],
    )
    share_e = Share(lambda k: (we.at[r, 2 * k + y],), lambda h: we.at[0, pl.ds(0, 4)])
    share_o = Share(lambda k: (we.at[xp[1], 2 * k + y],), lambda h: we.at[0, pl.ds(0, 4)])

    inner = ((z + 1) // 2) * (2 - (z + 1) // 2)

    def line_send(share, direct=False):
        for h, own in enumerate(share.parts(z)):

            def go(slot, dev, own=own):
                copy(own, own, share.send, slot, dev).start()

            go(share.along_z[h], on_line(2))
            go(share.along_z[h] + 2 - inner, on_line(1))

            @pl.when(middle)
            def _(go=go, h=h):
                go(share.along_z[h] + 1, on_line(-1))

            if direct:

                @pl.when(jnp.logical_not(middle))
                def _(go=go, h=h):
                    go(share.along_z[h] + 2, on_line(3))

    def line_over(share):
        for h, own in enumerate(share.parts(z)):
            copy(own, own, share.send, share.along_y[h], yp).start()

    def line_pass(share, h, send=None, which=(0, 1, 2)):
        relayed = send is None
        send = share.send if relayed else send

        def take(places, slot, on=False):
            if slot not in which:
                return
            ref = share.parts(z + places * step)[h]
            got(ref, share.along_z[h] + slot)
            if on:
                copy(ref, ref, send, share.along_z[h] + 2, on_line(-1)).start()
            copy(ref, ref, send, share.along_y[h], yp).start()

        @pl.when(middle)
        def _():
            take(2, 0, relayed)
            take(1, 1)
            take(-1, 2)

        @pl.when(jnp.logical_not(middle))
        def _():
            take(2, 0)
            take(1, 1)
            take(3, 2)

    def line_got(share):
        for h, slot in enumerate(share.along_y):
            got(share.others(h), slot)

    def line_sent(send, for_middle, for_end):
        @pl.when(middle)
        def _():
            sent(for_middle, send)

        @pl.when(jnp.logical_not(middle))
        def _():
            sent(for_end, send)

    @pl.when(y == c)
    def _():
        stored(wr.at[r, z], l_wr)
        line_send(share_r, True)
        line_over(share_r)

    s_sx, s_rx = ((new(), new()), (new(), new())), ((new(), new()), (new(), new()))

    def spread_v(src, dst, s, devs):
        for dev in devs:
            for k in range(4):
                copy(src.at[:, :, lanes(k, dev[1] // 2, dev[1] % 2)], dst.at[:, r, :, kl(k)], s_sx[s][0], s_rx[s][0], dev).start()

    def spread_c(src, dst, s, devs):
        for dev in devs:
            for k in range(4):
                copy(src.at[:, :, lanes(k, dev[1] // 2, dev[1] % 2)], dst.at[r, :, :, kl(k)], s_sx[s][1], s_rx[s][1], dev).start()

    spread_v(views, xv, 0, rest)
    spread_c(crops, xc4, 0, rest)
    spread_v(cot_views, cv, 1, rest[:1])
    spread_c(cot_crops, cc4, 1, rest[:1])
    stored(ws.at[:, i], l_ws)
    line_over(share_s)

    for n in range(6):
        stored(raw[n], l_gain + n)
    pg[i] = jnp.zeros((8, 128), F32)
    for n in range(4):
        vec = raw[n][...].reshape(1, 64).astype(F32)
        pg[i, n : n + 1, :] = jnp.concatenate([vec, vec], axis=1)
    for n in range(2):
        for m in range(2):
            pg[i, 4 + 2 * n + m : 5 + 2 * n + m, :] = raw[4 + n][128 * m : 128 * m + 128].reshape(1, 128).astype(F32)
    s_pg, r_pg = new(), new()
    for dev in peers[:7]:
        copy(pg.at[i], pg.at[i], s_pg, r_pg, dev).start()

    @pl.when(y == c)
    def _():
        line_pass(share_r, 0, share_r.passed)

    got(pg.at[pl.ds(0, 7)], r_pg)
    line_send(share_s)
    stored(xv.at[:, r], l_x[0])
    got(xv.at[:, pl.ds(0, 3)], s_rx[0][0])

    @pl.when(y != c)
    def _():
        got(wr.at[r], share_r.along_y[0])

    s_cs, r_cs = new(3), new(12)
    s_xs, r_xs = new(3), new(12)
    s_ag, r_ag = new(3), new(8)

    def scatter_start(op, kind, sums):
        rows = kind_rows(kind)
        n = pl.ds(0, KINDS[kind][1])
        if op == 0:
            sums = sums - jnp.sum(sums, axis=0, keepdims=True) / KINDS[kind][1]
        for s in range(4):
            part[op, s, rows, :] = sums[:, 128 * s : 128 * s + 128]
        for near, xx in enumerate((1 - x, x)):
            csend[op, kind, xx, n, :] = part[op, 2 * xx + 1 - c, rows, :].astype(BF16)
            own = csend.at[op, kind, xx, n]
            copy(own, crecv.at[op, kind, xx, n], s_cs + op, r_cs + 4 * op + 2 * kind + near, cp).start()

    def scatter_mid(op, kind):
        rows = kind_rows(kind)
        n = pl.ds(0, KINDS[kind][1])
        got(crecv.at[op, kind, 1 - x, n], r_cs + 4 * op + 2 * kind)
        far = part[op, 2 * (1 - x) + c, rows, :] + crecv[op, kind, 1 - x, n, :].astype(F32)
        xsend[op, kind, 0, n, :] = far.astype(BF16)
        copy(xsend.at[op, kind, 0, n], xrecv.at[op, kind, 0, n], s_xs + op, r_xs + 4 * op + 2 * kind, xp).start()

    def scatter_end(op, kind):
        rows = kind_rows(kind)
        n = pl.ds(0, KINDS[kind][1])
        got(crecv.at[op, kind, x, n], r_cs + 4 * op + 2 * kind + 1)
        near = part[op, 2 * x + c, rows, :] + crecv[op, kind, x, n, :].astype(F32)
        got(xrecv.at[op, kind, 0, n], r_xs + 4 * op + 2 * kind)
        return near + xrecv[op, kind, 0, n, :].astype(F32)

    def gather_start(kind, buf, value):
        rows = kind_rows(kind)
        buf[r, rows, :] = value
        own = buf.at[r, rows]
        copy(own, own, s_ag + 1, r_ag + 6 + kind, xp).start()
        copy(own, own, s_ag + 1, r_ag + 2 + kind, cp).start()

    def gather_mid(kind, buf):
        far = buf.at[xp[1], kind_rows(kind)]
        got(far, r_ag + 6 + kind)
        copy(far, far, s_ag + 1, r_ag + 2 + kind, cp).start()

    def gather_end(op, kind, buf):
        rows = kind_rows(kind)
        got(buf.at[pl.ds(0, 2), rows], r_ag + 2 * op + kind)
        return jnp.concatenate([buf[s, rows, :] for s in range(4)], axis=1)

    def both_mid(op, kind):
        rows = kind_rows(kind)
        n = pl.ds(0, KINDS[kind][1])
        for near, xx in enumerate((1 - x, x)):
            got(crecv.at[op, kind, xx, n], r_cs + 4 * op + 2 * kind + near)
        for xx in range(2):
            total = part[op, 2 * xx + c, rows, :] + crecv[op, kind, xx, n, :].astype(F32)
            part[op, 2 * xx + c, rows, :] = total
            xsend[op, kind, xx, n, :] = total.astype(BF16)
            one = xsend.at[op, kind, xx, n]
            copy(one, xrecv.at[op, kind, xx, n], s_xs + op, r_xs + 4 * op + 2 * kind + xx, xp).start()

    def both_end(op, kind, xx):
        n = pl.ds(0, KINDS[kind][1])
        got(xrecv.at[op, kind, xx, n], r_xs + 4 * op + 2 * kind + xx)
        return part[op, 2 * xx + c, kind_rows(kind), :] + xrecv[op, kind, xx, n, :].astype(F32)

    def both_out(op, kind, xx, buf, value):
        rows = kind_rows(kind)
        buf[2 * xx + c, rows, :] = value
        own = buf.at[2 * xx + c, rows]
        copy(own, own, s_ag + op, r_ag + 2 * op + kind, cp).start()

    weight_r = wr[r].reshape(512, 512)
    scatter_start(0, 0, dot(xv[...].reshape(NV, 512), weight_r))
    stored(xc4.at[r], l_x[1])
    got(xc4.at[pl.ds(0, 3)], s_rx[0][1])
    xc[...] = xc4[...].reshape(4, 64, 512)
    scatter_start(0, 1, dot(xc[...].reshape(NC, 512), weight_r))
    line_pass(share_s, 0, None, (0, 1))
    both_mid(0, 0)
    both_mid(0, 1)

    half = lax.broadcasted_iota(jnp.int32, (1, 128), 1) < 64

    def slice_of(s, q):
        return jnp.where(half, pg[2 * s, q : q + 1, :], pg[2 * s + 1, q : q + 1, :])

    gain1, shift1 = [[slice_of(2 * xx + c, q) for xx in range(2)] for q in range(2)]
    gain2, shift2 = slice_of(r, 2), slice_of(r, 3)
    gain3 = jnp.concatenate([pg[2 * k + c, pl.ds(4 + x, 1), :] for k in range(4)], axis=1)
    shift3 = jnp.concatenate([pg[2 * k + c, pl.ds(6 + x, 1), :] for k in range(4)], axis=1)

    def norm_act(values, rows, gain, shift):
        mean = jnp.sum(values, axis=0, keepdims=True) / rows
        second = jnp.sum(values * values, axis=0, keepdims=True) / rows
        rstd = lax.rsqrt(second - mean * mean + EPSILON)
        xhat = (values - mean) * rstd
        norm = gain * xhat + shift
        sig = sigmoid(norm)
        return rstd, xhat, sig * (1.0 + norm * (1.0 - sig)), (norm * sig).astype(BF16)

    for h, which in ((1, (0, 1)), (0, (2,)), (2, (0, 1)), (1, (2,)), (2, (2,))):
        line_pass(share_s, h, None, which)
    stored(we.at[r, i], l_we)
    stored(we.at[r, i], l_we2)
    for share in (share_e, share_o):
        line_send(share, True)
        line_over(share)
    rstd1, rstd2 = [[None, None], [None, None]], [None, None]
    for kind in range(2):
        rows = KINDS[kind][1]
        for xx in range(2):
            rstd1[kind][xx], xh, sl, act = norm_act(both_end(0, kind, xx), rows, gain1[xx], shift1[xx])
            both_out(0, kind, xx, act1, act)
            xhat1[xx, kind_rows(kind), :] = xh
            slope1[xx, kind_rows(kind), :] = sl
        if kind == 0:
            spread_v(cot_views, cv, 1, rest[1:])

    s_ow, s_xw, r_xw, r_ow = new(), new(), new(), new(2)

    def over_x(k):
        copy(wr.at[r, k], wr.at[r, k], s_xw, r_xw, xp).start()

    def between(ref, n):
        copy(ref, ref, s_ow, r_ow + n, cp).start()

    between(wr.at[r], 0)
    line_pass(share_e, 0, share_e.passed, (0,))
    line_got(share_s)
    line_pass(share_e, 0, share_e.passed, (1,))

    def weight_s():
        return jnp.concatenate([ws[t].reshape(512, 128) for t in range(9)], axis=1)

    for kind in range(2):
        rows = KINDS[kind][1]
        conv[kind_rows(kind), :] = dot(gather_end(0, kind, act1), weight_s())
        taps = [conv[kind_rows(kind), 128 * t : 128 * t + 128] for t in range(9)]
        spatial = None
        for j in range(3):
            col = taps[3 + j] + moved(taps[j], kind, 1) + moved(taps[6 + j], kind, -1)
            col = turned(col, kind, 1 - j)
            spatial = col if spatial is None else spatial + col
        rstd2[kind], xh, sl, act = norm_act(spatial, rows, gain2, shift2)
        gather_start(kind, act2, act)
        xhat2[kind_rows(kind), :] = xh
        slope2[kind_rows(kind), :] = sl
        if kind == 0:
            line_pass(share_e, 0, share_e.passed, (2,))
    spread_c(cot_crops, cc4, 1, rest[1:])
    over_x(0)
    pool[...] = jnp.zeros_like(pool)
    gather_mid(0, act2)
    stored(cv.at[:, r], l_cot[0])
    got(cv.at[:, pl.ds(0, 3)], s_rx[1][0])
    line_got(share_e)
    line_pass(share_o, 0, share_o.passed)
    between(we.at[r], 1)
    weight_e = we[r].reshape(512, 512)

    sum_x3, sum_d3 = [], []
    zero8 = jnp.zeros((8, 512), F32)

    def expand(kind):
        start, rows = KINDS[kind]
        ex[kind_rows(kind), :] = dot(gather_end(1, kind, act2), weight_e)

        def moments(b, acc):
            e = ex[pl.ds(pl.multiple_of(start + 32 * b, 32), 32), :].reshape(4, 8, 512)
            return acc[0] + jnp.sum(e, axis=0), acc[1] + jnp.sum(e * e, axis=0)

        tot, sq = lax.fori_loop(0, rows // 32, moments, (zero8, zero8))
        if kind == 0:
            gather_mid(1, act2)
        mean = jnp.sum(tot, axis=0, keepdims=True) / rows
        rstd = lax.rsqrt(jnp.sum(sq, axis=0, keepdims=True) / rows - mean * mean + EPSILON)

        def finish(b, acc):
            rs = pl.ds(pl.multiple_of(start + 16 * b, 16), 16)
            qs = pl.ds(pl.multiple_of(16 * (b % 4), 16), 16)
            xhat = (ex[rs, :] - mean) * rstd
            ex[rs, :] = xhat
            src = xv[b // 4, b % 4] if kind == 0 else xc[b // 4, qs, :]
            cot = cv[b // 4, b % 4] if kind == 0 else cc[b // 4, qs, :]
            pre = src.astype(F32) + (gain3 * xhat + shift3)
            sig = sigmoid(pre)
            activation = pre * sig
            d = cot.astype(F32) * (sig * (1.0 + pre * (1.0 - sig)))
            dpre[rs, :] = d
            if kind == 0:
                pool[b // 4] += activation[:8] + activation[8:]
            else:
                pool[8 + 2 * (b % 4)] += activation[:8]
                pool[9 + 2 * (b % 4)] += activation[8:]
            dx = d * xhat
            return acc[0] + (d[:8] + d[8:]), acc[1] + (dx[:8] + dx[8:])

        sd, sxx = lax.fori_loop(0, rows // 16, finish, (zero8, zero8), unroll=2)
        sd, sxx = jnp.sum(sd, axis=0, keepdims=True), jnp.sum(sxx, axis=0, keepdims=True)
        sum_d3.append(sd)
        sum_x3.append(sxx)
        scale = gain3 * rstd
        mean_d, mean_x = sd / rows, sxx / rows
        aff[r, 2 * kind : 2 * kind + 1, :] = scale
        aff[r, 2 * kind + 1 : 2 * kind + 2, :] = shift3 - scale * mean

        def back(b, _):
            rs = pl.ds(pl.multiple_of(start + 32 * b, 32), 32)
            dex[rs, :] = (scale * (dpre[rs, :] - mean_d - ex[rs, :] * mean_x)).astype(BF16)
            return 0

        lax.fori_loop(0, rows // 32, back, 0)

    def own_rows(buf):
        slices = []
        for s in range(4):
            rows = [buf[s, pl.ds(pl.multiple_of(64 * m + 16 * r, 16), 16), :] for m in range(8)]
            rows.append(buf[s, pl.ds(pl.multiple_of(NV + 64 * r, 64), 64), :])
            slices.append(jnp.concatenate(rows, axis=0))
        return jnp.concatenate(slices, axis=1)

    def own_blocks(values, s):
        for k in range(4):
            lo = 512 * k + 256 * (s % 2) + 128 * (s // 2)
            yield k, slice(lo, lo + 128), (values[:128, 128 * k : 128 * k + 128], values[128:, 128 * k : 128 * k + 128])

    def own_output():
        act = own_rows(act2)
        for s in range(4):
            for k, cols, blocks in own_blocks(dot(act, we[s].reshape(512, 512)), s):
                for kind, block in enumerate(blocks):
                    scale = aff[s, 2 * kind : 2 * kind + 1, 128 * k : 128 * k + 128]
                    shift = aff[s, 2 * kind + 1 : 2 * kind + 2, 128 * k : 128 * k + 128]
                    src = (xo_v if kind == 0 else xo_c)[:, :, cols].reshape(block.shape).astype(F32)
                    cot = (co_v if kind == 0 else co_c)[:, :, cols].reshape(block.shape).astype(F32)
                    pre = src + (scale * block + shift)
                    sig = sigmoid(pre)
                    if kind == 0:
                        out_views[:, :, cols] = (pre * sig).astype(BF16).reshape(8, 16, 128)
                    else:
                        out_crops[:, cols] = (pre * sig).astype(BF16)
                    dpo[128 * kind : 128 * kind + block.shape[0], cols] = cot * (sig * (1.0 + pre * (1.0 - sig)))

    def own_gradient():
        back = own_rows(dred)
        for s in range(4):
            for _, cols, blocks in own_blocks(dot(back, wr[s].reshape(512, 512), NT), s):
                grad_views[:, :, cols] = (dpo[:128, cols] + blocks[0]).astype(BF16).reshape(8, 16, 128)
                grad_crops[:, cols] = (dpo[128:, cols] + blocks[1]).astype(BF16)

    far_of = jnp.where(middle, z + 2 * step, z + 3 * step)
    mid_of = jnp.where(middle, z - step, z + 2 * step)
    order = [far_of, mid_of, z + step, z]

    class Grad:
        def __init__(self, full, ysend, yrecv, zsend, zrecv, acc, relay=None, both=True):
            self.full, self.ysend, self.yrecv, self.zsend, self.zrecv = full, ysend, yrecv, zsend, zrecv
            self.acc, self.relay, self.both = acc, relay, both
            self.s_y, self.r_y, self.s_z, self.r_z, self.r_relay = new(), new(4), new(), new(), new()

        def start(self):
            for k in order:
                self.ysend[k] = (self.full[k, 1 - y] if self.both else self.full[k]).astype(BF16)
                copy(self.ysend.at[k], self.yrecv.at[k], self.s_y, self.r_y + k, yp).start()

        def add(self, k):
            got(self.yrecv.at[k], self.r_y + k)
            return (self.full[k, y] if self.both else self.full[k]) + self.yrecv[k].astype(F32)

        def send(self, k, value):
            self.zsend[k] = value.astype(BF16)
            copy(self.zsend.at[k], self.zrecv.at[z], self.s_z, self.r_z, (2 * k + y, r)).start()

        def along(self):
            if self.relay is None:
                self.send(order[0], self.add(order[0]))
            else:

                @pl.when(jnp.logical_not(middle))
                def _():
                    self.zsend[order[0]] = self.add(order[0]).astype(BF16)
                    copy(self.zsend.at[order[0]], self.relay, self.s_z, self.r_relay, on_line(1)).start()

            self.send(order[1], self.add(order[1]))
            self.send(order[2], self.add(order[2]))

        def hand_on(self):
            @pl.when(middle)
            def _():
                total = self.add(order[0])
                got(self.relay, self.r_relay)
                self.send(order[0], total + self.relay[...].astype(F32))

        def total(self):
            self.acc[...] = self.add(z)
            if self.relay is None:
                got(self.zrecv.at[pl.ds(0, 3)], self.r_z)
                self.acc[...] += self.zrecv[order[0]].astype(F32) + self.zrecv[order[1]].astype(F32)
                return self.acc[...] + self.zrecv[order[2]].astype(F32)

            @pl.when(middle)
            def _():
                got(self.zrecv.at[pl.ds(0, 3)], self.r_z)
                self.acc[...] += self.zrecv[z - step].astype(F32)

            @pl.when(jnp.logical_not(middle))
            def _():
                got(self.zrecv.at[pl.ds(0, 2)], self.r_z)

            return self.acc[...] + self.zrecv[z + step].astype(F32) + self.zrecv[z + 2 * step].astype(F32)

        def sent(self):
            sent(self.zsend.at[pl.ds(0, 3)], self.s_z)

    class Slices:
        def __init__(self, buf, straight=False):
            self.buf, self.straight, self.send, self.near, self.far = buf, straight, new(), new(), new()

        def start(self, value):
            self.buf[r] = value.astype(BF16)
            for dev, come in ((xp, self.near if self.straight else self.far), (cp, self.near), (xcp, self.near)):
                if dev is not xcp or self.straight:
                    copy(self.buf.at[r], self.buf.at[r], self.send, come, dev).start()

        def mid(self):
            far = self.buf.at[xp[1]]
            got(far, self.far)
            copy(far, far, self.send, self.near, cp).start()

        def end(self):
            got(self.buf.at[pl.ds(0, 3 if self.straight else 2)], self.near)
            sent(self.buf.at[pl.ds(0, 3)], self.send)

    grad_e = Grad(ge, ysend_e, yrecv_e, zsend_e, zrecv_e, acc_e, relay_e)
    grad_s = [
        Grad(*(one.at[q] for one in (gs, ysend_s, yrecv_s, zsend_s, zrecv_s, acc_s, relay_s))) for q in range(3)
    ]
    grad_r = [Grad(*(one.at[q] for one in (gr, ysend_r, yrecv_r, zsend_r, zrecv_r, acc_r)), both=False) for q in range(2)]
    slices_p, slices_e, slices_s = Slices(fin_p), Slices(fin_e), [Slices(fin_s.at[q], q == 2) for q in range(3)]

    expand(0)
    scatter_start(1, 0, dot(dex[kind_rows(0), :], weight_e, NT))
    stored(cc4.at[r], l_cot[1])
    got(cc4.at[pl.ds(0, 3)], s_rx[1][1])
    cc[...] = cc4[...].reshape(4, 64, 512)
    expand(1)
    scatter_mid(1, 0)
    scatter_start(1, 1, dot(dex[kind_rows(1), :], weight_e, NT))
    ge[...] = dot(jnp.concatenate([act2[s] for s in range(4)], axis=1), dex[...], TN).reshape(4, 2, 64, 512)
    grad_e.start()
    scatter_mid(1, 1)
    s_af, r_af = new(), new()
    for dev in rest:
        copy(aff.at[r], aff.at[r], s_af, r_af, dev).start()
    over_x(1)

    def norm_back(d, xhat, rstd, gain, rows):
        sd = jnp.sum(d, axis=0, keepdims=True)
        sxx = jnp.sum(d * xhat, axis=0, keepdims=True)
        return (gain * rstd) * (d - sd / rows - xhat * (sxx / rows)), sd, sxx

    def weight_grad(q):
        full = jnp.concatenate([act1[s] for s in range(4)], axis=1)
        gs[q] = dot(full, pat[:, 384 * q : 384 * q + 384], TN).reshape(4, 2, 64, 384)
        grad_s[q].start()

    sum_d2, sum_x2 = [], []
    for kind in range(2):
        rows = KINDS[kind][1]
        d = scatter_end(1, kind) * slope2[kind_rows(kind), :]
        dz_, sd, sxx = norm_back(d, xhat2[kind_rows(kind), :], rstd2[kind], gain2, rows)
        sum_d2.append(sd)
        sum_x2.append(sxx)
        dz_ = dz_.astype(BF16).astype(F32)
        for tj in range(3):
            col = turned(dz_, kind, tj - 1)
            for ti in range(3):
                t = 3 * ti + tj
                pat[kind_rows(kind), 128 * t : 128 * t + 128] = moved(col, kind, ti - 1).astype(BF16)
        if kind == 1:
            weight_grad(0)
            both_mid(2, 0)
        scatter_start(2, kind, dot(pat[kind_rows(kind), :], weight_s(), NT))
    grad_e.along()
    weight_grad(1)
    weight_grad(2)
    both_mid(2, 1)
    over_x(2)
    over_x(3)
    line_got(share_o)
    between(we.at[xp[1]], 1)
    grad_s[0].along()
    grad_e.hand_on()
    grad_s[0].hand_on()

    sum_1 = [[0.0, 0.0], [0.0, 0.0]]
    for kind in range(2):
        rows = KINDS[kind][1]
        for xx in range(2):
            d = both_end(2, kind, xx) * slope1[xx, kind_rows(kind), :]
            dz_, sd, sxx = norm_back(d, xhat1[xx, kind_rows(kind), :], rstd1[kind][xx], gain1[xx], rows)
            sum_1[xx][0] += sxx
            sum_1[xx][1] += sd
            both_out(2, kind, xx, dred, dz_.astype(BF16))
        if kind == 0:
            grad_s[1].along()

    rows12 = [jnp.where(x == 0, sum_1[0][n], sum_1[1][n]) for n in range(2)]
    rows12 += [sum_x2[0] + sum_x2[1], sum_d2[0] + sum_d2[1]]
    gx3, gd3 = sum_x3[0] + sum_x3[1], sum_d3[0] + sum_d3[1]
    rows3 = [g[:, 128 * k : 128 * k + 128] for g in (gx3, gd3) for k in range(4)]
    pgr[i] = jnp.concatenate(rows12 + rows3 + [jnp.zeros((4, 128), F32)], axis=0)
    s_pp, r_pp, s_ps, r_ps = new(), new(), new(), new()
    for dev in peers[:7]:
        copy(pgr.at[i], pgr.at[i], s_pp, r_pp, dev).start()

    rows_pool[...] = jnp.zeros_like(rows_pool)
    for n in range(8):
        row = 4 * (n % 2) + n // 2
        rows_pool[row : row + 1, :] = jnp.sum(pool[n], axis=0, keepdims=True) / 64.0
        for m in range(2):
            row = 4 * (2 + 2 * (n % 2) + m) + n // 2
            rows_pool[row : row + 1, :] = jnp.sum(pool[8 + n, 4 * m : 4 * m + 4, :], axis=0, keepdims=True) / 16.0
    slices_p.start(rows_pool[...])
    grad_s[1].hand_on()
    full_d = [gather_end(2, kind, dred) for kind in range(2)]

    for m in range(4):
        col = dot(xv[:, :, :, 128 * m : 128 * m + 128].reshape(NV, 128), full_d[0], TN)
        col = col + dot(xc[:, :, 128 * m : 128 * m + 128].reshape(NC, 128), full_d[1], TN)
        for q in range(2):
            gr[q, m] = col[:, 256 * q : 256 * q + 256]

    @pl.when(y != c)
    def _():
        for one in grad_r:
            one.start()

    for n, ref in enumerate((xo_v, xo_c, co_v, co_c)):
        stored(ref, l_own + n)
    got(aff.at[pl.ds(0, 3)], r_af)
    got(we.at[pl.ds(0, 2)], r_ow + 1)
    own_output()
    grad_s[2].along()
    slices_s[0].start(grad_s[0].total())
    slices_e.start(grad_e.total())
    grad_s[2].hand_on()

    @pl.when(y == c)
    def _():
        grad_r[0].along()
        grad_r[1].along()

    slices_s[1].start(grad_s[1].total())
    slices_p.mid()
    slices_s[0].mid()
    slices_e.mid()
    got(wr.at[0], r_xw)
    between(wr.at[xp[1]], 0)

    got(pgr.at[pl.ds(0, 7)], r_pp)
    total = pgr[0]
    for n in range(1, 8):
        total = total + pgr[n]
    pgs[r] = total
    for dev in rest:
        copy(pgs.at[r], pgs.at[r], s_ps, r_ps, dev).start()
    slices_s[2].start(grad_s[2].total())
    slices_s[1].mid()
    got(wr.at[pl.ds(0, 2)], r_ow)
    own_gradient()

    s_fr, r_fr = new(2), new(2)
    for q in range(2):

        @pl.when(y == c)
        def _(q=q):
            fin_r[q, x] = grad_r[q].total().astype(BF16)
            for dev in rest:
                copy(fin_r.at[q, x], fin_r.at[q, x], s_fr + q, r_fr + q, dev).start()

    for one in (slices_p, slices_e, *slices_s):
        one.end()
    got(pgs.at[pl.ds(0, 3)], r_ps)
    sent(aff.at[pl.ds(0, 3)], s_af)
    sent(we, s_ow)
    sent(wr.at[0], s_xw)
    for s, (own_v, own_c) in enumerate(((xv, xc4), (cv, cc4))):
        sent(own_v.at[:, pl.ds(0, 3)], s_sx[s][0])
        sent(own_c.at[pl.ds(0, 3)], s_sx[s][1])
    sent(pg.at[pl.ds(0, 7)], s_pg)
    sent(pgr.at[pl.ds(0, 7)], s_pp)
    sent(pgs.at[pl.ds(0, 3)], s_ps)
    line_sent(share_s.send, ws, ws.at[:, pl.ds(0, 6)])
    for share in (share_e, share_o):
        sent(we.at[0, pl.ds(0, 4)], share.send)
        sent(we.at[0, pl.ds(0, 3)], share.passed)
    for op in range(3):
        sent(act1.at[pl.ds(0, 2)], s_cs + op)
        sent(act1.at[pl.ds(0, 1 if op == 1 else 2)], s_xs + op)
        sent(act1.at[pl.ds(0, 3 if op == 1 else 2)], s_ag + op)
    for one in (grad_e, *grad_s):
        sent(one.ysend, one.s_y)
        one.sent()

    @pl.when(y != c)
    def _():
        for q, one in enumerate(grad_r):
            sent(one.ysend, one.s_y)
            got(fin_r.at[q], r_fr + q)

    @pl.when(y == c)
    def _():
        sent(wr.at[0], share_r.send)
        sent(wr.at[0, pl.ds(0, 3)], share_r.passed)
        for q, one in enumerate(grad_r):
            one.sent()
            sent(one.zsend.at[pl.ds(0, 3)], s_fr + q)
            got(fin_r.at[q, 1 - x], r_fr + q)

    assert taken[0] == SEMAPHORES, taken


def store_kernel(
    out_v, out_c, pool, grad_v, grad_c, fin_e, fin_s, fin_r, sums,
    out_views, out_crops, pooled, grad_views, grad_crops, grad_reduce, grad_spatial, grad_expand,
    gain_a, shift_a, gain_b, shift_b, gain_c, shift_c,
    oc, pl_, gc, gr, gs, ge, sem,
):
    i = lax.axis_index("dp")
    z, y = i // 2, i % 2
    copies = []

    def store(src, dst):
        one = pltpu.make_async_copy(src, dst, sem.at[len(copies)])
        one.start()
        copies.append(one)

    store(out_v, out_views)
    store(grad_v, grad_views)
    for s in range(4):
        for t in range(9):
            gs[t, :, 128 * s : 128 * s + 128] = fin_s[t // 3, s, :, 128 * (t % 3) : 128 * (t % 3) + 128].astype(F32)
    store(gs, grad_spatial)
    for s in range(4):
        for k in range(4):
            lo = 512 * k + 256 * (s % 2) + 128 * (s // 2)
            ge[:, lo : lo + 128] = fin_e[s, :, 128 * k : 128 * k + 128].astype(F32)
    store(ge, grad_expand)
    for n in range(2):
        gr[:, 256 * n : 256 * n + 256] = fin_r[n].astype(F32).reshape(256, 256)
    store(gr, grad_reduce)
    oc[...] = out_c[...].reshape(16, 4, 2048)
    store(oc, out_crops)
    gc[...] = grad_c[...].reshape(16, 4, 2048)
    store(gc, grad_crops)
    for s in range(4):
        for k in range(4):
            lo = 512 * k + 256 * (s % 2) + 128 * (s // 2)
            pl_[:, :, lo : lo + 128] = pool[s, 0:24, 128 * k : 128 * k + 128].astype(F32).reshape(6, 4, 128)
    store(pl_, pooled)
    for n, out in enumerate((gain_a, shift_a, gain_b, shift_b)):
        row = sums[i // 2, n : n + 1, :]
        out[...] = jnp.where(i % 2 == 0, row[:, :64], row[:, 64:]).reshape(64)
    for n, out in enumerate((gain_c, shift_c)):
        out[...] = jnp.concatenate([sums[2 * m + y, pl.ds(4 + 4 * n + z, 1), :] for m in range(2)], axis=1).reshape(256)
    for one in copies:
        one.wait()


def fused(views, crops, w_reduce, w_spatial, w_expand, cot_views, cot_crops, *params):
    hbm, vmem = pl.BlockSpec(memory_space=pltpu.HBM), pl.BlockSpec(memory_space=pltpu.VMEM)

    def shape(dims, dtype):
        return jax.ShapeDtypeStruct(dims, dtype)

    def buf(dims, dtype=BF16):
        return pltpu.VMEM(dims, dtype)

    def dma(*dims):
        return pltpu.SemaphoreType.DMA(dims)

    held = pl.pallas_call(
        block_kernel,
        out_shape=[
            buf((8, 16, 2048)), buf((64, 2048)), buf((4, 32, 512)), buf((8, 16, 2048)), buf((64, 2048)),
            buf((4, 64, 512)), buf((3, 4, 64, 384)), buf((2, 2, 128, 256)), buf((4, 16, 128), F32),
        ],
        in_specs=[hbm] * 13,
        out_specs=[vmem] * 9,
        scratch_shapes=[
            buf((8, 4, 16, 512)), buf((4, 16, 4, 512)), buf((4, 64, 512)),
            buf((8, 4, 16, 512)), buf((4, 16, 4, 512)), buf((4, 64, 512)),
            buf((8, 16, 2048)), buf((16, 4, 2048)), buf((8, 16, 2048)), buf((16, 4, 2048)),
            buf((4, 4, 128, 512)), buf((9, 8, 64, 128)), buf((4, 8, 64, 512)), buf((4, 8, 512), F32), buf((64,)), buf((64,)), buf((64,)), buf((64,)), buf((256,)), buf((256,)), buf((8, 8, 128), F32),
            buf((3, 4, N, 128), F32), buf((3, 2, 2, NV, 128)), buf((3, 2, 2, NV, 128)),
            buf((3, 2, 2, NV, 128)), buf((3, 2, 2, NV, 128)),
            buf((4, N, 128)), buf((4, N, 128)), buf((4, N, 128)), buf((N, 1152), F32),
            buf((2, N, 128), F32), buf((2, N, 128), F32), buf((N, 128), F32), buf((N, 128), F32),
            buf((N, 512), F32), buf((N, 512), F32), buf((N, 512)), buf((N, 1152)),
            buf((192, 2048), F32), buf((16, 8, 512), F32), buf((32, 512), F32),
            buf((4, 2, 64, 512), F32), buf((3, 4, 2, 64, 384), F32), buf((2, 4, 128, 256), F32),
            buf((4, 64, 512)), buf((4, 64, 512)), buf((4, 64, 512)), buf((4, 64, 512)),
            buf((3, 4, 64, 384)), buf((3, 4, 64, 384)), buf((3, 4, 64, 384)), buf((3, 4, 64, 384)),
            buf((2, 4, 128, 256)), buf((2, 4, 128, 256)), buf((2, 4, 128, 256)), buf((2, 4, 128, 256)),
            buf((64, 512)), buf((3, 64, 384)), buf((64, 512), F32), buf((3, 64, 384), F32), buf((2, 128, 256), F32),
            buf((8, 16, 128), F32),
            dma(SEMAPHORES),
        ],
        compiler_params=pltpu.CompilerParams(collective_id=0, has_side_effects=True, vmem_limit_bytes=58 << 20),
        cost_estimate=pl.CostEstimate(flops=5_200_000_000, bytes_accessed=8_000_000, transcendentals=2_000_000),
    )(views, crops, w_reduce, w_spatial, w_expand, cot_views, cot_crops, *params)
    held = [pltpu.with_memory_space_constraint(one, pltpu.VMEM) for one in held]
    return pl.pallas_call(
        store_kernel,
        out_shape=[
            shape((8, 16, 2048), BF16), shape((16, 4, 2048), BF16), shape((6, 4, 2048), F32),
            shape((8, 16, 2048), BF16), shape((16, 4, 2048), BF16),
            shape((256, 512), F32), shape((9, 64, 512), F32), shape((64, 2048), F32),
            shape((64,), F32), shape((64,), F32), shape((64,), F32), shape((64,), F32), shape((256,), F32), shape((256,), F32),
        ],
        in_specs=[vmem] * 9,
        out_specs=[hbm] * 8 + [vmem] * 6,
        scratch_shapes=[
            buf((16, 4, 2048)), buf((6, 4, 2048), F32), buf((16, 4, 2048)),
            buf((256, 512), F32), buf((9, 64, 512), F32), buf((64, 2048), F32), dma(8),
        ],
        compiler_params=pltpu.CompilerParams(vmem_limit_bytes=16 << 20),
    )(*held)


def step(
    dp, rows, views, crops, w_reduce, gain_one, shift_one, w_spatial, gain_two, shift_two, w_expand, gain_three, shift_three,
    cot_views, cot_crops,
):
    args = (
        views, crops, w_reduce, gain_one, shift_one, w_spatial, gain_two, shift_two, w_expand, gain_three, shift_three,
        cot_views, cot_crops,
    )
    if (dp, rows) != (8, 4) or views.shape != (4, 2, 2, 8, 2048) or crops.shape != (4, 4, 1, 4, 2048):
        return body(*args)
    out_v, out_c, pooled, grad_v, grad_c, grad_r, grad_s, grad_e, ga, sa, gb, sb, gc, sc = fused(
        views.reshape(8, 16, 2048), crops.reshape(16, 4, 2048), w_reduce, w_spatial.reshape(9, 64, 512), w_expand,
        cot_views.reshape(8, 16, 2048), cot_crops.reshape(16, 4, 2048),
        gain_one, shift_one, gain_two, shift_two, gain_three, shift_three,
    )
    return (
        out_v.reshape(views.shape),
        out_c.reshape(crops.shape),
        jnp.transpose(pooled, (1, 0, 2)),
        grad_v.reshape(views.shape),
        grad_c.reshape(crops.shape),
        grad_r,
        ga,
        sa,
        grad_s.reshape(w_spatial.shape[:3] + (512,)),
        gb,
        sb,
        grad_e,
        gc,
        sc,
    )


def solution(mesh):
    return jax.shard_map(
        functools.partial(step, mesh.shape["dp"], mesh.shape["rows"]),
        mesh=mesh,
        in_specs=(
            P("dp", None, "rows", None, None),
            P("dp", None, "rows", None, None),
            P("dp", None),
            P("dp"),
            P("dp"),
            P(None, None, "dp", None),
            P("dp"),
            P("dp"),
            P("dp", None),
            P("dp"),
            P("dp"),
            P("dp", None, "rows", None, None),
            P("dp", None, "rows", None, None),
        ),
        out_specs=(
            P("dp", None, "rows", None, None),
            P("dp", None, "rows", None, None),
            P("dp", None, None),
            P("dp", None, "rows", None, None),
            P("dp", None, "rows", None, None),
            P("dp", None),
            P("dp"),
            P("dp"),
            P(None, None, "dp", None),
            P("dp"),
            P("dp"),
            P("dp", None),
            P("dp"),
            P("dp"),
        ),
        check_vma=False,
    )
```

```python
import functools

import jax
import jax.numpy as jnp
from jax import lax
from jax.experimental import pallas as pl
from jax.experimental.pallas import tpu as pltpu
from jax.sharding import PartitionSpec as P

EPSILON = 1e-05


def extended(cells, sides, width):
    for axis, dim in sides:
        count = lax.axis_size(axis)
        ends = count - 1
        head = lax.slice_in_dim(cells, 0, width, axis=dim)
        tail = lax.slice_in_dim(cells, cells.shape[dim] - width, cells.shape[dim], axis=dim)
        cells = jnp.concatenate(
            [
                lax.ppermute(tail, axis, [(i, (i + 1) % count) for i in range(ends)]),
                cells,
                lax.ppermute(head, axis, [((i + 1) % count, i) for i in range(ends)]),
            ],
            axis=dim,
        )
    return cells


def silu_slope(values):
    sigmoid_val = jax.nn.sigmoid(values)
    return sigmoid_val * (1.0 + values * (1.0 - sigmoid_val))


def standardize(reduced_pair, gain_vec, shift_vec):
    left_map = reduced_pair[0]
    right_map = reduced_pair[1]
    totals = lax.psum(
        (
            jnp.sum(left_map, 0),
            jnp.sum(left_map * left_map, 0),
            jnp.sum(right_map, 0),
            jnp.sum(right_map * right_map, 0),
        ),
        "rows",
    )
    results = []
    for member in range(2):
        values = reduced_pair[member]
        pixel_count = values.shape[0] * lax.axis_size("rows")
        channel_mean = totals[2 * member] / pixel_count
        inverse_scale = lax.rsqrt(
            totals[2 * member + 1] / pixel_count - channel_mean * channel_mean + EPSILON
        )
        centred = (values - channel_mean) * inverse_scale
        results.append((centred, inverse_scale, gain_vec * centred + shift_vec))
    return results


def unstandardize(slopes, saved, gain_vec):
    shift_left = jnp.sum(slopes[0], 0)
    gain_left = jnp.sum(slopes[0] * saved[0][0], 0)
    shift_right = jnp.sum(slopes[1], 0)
    gain_right = jnp.sum(slopes[1] * saved[1][0], 0)
    totals = lax.psum((shift_left, gain_left, shift_right, gain_right), "rows")
    results = []
    for member in range(2):
        pixel_count = slopes[member].shape[0] * lax.axis_size("rows")
        centred = saved[member][0]
        inverse_scale = saved[member][1]
        mean_slope = gain_vec * totals[2 * member] / pixel_count
        mean_cross = gain_vec * totals[2 * member + 1] / pixel_count
        results.append(
            inverse_scale * (gain_vec * slopes[member] - mean_slope - centred * mean_cross)
        )
    return (results, gain_left + gain_right, shift_left + shift_right)


def spread_rows(activity):
    return extended(activity, (("rows", 1),), 1)


def spread_grads(slopes):
    return extended(slopes, (("rows", 1),), 1)


def patches(padded, row_count, col_count, flipped):
    widened = jnp.pad(padded, ((0, 0), (0, 0), (1, 1), (0, 0)))
    tap_list = []
    for row_tap in range(3):
        for col_tap in range(3):
            row_start = 2 - row_tap if flipped else row_tap
            col_start = 2 - col_tap if flipped else col_tap
            tap_list.append(
                widened[:, row_start : row_start + row_count, col_start : col_start + col_count, :]
            )
    return jnp.concatenate(tap_list, axis=-1).reshape(-1, 9 * widened.shape[-1])


def body(
    views,
    crops,
    w_reduce,
    gain_one,
    shift_one,
    w_spatial,
    gain_two,
    shift_two,
    w_expand,
    gain_three,
    shift_three,
    cot_views,
    cot_crops,
):
    gathered = (
        lax.all_gather(w_reduce, "dp", axis=0, tiled=True),
        lax.all_gather(gain_one, "dp", axis=0, tiled=True),
        lax.all_gather(shift_one, "dp", axis=0, tiled=True),
        lax.all_gather(w_spatial, "dp", axis=2, tiled=True),
        lax.all_gather(gain_two, "dp", axis=0, tiled=True),
        lax.all_gather(shift_two, "dp", axis=0, tiled=True),
        lax.all_gather(w_expand, "dp", axis=0, tiled=True),
        lax.all_gather(gain_three, "dp", axis=0, tiled=True),
        lax.all_gather(shift_three, "dp", axis=0, tiled=True),
    )
    weight_reduce = gathered[0]
    weight_spatial = gathered[3]
    weight_expand = gathered[6]
    gain_first = gathered[1].astype(jnp.float32)
    shift_first = gathered[2].astype(jnp.float32)
    gain_second = gathered[4].astype(jnp.float32)
    shift_second = gathered[5].astype(jnp.float32)
    gain_third = gathered[7].astype(jnp.float32)
    shift_third = gathered[8].astype(jnp.float32)
    channels = views.shape[4]
    middle = weight_reduce.shape[1]
    map_shapes = [
        (views.shape[0] * views.shape[1], views.shape[2], views.shape[3]),
        (crops.shape[0] * crops.shape[1], crops.shape[2], crops.shape[3]),
    ]
    flat_inputs = [views.reshape(-1, channels), crops.reshape(-1, channels)]
    reduced = [
        jnp.dot(source, weight_reduce, preferred_element_type=jnp.float32) for source in flat_inputs
    ]
    first_norm = standardize(reduced, gain_first, shift_first)
    first_act = [jax.nn.silu(saved[2]).astype(jnp.bfloat16) for saved in first_norm]
    padded_act = [
        spread_rows(act.reshape(shape[0], shape[1], shape[2], middle))
        for act, shape in zip(first_act, map_shapes)
    ]
    patch_rows = [
        patches(padded, shape[1], shape[2], False) for padded, shape in zip(padded_act, map_shapes)
    ]
    kernel = weight_spatial.reshape(9 * middle, middle)
    spatial = [jnp.dot(patch, kernel, preferred_element_type=jnp.float32) for patch in patch_rows]
    second_norm = standardize(spatial, gain_second, shift_second)
    second_act = [jax.nn.silu(saved[2]).astype(jnp.bfloat16) for saved in second_norm]
    expanded = [
        jnp.dot(act, weight_expand, preferred_element_type=jnp.float32) for act in second_act
    ]
    third_norm = standardize(expanded, gain_third, shift_third)
    pre_list = [
        source.astype(jnp.float32) + saved[2] for source, saved in zip(flat_inputs, third_norm)
    ]
    activation = [jax.nn.silu(pre) for pre in pre_list]
    view_sums = jnp.sum(activation[0].reshape(views.shape[0], views.shape[1], -1, channels), axis=2)
    crop_sums = jnp.sum(activation[1].reshape(crops.shape[0], crops.shape[1], -1, channels), axis=2)
    pooled_sums = lax.psum((view_sums, crop_sums), "rows")
    pooled = jnp.concatenate(
        [
            pooled_sums[0] / (views.shape[3] * views.shape[3]),
            pooled_sums[1] / (crops.shape[3] * crops.shape[3]),
        ],
        axis=1,
    )
    cotangent = [
        cot_views.reshape(-1, channels).astype(jnp.float32),
        cot_crops.reshape(-1, channels).astype(jnp.float32),
    ]
    d_pre = [cot * silu_slope(pre) for cot, pre in zip(cotangent, pre_list)]
    d_expanded_f, gain_third_grad, shift_third_grad = unstandardize(d_pre, third_norm, gain_third)
    d_expanded = [grad.astype(jnp.bfloat16) for grad in d_expanded_f]
    expand_grad = jnp.einsum(
        "pm,pc->mc", second_act[0], d_expanded[0], preferred_element_type=jnp.float32
    ) + jnp.einsum("pm,pc->mc", second_act[1], d_expanded[1], preferred_element_type=jnp.float32)
    d_norm_two = [
        jnp.einsum("pc,mc->pm", grad, weight_expand, preferred_element_type=jnp.float32)
        * silu_slope(saved[2])
        for grad, saved in zip(d_expanded, second_norm)
    ]
    d_spatial_f, gain_second_grad, shift_second_grad = unstandardize(
        d_norm_two, second_norm, gain_second
    )
    d_spatial = [grad.astype(jnp.bfloat16) for grad in d_spatial_f]
    spatial_grad = (
        jnp.einsum("pk,pm->km", patch_rows[0], d_spatial[0], preferred_element_type=jnp.float32)
        + jnp.einsum("pk,pm->km", patch_rows[1], d_spatial[1], preferred_element_type=jnp.float32)
    ).reshape(3, 3, middle, middle)
    back_kernel = jnp.transpose(weight_spatial, (0, 1, 3, 2)).reshape(9 * middle, middle)
    padded_grads = [
        spread_grads(grad.reshape(shape[0], shape[1], shape[2], middle))
        for grad, shape in zip(d_spatial, map_shapes)
    ]
    d_norm_one = [
        jnp.dot(
            patches(padded, shape[1], shape[2], True),
            back_kernel,
            preferred_element_type=jnp.float32,
        )
        * silu_slope(saved[2])
        for padded, shape, saved in zip(padded_grads, map_shapes, first_norm)
    ]
    d_reduced_f, gain_first_grad, shift_first_grad = unstandardize(
        d_norm_one, first_norm, gain_first
    )
    d_reduced = [grad.astype(jnp.bfloat16) for grad in d_reduced_f]
    reduce_grad = jnp.einsum(
        "pc,pm->cm", flat_inputs[0], d_reduced[0], preferred_element_type=jnp.float32
    ) + jnp.einsum("pc,pm->cm", flat_inputs[1], d_reduced[1], preferred_element_type=jnp.float32)
    input_grads = [
        (
            pre_grad
            + jnp.einsum("pm,cm->pc", grad, weight_reduce, preferred_element_type=jnp.float32)
        ).astype(jnp.bfloat16)
        for pre_grad, grad in zip(d_pre, d_reduced)
    ]
    shares = (
        lax.psum_scatter(reduce_grad, "dp", scatter_dimension=0, tiled=True),
        lax.psum_scatter(gain_first_grad, "dp", scatter_dimension=0, tiled=True),
        lax.psum_scatter(shift_first_grad, "dp", scatter_dimension=0, tiled=True),
        lax.psum_scatter(spatial_grad, "dp", scatter_dimension=2, tiled=True),
        lax.psum_scatter(gain_second_grad, "dp", scatter_dimension=0, tiled=True),
        lax.psum_scatter(shift_second_grad, "dp", scatter_dimension=0, tiled=True),
        lax.psum_scatter(expand_grad, "dp", scatter_dimension=0, tiled=True),
        lax.psum_scatter(gain_third_grad, "dp", scatter_dimension=0, tiled=True),
        lax.psum_scatter(shift_third_grad, "dp", scatter_dimension=0, tiled=True),
    )
    summed = lax.psum(
        (
            shares[0],
            shares[1],
            shares[2],
            shares[3],
            shares[4],
            shares[5],
            shares[6],
            shares[7],
            shares[8],
        ),
        "rows",
    )
    return (
        activation[0].astype(jnp.bfloat16).reshape(views.shape),
        activation[1].astype(jnp.bfloat16).reshape(crops.shape),
        pooled,
        input_grads[0].reshape(views.shape),
        input_grads[1].reshape(crops.shape),
        summed[0],
        summed[1],
        summed[2],
        summed[3],
        summed[4],
        summed[5],
        summed[6],
        summed[7],
        summed[8],
    )


MESH = pl.DeviceIdType.MESH
SEMAPHORES = 179
F32 = jnp.float32
BF16 = jnp.bfloat16
NV = 512
NC = 256
N = NV + NC
KINDS = ((0, NV), (NV, NC))
NT = (((1,), (1,)), ((), ()))
TN = (((0,), (0,)), ((), ()))


def sigmoid(values):
    return 0.5 * jnp.tanh(0.5 * values) + 0.5


def dot(left, right, dims=(((1,), (0,)), ((), ()))):
    return lax.dot_general(left, right, dims, preferred_element_type=F32)


def moved(values, kind, step):
    rows, lanes = values.shape
    if step == 0:
        return values
    if kind == 0:
        maps = values.reshape(rows // 64, 64, lanes)
        gap = jnp.zeros((rows // 64, 8, lanes), values.dtype)
        parts = [gap, maps[:, :-8]] if step > 0 else [maps[:, 8:], gap]
        return jnp.concatenate(parts, axis=1).reshape(rows, lanes)
    gap = jnp.zeros((64, lanes), values.dtype)
    return jnp.concatenate([gap, values[:-64]] if step > 0 else [values[64:], gap], axis=0)


def turned(values, kind, step):
    if step == 0:
        return values
    rows, lanes = values.shape
    width = 8 if kind == 0 else 4
    col = lax.rem(lax.broadcasted_iota(jnp.int32, (rows, lanes), 0), width)
    edge = 0 if step > 0 else width - 1
    return jnp.where(col == edge, 0.0, pltpu.roll(values, 1 if step > 0 else rows - 1, axis=0))


def block_kernel(
    views, crops, w_reduce, w_spatial, w_expand, cot_views, cot_crops, gain_a, shift_a, gain_b, shift_b, gain_c, shift_c,
    out_views, out_crops, fin_p, grad_views, grad_crops, fin_e, fin_s, fin_r, pgs,
    xv, xc4, xc, cv, cc4, cc, xo_v, xo_c, co_v, co_c, wr, ws, we, aff, raw_a, raw_b, raw_c, raw_d, raw_e, raw_f, pg,
    part, csend, crecv, xsend, xrecv,
    act1, act2, dred, conv, xhat1, slope1, xhat2, slope2, ex, dpre, dex, pat, dpo, pool, rows_pool,
    ge, gs, gr, ysend_e, yrecv_e, zsend_e, zrecv_e, ysend_s, yrecv_s, zsend_s, zrecv_s, ysend_r, yrecv_r, zsend_r, zrecv_r,
    relay_e, relay_s, acc_e, acc_s, acc_r, pgr,
    sem,
):
    i, r = lax.axis_index("dp"), lax.axis_index("rows")
    z, y = i // 2, i % 2
    x, c = r // 2, r % 2
    yp = (i + 1 - 2 * y, r)
    cp = (i, 2 * x + 1 - c)
    xp = (i, 2 * (1 - x) + c)
    xcp = (i, 2 * (1 - x) + 1 - c)
    rest = (xp, xcp, cp)

    middle = (z + 1) // 2 == 1
    step = 1 - 2 * (z // 2)

    def on_line(places):
        return (2 * (z + places * step) + y, r)

    taken = [0]

    def new(count=1):
        taken[0] += count
        return taken[0] - count

    def copy(src, dst, send, recv, dev):
        return pltpu.make_async_remote_copy(
            src_ref=src, dst_ref=dst, send_sem=sem.at[send], recv_sem=sem.at[recv], device_id=dev, device_id_type=MESH
        )

    def got(ref, recv):
        copy(ref, ref, recv, recv, cp).wait_recv()

    def sent(ref, send):
        copy(ref, ref, send, send, cp).wait_send()

    def stored(ref, one):
        pltpu.make_async_copy(ref, ref, sem.at[one]).wait()

    def lanes(k, xx, cc_):
        return pl.ds(pl.multiple_of(512 * k + 256 * cc_ + 128 * xx, 128), 128)

    def kl(k):
        return pl.ds(128 * k, 128)

    def kind_rows(kind):
        return pl.ds(*KINDS[kind])

    bar = pltpu.get_barrier_semaphore()
    peers = [((i + n) % 8, r) for n in range(1, 8)] + [cp, xp, xcp]
    for dev in peers:
        pl.semaphore_signal(bar, inc=1, device_id=dev, device_id_type=MESH)

    def stage(src, dst, one):
        pltpu.make_async_copy(src, dst, sem.at[one]).start()

    l_wr, l_ws, l_we, l_we2, l_gain = new(), new(), new(), new(), new(6)
    l_x, l_cot, l_own = (new(), new()), (new(), new()), new(4)

    @pl.when(y == c)
    def _():
        stage(w_reduce.at[pl.ds(pl.multiple_of(128 * x, 128), 128)], wr.at[r, z], l_wr)

    stage(w_spatial.at[:, :, pl.ds(pl.multiple_of(128 * r, 128), 128)], ws.at[:, i], l_ws)
    raw = (raw_a, raw_b, raw_c, raw_d, raw_e, raw_f)
    for n, vec in enumerate((gain_a, shift_a, gain_b, shift_b, gain_c, shift_c)):
        stage(vec, raw[n], l_gain + n)
    for k in range(4):
        stage(views.at[:, :, lanes(k, x, c)], xv.at[:, r, :, kl(k)], l_x[0])
        stage(crops.at[:, :, lanes(k, x, c)], xc4.at[r, :, :, kl(k)], l_x[1])
    for k in range(4):
        stage(w_expand.at[:, lanes(k, x, c)], we.at[r, i, :, kl(k)], l_we)
        stage(w_expand.at[:, lanes(k, 1 - x, c)], we.at[xp[1], i, :, kl(k)], l_we2)
    for k in range(4):
        stage(cot_views.at[:, :, lanes(k, x, c)], cv.at[:, r, :, kl(k)], l_cot[0])
        stage(cot_crops.at[:, :, lanes(k, x, c)], cc4.at[r, :, :, kl(k)], l_cot[1])
    for n, (src, dst) in enumerate(((views, xo_v), (crops, xo_c), (cot_views, co_v), (cot_crops, co_c))):
        stage(src, dst, l_own + n)

    pl.semaphore_wait(bar, len(peers))

    class Share:
        def __init__(self, parts, others):
            self.parts, self.others = parts, others
            count = len(parts(0))
            self.send, self.passed = new(), new()
            self.along_z = [new(3) for _ in range(count)]
            self.along_y = [new() for _ in range(count)]

    share_r = Share(lambda k: (wr.at[r, k],), None)
    share_s = Share(
        lambda k: tuple(ws.at[pl.ds(3 * h, 3), 2 * k + y] for h in range(3)),
        lambda h: ws.at[pl.ds(3 * h, 3), pl.ds(0, 4)],
    )
    share_e = Share(lambda k: (we.at[r, 2 * k + y],), lambda h: we.at[0, pl.ds(0, 4)])
    share_o = Share(lambda k: (we.at[xp[1], 2 * k + y],), lambda h: we.at[0, pl.ds(0, 4)])

    inner = ((z + 1) // 2) * (2 - (z + 1) // 2)

    def line_send(share, direct=False):
        for h, own in enumerate(share.parts(z)):

            def go(slot, dev, own=own):
                copy(own, own, share.send, slot, dev).start()

            go(share.along_z[h], on_line(2))
            go(share.along_z[h] + 2 - inner, on_line(1))

            @pl.when(middle)
            def _(go=go, h=h):
                go(share.along_z[h] + 1, on_line(-1))

            if direct:

                @pl.when(jnp.logical_not(middle))
                def _(go=go, h=h):
                    go(share.along_z[h] + 2, on_line(3))

    def line_over(share):
        for h, own in enumerate(share.parts(z)):
            copy(own, own, share.send, share.along_y[h], yp).start()

    def line_pass(share, h, send=None, which=(0, 1, 2)):
        relayed = send is None
        send = share.send if relayed else send

        def take(places, slot, on=False):
            if slot not in which:
                return
            ref = share.parts(z + places * step)[h]
            got(ref, share.along_z[h] + slot)
            if on:
                copy(ref, ref, send, share.along_z[h] + 2, on_line(-1)).start()
            copy(ref, ref, send, share.along_y[h], yp).start()

        @pl.when(middle)
        def _():
            take(2, 0, relayed)
            take(1, 1)
            take(-1, 2)

        @pl.when(jnp.logical_not(middle))
        def _():
            take(2, 0)
            take(1, 1)
            take(3, 2)

    def line_got(share):
        for h, slot in enumerate(share.along_y):
            got(share.others(h), slot)

    def line_sent(send, for_middle, for_end):
        @pl.when(middle)
        def _():
            sent(for_middle, send)

        @pl.when(jnp.logical_not(middle))
        def _():
            sent(for_end, send)

    @pl.when(y == c)
    def _():
        stored(wr.at[r, z], l_wr)
        line_send(share_r, True)
        line_over(share_r)

    s_sx, s_rx = ((new(), new()), (new(), new())), ((new(), new()), (new(), new()))

    def spread_v(src, dst, s, devs):
        for dev in devs:
            for k in range(4):
                copy(src.at[:, :, lanes(k, dev[1] // 2, dev[1] % 2)], dst.at[:, r, :, kl(k)], s_sx[s][0], s_rx[s][0], dev).start()

    def spread_c(src, dst, s, devs):
        for dev in devs:
            for k in range(4):
                copy(src.at[:, :, lanes(k, dev[1] // 2, dev[1] % 2)], dst.at[r, :, :, kl(k)], s_sx[s][1], s_rx[s][1], dev).start()

    spread_v(views, xv, 0, rest)
    spread_c(crops, xc4, 0, rest)
    spread_v(cot_views, cv, 1, rest[:1])
    spread_c(cot_crops, cc4, 1, rest[:1])
    stored(ws.at[:, i], l_ws)
    line_over(share_s)

    for n in range(6):
        stored(raw[n], l_gain + n)
    pg[i] = jnp.zeros((8, 128), F32)
    for n in range(4):
        vec = raw[n][...].reshape(1, 64).astype(F32)
        pg[i, n : n + 1, :] = jnp.concatenate([vec, vec], axis=1)
    for n in range(2):
        for m in range(2):
            pg[i, 4 + 2 * n + m : 5 + 2 * n + m, :] = raw[4 + n][128 * m : 128 * m + 128].reshape(1, 128).astype(F32)
    s_pg, r_pg = new(), new()
    for dev in peers[:7]:
        copy(pg.at[i], pg.at[i], s_pg, r_pg, dev).start()

    @pl.when(y == c)
    def _():
        line_pass(share_r, 0, share_r.passed)

    got(pg.at[pl.ds(0, 7)], r_pg)
    line_send(share_s)
    stored(xv.at[:, r], l_x[0])
    got(xv.at[:, pl.ds(0, 3)], s_rx[0][0])

    @pl.when(y != c)
    def _():
        got(wr.at[r], share_r.along_y[0])

    s_cs, r_cs = new(3), new(12)
    s_xs, r_xs = new(3), new(12)
    s_ag, r_ag = new(3), new(8)

    def scatter_start(op, kind, sums):
        rows = kind_rows(kind)
        n = pl.ds(0, KINDS[kind][1])
        if op == 0:
            sums = sums - jnp.sum(sums, axis=0, keepdims=True) / KINDS[kind][1]
        for s in range(4):
            part[op, s, rows, :] = sums[:, 128 * s : 128 * s + 128]
        for near, xx in enumerate((1 - x, x)):
            csend[op, kind, xx, n, :] = part[op, 2 * xx + 1 - c, rows, :].astype(BF16)
            own = csend.at[op, kind, xx, n]
            copy(own, crecv.at[op, kind, xx, n], s_cs + op, r_cs + 4 * op + 2 * kind + near, cp).start()

    def scatter_mid(op, kind):
        rows = kind_rows(kind)
        n = pl.ds(0, KINDS[kind][1])
        got(crecv.at[op, kind, 1 - x, n], r_cs + 4 * op + 2 * kind)
        far = part[op, 2 * (1 - x) + c, rows, :] + crecv[op, kind, 1 - x, n, :].astype(F32)
        xsend[op, kind, 0, n, :] = far.astype(BF16)
        copy(xsend.at[op, kind, 0, n], xrecv.at[op, kind, 0, n], s_xs + op, r_xs + 4 * op + 2 * kind, xp).start()

    def scatter_end(op, kind):
        rows = kind_rows(kind)
        n = pl.ds(0, KINDS[kind][1])
        got(crecv.at[op, kind, x, n], r_cs + 4 * op + 2 * kind + 1)
        near = part[op, 2 * x + c, rows, :] + crecv[op, kind, x, n, :].astype(F32)
        got(xrecv.at[op, kind, 0, n], r_xs + 4 * op + 2 * kind)
        return near + xrecv[op, kind, 0, n, :].astype(F32)

    def gather_start(kind, buf, value):
        rows = kind_rows(kind)
        buf[r, rows, :] = value
        own = buf.at[r, rows]
        copy(own, own, s_ag + 1, r_ag + 6 + kind, xp).start()
        copy(own, own, s_ag + 1, r_ag + 2 + kind, cp).start()

    def gather_mid(kind, buf):
        far = buf.at[xp[1], kind_rows(kind)]
        got(far, r_ag + 6 + kind)
        copy(far, far, s_ag + 1, r_ag + 2 + kind, cp).start()

    def gather_end(op, kind, buf):
        rows = kind_rows(kind)
        got(buf.at[pl.ds(0, 2), rows], r_ag + 2 * op + kind)
        return jnp.concatenate([buf[s, rows, :] for s in range(4)], axis=1)

    def both_mid(op, kind):
        rows = kind_rows(kind)
        n = pl.ds(0, KINDS[kind][1])
        for near, xx in enumerate((1 - x, x)):
            got(crecv.at[op, kind, xx, n], r_cs + 4 * op + 2 * kind + near)
        for xx in range(2):
            total = part[op, 2 * xx + c, rows, :] + crecv[op, kind, xx, n, :].astype(F32)
            part[op, 2 * xx + c, rows, :] = total
            xsend[op, kind, xx, n, :] = total.astype(BF16)
            one = xsend.at[op, kind, xx, n]
            copy(one, xrecv.at[op, kind, xx, n], s_xs + op, r_xs + 4 * op + 2 * kind + xx, xp).start()

    def both_end(op, kind, xx):
        n = pl.ds(0, KINDS[kind][1])
        got(xrecv.at[op, kind, xx, n], r_xs + 4 * op + 2 * kind + xx)
        return part[op, 2 * xx + c, kind_rows(kind), :] + xrecv[op, kind, xx, n, :].astype(F32)

    def both_out(op, kind, xx, buf, value):
        rows = kind_rows(kind)
        buf[2 * xx + c, rows, :] = value
        own = buf.at[2 * xx + c, rows]
        copy(own, own, s_ag + op, r_ag + 2 * op + kind, cp).start()

    weight_r = wr[r].reshape(512, 512)
    scatter_start(0, 0, dot(xv[...].reshape(NV, 512), weight_r))
    stored(xc4.at[r], l_x[1])
    got(xc4.at[pl.ds(0, 3)], s_rx[0][1])
    xc[...] = xc4[...].reshape(4, 64, 512)
    scatter_start(0, 1, dot(xc[...].reshape(NC, 512), weight_r))
    line_pass(share_s, 0, None, (0, 1))
    both_mid(0, 0)
    both_mid(0, 1)

    half = lax.broadcasted_iota(jnp.int32, (1, 128), 1) < 64

    def slice_of(s, q):
        return jnp.where(half, pg[2 * s, q : q + 1, :], pg[2 * s + 1, q : q + 1, :])

    gain1, shift1 = [[slice_of(2 * xx + c, q) for xx in range(2)] for q in range(2)]
    gain2, shift2 = slice_of(r, 2), slice_of(r, 3)
    gain3 = jnp.concatenate([pg[2 * k + c, pl.ds(4 + x, 1), :] for k in range(4)], axis=1)
    shift3 = jnp.concatenate([pg[2 * k + c, pl.ds(6 + x, 1), :] for k in range(4)], axis=1)

    def norm_act(values, rows, gain, shift):
        mean = jnp.sum(values, axis=0, keepdims=True) / rows
        second = jnp.sum(values * values, axis=0, keepdims=True) / rows
        rstd = lax.rsqrt(second - mean * mean + EPSILON)
        xhat = (values - mean) * rstd
        norm = gain * xhat + shift
        sig = sigmoid(norm)
        return rstd, xhat, sig * (1.0 + norm * (1.0 - sig)), (norm * sig).astype(BF16)

    for h, which in ((1, (0, 1)), (0, (2,)), (2, (0, 1)), (1, (2,)), (2, (2,))):
        line_pass(share_s, h, None, which)
    stored(we.at[r, i], l_we)
    stored(we.at[r, i], l_we2)
    line_send(share_e, True)
    line_over(share_e)
    rstd1, rstd2 = [[None, None], [None, None]], [None, None]
    for kind in range(2):
        rows = KINDS[kind][1]
        for xx in range(2):
            rstd1[kind][xx], xh, sl, act = norm_act(both_end(0, kind, xx), rows, gain1[xx], shift1[xx])
            both_out(0, kind, xx, act1, act)
            xhat1[xx, kind_rows(kind), :] = xh
            slope1[xx, kind_rows(kind), :] = sl
        if kind == 0:
            spread_v(cot_views, cv, 1, rest[1:])

    s_ow, s_xw, r_xw, r_ow = new(), new(), new(), new(2)

    def over_x(k):
        copy(wr.at[r, k], wr.at[r, k], s_xw, r_xw, xp).start()

    def between(ref, n):
        copy(ref, ref, s_ow, r_ow + n, cp).start()

    between(wr.at[r], 0)
    line_send(share_o, True)
    line_over(share_o)
    line_pass(share_e, 0, share_e.passed, (0,))
    line_got(share_s)
    line_pass(share_e, 0, share_e.passed, (1,))

    def weight_s():
        return jnp.concatenate([ws[t].reshape(512, 128) for t in range(9)], axis=1)

    for kind in range(2):
        rows = KINDS[kind][1]
        conv[kind_rows(kind), :] = dot(gather_end(0, kind, act1), weight_s())
        taps = [conv[kind_rows(kind), 128 * t : 128 * t + 128] for t in range(9)]
        spatial = None
        for j in range(3):
            col = taps[3 + j] + moved(taps[j], kind, 1) + moved(taps[6 + j], kind, -1)
            col = turned(col, kind, 1 - j)
            spatial = col if spatial is None else spatial + col
        rstd2[kind], xh, sl, act = norm_act(spatial, rows, gain2, shift2)
        gather_start(kind, act2, act)
        xhat2[kind_rows(kind), :] = xh
        slope2[kind_rows(kind), :] = sl
        if kind == 0:
            line_pass(share_e, 0, share_e.passed, (2,))
    spread_c(cot_crops, cc4, 1, rest[1:])
    over_x(0)
    pool[...] = jnp.zeros_like(pool)
    gather_mid(0, act2)
    stored(cv.at[:, r], l_cot[0])
    got(cv.at[:, pl.ds(0, 3)], s_rx[1][0])
    line_got(share_e)
    line_pass(share_o, 0, share_o.passed)
    between(we.at[r], 1)
    weight_e = we[r].reshape(512, 512)

    sum_x3, sum_d3 = [], []
    zero8 = jnp.zeros((8, 512), F32)

    def expand(kind):
        start, rows = KINDS[kind]
        ex[kind_rows(kind), :] = dot(gather_end(1, kind, act2), weight_e)

        def moments(b, acc):
            e = ex[pl.ds(pl.multiple_of(start + 32 * b, 32), 32), :].reshape(4, 8, 512)
            return acc[0] + jnp.sum(e, axis=0), acc[1] + jnp.sum(e * e, axis=0)

        tot, sq = lax.fori_loop(0, rows // 32, moments, (zero8, zero8))
        if kind == 0:
            gather_mid(1, act2)
        mean = jnp.sum(tot, axis=0, keepdims=True) / rows
        rstd = lax.rsqrt(jnp.sum(sq, axis=0, keepdims=True) / rows - mean * mean + EPSILON)

        def finish(b, acc):
            rs = pl.ds(pl.multiple_of(start + 16 * b, 16), 16)
            qs = pl.ds(pl.multiple_of(16 * (b % 4), 16), 16)
            xhat = (ex[rs, :] - mean) * rstd
            ex[rs, :] = xhat
            src = xv[b // 4, b % 4] if kind == 0 else xc[b // 4, qs, :]
            cot = cv[b // 4, b % 4] if kind == 0 else cc[b // 4, qs, :]
            pre = src.astype(F32) + (gain3 * xhat + shift3)
            sig = sigmoid(pre)
            activation = pre * sig
            d = cot.astype(F32) * (sig * (1.0 + pre * (1.0 - sig)))
            dpre[rs, :] = d
            if kind == 0:
                pool[b // 4] += activation[:8] + activation[8:]
            else:
                pool[8 + 2 * (b % 4)] += activation[:8]
                pool[9 + 2 * (b % 4)] += activation[8:]
            dx = d * xhat
            return acc[0] + (d[:8] + d[8:]), acc[1] + (dx[:8] + dx[8:])

        sd, sxx = lax.fori_loop(0, rows // 16, finish, (zero8, zero8), unroll=2)
        sd, sxx = jnp.sum(sd, axis=0, keepdims=True), jnp.sum(sxx, axis=0, keepdims=True)
        sum_d3.append(sd)
        sum_x3.append(sxx)
        scale = gain3 * rstd
        mean_d, mean_x = sd / rows, sxx / rows
        aff[r, 2 * kind : 2 * kind + 1, :] = scale
        aff[r, 2 * kind + 1 : 2 * kind + 2, :] = shift3 - scale * mean

        def back(b, _):
            rs = pl.ds(pl.multiple_of(start + 32 * b, 32), 32)
            dex[rs, :] = (scale * (dpre[rs, :] - mean_d - ex[rs, :] * mean_x)).astype(BF16)
            return 0

        lax.fori_loop(0, rows // 32, back, 0)

    def own_rows(buf):
        slices = []
        for s in range(4):
            rows = [buf[s, pl.ds(pl.multiple_of(64 * m + 16 * r, 16), 16), :] for m in range(8)]
            rows.append(buf[s, pl.ds(pl.multiple_of(NV + 64 * r, 64), 64), :])
            slices.append(jnp.concatenate(rows, axis=0))
        return jnp.concatenate(slices, axis=1)

    def own_blocks(values, s):
        for k in range(4):
            lo = 512 * k + 256 * (s % 2) + 128 * (s // 2)
            yield k, slice(lo, lo + 128), (values[:128, 128 * k : 128 * k + 128], values[128:, 128 * k : 128 * k + 128])

    def own_output():
        act = own_rows(act2)
        for s in range(4):
            for k, cols, blocks in own_blocks(dot(act, we[s].reshape(512, 512)), s):
                for kind, block in enumerate(blocks):
                    scale = aff[s, 2 * kind : 2 * kind + 1, 128 * k : 128 * k + 128]
                    shift = aff[s, 2 * kind + 1 : 2 * kind + 2, 128 * k : 128 * k + 128]
                    src = (xo_v if kind == 0 else xo_c)[:, :, cols].reshape(block.shape).astype(F32)
                    cot = (co_v if kind == 0 else co_c)[:, :, cols].reshape(block.shape).astype(F32)
                    pre = src + (scale * block + shift)
                    sig = sigmoid(pre)
                    if kind == 0:
                        out_views[:, :, cols] = (pre * sig).astype(BF16).reshape(8, 16, 128)
                    else:
                        out_crops[:, cols] = (pre * sig).astype(BF16)
                    dpo[128 * kind : 128 * kind + block.shape[0], cols] = cot * (sig * (1.0 + pre * (1.0 - sig)))

    def own_gradient():
        back = own_rows(dred)
        for s in range(4):
            for _, cols, blocks in own_blocks(dot(back, wr[s].reshape(512, 512), NT), s):
                grad_views[:, :, cols] = (dpo[:128, cols] + blocks[0]).astype(BF16).reshape(8, 16, 128)
                grad_crops[:, cols] = (dpo[128:, cols] + blocks[1]).astype(BF16)

    far_of = jnp.where(middle, z + 2 * step, z + 3 * step)
    mid_of = jnp.where(middle, z - step, z + 2 * step)
    order = [far_of, mid_of, z + step, z]

    class Grad:
        def __init__(self, full, ysend, yrecv, zsend, zrecv, acc, relay=None, both=True):
            self.full, self.ysend, self.yrecv, self.zsend, self.zrecv = full, ysend, yrecv, zsend, zrecv
            self.acc, self.relay, self.both = acc, relay, both
            self.s_y, self.r_y, self.s_z, self.r_z, self.r_relay = new(), new(4), new(), new(), new()

        def start(self):
            for k in order:
                self.ysend[k] = (self.full[k, 1 - y] if self.both else self.full[k]).astype(BF16)
                copy(self.ysend.at[k], self.yrecv.at[k], self.s_y, self.r_y + k, yp).start()

        def add(self, k):
            got(self.yrecv.at[k], self.r_y + k)
            return (self.full[k, y] if self.both else self.full[k]) + self.yrecv[k].astype(F32)

        def send(self, k, value):
            self.zsend[k] = value.astype(BF16)
            copy(self.zsend.at[k], self.zrecv.at[z], self.s_z, self.r_z, (2 * k + y, r)).start()

        def along(self):
            if self.relay is None:
                self.send(order[0], self.add(order[0]))
            else:

                @pl.when(jnp.logical_not(middle))
                def _():
                    self.zsend[order[0]] = self.add(order[0]).astype(BF16)
                    copy(self.zsend.at[order[0]], self.relay, self.s_z, self.r_relay, on_line(1)).start()

            self.send(order[1], self.add(order[1]))
            self.send(order[2], self.add(order[2]))

        def hand_on(self):
            @pl.when(middle)
            def _():
                total = self.add(order[0])
                got(self.relay, self.r_relay)
                self.send(order[0], total + self.relay[...].astype(F32))

        def total(self):
            self.acc[...] = self.add(z)
            if self.relay is None:
                got(self.zrecv.at[pl.ds(0, 3)], self.r_z)
                self.acc[...] += self.zrecv[order[0]].astype(F32) + self.zrecv[order[1]].astype(F32)
                return self.acc[...] + self.zrecv[order[2]].astype(F32)

            @pl.when(middle)
            def _():
                got(self.zrecv.at[pl.ds(0, 3)], self.r_z)
                self.acc[...] += self.zrecv[z - step].astype(F32)

            @pl.when(jnp.logical_not(middle))
            def _():
                got(self.zrecv.at[pl.ds(0, 2)], self.r_z)

            return self.acc[...] + self.zrecv[z + step].astype(F32) + self.zrecv[z + 2 * step].astype(F32)

        def sent(self):
            sent(self.zsend.at[pl.ds(0, 3)], self.s_z)

    class Slices:
        def __init__(self, buf, straight=False):
            self.buf, self.straight, self.send, self.near, self.far = buf, straight, new(), new(), new()

        def start(self, value):
            self.buf[r] = value.astype(BF16)
            for dev, come in ((xp, self.near if self.straight else self.far), (cp, self.near), (xcp, self.near)):
                if dev is not xcp or self.straight:
                    copy(self.buf.at[r], self.buf.at[r], self.send, come, dev).start()

        def mid(self):
            far = self.buf.at[xp[1]]
            got(far, self.far)
            copy(far, far, self.send, self.near, cp).start()

        def end(self):
            got(self.buf.at[pl.ds(0, 3 if self.straight else 2)], self.near)
            sent(self.buf.at[pl.ds(0, 3)], self.send)

    grad_e = Grad(ge, ysend_e, yrecv_e, zsend_e, zrecv_e, acc_e, relay_e)
    grad_s = [
        Grad(*(one.at[q] for one in (gs, ysend_s, yrecv_s, zsend_s, zrecv_s, acc_s, relay_s))) for q in range(3)
    ]
    grad_r = [Grad(*(one.at[q] for one in (gr, ysend_r, yrecv_r, zsend_r, zrecv_r, acc_r)), both=False) for q in range(2)]
    slices_p, slices_e, slices_s = Slices(fin_p), Slices(fin_e), [Slices(fin_s.at[q], q == 2) for q in range(3)]

    expand(0)
    scatter_start(1, 0, dot(dex[kind_rows(0), :], weight_e, NT))
    stored(cc4.at[r], l_cot[1])
    got(cc4.at[pl.ds(0, 3)], s_rx[1][1])
    cc[...] = cc4[...].reshape(4, 64, 512)
    expand(1)
    scatter_mid(1, 0)
    scatter_start(1, 1, dot(dex[kind_rows(1), :], weight_e, NT))
    ge[...] = dot(jnp.concatenate([act2[s] for s in range(4)], axis=1), dex[...], TN).reshape(4, 2, 64, 512)
    grad_e.start()
    scatter_mid(1, 1)
    s_af, r_af = new(), new()
    for dev in rest:
        copy(aff.at[r], aff.at[r], s_af, r_af, dev).start()
    over_x(1)

    def norm_back(d, xhat, rstd, gain, rows):
        sd = jnp.sum(d, axis=0, keepdims=True)
        sxx = jnp.sum(d * xhat, axis=0, keepdims=True)
        return (gain * rstd) * (d - sd / rows - xhat * (sxx / rows)), sd, sxx

    def weight_grad(q):
        full = jnp.concatenate([act1[s] for s in range(4)], axis=1)
        gs[q] = dot(full, pat[:, 384 * q : 384 * q + 384], TN).reshape(4, 2, 64, 384)
        grad_s[q].start()

    sum_d2, sum_x2 = [], []
    for kind in range(2):
        rows = KINDS[kind][1]
        d = scatter_end(1, kind) * slope2[kind_rows(kind), :]
        dz_, sd, sxx = norm_back(d, xhat2[kind_rows(kind), :], rstd2[kind], gain2, rows)
        sum_d2.append(sd)
        sum_x2.append(sxx)
        dz_ = dz_.astype(BF16).astype(F32)
        for tj in range(3):
            col = turned(dz_, kind, tj - 1)
            for ti in range(3):
                t = 3 * ti + tj
                pat[kind_rows(kind), 128 * t : 128 * t + 128] = moved(col, kind, ti - 1).astype(BF16)
        if kind == 1:
            weight_grad(0)
            both_mid(2, 0)
        scatter_start(2, kind, dot(pat[kind_rows(kind), :], weight_s(), NT))
    grad_e.along()
    weight_grad(1)
    weight_grad(2)
    both_mid(2, 1)
    over_x(2)
    over_x(3)
    line_got(share_o)
    between(we.at[xp[1]], 1)
    grad_s[0].along()
    grad_e.hand_on()
    grad_s[0].hand_on()

    sum_1 = [[0.0, 0.0], [0.0, 0.0]]
    for kind in range(2):
        rows = KINDS[kind][1]
        for xx in range(2):
            d = both_end(2, kind, xx) * slope1[xx, kind_rows(kind), :]
            dz_, sd, sxx = norm_back(d, xhat1[xx, kind_rows(kind), :], rstd1[kind][xx], gain1[xx], rows)
            sum_1[xx][0] += sxx
            sum_1[xx][1] += sd
            both_out(2, kind, xx, dred, dz_.astype(BF16))
        if kind == 0:
            grad_s[1].along()

    rows12 = [jnp.where(x == 0, sum_1[0][n], sum_1[1][n]) for n in range(2)]
    rows12 += [sum_x2[0] + sum_x2[1], sum_d2[0] + sum_d2[1]]
    gx3, gd3 = sum_x3[0] + sum_x3[1], sum_d3[0] + sum_d3[1]
    rows3 = [g[:, 128 * k : 128 * k + 128] for g in (gx3, gd3) for k in range(4)]
    pgr[i] = jnp.concatenate(rows12 + rows3 + [jnp.zeros((4, 128), F32)], axis=0)
    s_pp, r_pp, s_ps, r_ps = new(), new(), new(), new()
    for dev in peers[:7]:
        copy(pgr.at[i], pgr.at[i], s_pp, r_pp, dev).start()

    rows_pool[...] = jnp.zeros_like(rows_pool)
    for n in range(8):
        row = 4 * (n % 2) + n // 2
        rows_pool[row : row + 1, :] = jnp.sum(pool[n], axis=0, keepdims=True) / 64.0
        for m in range(2):
            row = 4 * (2 + 2 * (n % 2) + m) + n // 2
            rows_pool[row : row + 1, :] = jnp.sum(pool[8 + n, 4 * m : 4 * m + 4, :], axis=0, keepdims=True) / 16.0
    grad_s[1].hand_on()
    full_d = [gather_end(2, kind, dred) for kind in range(2)]

    for m in range(4):
        col = dot(xv[:, :, :, 128 * m : 128 * m + 128].reshape(NV, 128), full_d[0], TN)
        col = col + dot(xc[:, :, 128 * m : 128 * m + 128].reshape(NC, 128), full_d[1], TN)
        for q in range(2):
            gr[q, m] = col[:, 256 * q : 256 * q + 256]

    @pl.when(y != c)
    def _():
        for one in grad_r:
            one.start()

    for n, ref in enumerate((xo_v, xo_c, co_v, co_c)):
        stored(ref, l_own + n)
    got(aff.at[pl.ds(0, 3)], r_af)
    got(we.at[pl.ds(0, 2)], r_ow + 1)
    own_output()
    grad_s[2].along()
    slices_p.start(rows_pool[...])
    slices_s[0].start(grad_s[0].total())
    slices_e.start(grad_e.total())
    grad_s[2].hand_on()

    @pl.when(y == c)
    def _():
        grad_r[0].along()
        grad_r[1].along()

    slices_s[1].start(grad_s[1].total())
    slices_p.mid()
    slices_s[0].mid()
    slices_e.mid()
    got(wr.at[0], r_xw)
    between(wr.at[xp[1]], 0)

    got(pgr.at[pl.ds(0, 7)], r_pp)
    total = pgr[0]
    for n in range(1, 8):
        total = total + pgr[n]
    pgs[r] = total
    for dev in rest:
        copy(pgs.at[r], pgs.at[r], s_ps, r_ps, dev).start()
    slices_s[2].start(grad_s[2].total())
    slices_s[1].mid()
    got(wr.at[pl.ds(0, 2)], r_ow)
    own_gradient()

    s_fr, r_fr = new(2), new(2)
    for q in range(2):

        @pl.when(y == c)
        def _(q=q):
            fin_r[q, x] = grad_r[q].total().astype(BF16)
            for dev in rest:
                copy(fin_r.at[q, x], fin_r.at[q, x], s_fr + q, r_fr + q, dev).start()

    for one in (slices_p, slices_e, *slices_s):
        one.end()
    got(pgs.at[pl.ds(0, 3)], r_ps)
    sent(aff.at[pl.ds(0, 3)], s_af)
    sent(we, s_ow)
    sent(wr.at[0], s_xw)
    for s, (own_v, own_c) in enumerate(((xv, xc4), (cv, cc4))):
        sent(own_v.at[:, pl.ds(0, 3)], s_sx[s][0])
        sent(own_c.at[pl.ds(0, 3)], s_sx[s][1])
    sent(pg.at[pl.ds(0, 7)], s_pg)
    sent(pgr.at[pl.ds(0, 7)], s_pp)
    sent(pgs.at[pl.ds(0, 3)], s_ps)
    line_sent(share_s.send, ws, ws.at[:, pl.ds(0, 6)])
    for share in (share_e, share_o):
        sent(we.at[0, pl.ds(0, 4)], share.send)
        sent(we.at[0, pl.ds(0, 3)], share.passed)
    for op in range(3):
        sent(act1.at[pl.ds(0, 2)], s_cs + op)
        sent(act1.at[pl.ds(0, 1 if op == 1 else 2)], s_xs + op)
        sent(act1.at[pl.ds(0, 3 if op == 1 else 2)], s_ag + op)
    for one in (grad_e, *grad_s):
        sent(one.ysend, one.s_y)
        one.sent()

    @pl.when(y != c)
    def _():
        for q, one in enumerate(grad_r):
            sent(one.ysend, one.s_y)
            got(fin_r.at[q], r_fr + q)

    @pl.when(y == c)
    def _():
        sent(wr.at[0], share_r.send)
        sent(wr.at[0, pl.ds(0, 3)], share_r.passed)
        for q, one in enumerate(grad_r):
            one.sent()
            sent(one.zsend.at[pl.ds(0, 3)], s_fr + q)
            got(fin_r.at[q, 1 - x], r_fr + q)

    assert taken[0] == SEMAPHORES, taken


def store_kernel(
    out_v, out_c, pool, grad_v, grad_c, fin_e, fin_s, fin_r, sums,
    out_views, out_crops, pooled, grad_views, grad_crops, grad_reduce, grad_spatial, grad_expand,
    gain_a, shift_a, gain_b, shift_b, gain_c, shift_c,
    oc, pl_, gc, gr, gs, ge, sem,
):
    i = lax.axis_index("dp")
    z, y = i // 2, i % 2
    copies = []

    def store(src, dst):
        one = pltpu.make_async_copy(src, dst, sem.at[len(copies)])
        one.start()
        copies.append(one)

    store(out_v, out_views)
    store(grad_v, grad_views)
    for s in range(4):
        for t in range(9):
            gs[t, :, 128 * s : 128 * s + 128] = fin_s[t // 3, s, :, 128 * (t % 3) : 128 * (t % 3) + 128].astype(F32)
    store(gs, grad_spatial)
    for s in range(4):
        for k in range(4):
            lo = 512 * k + 256 * (s % 2) + 128 * (s // 2)
            ge[:, lo : lo + 128] = fin_e[s, :, 128 * k : 128 * k + 128].astype(F32)
    store(ge, grad_expand)
    for n in range(2):
        gr[:, 256 * n : 256 * n + 256] = fin_r[n].astype(F32).reshape(256, 256)
    store(gr, grad_reduce)
    oc[...] = out_c[...].reshape(16, 4, 2048)
    store(oc, out_crops)
    gc[...] = grad_c[...].reshape(16, 4, 2048)
    store(gc, grad_crops)
    for s in range(4):
        for k in range(4):
            lo = 512 * k + 256 * (s % 2) + 128 * (s // 2)
            pl_[:, :, lo : lo + 128] = pool[s, 0:24, 128 * k : 128 * k + 128].astype(F32).reshape(6, 4, 128)
    store(pl_, pooled)
    for n, out in enumerate((gain_a, shift_a, gain_b, shift_b)):
        row = sums[i // 2, n : n + 1, :]
        out[...] = jnp.where(i % 2 == 0, row[:, :64], row[:, 64:]).reshape(64)
    for n, out in enumerate((gain_c, shift_c)):
        out[...] = jnp.concatenate([sums[2 * m + y, pl.ds(4 + 4 * n + z, 1), :] for m in range(2)], axis=1).reshape(256)
    for one in copies:
        one.wait()


def fused(views, crops, w_reduce, w_spatial, w_expand, cot_views, cot_crops, *params):
    hbm, vmem = pl.BlockSpec(memory_space=pltpu.HBM), pl.BlockSpec(memory_space=pltpu.VMEM)

    def shape(dims, dtype):
        return jax.ShapeDtypeStruct(dims, dtype)

    def buf(dims, dtype=BF16):
        return pltpu.VMEM(dims, dtype)

    def dma(*dims):
        return pltpu.SemaphoreType.DMA(dims)

    held = pl.pallas_call(
        block_kernel,
        out_shape=[
            buf((8, 16, 2048)), buf((64, 2048)), buf((4, 32, 512)), buf((8, 16, 2048)), buf((64, 2048)),
            buf((4, 64, 512)), buf((3, 4, 64, 384)), buf((2, 2, 128, 256)), buf((4, 16, 128), F32),
        ],
        in_specs=[hbm] * 13,
        out_specs=[vmem] * 9,
        scratch_shapes=[
            buf((8, 4, 16, 512)), buf((4, 16, 4, 512)), buf((4, 64, 512)),
            buf((8, 4, 16, 512)), buf((4, 16, 4, 512)), buf((4, 64, 512)),
            buf((8, 16, 2048)), buf((16, 4, 2048)), buf((8, 16, 2048)), buf((16, 4, 2048)),
            buf((4, 4, 128, 512)), buf((9, 8, 64, 128)), buf((4, 8, 64, 512)), buf((4, 8, 512), F32), buf((64,)), buf((64,)), buf((64,)), buf((64,)), buf((256,)), buf((256,)), buf((8, 8, 128), F32),
            buf((3, 4, N, 128), F32), buf((3, 2, 2, NV, 128)), buf((3, 2, 2, NV, 128)),
            buf((3, 2, 2, NV, 128)), buf((3, 2, 2, NV, 128)),
            buf((4, N, 128)), buf((4, N, 128)), buf((4, N, 128)), buf((N, 1152), F32),
            buf((2, N, 128), F32), buf((2, N, 128), F32), buf((N, 128), F32), buf((N, 128), F32),
            buf((N, 512), F32), buf((N, 512), F32), buf((N, 512)), buf((N, 1152)),
            buf((192, 2048), F32), buf((16, 8, 512), F32), buf((32, 512), F32),
            buf((4, 2, 64, 512), F32), buf((3, 4, 2, 64, 384), F32), buf((2, 4, 128, 256), F32),
            buf((4, 64, 512)), buf((4, 64, 512)), buf((4, 64, 512)), buf((4, 64, 512)),
            buf((3, 4, 64, 384)), buf((3, 4, 64, 384)), buf((3, 4, 64, 384)), buf((3, 4, 64, 384)),
            buf((2, 4, 128, 256)), buf((2, 4, 128, 256)), buf((2, 4, 128, 256)), buf((2, 4, 128, 256)),
            buf((64, 512)), buf((3, 64, 384)), buf((64, 512), F32), buf((3, 64, 384), F32), buf((2, 128, 256), F32),
            buf((8, 16, 128), F32),
            dma(SEMAPHORES),
        ],
        compiler_params=pltpu.CompilerParams(collective_id=0, has_side_effects=True, vmem_limit_bytes=58 << 20),
        cost_estimate=pl.CostEstimate(flops=5_200_000_000, bytes_accessed=8_000_000, transcendentals=2_000_000),
    )(views, crops, w_reduce, w_spatial, w_expand, cot_views, cot_crops, *params)
    held = [pltpu.with_memory_space_constraint(one, pltpu.VMEM) for one in held]
    return pl.pallas_call(
        store_kernel,
        out_shape=[
            shape((8, 16, 2048), BF16), shape((16, 4, 2048), BF16), shape((6, 4, 2048), F32),
            shape((8, 16, 2048), BF16), shape((16, 4, 2048), BF16),
            shape((256, 512), F32), shape((9, 64, 512), F32), shape((64, 2048), F32),
            shape((64,), F32), shape((64,), F32), shape((64,), F32), shape((64,), F32), shape((256,), F32), shape((256,), F32),
        ],
        in_specs=[vmem] * 9,
        out_specs=[hbm] * 8 + [vmem] * 6,
        scratch_shapes=[
            buf((16, 4, 2048)), buf((6, 4, 2048), F32), buf((16, 4, 2048)),
            buf((256, 512), F32), buf((9, 64, 512), F32), buf((64, 2048), F32), dma(8),
        ],
        compiler_params=pltpu.CompilerParams(vmem_limit_bytes=16 << 20),
    )(*held)


def step(
    dp, rows, views, crops, w_reduce, gain_one, shift_one, w_spatial, gain_two, shift_two, w_expand, gain_three, shift_three,
    cot_views, cot_crops,
):
    args = (
        views, crops, w_reduce, gain_one, shift_one, w_spatial, gain_two, shift_two, w_expand, gain_three, shift_three,
        cot_views, cot_crops,
    )
    if (dp, rows) != (8, 4) or views.shape != (4, 2, 2, 8, 2048) or crops.shape != (4, 4, 1, 4, 2048):
        return body(*args)
    out_v, out_c, pooled, grad_v, grad_c, grad_r, grad_s, grad_e, ga, sa, gb, sb, gc, sc = fused(
        views.reshape(8, 16, 2048), crops.reshape(16, 4, 2048), w_reduce, w_spatial.reshape(9, 64, 512), w_expand,
        cot_views.reshape(8, 16, 2048), cot_crops.reshape(16, 4, 2048),
        gain_one, shift_one, gain_two, shift_two, gain_three, shift_three,
    )
    return (
        out_v.reshape(views.shape),
        out_c.reshape(crops.shape),
        jnp.transpose(pooled, (1, 0, 2)),
        grad_v.reshape(views.shape),
        grad_c.reshape(crops.shape),
        grad_r,
        ga,
        sa,
        grad_s.reshape(w_spatial.shape[:3] + (512,)),
        gb,
        sb,
        grad_e,
        gc,
        sc,
    )


def solution(mesh):
    return jax.shard_map(
        functools.partial(step, mesh.shape["dp"], mesh.shape["rows"]),
        mesh=mesh,
        in_specs=(
            P("dp", None, "rows", None, None),
            P("dp", None, "rows", None, None),
            P("dp", None),
            P("dp"),
            P("dp"),
            P(None, None, "dp", None),
            P("dp"),
            P("dp"),
            P("dp", None),
            P("dp"),
            P("dp"),
            P("dp", None, "rows", None, None),
            P("dp", None, "rows", None, None),
        ),
        out_specs=(
            P("dp", None, "rows", None, None),
            P("dp", None, "rows", None, None),
            P("dp", None, None),
            P("dp", None, "rows", None, None),
            P("dp", None, "rows", None, None),
            P("dp", None),
            P("dp"),
            P("dp"),
            P(None, None, "dp", None),
            P("dp"),
            P("dp"),
            P("dp", None),
            P("dp"),
            P("dp"),
        ),
        check_vma=False,
    )
```
